32 devices in a mesh: view: 4 (over z), gx: 4 (over y, x), gy: 2 (over core).
Axes of the slice: x: 2, y: 2, z: 4, core: 2. Of those that a mesh axis runs over, the one named last changes fastest.
Arguments:
- velocity: float32 [3, 128, 256, 512], P(None, 'gx', 'gy', 'view'), may hold values from -6 to 6
- occupied: int32 [16, 32, 4], P('gx', 'gy', 'view'), may hold values 0 or 1
- q_floor: float32 [1], replicated, may hold values from -1 to 0
- q_span: float32 [1], replicated, may hold values from 1 to 4
Outputs:
- image: float32 [4, 2, 4, 32, 128], P('gx', 'gy', None, 'view')
The draws below stay inside these ranges and needn't reach their ends.
All inputs are finite; a program needn't handle non-finite values. No bound on the sum of `occupied` on one device may be relied on, other than what follows from the above.
Results may differ from the reference program's by a relative error of at most 0.0003.
Values sent between devices are 32-bit elements; how exact they have to be, the bound alone decides.
No kernel may reach another device: no remote copies, remote signals or barrier semaphores. Data moves between devices by JAX's collectives and lax.ppermute only.
A program may use at most 128 MiB of HBM per device.

```python
import math
import jax
import jax.numpy as jnp
from jax import lax

BX = 32
BY = 128
BZ = 128
SUB = 8
NX = 128
NY = 256
NZ = 512
N_VIEW = 4
N_GX = 4
N_GY = 2


def touch_ends(result, key, smallest, high):
    spot = [jax.random.randint(jax.random.fold_in(key, axis), (), 0, length) for axis, length in enumerate(result.shape)]
    longest = result.shape.index(max(result.shape))
    beside = spot[:longest] + [(spot[longest] + 1) % result.shape[longest]] + spot[longest + 1:]
    return result.at[tuple(spot)].set(smallest).at[tuple(beside)].set(high)


def shard_levels(own_key, shape, split, low, top_value):
    def one(dim, parts):
        heights = jax.random.uniform(jax.random.fold_in(jax.random.fold_in(own_key, 6), dim), (parts,), jnp.float32, low / len(split), top_value / len(split))
        return jnp.repeat(jnp.exp(heights), shape[dim] // parts).reshape((-1,) + (1,) * (len(shape) - dim - 1))

    gain = one(*split[0])
    for cut in split[1:]:
        gain = gain * one(*cut)
    return gain


def scatter_about(key, extent, width, limit, cuts=(), kind=jnp.bfloat16):
    loudness = shard_levels(key, extent, cuts, -0.22, 0.18) if cuts else 1.0
    values = jax.random.normal(key, extent, jnp.float32) * width * loudness
    return jnp.minimum(jnp.maximum(values, -limit), limit).astype(kind)


def setup_inputs(seed: int = 0) -> dict:
    streams_of = jax.random.split(jax.random.key(seed), 5)
    velocity = scatter_about(streams_of[0], (3, NX, NY, NZ), 1.0, 6.0, ((1, 4), (2, 2), (3, 4)), jnp.float32)
    occupied = touch_ends((jax.random.randint(streams_of[1], (NX // SUB, NY // SUB, N_VIEW), 0, 4) < 3).astype(jnp.int32), jax.random.fold_in(streams_of[1], 1), 0, 1)
    q_floor = jnp.clip(jax.random.uniform(streams_of[2], (1,), jnp.float32, -1.0, 0.0), -1.0, 0.0)
    q_span = jnp.clip(jnp.exp(jax.random.uniform(streams_of[3], (1,), jnp.float32, math.log(1.0), math.log(4.0))), 1.0, 4.0)
    return dict(velocity=velocity, occupied=occupied, q_floor=q_floor, q_span=q_span)


slab_rows = 8


def derivative(padded_field, direction):
    length_inner = padded_field.shape[direction] - 4

    def shifted(offset):
        return lax.slice_in_dim(padded_field, offset, offset + length_inner, axis=direction)

    return (shifted(0) - 8.0 * shifted(1) + 8.0 * shifted(3) - shifted(4)) / 12.0


def criterion(padded_sets):
    gradient = [[derivative(padded_sets[column][component], column) for column in range(3)] for component in range(3)]
    diagonal_part = gradient[0][0] * gradient[0][0] + gradient[1][1] * gradient[1][1] + gradient[2][2] * gradient[2][2]
    cross_part = gradient[0][1] * gradient[1][0] + gradient[0][2] * gradient[2][0] + gradient[1][2] * gradient[2][1]
    return -0.5 * diagonal_part - cross_part


def reference(velocity, occupied, q_floor, q_span):
    density = 5.0 / NZ
    row_total = velocity.shape[1]

    def one_slab(slab_index):
        first_row = slab_index * slab_rows
        row_index = (first_row - 2 + jnp.arange(slab_rows + 4, dtype=jnp.int32)) % row_total
        slab_cells = jnp.take(velocity, row_index, axis=1)
        middle = slab_cells[:, 2:-2]
        pad_down = jnp.pad(middle, ((0, 0), (0, 0), (2, 2), (0, 0)), mode="wrap")
        pad_depth = jnp.pad(middle, ((0, 0), (0, 0), (0, 0), (2, 2)), mode="wrap")
        qvalue = criterion((slab_cells, pad_down, pad_depth))
        mask_rows = (first_row + jnp.arange(slab_rows, dtype=jnp.int32)) // SUB
        occupancy = jnp.take(occupied, mask_rows, axis=0)
        occupancy = jnp.repeat(jnp.repeat(occupancy, SUB, axis=1), BZ, axis=2).astype(jnp.float32)
        shade_level = jnp.clip((qvalue - q_floor[0]) / q_span[0], 0.0, 1.0) * occupancy
        optical = density * shade_level
        coverage = 1.0 - jnp.exp(-optical)
        passing = jnp.exp(-(jnp.cumsum(optical, axis=-1) - optical))
        weight = passing * coverage
        red = jnp.sum(weight * shade_level, axis=-1)
        green = jnp.sum(weight * 4.0 * shade_level * (1.0 - shade_level), axis=-1)
        blue = jnp.sum(weight * (1.0 - shade_level), axis=-1)
        opacity = 1.0 - jnp.exp(-jnp.sum(optical, axis=-1))
        return jnp.stack([red, green, blue, opacity], axis=0)

    slabs = lax.map(one_slab, jnp.arange(NX // slab_rows, dtype=jnp.int32))
    whole = jnp.moveaxis(slabs, 1, 0).reshape(4, NX, NY)
    return whole.reshape(4, N_GX, BX, N_GY, BY).transpose(1, 3, 0, 2, 4)
```

```python
import functools

import jax
import jax.numpy as jnp
from jax import lax
from jax.experimental import pallas as pl
from jax.experimental.pallas import tpu as pltpu
from jax.sharding import PartitionSpec as P

SUB = 8
PAD = 8
ROWS = 32


def faces_kernel(u_hbm, yface_ref, zface_ref, u_ref, turned_ref, sems):
    comps, nx, ny, nz = u_ref.shape
    copies = [pltpu.make_async_copy(u_hbm.at[c], u_ref.at[c], sems.at[c]) for c in range(comps)]
    for copy in copies:
        copy.start()
    lane = lax.broadcasted_iota(jnp.int32, (8, nz), 1)
    for c in range(comps):
        copies[c].wait()
        for x in range(nx):
            yface_ref[0, c, pl.ds(2 * x, 2), :] = u_ref[c, x, pl.ds(ny - 2, 2), :]
            yface_ref[1, c, pl.ds(2 * x, 2), :] = u_ref[c, x, pl.ds(0, 2), :]

        def gather(group, carry):
            rows = pl.ds(pl.multiple_of(group * 8, 8), 8)
            packed = jnp.zeros((8, nz), jnp.float32)
            for x in range(nx):
                moved = pltpu.roll(u_ref[c, x, rows, :], (4 * x + 2) % nz, 1)
                packed = jnp.where((lane >= 4 * x) & (lane < 4 * x + 4), moved, packed)
            turned_ref[rows, :] = packed
            return carry

        lax.fori_loop(0, ny // 8, gather, 0)
        turned_ref[...] = turned_ref[...].T
        for layer in range(4):
            zface_ref[layer // 2, c, layer % 2] = turned_ref[pl.ds(layer, nx, stride=4), :]


def faces(u):
    comps, nx, ny, nz = u.shape
    return pl.pallas_call(
        faces_kernel,
        out_shape=(
            jax.ShapeDtypeStruct((2, comps, 2 * nx, nz), jnp.float32),
            jax.ShapeDtypeStruct((2, comps, 2, nx, ny), jnp.float32),
        ),
        in_specs=[pl.BlockSpec(memory_space=pl.ANY)],
        out_specs=(pl.BlockSpec(memory_space=pltpu.VMEM), pl.BlockSpec(memory_space=pltpu.VMEM)),
        scratch_shapes=[
            pltpu.VMEM(u.shape, jnp.float32),
            pltpu.VMEM((ny, nz), jnp.float32),
            pltpu.SemaphoreType.DMA((comps,)),
        ],
        compiler_params=pltpu.CompilerParams(vmem_limit_bytes=32 << 20),
        cost_estimate=pl.CostEstimate(flops=4 * u.size, bytes_accessed=4 * u.size, transcendentals=0),
    )(u)


def border_corrections(own_ref, left_ref, right_ref, corr_ref):
    comps, _, nx, ny = left_ref.shape
    for c in range(comps):
        right0 = right_ref[c, 0] - own_ref[1, c, 0]
        right1 = right_ref[c, 1] - own_ref[1, c, 1]
        left0 = left_ref[c, 0] - own_ref[0, c, 0]
        left1 = left_ref[c, 1] - own_ref[0, c, 1]
        corr_ref[c, pl.ds(0, nx, stride=4), :] = -right0
        corr_ref[c, pl.ds(1, nx, stride=4), :] = 8.0 * right0 - right1
        corr_ref[c, pl.ds(2, nx, stride=4), :] = left0 - 8.0 * left1
        corr_ref[c, pl.ds(3, nx, stride=4), :] = left1
        corr_ref[c] = corr_ref[c].T


def shade_row(pad_ref, slot, x, corr_ref, scale_ref, offset_ref, level_ref):
    comps, _, padded, nz = pad_ref.shape
    ny = padded - 2 * PAD
    lane = lax.broadcasted_iota(jnp.int32, (ROWS, nz), 1)
    border = (lane >= nz - 2) | (lane < 2)
    shift = lax.rem(2 * nz - 2 - 4 * x, nz)
    for y in range(0, ny, ROWS):
        across, down, depth = [], [], []
        for c in range(comps):
            def at(dx, dy):
                return pad_ref[c, slot + dx, pl.ds(PAD + y + dy, ROWS), :]

            across.append(8.0 * (at(1, 0) - at(-1, 0)) - (at(2, 0) - at(-2, 0)))
            down.append(8.0 * (at(0, 1) - at(0, -1)) - (at(0, 2) - at(0, -2)))
            here = at(0, 0)
            step = here - pltpu.roll(here, 2, 1)
            wrapped = 8.0 * pltpu.roll(step, nz - 1, 1) - pltpu.roll(step, nz - 2, 1) - step
            fix = pltpu.roll(corr_ref[c, pl.ds(y, ROWS), :], shift, 1)
            depth.append(wrapped + jnp.where(border, fix, 0.0))
        total = 0.5 * (across[0] * across[0] + down[1] * down[1] + depth[2] * depth[2])
        total = total + across[1] * down[0] + across[2] * depth[0] + down[2] * depth[1]
        block = x // SUB
        level = total * scale_ref[block, pl.ds(y, ROWS), :] + offset_ref[block, pl.ds(y, ROWS), :]
        level_ref[pl.ds(y, ROWS), :] = jnp.clip(level, 0.0, 1.0)


def blend_row(density, level_ref, store):
    ny, nz = level_ref.shape
    row = lax.broadcasted_iota(jnp.int32, (2 * nz, nz), 0)
    col = lax.broadcasted_iota(jnp.int32, (2 * nz, nz), 1)
    before = jnp.where((row < col) | ((row >= nz) & (row < col + nz)), -1.0, 0.0).astype(jnp.bfloat16)
    level = level_ref[...]
    optical = density * level
    high = optical.astype(jnp.bfloat16)
    low = (optical - high.astype(jnp.float32)).astype(jnp.bfloat16)
    parts = jnp.concatenate([high, low], axis=1)
    passing = jnp.exp(jnp.dot(parts, before, preferred_element_type=jnp.float32))
    weight = passing * (1.0 - jnp.exp(-optical))
    first = weight * level
    second = first * level
    lane_group = lax.broadcasted_iota(jnp.int32, (8, ny), 1) // 8
    eye = lax.broadcasted_iota(jnp.int32, (8, ny), 1) % 8 == lax.broadcasted_iota(jnp.int32, (8, ny), 0)

    def lanes(cells):
        total = jnp.zeros((8, ny), jnp.float32)
        for group in range(ny // 8):
            part = jnp.sum(cells[8 * group : 8 * group + 8], axis=1, keepdims=True)
            total = jnp.where(lane_group == group, part, total)
        return jnp.sum(jnp.where(eye, total, 0.0), axis=0, keepdims=True)

    red = lanes(first)
    square = lanes(second)
    through = jnp.exp(-density * lanes(level))
    store(jnp.concatenate([red, 4.0 * (red - square), 1.0 - through - red, through], axis=0))


def inner_kernel(
    density, u_hbm, yleft_ref, yright_ref, zown_ref, zleft_ref, zright_ref, scale_ref, offset_ref,
    image_ref, pad_ref, corr_ref, level0_ref, level1_ref, sems,
):
    comps, nx, padded, nz = pad_ref.shape
    ny = padded - 2 * PAD
    chunks = sems.shape[1]
    size = nx // chunks
    copies = [
        [
            pltpu.make_async_copy(
                u_hbm.at[c, pl.ds(k * size, size)],
                pad_ref.at[c, pl.ds(k * size, size), pl.ds(PAD, ny)],
                sems.at[c, k],
            )
            for c in range(comps)
        ]
        for k in range(chunks)
    ]
    for chunk in copies:
        for copy in chunk:
            copy.start()
    for c in range(comps):
        for x in range(nx):
            pad_ref[c, x, pl.ds(PAD - 2, 2), :] = yleft_ref[c, pl.ds(2 * x, 2), :]
            pad_ref[c, x, pl.ds(PAD + ny, 2), :] = yright_ref[c, pl.ds(2 * x, 2), :]
    border_corrections(zown_ref, zleft_ref, zright_ref, corr_ref)
    for chunk in copies:
        for copy in chunk:
            copy.wait()
    image_ref[...] = jnp.zeros(image_ref.shape, jnp.float32)

    def store(x):
        def put(values):
            for k in range(4):
                image_ref[k, pl.ds(x, 1), :] = values[k : k + 1]

        return put

    def pair(i, carry):
        x = 2 * i + 2
        shade_row(pad_ref, x, x, corr_ref, scale_ref, offset_ref, level0_ref)
        blend_row(density, level0_ref, store(x))
        shade_row(pad_ref, x + 1, x + 1, corr_ref, scale_ref, offset_ref, level1_ref)
        blend_row(density, level1_ref, store(x + 1))
        return carry

    lax.fori_loop(0, (nx - 4) // 2, pair, 0)


def inner(density, u, yleft, yright, zown, zleft, zright, scale, offset):
    comps, nx, ny, nz = u.shape
    chunks = 4
    vmem = pl.BlockSpec(memory_space=pltpu.VMEM)
    return pl.pallas_call(
        functools.partial(inner_kernel, density),
        out_shape=jax.ShapeDtypeStruct((4, nx, ny), jnp.float32),
        in_specs=[pl.BlockSpec(memory_space=pl.ANY)] + [vmem] * 7,
        out_specs=vmem,
        scratch_shapes=[
            pltpu.VMEM((comps, nx, ny + 2 * PAD, nz), jnp.float32),
            pltpu.VMEM((comps, 4 * nx, ny), jnp.float32),
            pltpu.VMEM((ny, nz), jnp.float32),
            pltpu.VMEM((ny, nz), jnp.float32),
            pltpu.SemaphoreType.DMA((comps, chunks)),
        ],
        compiler_params=pltpu.CompilerParams(vmem_limit_bytes=32 << 20),
        cost_estimate=pl.CostEstimate(flops=100 * u.size, bytes_accessed=4 * u.size, transcendentals=2 * u.size),
    )(u, yleft, yright, zown, zleft, zright, scale, offset)


def edge_kernel(
    density, u_hbm, xleft_hbm, xright_hbm, yleft_ref, yright_ref, zown_ref, zleft_ref, zright_ref, scale_ref, offset_ref,
    image_ref, pad_ref, corr_ref, level0_ref, level1_ref, sems,
):
    comps, _, padded, nz = pad_ref.shape
    ny = padded - 2 * PAD
    nx = zown_ref.shape[3]
    parts = (
        (u_hbm, 0, 4, 2),
        (u_hbm, nx - 4, 4, 6),
        (xleft_hbm, 0, 2, 0),
        (xright_hbm, 0, 2, 10),
    )
    copies = [
        pltpu.make_async_copy(
            source.at[c, pl.ds(start, count)], pad_ref.at[c, pl.ds(slot, count), pl.ds(PAD, ny)], sems.at[c, k]
        )
        for k, (source, start, count, slot) in enumerate(parts)
        for c in range(comps)
    ]
    for copy in copies:
        copy.start()
    places = ((2, 0), (3, 1), (8, nx - 2), (9, nx - 1))
    for c in range(comps):
        for slot, x in places:
            pad_ref[c, slot, pl.ds(PAD - 2, 2), :] = yleft_ref[c, pl.ds(2 * x, 2), :]
            pad_ref[c, slot, pl.ds(PAD + ny, 2), :] = yright_ref[c, pl.ds(2 * x, 2), :]
    border_corrections(zown_ref, zleft_ref, zright_ref, corr_ref)
    for copy in copies:
        copy.wait()

    def store(place):
        def put(values):
            for k in range(4):
                image_ref[k, place : place + 1, :] = values[k : k + 1]

        return put

    for place, (slot, x) in enumerate(places):
        level_ref = (level0_ref, level1_ref)[place % 2]
        shade_row(pad_ref, slot, x, corr_ref, scale_ref, offset_ref, level_ref)
        blend_row(density, level_ref, store(place))


def edge(density, u, xleft, xright, yleft, yright, zown, zleft, zright, scale, offset):
    comps, nx, ny, nz = u.shape
    vmem = pl.BlockSpec(memory_space=pltpu.VMEM)
    hbm = pl.BlockSpec(memory_space=pl.ANY)
    return pl.pallas_call(
        functools.partial(edge_kernel, density),
        out_shape=jax.ShapeDtypeStruct((4, 4, ny), jnp.float32),
        in_specs=[hbm] * 3 + [vmem] * 7,
        out_specs=vmem,
        scratch_shapes=[
            pltpu.VMEM((comps, 12, ny + 2 * PAD, nz), jnp.float32),
            pltpu.VMEM((comps, 4 * nx, ny), jnp.float32),
            pltpu.VMEM((ny, nz), jnp.float32),
            pltpu.VMEM((ny, nz), jnp.float32),
            pltpu.SemaphoreType.DMA((comps, 4)),
        ],
        compiler_params=pltpu.CompilerParams(vmem_limit_bytes=32 << 20),
        cost_estimate=pl.CostEstimate(flops=12 * u.size, bytes_accessed=2 * u.size, transcendentals=u.size // 4),
    )(u, xleft, xright, yleft, yright, zown, zleft, zright, scale, offset)


def turn(block, axis, by):
    count = lax.axis_size(axis)
    return lax.ppermute(block, axis, [(i, (i + by) % count) for i in range(count)])


def both_sides(tail_head, axis):
    if lax.axis_size(axis) == 2:
        other = turn(tail_head, axis, 1)
        return other[0], other[1]
    return turn(tail_head[0], axis, 1), turn(tail_head[1], axis, -1)


def local(velocity, occupied, q_floor, q_span):
    comps, nx, ny, nz = velocity.shape
    views = lax.axis_size("view")
    density = 5.0 / (nz * views)
    xleft = turn(velocity[:, nx - 2 :], "gx", 1)
    xright = turn(velocity[:, :2], "gx", -1)
    yface, zface = faces(velocity)
    yleft, yright = both_sides(yface, "gy")
    zleft = turn(zface[0], "view", 1)
    zright = turn(zface[1], "view", -1)
    zown = zface
    mask = jnp.repeat(occupied[:, :, 0].astype(jnp.float32), SUB, axis=1)
    spread = (nx // SUB, ny, nz)
    scale = jnp.broadcast_to((mask * (-1.0 / 144.0 / q_span[0]))[:, :, None], spread)
    offset = jnp.broadcast_to((mask * (-q_floor[0] / q_span[0]))[:, :, None], spread)
    middle = inner(density, velocity, yleft, yright, zown, zleft, zright, scale, offset)
    border = edge(density, velocity, xleft, xright, yleft, yright, zown, zleft, zright, scale, offset)
    partial_image = jnp.concatenate([border[:, :2], middle[:, 2:-2], border[:, 2:]], axis=1)
    rows = nx // views
    blocks = partial_image.reshape(4, views, rows, ny)
    me = lax.axis_index("view")
    sources, images = [me], [lax.dynamic_index_in_dim(blocks, me, 1, keepdims=False)]
    for by in range(1, views):
        sent = lax.dynamic_index_in_dim(blocks, (me + by) % views, 1, keepdims=False)
        images.append(turn(sent, "view", by))
        sources.append((me - by) % views)
    colour = jnp.zeros((3, rows, ny), jnp.float32)
    through = jnp.ones((rows, ny), jnp.float32)
    for source, image in zip(sources, images):
        passing = jnp.ones((rows, ny), jnp.float32)
        for other, behind in zip(sources, images):
            passing = passing * jnp.where(other < source, behind[3], 1.0)
        colour = colour + passing * image[:3]
        through = through * image[3]
    finished = jnp.concatenate([colour, 1.0 - through[None]], axis=0)
    return finished.reshape(1, 1, 4, rows, ny)


def solution(mesh):
    placed = (P(None, "gx", "gy", "view"), P("gx", "gy", "view"), P(), P())
    return jax.shard_map(
        local,
        mesh=mesh,
        in_specs=placed,
        out_specs=P("gx", "gy", None, "view", None),
        check_vma=False,
    )
```

```python
import functools
import math

import jax
import jax.numpy as jnp
from jax import lax
from jax.experimental import pallas as pl
from jax.experimental.pallas import tpu as pltpu
from jax.sharding import PartitionSpec as P

SUB = 8
ROWS = 32
VMEM = pl.BlockSpec(memory_space=pltpu.VMEM)
HBM = pl.BlockSpec(memory_space=pl.ANY)
PARAMS = pltpu.CompilerParams(vmem_limit_bytes=32 << 20)


def split(values):
    high = values.astype(jnp.bfloat16)
    low = (values - high.astype(jnp.float32)).astype(jnp.bfloat16)
    return high, low


def iota(shape, dim):
    return lax.broadcasted_iota(jnp.int32, shape, dim)


def faces_kernel(u_hbm, u_ref, yface_ref, tail_ref, head_ref, sems):
    comps, nx, ny, nz = u_ref.shape
    quarters = sems.shape[1]
    rows = ny // quarters

    def fetch(c, k):
        span = pl.ds(k * rows if isinstance(k, int) else pl.multiple_of(k * rows, rows), rows)
        return pltpu.make_async_copy(u_hbm.at[c, :, span], u_ref.at[c, :, span], sems.at[c, k])

    for k in range(quarters):
        for c in (0, 1):
            fetch(c, k).start()
    for k in range(quarters):
        fetch(2, k).start()
    pair = iota((8, nz), 1) // 2

    def pack(members, y, out, first):
        out_rows = pl.ds(out, 8)
        tail = jnp.zeros((8, nz), jnp.float32)
        head = jnp.zeros((8, nz), jnp.float32)
        for c, base in members:
            for x in range(nx):
                place = base // 2 + x
                moved = pltpu.roll(u_ref[c, x, pl.ds(y, 8), :], (base + 2 * x + 2) % nz, 1)
                tail = jnp.where(pair == place, moved, tail)
                head = jnp.where(pair == (place + 1) % (nz // 2), moved, head)
        head = pltpu.roll(head, nz - 2, 1)
        if first:
            tail_ref[out_rows, :] = tail
            head_ref[out_rows, :] = head
        else:
            half = pair < nz // 4
            tail_ref[out_rows, :] = jnp.where(half, tail_ref[out_rows, :], tail)
            head_ref[out_rows, :] = jnp.where(half, head_ref[out_rows, :], head)

    def both(k, carry):
        fetch(0, k).wait()
        fetch(1, k).wait()
        for part in range(rows // 8):
            y = pl.multiple_of(k * rows + part * 8, 8)
            pack(((0, 0), (1, nz // 2)), y, y, True)
        return carry

    lax.fori_loop(0, quarters, both, 0)

    def last(base, offset, first):
        def step(k, carry):
            fetch(2, k).wait()
            for part in range(rows // 8):
                y = pl.multiple_of(k * rows + part * 8, 8)
                pack(((2, base),), y, pl.multiple_of(y + offset, 8), first)
            return carry

        return step

    lax.fori_loop(0, quarters // 2, last(0, ny, True), 0)
    lax.fori_loop(quarters // 2, quarters, last(nz // 2, ny // 2, False), 0)
    for c in range(comps):
        for x in range(nx):
            end = u_ref[c, x, pl.ds(ny - 8, 8), :]
            start = u_ref[c, x, pl.ds(0, 8), :]
            yface_ref[0, c, pl.ds(2 * x, 2), :] = jnp.concatenate([end[6:7] - 8.0 * end[7:8], end[7:8]], axis=0)
            yface_ref[1, c, pl.ds(2 * x, 2), :] = jnp.concatenate([-start[0:1], 8.0 * start[0:1] - start[1:2]], axis=0)


def faces(u):
    comps, nx, ny, nz = u.shape
    packed = jax.ShapeDtypeStruct((ny + ny // 2, nz), jnp.float32)
    return pl.pallas_call(
        faces_kernel,
        out_shape=(
            jax.ShapeDtypeStruct(u.shape, jnp.float32),
            jax.ShapeDtypeStruct((2, comps, 2 * nx, nz), jnp.float32),
            packed,
            packed,
        ),
        in_specs=[HBM],
        out_specs=(VMEM,) * 4,
        scratch_shapes=[pltpu.SemaphoreType.DMA((comps, 4))],
        compiler_params=pltpu.CompilerParams(vmem_limit_bytes=52 << 20),
        cost_estimate=pl.CostEstimate(flops=4 * u.size, bytes_accessed=4 * u.size, transcendentals=0),
    )(u)


def stencil(far):
    one = jnp.where(far == 1, 8.0, 0.0) - jnp.where(far == -1, 8.0, 0.0)
    return (one - jnp.where(far == 2, 1.0, 0.0) + jnp.where(far == -2, 1.0, 0.0)).astype(jnp.bfloat16)


def prepare(u_shape, yleft_ref, yright_ref, zleft_ref, zright_ref, top_ref, low_ref, fix_ref, dz_ref, dy_ref, sum_ref):
    comps, nx, ny, nz = u_shape
    dz_ref[...] = stencil(iota((2 * nz, nz), 0) % nz - iota((2 * nz, nz), 1))
    dy_ref[...] = stencil(iota((ny, 2 * ny), 1) % ny - iota((ny, 2 * ny), 0))
    row = iota((2 * nz, 2 * nz), 0) % nz
    col = iota((2 * nz, 2 * nz), 1)
    sum_ref[...] = jnp.where((row < col) & (col < nz) | (row <= col - nz), -1.0, 0.0).astype(jnp.bfloat16)
    source, target = iota((2 * nz, nz), 0) % nz, iota((2 * nz, nz), 1)
    side, place, layer = source // (2 * nx), source % (2 * nx) // 2, source % 2
    where = jnp.where(place == target // 4, 4 * side + 2 * layer, -1000) + 10 * (target % 4)
    weights = jnp.zeros((2 * nz, nz), jnp.float32)
    for value, (s, l, t) in (
        (1.0, (0, 0, 2)),
        (-8.0, (0, 1, 2)),
        (1.0, (0, 1, 3)),
        (-1.0, (1, 0, 0)),
        (8.0, (1, 0, 1)),
        (-1.0, (1, 1, 1)),
    ):
        weights = jnp.where(where == 4 * s + 2 * l + 10 * t, value, weights)
    weights = weights.astype(jnp.bfloat16)
    first = iota((ny, nz), 1) < nz // 2
    left, right = zleft_ref[:ny], zright_ref[:ny]
    left2, right2 = zleft_ref[ny:], zright_ref[ny:]
    turned_left2, turned_right2 = pltpu.roll(left2, nz // 2, 1), pltpu.roll(right2, nz // 2, 1)
    ghosts = (
        jnp.where(first, left, pltpu.roll(right, nz // 2, 1)),
        jnp.where(first, pltpu.roll(left, nz // 2, 1), right),
        jnp.where(
            first,
            jnp.concatenate([left2, turned_left2], axis=0),
            jnp.concatenate([turned_right2, right2], axis=0),
        ),
    )
    for c in range(comps):
        parts = jnp.concatenate(split(ghosts[c]), axis=1)
        fix_ref[c] = jnp.dot(parts, weights, preferred_element_type=jnp.float32)
    sub = iota((8, nz), 0)
    for c in range(comps):
        for group in range(nx // 4):
            left8 = yleft_ref[c, pl.ds(8 * group, 8), :]
            right8 = yright_ref[c, pl.ds(8 * group, 8), :]
            for k in range(4):
                top = left8 if k == 0 else pltpu.roll(left8, 8 - 2 * k, 0)
                low = right8 if k == 3 else pltpu.roll(right8, 6 - 2 * k, 0)
                top_ref[c, 4 * group + k] = jnp.where(sub < 2, top, 0.0)
                low_ref[c, 4 * group + k] = jnp.where(sub >= 6, low, 0.0)


def slopes(slab, x, refs, slope_ref):
    top_ref, low_ref, fix_ref, dz_ref, dy_ref = refs
    comps, ny, nz = slope_ref.shape[1:]
    lane = iota((ny, nz), 1)
    border = (lane >= nz - 2) | (lane < 2)
    shift = (2 * nz - 2 - 4 * x) % nz if isinstance(x, int) else lax.rem(2 * nz - 2 - 4 * x, nz)
    for c in range(comps):
        high, low = split(slab(c))
        depth = jnp.dot(jnp.concatenate([high, low], axis=1), dz_ref[...], preferred_element_type=jnp.float32)
        fix = pltpu.roll(fix_ref[c], shift, 1)
        slope_ref[1, c] = depth + jnp.where(border, fix, 0.0)
        down = jnp.dot(dy_ref[...], jnp.concatenate([high, low], axis=0), preferred_element_type=jnp.float32)
        slope_ref[0, c, pl.ds(0, 8), :] = down[:8] + top_ref[c, x]
        slope_ref[0, c, pl.ds(8, ny - 16), :] = down[8 : ny - 8]
        slope_ref[0, c, pl.ds(ny - 8, 8), :] = down[ny - 8 :] + low_ref[c, x]


def shade(near, x, slope_ref, scale_ref, offset_ref, level_ref):
    comps, ny, nz = slope_ref.shape[1:]
    block = x // SUB
    for y in range(0, ny, ROWS):
        rows = pl.ds(y, ROWS)
        across = [
            8.0 * (near(c, 1, rows) - near(c, -1, rows)) - (near(c, 2, rows) - near(c, -2, rows)) for c in range(comps)
        ]
        down = [slope_ref[0, c, rows, :] for c in range(comps)]
        depth = [slope_ref[1, c, rows, :] for c in range(comps)]
        total = 0.5 * (across[0] * across[0] + down[1] * down[1] + depth[2] * depth[2])
        total = total + across[1] * down[0] + across[2] * depth[0] + down[2] * depth[1]
        level = total * scale_ref[block, rows, :] + offset_ref[block, rows, :]
        level_ref[rows, :] = jnp.clip(level, 0.0, 1.0)


def blend(density, level_ref, sum_ref, store):
    ny, nz = level_ref.shape
    level = level_ref[...]
    binary = density / math.log(2.0)
    parts = jnp.concatenate(split(binary * level), axis=1)
    sums = jnp.dot(parts, sum_ref[...], preferred_element_type=jnp.float32)
    first = (jnp.exp2(sums[:, :nz]) - jnp.exp2(sums[:, nz:])) * level
    second = first * level
    lane_group = iota((8, ny), 1) // 8
    eye = iota((8, ny), 1) % 8 == iota((8, ny), 0)

    def lanes(cells):
        total = jnp.zeros((8, ny), jnp.float32)
        for group in range(ny // 8):
            part = jnp.sum(cells[8 * group : 8 * group + 8], axis=1, keepdims=True)
            total = jnp.where(lane_group == group, part, total)
        return jnp.sum(jnp.where(eye, total, 0.0), axis=0, keepdims=True)

    red = lanes(first)
    square = lanes(second)
    through = jnp.exp2(-binary * lanes(level))
    store(red, 4.0 * (red - square), 1.0 - through - red, through)


def put(image_ref, row):
    def store(*channels):
        for k, values in enumerate(channels):
            image_ref[k, pl.ds(row, 1), :] = values

    return store


def inner_kernel(
    density, u_ref, yleft_ref, yright_ref, zleft_ref, zright_ref, scale_ref, offset_ref,
    image_ref, top_ref, low_ref, fix_ref, dz_ref, dy_ref, sum_ref, slope0_ref, slope1_ref, level0_ref, level1_ref,
):
    comps, nx, ny, nz = u_ref.shape
    prepare(u_ref.shape, yleft_ref, yright_ref, zleft_ref, zright_ref, top_ref, low_ref, fix_ref, dz_ref, dy_ref, sum_ref)
    refs = (top_ref, low_ref, fix_ref, dz_ref, dy_ref)
    level1_ref[...] = jnp.zeros(level1_ref.shape, jnp.float32)

    def slab(x):
        return lambda c: u_ref[c, x]

    def near(x):
        return lambda c, d, rows: u_ref[c, x + d, rows, :]

    slopes(slab(2), 2, refs, slope0_ref)

    def pair(i, carry):
        x = 2 * i + 2
        slopes(slab(x + 1), x + 1, refs, slope1_ref)
        shade(near(x), x, slope0_ref, scale_ref, offset_ref, level0_ref)
        blend(density, level1_ref, sum_ref, put(image_ref, x - 1))
        slopes(slab(x + 2), x + 2, refs, slope0_ref)
        shade(near(x + 1), x + 1, slope1_ref, scale_ref, offset_ref, level1_ref)
        blend(density, level0_ref, sum_ref, put(image_ref, x))
        return carry

    lax.fori_loop(0, (nx - 4) // 2, pair, 0)
    blend(density, level1_ref, sum_ref, put(image_ref, nx - 3))


def tables(u):
    comps, nx, ny, nz = u.shape
    return [
        pltpu.VMEM((comps, nx, 8, nz), jnp.float32),
        pltpu.VMEM((comps, nx, 8, nz), jnp.float32),
        pltpu.VMEM((comps, ny, nz), jnp.float32),
        pltpu.VMEM((2 * nz, nz), jnp.bfloat16),
        pltpu.VMEM((ny, 2 * ny), jnp.bfloat16),
        pltpu.VMEM((2 * nz, 2 * nz), jnp.bfloat16),
        pltpu.VMEM((2, comps, ny, nz), jnp.float32),
        pltpu.VMEM((2, comps, ny, nz), jnp.float32),
        pltpu.VMEM((ny, nz), jnp.float32),
        pltpu.VMEM((ny, nz), jnp.float32),
    ]


def inner(density, u, *rest):
    comps, nx, ny, nz = u.shape
    return pl.pallas_call(
        functools.partial(inner_kernel, density),
        out_shape=jax.ShapeDtypeStruct((4, nx, ny), jnp.float32),
        in_specs=[VMEM] * 7,
        out_specs=VMEM,
        scratch_shapes=tables(u),
        compiler_params=PARAMS,
        cost_estimate=pl.CostEstimate(flops=100 * u.size, bytes_accessed=4 * u.size, transcendentals=2 * u.size),
    )(u, *rest)


def edge_kernel(
    density, u_ref, xleft_ref, xright_ref, yleft_ref, yright_ref, zleft_ref, zright_ref, scale_ref, offset_ref,
    image_ref, top_ref, low_ref, fix_ref, dz_ref, dy_ref, sum_ref, slope0_ref, slope1_ref, level0_ref, level1_ref,
):
    comps, nx, ny, nz = u_ref.shape
    prepare(u_ref.shape, yleft_ref, yright_ref, zleft_ref, zright_ref, top_ref, low_ref, fix_ref, dz_ref, dy_ref, sum_ref)
    refs = (top_ref, low_ref, fix_ref, dz_ref, dy_ref)

    def near(x):
        def read(c, d, rows):
            if x + d < 0:
                return xleft_ref[c, x + d + 2, rows, :]
            if x + d >= nx:
                return xright_ref[c, x + d - nx, rows, :]
            return u_ref[c, x + d, rows, :]

        return read

    def slab(x):
        return lambda c: u_ref[c, x]

    for place, x in enumerate((0, 1, nx - 2, nx - 1)):
        slope_ref = (slope0_ref, slope1_ref)[place % 2]
        level_ref = (level0_ref, level1_ref)[place % 2]
        slopes(slab(x), x, refs, slope_ref)
        shade(near(x), x, slope_ref, scale_ref, offset_ref, level_ref)
        blend(density, level_ref, sum_ref, put(image_ref, place))


def edge(density, u, *rest):
    comps, nx, ny, nz = u.shape
    return pl.pallas_call(
        functools.partial(edge_kernel, density),
        out_shape=jax.ShapeDtypeStruct((4, 4, ny), jnp.float32),
        in_specs=[VMEM] * 9,
        out_specs=VMEM,
        scratch_shapes=tables(u),
        compiler_params=PARAMS,
        cost_estimate=pl.CostEstimate(flops=12 * u.size, bytes_accessed=2 * u.size, transcendentals=u.size // 4),
    )(u, *rest)


def turn(block, axis, by):
    count = lax.axis_size(axis)
    return lax.ppermute(block, axis, [(i, (i + by) % count) for i in range(count)])


def both_sides(tail_head, axis):
    if lax.axis_size(axis) == 2:
        other = turn(tail_head, axis, 1)
        return other[0], other[1]
    return turn(tail_head[0], axis, 1), turn(tail_head[1], axis, -1)


def local(velocity, occupied, q_floor, q_span):
    comps, nx, ny, nz = velocity.shape
    views = lax.axis_size("view")
    density = 5.0 / (nz * views)
    xleft = turn(velocity[:, nx - 2 :], "gx", 1)
    xright = turn(velocity[:, :2], "gx", -1)
    u, yface, tail, head = faces(velocity)
    yleft, yright = both_sides(yface, "gy")
    zleft = turn(tail, "view", 1)
    zright = turn(head, "view", -1)
    mask = jnp.repeat(occupied[:, :, 0].astype(jnp.float32), SUB, axis=1)
    spread = (nx // SUB, ny, nz)
    scale = jnp.broadcast_to((mask * (-1.0 / 144.0 / q_span[0]))[:, :, None], spread)
    offset = jnp.broadcast_to((mask * (-q_floor[0] / q_span[0]))[:, :, None], spread)
    middle = inner(density, u, yleft, yright, zleft, zright, scale, offset)
    border = edge(density, u, xleft, xright, yleft, yright, zleft, zright, scale, offset)
    partial_image = jnp.concatenate([border[:, :2], middle[:, 2:-2], border[:, 2:]], axis=1)
    rows = nx // views
    blocks = partial_image.reshape(4, views, rows, ny)
    me = lax.axis_index("view")
    sources, images = [me], [lax.dynamic_index_in_dim(blocks, me, 1, keepdims=False)]
    for by in range(1, views):
        sent = lax.dynamic_index_in_dim(blocks, (me + by) % views, 1, keepdims=False)
        images.append(turn(sent, "view", by))
        sources.append((me - by) % views)
    colour = jnp.zeros((3, rows, ny), jnp.float32)
    through = jnp.ones((rows, ny), jnp.float32)
    for source, image in zip(sources, images):
        passing = jnp.ones((rows, ny), jnp.float32)
        for other, behind in zip(sources, images):
            passing = passing * jnp.where(other < source, behind[3], 1.0)
        colour = colour + passing * image[:3]
        through = through * image[3]
    finished = jnp.concatenate([colour, 1.0 - through[None]], axis=0)
    return finished.reshape(1, 1, 4, rows, ny)


def solution(mesh):
    placed = (P(None, "gx", "gy", "view"), P("gx", "gy", "view"), P(), P())
    return jax.shard_map(
        local,
        mesh=mesh,
        in_specs=placed,
        out_specs=P("gx", "gy", None, "view", None),
        check_vma=False,
    )
```

```python
import functools
import math

import jax
import jax.numpy as jnp
from jax import lax
from jax.experimental import pallas as pl
from jax.experimental.pallas import tpu as pltpu
from jax.sharding import PartitionSpec as P

SUB = 8
ROWS = 32
VMEM = pl.BlockSpec(memory_space=pltpu.VMEM)
HBM = pl.BlockSpec(memory_space=pltpu.HBM)
COST = pl.CostEstimate(flops=1 << 20, bytes_accessed=1 << 20, transcendentals=0)
PARAMS = pltpu.CompilerParams(vmem_limit_bytes=32 << 20)


def split(values):
    high = values.astype(jnp.bfloat16)
    low = (values - high.astype(jnp.float32)).astype(jnp.bfloat16)
    return high, low


def iota(shape, dim):
    return lax.broadcasted_iota(jnp.int32, shape, dim)


def faces_kernel(
    u_hbm, u_ref, xtail_ref, xhead_ref, yface_ref, tail_ref, head_ref, sems, side_sems
):
    comps, nx, ny, nz = u_ref.shape
    sides = [
        pltpu.make_async_copy(source, target, side_sems.at[k])
        for k, (source, target) in enumerate(
            (
                (u_hbm.at[:, pl.ds(nx - 2, 2)], xtail_ref),
                (u_hbm.at[:, pl.ds(0, 2)], xhead_ref),
            )
        )
    ]
    quarters = sems.shape[1]
    rows = ny // quarters

    def fetch(c, k):
        span = pl.ds(k * rows if isinstance(k, int) else pl.multiple_of(k * rows, rows), rows)
        return pltpu.make_async_copy(u_hbm.at[c, :, span], u_ref.at[c, :, span], sems.at[c, k])

    for k in range(quarters):
        for c in (0, 1):
            fetch(c, k).start()
    for k in range(quarters):
        fetch(2, k).start()
    for copy in sides:
        copy.start()
    pair = iota((8, nz), 1) // 2

    def pack(members, y, out, first):
        out_rows = pl.ds(out, 8)
        tail = jnp.zeros((8, nz), jnp.float32)
        head = jnp.zeros((8, nz), jnp.float32)
        for c, base in members:
            for x in range(nx):
                place = base // 2 + x
                moved = pltpu.roll(u_ref[c, x, pl.ds(y, 8), :], (base + 2 * x + 2) % nz, 1)
                tail = jnp.where(pair == place, moved, tail)
                head = jnp.where(pair == (place + 1) % (nz // 2), moved, head)
        head = pltpu.roll(head, nz - 2, 1)
        if first:
            tail_ref[out_rows, :] = tail
            head_ref[out_rows, :] = head
        else:
            half = pair < nz // 4
            tail_ref[out_rows, :] = jnp.where(half, tail_ref[out_rows, :], tail)
            head_ref[out_rows, :] = jnp.where(half, head_ref[out_rows, :], head)

    def both(k, carry):
        fetch(0, k).wait()
        fetch(1, k).wait()
        for part in range(rows // 8):
            y = pl.multiple_of(k * rows + part * 8, 8)
            pack(((0, 0), (1, nz // 2)), y, y, True)
        return carry

    lax.fori_loop(0, quarters, both, 0)

    def last(base, offset, first):
        def step(k, carry):
            fetch(2, k).wait()
            for part in range(rows // 8):
                y = pl.multiple_of(k * rows + part * 8, 8)
                pack(((2, base),), y, pl.multiple_of(y + offset, 8), first)
            return carry

        return step

    lax.fori_loop(0, quarters // 2, last(0, ny, True), 0)
    lax.fori_loop(quarters // 2, quarters, last(nz // 2, ny // 2, False), 0)
    for c in range(comps):
        for x in range(nx):
            end = u_ref[c, x, pl.ds(ny - 8, 8), :]
            start = u_ref[c, x, pl.ds(0, 8), :]
            yface_ref[0, c, pl.ds(2 * x, 2), :] = jnp.concatenate([end[6:7] - 8.0 * end[7:8], end[7:8]], axis=0)
            yface_ref[1, c, pl.ds(2 * x, 2), :] = jnp.concatenate([-start[0:1], 8.0 * start[0:1] - start[1:2]], axis=0)
    for copy in sides:
        copy.wait()


def faces(u):
    comps, nx, ny, nz = u.shape

    def shaped(*shape):
        return jax.ShapeDtypeStruct(shape, jnp.float32)

    return pl.pallas_call(
        faces_kernel,
        out_shape=(
            shaped(*u.shape),
            shaped(comps, 2, ny, nz),
            shaped(comps, 2, ny, nz),
            shaped(2, comps, 2 * nx, nz),
            shaped(ny + ny // 2, nz),
            shaped(ny + ny // 2, nz),
        ),
        in_specs=[HBM],
        out_specs=(VMEM,) * 6,
        scratch_shapes=[
            pltpu.SemaphoreType.DMA((comps, 4)),
            pltpu.SemaphoreType.DMA((2,)),
        ],
        compiler_params=pltpu.CompilerParams(vmem_limit_bytes=45 << 20),
        cost_estimate=COST,
    )(u)


def stencil(far):
    one = jnp.where(far == 1, 8.0, 0.0) - jnp.where(far == -1, 8.0, 0.0)
    return (one - jnp.where(far == 2, 1.0, 0.0) + jnp.where(far == -2, 1.0, 0.0)).astype(jnp.bfloat16)


def sides_down(yleft_ref, yright_ref, top_ref, low_ref):
    comps, nx, _, nz = top_ref.shape
    sub = iota((8, nz), 0)
    for c in range(comps):
        for group in range(nx // 4):
            left8 = yleft_ref[c, pl.ds(8 * group, 8), :]
            right8 = yright_ref[c, pl.ds(8 * group, 8), :]
            for k in range(4):
                top = left8 if k == 0 else pltpu.roll(left8, 8 - 2 * k, 0)
                low = right8 if k == 3 else pltpu.roll(right8, 6 - 2 * k, 0)
                top_ref[c, 4 * group + k] = jnp.where(sub < 2, top, 0.0)
                low_ref[c, 4 * group + k] = jnp.where(sub >= 6, low, 0.0)


def shading(occupied_ref, floor, span, scale_ref, offset_ref):
    blocks, ny, nz = scale_ref.shape
    groups = ny // SUB
    mine = iota((ny, groups), 0) // SUB == iota((ny, groups), 1)
    shrink = 1.0 / span
    for block in range(blocks):
        row = occupied_ref[block : block + 1, :].astype(jnp.float32)
        column = jnp.sum(jnp.where(mine, row, 0.0), axis=1, keepdims=True)
        scale_ref[block] = jnp.broadcast_to(column * (shrink * (-1.0 / 144.0)), (ny, nz))
        offset_ref[block] = jnp.broadcast_to(column * (shrink * -floor), (ny, nz))


def lane_shift(x, nz, back):
    if isinstance(x, int):
        return (4 * x + 2 if back else 2 * nz - 2 - 4 * x) % nz
    return lax.rem(4 * x + 2 if back else 2 * nz - 2 - 4 * x, nz)


def slopes(u_ref, x, tables, slope_ref):
    top_ref, low_ref, dz_ref, dy_ref = tables
    comps, ny, nz = slope_ref.shape[1:]
    for c in range(comps):
        high, low = split(u_ref[c, x])
        slope_ref[1, c] = jnp.dot(
            jnp.concatenate([high, low], axis=1), dz_ref[...], preferred_element_type=jnp.float32
        )
        down = jnp.dot(dy_ref[...], jnp.concatenate([high, low], axis=0), preferred_element_type=jnp.float32)
        slope_ref[0, c, pl.ds(0, 8), :] = down[:8] + top_ref[c, x]
        slope_ref[0, c, pl.ds(8, ny - 16), :] = down[8 : ny - 8]
        slope_ref[0, c, pl.ds(ny - 8, 8), :] = down[ny - 8 :] + low_ref[c, x]


def shade(u_ref, x, slope_ref, scale_ref, offset_ref, raw_ref, pack_ref, kept_ref=None, place=None):
    comps, nx, ny, nz = u_ref.shape
    block = x // SUB
    back = lane_shift(x, nz, True)

    def across(c, rows):
        def part(d):
            inside = not isinstance(x, int) or 0 <= x + d < nx
            return u_ref[c, x + d, rows, :] if inside else None

        def difference(high, low):
            if high is None:
                return 0.0 if low is None else -low
            return high if low is None else high - low

        return 8.0 * difference(part(1), part(-1)) - difference(part(2), part(-2))

    for y in range(0, ny, ROWS):
        rows = pl.ds(y, ROWS)
        mine = iota((ROWS, nz), 1) // 4 == x
        side = [across(c, rows) for c in range(comps)]
        down = [slope_ref[0, c, rows, :] for c in range(comps)]
        depth = [slope_ref[1, c, rows, :] for c in range(comps)]
        total = 0.5 * (side[0] * side[0] + down[1] * down[1] + depth[2] * depth[2])
        total = total + side[1] * down[0] + side[2] * depth[0] + down[2] * depth[1]
        raw_ref[x, rows, :] = total * scale_ref[block, rows, :] + offset_ref[block, rows, :]
        for k, values in enumerate((side[2], down[2], depth[2])):
            pack_ref[k, rows, :] = jnp.where(mine, pltpu.roll(values, back, 1), pack_ref[k, rows, :])
        if kept_ref is not None:
            for k, values in enumerate((side[0], down[0], depth[0])):
                kept_ref[place, k, rows, :] = values


def edge_rows(nx):
    return (0, 1, nx - 2, nx - 1)


def shade_kernel(
    u_ref, yleft_ref, yright_ref, occupied_ref, floor_ref, span_ref,
    raw_ref, pack_ref, kept_ref, scale_ref, offset_ref, top_ref, low_ref, dz_ref, dy_ref, slope0_ref, slope1_ref,
):
    comps, nx, ny, nz = u_ref.shape
    dz_ref[...] = stencil(iota((2 * nz, nz), 0) % nz - iota((2 * nz, nz), 1))
    dy_ref[...] = stencil(iota((ny, 2 * ny), 1) % ny - iota((ny, 2 * ny), 0))
    sides_down(yleft_ref, yright_ref, top_ref, low_ref)
    shading(occupied_ref, floor_ref[...].reshape(1, 1), span_ref[...].reshape(1, 1), scale_ref, offset_ref)
    pack_ref[...] = jnp.zeros(pack_ref.shape, jnp.float32)
    tables = (top_ref, low_ref, dz_ref, dy_ref)
    outs = (scale_ref, offset_ref, raw_ref, pack_ref)
    slopes(u_ref, 0, tables, slope0_ref)
    slopes(u_ref, 1, tables, slope1_ref)
    shade(u_ref, 0, slope0_ref, *outs, kept_ref, 0)
    slopes(u_ref, 2, tables, slope0_ref)
    shade(u_ref, 1, slope1_ref, *outs, kept_ref, 1)

    def pair(i, carry):
        x = 2 * i + 2
        slopes(u_ref, x + 1, tables, slope1_ref)
        shade(u_ref, x, slope0_ref, *outs)
        slopes(u_ref, x + 2, tables, slope0_ref)
        shade(u_ref, x + 1, slope1_ref, *outs)
        return carry

    lax.fori_loop(0, (nx - 4) // 2, pair, 0)
    slopes(u_ref, nx - 1, tables, slope1_ref)
    shade(u_ref, nx - 2, slope0_ref, *outs, kept_ref, 2)
    shade(u_ref, nx - 1, slope1_ref, *outs, kept_ref, 3)


def shaded(u, *rest):
    comps, nx, ny, nz = u.shape
    return pl.pallas_call(
        shade_kernel,
        out_shape=(
            jax.ShapeDtypeStruct((nx, ny, nz), jnp.float32),
            jax.ShapeDtypeStruct((comps, ny, nz), jnp.float32),
            jax.ShapeDtypeStruct((4, comps, ny, nz), jnp.float32),
            jax.ShapeDtypeStruct((nx // SUB, ny, nz), jnp.float32),
        ),
        in_specs=[VMEM] * 6,
        out_specs=(VMEM,) * 4,
        scratch_shapes=[
            pltpu.VMEM((nx // SUB, ny, nz), jnp.float32),
            pltpu.VMEM((comps, nx, 8, nz), jnp.float32),
            pltpu.VMEM((comps, nx, 8, nz), jnp.float32),
            pltpu.VMEM((2 * nz, nz), jnp.bfloat16),
            pltpu.VMEM((ny, 2 * ny), jnp.bfloat16),
            pltpu.VMEM((2, comps, ny, nz), jnp.float32),
            pltpu.VMEM((2, comps, ny, nz), jnp.float32),
        ],
        compiler_params=PARAMS,
        cost_estimate=COST,
    )(u, *rest)


def sides_deep(nx, ny, nz, zleft_ref, zright_ref):
    source, target = iota((2 * nz, nz), 0) % nz, iota((2 * nz, nz), 1)
    side, place, layer = source // (2 * nx), source % (2 * nx) // 2, source % 2
    where = jnp.where(place == target // 4, 4 * side + 2 * layer, -1000) + 10 * (target % 4)
    weights = jnp.zeros((2 * nz, nz), jnp.float32)
    for value, (s, l, t) in (
        (1.0, (0, 0, 2)),
        (-8.0, (0, 1, 2)),
        (1.0, (0, 1, 3)),
        (-1.0, (1, 0, 0)),
        (8.0, (1, 0, 1)),
        (-1.0, (1, 1, 1)),
    ):
        weights = jnp.where(where == 4 * s + 2 * l + 10 * t, value, weights)
    weights = weights.astype(jnp.bfloat16)
    first = iota((ny, nz), 1) < nz // 2
    left, right = zleft_ref[:ny], zright_ref[:ny]
    left2, right2 = zleft_ref[ny:], zright_ref[ny:]
    turned_left2, turned_right2 = pltpu.roll(left2, nz // 2, 1), pltpu.roll(right2, nz // 2, 1)
    ghosts = (
        jnp.where(first, left, pltpu.roll(right, nz // 2, 1)),
        jnp.where(first, pltpu.roll(left, nz // 2, 1), right),
        jnp.where(
            first,
            jnp.concatenate([left2, turned_left2], axis=0),
            jnp.concatenate([turned_right2, right2], axis=0),
        ),
    )
    return [
        jnp.dot(jnp.concatenate(split(ghost), axis=1), weights, preferred_element_type=jnp.float32) for ghost in ghosts
    ]


def on_border(packed, x, rows=None):
    ny, nz = packed.shape
    lane = iota((ny, nz), 1)
    return jnp.where((lane >= nz - 2) | (lane < 2), pltpu.roll(packed, lane_shift(x, nz, False), 1), 0.0)


def gather(density, raw, level_ref, sums_ref, sum_ref):
    level = jnp.clip(raw, 0.0, 1.0)
    level_ref[...] = level
    parts = jnp.concatenate(split((density / math.log(2.0)) * level), axis=1)
    sums_ref[...] = jnp.dot(parts, sum_ref[...], preferred_element_type=jnp.float32)


def blend(density, level_ref, sums_ref, store):
    ny, nz = level_ref.shape
    lane_group = iota((8, ny), 1) // 8
    eye = iota((8, ny), 1) % 8 == iota((8, ny), 0)
    totals = [jnp.zeros((8, ny), jnp.float32)] * 3
    for group in range(ny // 8):
        rows = pl.ds(8 * group, 8)
        level = level_ref[rows, :]
        first = (jnp.exp2(sums_ref[rows, pl.ds(0, nz)]) - jnp.exp2(sums_ref[rows, pl.ds(nz, nz)])) * level
        for k, cells in enumerate((first, first * level, level)):
            totals[k] = jnp.where(lane_group == group, jnp.sum(cells, axis=1, keepdims=True), totals[k])
    red, square, whole = [jnp.sum(jnp.where(eye, total, 0.0), axis=0, keepdims=True) for total in totals]
    through = jnp.exp2((-density / math.log(2.0)) * whole)
    store(red, 4.0 * (red - square), 1.0 - through - red, through)


def put(image_ref, x):
    per_view = image_ref.shape[2]
    view, row = (x // per_view, x % per_view) if isinstance(x, int) else (lax.div(x, per_view), lax.rem(x, per_view))

    def store(*channels):
        for k, values in enumerate(channels):
            image_ref[view, k, pl.ds(row, 1), :] = values

    return store


def summing(sum_ref):
    nz = sum_ref.shape[0] // 2
    row = iota((2 * nz, 2 * nz), 0) % nz
    col = iota((2 * nz, 2 * nz), 1)
    sum_ref[...] = jnp.where((row < col) & (col < nz) | (row <= col - nz), -1.0, 0.0).astype(jnp.bfloat16)


def blend_kernel(
    density, raw_ref, pack_ref, scale_ref, zleft_ref, zright_ref,
    image_ref, fix_ref, first_ref, sum_ref, level0_ref, level1_ref, sums0_ref, sums1_ref,
):
    nx, ny, nz = raw_ref.shape
    summing(sum_ref)
    ghosts = sides_deep(nx, ny, nz, zleft_ref, zright_ref)
    first_ref[...] = ghosts[0]
    fix = ghosts[2] * (0.5 * ghosts[2] + pack_ref[2]) + ghosts[0] * pack_ref[0] + ghosts[1] * pack_ref[1]
    per_block = 4 * SUB
    lane_block = iota((ny, nz), 1) // per_block
    scale = scale_ref[0]
    for block in range(1, nx // SUB):
        scale = jnp.where(lane_block == block, scale_ref[block], scale)
    fix_ref[...] = fix * scale
    image_ref[...] = jnp.zeros(image_ref.shape, jnp.float32)

    def load(x, level_ref, sums_ref):
        gather(density, raw_ref[x] + on_border(fix_ref[...], x), level_ref, sums_ref, sum_ref)

    load(2, level0_ref, sums0_ref)

    def pair(i, carry):
        x = 2 * i + 2
        load(x + 1, level1_ref, sums1_ref)
        blend(density, level0_ref, sums0_ref, put(image_ref, x))
        load(x + 2, level0_ref, sums0_ref)
        blend(density, level1_ref, sums1_ref, put(image_ref, x + 1))
        return carry

    lax.fori_loop(0, (nx - 4) // 2, pair, 0)


def row_tables(ny, nz):
    return [
        pltpu.VMEM((2 * nz, 2 * nz), jnp.bfloat16),
        pltpu.VMEM((ny, nz), jnp.float32),
        pltpu.VMEM((ny, nz), jnp.float32),
        pltpu.VMEM((ny, 2 * nz), jnp.float32),
        pltpu.VMEM((ny, 2 * nz), jnp.float32),
    ]


def blended(density, views, raw, *rest):
    nx, ny, nz = raw.shape
    return pl.pallas_call(
        functools.partial(blend_kernel, density),
        out_shape=(
            jax.ShapeDtypeStruct((views, 4, nx // views, ny), jnp.float32),
            jax.ShapeDtypeStruct((ny, nz), jnp.float32),
            jax.ShapeDtypeStruct((ny, nz), jnp.float32),
        ),
        in_specs=[VMEM] * 5,
        out_specs=(VMEM,) * 3,
        scratch_shapes=row_tables(ny, nz),
        compiler_params=PARAMS,
        cost_estimate=COST,
    )(raw, *rest)


def edge_kernel(
    density, middle_ref, raw_ref, kept_ref, scale_ref, fix_ref, first_ref, xleft_ref, xright_ref,
    image_ref, sum_ref, level0_ref, level1_ref, sums0_ref, sums1_ref,
):
    nx, ny, nz = raw_ref.shape
    summing(sum_ref)
    image_ref[...] = middle_ref[...]
    levels, sums = (level0_ref, level1_ref), (sums0_ref, sums1_ref)
    for place, x in enumerate(edge_rows(nx)):
        if place == 0:
            ghost = [xleft_ref[c, 0] - 8.0 * xleft_ref[c, 1] for c in range(3)]
        elif place == 1:
            ghost = [xleft_ref[c, 1] for c in range(3)]
        elif place == 2:
            ghost = [-xright_ref[c, 0] for c in range(3)]
        else:
            ghost = [8.0 * xright_ref[c, 0] - xright_ref[c, 1] for c in range(3)]
        depth = kept_ref[place, 2] + on_border(first_ref[...], x)
        more = ghost[0] * (0.5 * ghost[0] + kept_ref[place, 0]) + ghost[1] * kept_ref[place, 1] + ghost[2] * depth
        raw = raw_ref[x] + on_border(fix_ref[...], x) + more * scale_ref[x // SUB]
        gather(density, raw, levels[place % 2], sums[place % 2], sum_ref)
        blend(density, levels[place % 2], sums[place % 2], put(image_ref, x))


def edged(density, middle, raw, *rest):
    nx, ny, nz = raw.shape
    return pl.pallas_call(
        functools.partial(edge_kernel, density),
        out_shape=jax.ShapeDtypeStruct(middle.shape, jnp.float32),
        in_specs=[VMEM] * 8,
        out_specs=VMEM,
        scratch_shapes=row_tables(ny, nz),
        compiler_params=PARAMS,
        cost_estimate=COST,
    )(middle, raw, *rest)


def turn(block, axis, by):
    count = lax.axis_size(axis)
    return lax.ppermute(block, axis, [(i, (i + by) % count) for i in range(count)])


def both_sides(tail_head, axis):
    if lax.axis_size(axis) == 2:
        other = turn(tail_head, axis, 1)
        return other[0], other[1]
    return turn(tail_head[0], axis, 1), turn(tail_head[1], axis, -1)


def local(velocity, occupied, q_floor, q_span):
    comps, nx, ny, nz = velocity.shape
    views = lax.axis_size("view")
    density = 5.0 / (nz * views)
    u, xtail, xhead, yface, ztail, zhead = faces(velocity)
    xleft = turn(xtail, "gx", 1)
    xright = turn(xhead, "gx", -1)
    zleft = turn(ztail, "view", 1)
    zright = turn(zhead, "view", -1)
    yleft, yright = both_sides(yface, "gy")
    raw, pack, kept, scale = shaded(u, yleft, yright, occupied[:, :, 0], q_floor, q_span)
    middle, fix, first = blended(density, views, raw, pack, scale, zleft, zright)
    blocks = edged(density, middle, raw, kept, scale, fix, first, xleft, xright)
    images = lax.all_to_all(blocks, "view", 0, 0, tiled=True)
    colour, through = images[0, :3], images[0, 3:]
    for view in range(1, views):
        colour = colour + through * images[view, :3]
        through = through * images[view, 3:]
    finished = jnp.concatenate([colour, 1.0 - through], axis=0)
    return finished.reshape(1, 1, 4, nx // views, ny)


def solution(mesh):
    placed = (P(None, "gx", "gy", "view"), P("gx", "gy", "view"), P(), P())
    return jax.shard_map(
        local,
        mesh=mesh,
        in_specs=placed,
        out_specs=P("gx", "gy", None, "view", None),
        check_vma=False,
    )
```

```python
import functools
import math

import jax
import jax.numpy as jnp
from jax import lax
from jax.experimental import pallas as pl
from jax.experimental.pallas import tpu as pltpu
from jax.sharding import PartitionSpec as P

SUB = 8
ROWS = 32
VMEM = pl.BlockSpec(memory_space=pltpu.VMEM)
HBM = pl.BlockSpec(memory_space=pltpu.HBM)
COST = pl.CostEstimate(flops=1 << 20, bytes_accessed=1 << 20, transcendentals=0)
PARAMS = pltpu.CompilerParams(vmem_limit_bytes=24 << 20)


def split(values):
    high = values.astype(jnp.bfloat16)
    low = (values - high.astype(jnp.float32)).astype(jnp.bfloat16)
    return high, low


def iota(shape, dim):
    return lax.broadcasted_iota(jnp.int32, shape, dim)


def ends_kernel(u_hbm, xtail_ref, xhead_ref, yface_ref, sems):
    _, nx, ny, _ = u_hbm.shape
    pieces = (
        (u_hbm.at[:, pl.ds(nx - 2, 2)], xtail_ref),
        (u_hbm.at[:, pl.ds(0, 2)], xhead_ref),
        (u_hbm.at[:, :, pl.ds(ny - 8, 8)], yface_ref.at[0]),
        (u_hbm.at[:, :, pl.ds(0, 8)], yface_ref.at[1]),
    )
    copies = [pltpu.make_async_copy(source, target, sems.at[k]) for k, (source, target) in enumerate(pieces)]
    for copy in copies:
        copy.start()
    for copy in copies:
        copy.wait()


def ends(u):
    comps, nx, ny, nz = u.shape
    layers = jax.ShapeDtypeStruct((comps, 2, ny, nz), jnp.float32)
    return pl.pallas_call(
        ends_kernel,
        out_shape=(layers, layers, jax.ShapeDtypeStruct((2, comps, nx, 8, nz), jnp.float32)),
        in_specs=[HBM],
        out_specs=(VMEM,) * 3,
        scratch_shapes=[pltpu.SemaphoreType.DMA((4,))],
        compiler_params=pltpu.CompilerParams(vmem_limit_bytes=50 << 20),
        cost_estimate=COST,
    )(u)


def faces_kernel(u_hbm, u_ref, parts_ref, tail_ref, head_ref, sems):
    comps, nx, ny, nz = u_ref.shape
    quarters = sems.shape[1]
    rows = ny // quarters

    def fetch(c, k):
        span = pl.ds(k * rows if isinstance(k, int) else pl.multiple_of(k * rows, rows), rows)
        return pltpu.make_async_copy(u_hbm.at[c, :, span], u_ref.at[c, :, span], sems.at[c, k])

    for k in range(quarters):
        for c in (0, 1):
            fetch(c, k).start()
    for k in range(quarters):
        fetch(2, k).start()
    pair = iota((8, nz), 1) // 2

    def pack(members, y, out, first):
        out_rows = pl.ds(out, 8)
        tail = jnp.zeros((8, nz), jnp.float32)
        head = jnp.zeros((8, nz), jnp.float32)
        for c, base in members:
            for x in range(nx):
                place = base // 2 + x
                moved = pltpu.roll(u_ref[c, x, pl.ds(y, 8), :], (base + 2 * x + 2) % nz, 1)
                tail = jnp.where(pair == place, moved, tail)
                head = jnp.where(pair == (place + 1) % (nz // 2), moved, head)
        head = pltpu.roll(head, nz - 2, 1)
        if first:
            tail_ref[out_rows, :] = tail
            head_ref[out_rows, :] = head
        else:
            half = pair < nz // 4
            tail_ref[out_rows, :] = jnp.where(half, tail_ref[out_rows, :], tail)
            head_ref[out_rows, :] = jnp.where(half, head_ref[out_rows, :], head)

    def parted(c, k):
        span = pl.ds(pl.multiple_of(k * rows, rows), rows)
        for x in range(nx):
            high, low = split(u_ref[c, x, span, :])
            parts_ref[c, x, span, pl.ds(0, nz)] = high
            parts_ref[c, x, span, pl.ds(nz, nz)] = low

    def both(k, carry):
        fetch(0, k).wait()
        fetch(1, k).wait()
        parted(0, k)
        parted(1, k)
        for part in range(rows // 8):
            y = pl.multiple_of(k * rows + part * 8, 8)
            pack(((0, 0), (1, nz // 2)), y, y, True)
        return carry

    lax.fori_loop(0, quarters, both, 0)

    def last(base, offset, first):
        def step(k, carry):
            fetch(2, k).wait()
            parted(2, k)
            for part in range(rows // 8):
                y = pl.multiple_of(k * rows + part * 8, 8)
                pack(((2, base),), y, pl.multiple_of(y + offset, 8), first)
            return carry

        return step

    lax.fori_loop(0, quarters // 2, last(0, ny, True), 0)
    lax.fori_loop(quarters // 2, quarters, last(nz // 2, ny // 2, False), 0)


def faces(u):
    comps, nx, ny, nz = u.shape

    def shaped(*shape):
        return jax.ShapeDtypeStruct(shape, jnp.float32)

    return pl.pallas_call(
        faces_kernel,
        out_shape=(
            shaped(*u.shape),
            jax.ShapeDtypeStruct((comps, nx, ny, 2 * nz), jnp.bfloat16),
            shaped(ny + ny // 2, nz),
            shaped(ny + ny // 2, nz),
        ),
        in_specs=[HBM],
        out_specs=(VMEM,) * 4,
        scratch_shapes=[
            pltpu.SemaphoreType.DMA((comps, 4)),
        ],
        compiler_params=pltpu.CompilerParams(vmem_limit_bytes=37 << 20),
        cost_estimate=COST,
    )(u)


def stencil(far):
    one = jnp.where(far == 1, 8.0, 0.0) - jnp.where(far == -1, 8.0, 0.0)
    return (one - jnp.where(far == 2, 1.0, 0.0) + jnp.where(far == -2, 1.0, 0.0)).astype(jnp.bfloat16)


def shading(occupied_ref, floor, span, scale_ref, offset_ref):
    blocks, ny, nz = scale_ref.shape
    groups = ny // SUB
    mine = iota((ny, groups), 0) // SUB == iota((ny, groups), 1)
    shrink = 1.0 / span
    for block in range(blocks):
        row = occupied_ref[block : block + 1, :].astype(jnp.float32)
        column = jnp.sum(jnp.where(mine, row, 0.0), axis=1, keepdims=True)
        scale_ref[block] = jnp.broadcast_to(column * (shrink * (-1.0 / 144.0)), (ny, nz))
        offset_ref[block] = jnp.broadcast_to(column * (shrink * -floor), (ny, nz))


def lane_shift(x, nz, back):
    if isinstance(x, int):
        return (4 * x + 2 if back else 2 * nz - 2 - 4 * x) % nz
    return lax.rem(4 * x + 2 if back else 2 * nz - 2 - 4 * x, nz)


def slopes(parts_ref, x, tables, slope_ref):
    yleft_ref, yright_ref, dz_ref, dy_ref = tables
    comps, ny, nz = slope_ref.shape[2:]
    sub = iota((8, nz), 0)

    def top(left):
        return jnp.where(sub < 2, pltpu.roll(left, 2, 0) - jnp.where(sub == 0, 8.0 * pltpu.roll(left, 1, 0), 0.0), 0.0)

    def low(right):
        far = pltpu.roll(right, 6, 0)
        return jnp.where(sub >= 6, jnp.where(sub == 7, 8.0 * pltpu.roll(right, 7, 0), 0.0) - far, 0.0)

    parts = [[parts_ref[c, x + k] for k in range(2)] for c in range(comps)]
    depth = jnp.dot(
        jnp.concatenate([part for pair in parts for part in pair], axis=0),
        dz_ref[...],
        preferred_element_type=jnp.float32,
    )
    for c in range(comps):
        both = jnp.concatenate(
            [jnp.concatenate([part[:, half : half + nz] for part in parts[c]], axis=1) for half in (0, nz)], axis=0
        )
        down = jnp.dot(dy_ref[...], both, preferred_element_type=jnp.float32)
        for k in range(2):
            slope_ref[1, k, c] = depth[(2 * c + k) * ny : (2 * c + k + 1) * ny]
            mine = down[:, k * nz : (k + 1) * nz]
            slope_ref[0, k, c, pl.ds(0, 8), :] = mine[:8] + top(yleft_ref[c, x + k])
            slope_ref[0, k, c, pl.ds(8, ny - 16), :] = mine[8 : ny - 8]
            slope_ref[0, k, c, pl.ds(ny - 8, 8), :] = mine[ny - 8 :] + low(yright_ref[c, x + k])


def shade(u_ref, x, slope_ref, scale_ref, offset_ref, raw_ref, pack_ref, kept_ref=None, place=None):
    comps, nx, ny, nz = u_ref.shape
    block = x // SUB

    def difference(high, low):
        if high is None:
            return 0.0 if low is None else -low
        return high if low is None else high - low

    for y in range(0, ny, ROWS):
        rows = pl.ds(y, ROWS)
        slots = iota((ROWS, nz), 1) // 4
        across = []
        for c in range(comps):
            near = [
                u_ref[c, x + d, rows, :] if not isinstance(x, int) or 0 <= x + d < nx else None for d in range(-2, 4)
            ]
            across.append(
                [8.0 * difference(near[k + 3], near[k + 1]) - difference(near[k + 4], near[k]) for k in range(2)]
            )
        packs = [pack_ref[k, rows, :] for k in range(3)]
        for k in range(2):
            side = [across[c][k] for c in range(comps)]
            down = [slope_ref[0, k, c, rows, :] for c in range(comps)]
            depth = [slope_ref[1, k, c, rows, :] for c in range(comps)]
            total = 0.5 * (side[0] * side[0] + down[1] * down[1] + depth[2] * depth[2])
            total = total + side[1] * down[0] + side[2] * depth[0] + down[2] * depth[1]
            raw_ref[x + k, rows, :] = total * scale_ref[block, rows, :] + offset_ref[block, rows, :]
            back = lane_shift(x + k, nz, True)
            packs = [
                jnp.where(slots == x + k, pltpu.roll(values, back, 1), pack)
                for values, pack in zip((side[2], down[2], depth[2]), packs)
            ]
            if kept_ref is not None:
                for n, values in enumerate((side[0], down[0], depth[0])):
                    kept_ref[place + k, n, rows, :] = values
        for k in range(3):
            pack_ref[k, rows, :] = packs[k]


def edge_rows(nx):
    return (0, 1, nx - 2, nx - 1)


def shade_kernel(
    u_ref, parts_ref, yleft_ref, yright_ref, occupied_ref, floor_ref, span_ref,
    raw_ref, pack_ref, kept_ref, scale_ref, offset_ref, dz_ref, dy_ref, slope0_ref, slope1_ref,
):
    comps, nx, ny, nz = u_ref.shape
    dz_ref[...] = stencil(iota((2 * nz, nz), 0) % nz - iota((2 * nz, nz), 1))
    dy_ref[...] = stencil(iota((ny, 2 * ny), 1) % ny - iota((ny, 2 * ny), 0))
    shading(occupied_ref, floor_ref[...].reshape(1, 1), span_ref[...].reshape(1, 1), scale_ref, offset_ref)
    pack_ref[...] = jnp.zeros(pack_ref.shape, jnp.float32)
    tables = (yleft_ref, yright_ref, dz_ref, dy_ref)
    outs = (scale_ref, offset_ref, raw_ref, pack_ref)
    slopes(parts_ref, 0, tables, slope0_ref)
    slopes(parts_ref, 2, tables, slope1_ref)
    shade(u_ref, 0, slope0_ref, *outs, kept_ref, 0)

    def pairs(i, carry):
        x = 4 * i + 2
        slopes(parts_ref, x + 2, tables, slope0_ref)
        shade(u_ref, x, slope1_ref, *outs)
        slopes(parts_ref, x + 4, tables, slope1_ref)
        shade(u_ref, x + 2, slope0_ref, *outs)
        return carry

    lax.fori_loop(0, (nx - 4) // 4, pairs, 0)
    shade(u_ref, nx - 2, slope1_ref, *outs, kept_ref, 2)


def shaded(u, *rest):
    comps, nx, ny, nz = u.shape
    return pl.pallas_call(
        shade_kernel,
        out_shape=(
            jax.ShapeDtypeStruct((nx, ny, nz), jnp.float32),
            jax.ShapeDtypeStruct((comps, ny, nz), jnp.float32),
            jax.ShapeDtypeStruct((4, comps, ny, nz), jnp.float32),
            jax.ShapeDtypeStruct((nx // SUB, ny, nz), jnp.float32),
        ),
        in_specs=[VMEM] * 7,
        out_specs=(VMEM,) * 4,
        scratch_shapes=[
            pltpu.VMEM((nx // SUB, ny, nz), jnp.float32),
            pltpu.VMEM((2 * nz, nz), jnp.bfloat16),
            pltpu.VMEM((ny, 2 * ny), jnp.bfloat16),
            pltpu.VMEM((2, 2, comps, ny, nz), jnp.float32),
            pltpu.VMEM((2, 2, comps, ny, nz), jnp.float32),
        ],
        compiler_params=PARAMS,
        cost_estimate=COST,
    )(u, *rest)


def sides_deep(nx, ny, nz, zleft_ref, zright_ref):
    source, target = iota((2 * nz, nz), 0) % nz, iota((2 * nz, nz), 1)
    side, place, layer = source // (2 * nx), source % (2 * nx) // 2, source % 2
    where = jnp.where(place == target // 4, 4 * side + 2 * layer, -1000) + 10 * (target % 4)
    weights = jnp.zeros((2 * nz, nz), jnp.float32)
    for value, (s, l, t) in (
        (1.0, (0, 0, 2)),
        (-8.0, (0, 1, 2)),
        (1.0, (0, 1, 3)),
        (-1.0, (1, 0, 0)),
        (8.0, (1, 0, 1)),
        (-1.0, (1, 1, 1)),
    ):
        weights = jnp.where(where == 4 * s + 2 * l + 10 * t, value, weights)
    weights = weights.astype(jnp.bfloat16)
    first = iota((ny, nz), 1) < nz // 2
    left, right = zleft_ref[:ny], zright_ref[:ny]
    left2, right2 = zleft_ref[ny:], zright_ref[ny:]
    turned_left2, turned_right2 = pltpu.roll(left2, nz // 2, 1), pltpu.roll(right2, nz // 2, 1)
    ghosts = (
        jnp.where(first, left, pltpu.roll(right, nz // 2, 1)),
        jnp.where(first, pltpu.roll(left, nz // 2, 1), right),
        jnp.where(
            first,
            jnp.concatenate([left2, turned_left2], axis=0),
            jnp.concatenate([turned_right2, right2], axis=0),
        ),
    )
    return [
        jnp.dot(jnp.concatenate(split(ghost), axis=1), weights, preferred_element_type=jnp.float32) for ghost in ghosts
    ]


def on_border(packed, x, rows=None):
    ny, nz = packed.shape
    lane = iota((ny, nz), 1)
    return jnp.where((lane >= nz - 2) | (lane < 2), pltpu.roll(packed, lane_shift(x, nz, False), 1), 0.0)


def gather(density, raws, level_ref, sums_ref, sum_ref):
    parts = []
    for k, raw in enumerate(raws):
        level = jnp.clip(raw, 0.0, 1.0)
        level_ref[k] = level
        parts.append(jnp.concatenate(split((density / math.log(2.0)) * level), axis=1))
    ny, nz = level_ref.shape[1:]
    sums = jnp.dot(jnp.concatenate(parts, axis=0), sum_ref[...], preferred_element_type=jnp.float32)
    for k in range(len(raws)):
        sums_ref[k] = sums[k * ny : (k + 1) * ny]


def blend(level_ref, sums_ref, k, store):
    ny, nz = level_ref.shape[1:]
    lane_group = iota((8, ny), 1) // 8
    eye = iota((8, ny), 1) % 8 == iota((8, ny), 0)
    totals = [jnp.zeros((8, ny), jnp.float32)] * 3
    for group in range(ny // 8):
        rows = pl.ds(8 * group, 8)
        level = level_ref[k, rows, :]
        passing = jnp.exp2(sums_ref[k, rows, pl.ds(0, nz)])
        first = (passing - jnp.exp2(sums_ref[k, rows, pl.ds(nz, nz)])) * level
        red = jnp.sum(first, axis=1, keepdims=True)
        square = jnp.sum(first * level, axis=1, keepdims=True)
        whole = sums_ref[k, rows, pl.ds(2 * nz, ny)]
        totals = [jnp.where(lane_group == group, part, total) for part, total in zip((red, square, whole), totals)]
    red, square, whole = [jnp.sum(jnp.where(eye, total, 0.0), axis=0, keepdims=True) for total in totals]
    through = jnp.exp2(whole)
    store(red, 4.0 * (red - square), 1.0 - through - red, through)


def put(image_ref, x):
    per_view = image_ref.shape[2]
    view, row = (x // per_view, x % per_view) if isinstance(x, int) else (lax.div(x, per_view), lax.rem(x, per_view))

    def store(*channels):
        for k, values in enumerate(channels):
            image_ref[view, k, pl.ds(row, 1), :] = values

    return store


def summing(sum_ref):
    nz = sum_ref.shape[0] // 2
    row = iota(sum_ref.shape, 0) % nz
    col = iota(sum_ref.shape, 1)
    sum_ref[...] = jnp.where((row < col) & (col < nz) | (row <= col - nz), -1.0, 0.0).astype(jnp.bfloat16)


def blend_kernel(
    density, raw_ref, pack_ref, scale_ref, zleft_ref, zright_ref,
    image_ref, fix_ref, first_ref, sum_ref, level0_ref, level1_ref, sums0_ref, sums1_ref,
):
    nx, ny, nz = raw_ref.shape
    summing(sum_ref)
    ghosts = sides_deep(nx, ny, nz, zleft_ref, zright_ref)
    first_ref[...] = ghosts[0]
    fix = ghosts[2] * (0.5 * ghosts[2] + pack_ref[2]) + ghosts[0] * pack_ref[0] + ghosts[1] * pack_ref[1]
    per_block = 4 * SUB
    lane_block = iota((ny, nz), 1) // per_block
    scale = scale_ref[0]
    for block in range(1, nx // SUB):
        scale = jnp.where(lane_block == block, scale_ref[block], scale)
    fix_ref[...] = fix * scale
    image_ref[...] = jnp.zeros(image_ref.shape, jnp.float32)
    batch = level0_ref.shape[0]

    def load(x, level_ref, sums_ref):
        raws = [raw_ref[x + k] + on_border(fix_ref[...], x + k) for k in range(batch)]
        gather(density, raws, level_ref, sums_ref, sum_ref)

    def mix(x, level_ref, sums_ref):
        for k in range(batch):
            blend(level_ref, sums_ref, k, put(image_ref, x + k))

    load(2, level0_ref, sums0_ref)

    def batches(i, carry):
        x = 2 * batch * i + 2
        load(x + batch, level1_ref, sums1_ref)
        mix(x, level0_ref, sums0_ref)
        load(x + 2 * batch, level0_ref, sums0_ref)
        mix(x + batch, level1_ref, sums1_ref)
        return carry

    count = (nx - 4) // batch
    lax.fori_loop(0, (count - 1) // 2, batches, 0)
    if count % 2 == 0:
        load(nx - 2 - batch, level1_ref, sums1_ref)
        mix(nx - 2 - 2 * batch, level0_ref, sums0_ref)
        mix(nx - 2 - batch, level1_ref, sums1_ref)
    else:
        mix(nx - 2 - batch, level0_ref, sums0_ref)


def row_tables(batch, ny, nz, buffers):
    return (
        [pltpu.VMEM((2 * nz, 2 * nz + ny), jnp.bfloat16)]
        + [pltpu.VMEM((batch, ny, nz), jnp.float32)] * buffers
        + [pltpu.VMEM((batch, ny, 2 * nz + ny), jnp.float32)] * buffers
    )


def blended(density, views, raw, *rest):
    nx, ny, nz = raw.shape
    return pl.pallas_call(
        functools.partial(blend_kernel, density),
        out_shape=(
            jax.ShapeDtypeStruct((views, 4, nx // views, ny), jnp.float32),
            jax.ShapeDtypeStruct((ny, nz), jnp.float32),
            jax.ShapeDtypeStruct((ny, nz), jnp.float32),
        ),
        in_specs=[VMEM] * 5,
        out_specs=(VMEM,) * 3,
        scratch_shapes=row_tables(4, ny, nz, 2),
        compiler_params=PARAMS,
        cost_estimate=COST,
    )(raw, *rest)


def edge_kernel(
    density, middle_ref, raw_ref, kept_ref, scale_ref, fix_ref, first_ref, xleft_ref, xright_ref,
    image_ref, sum_ref, level_ref, sums_ref,
):
    nx, ny, nz = raw_ref.shape
    summing(sum_ref)
    image_ref[...] = middle_ref[...]
    raws = []
    for place, x in enumerate(edge_rows(nx)):
        if place == 0:
            ghost = [xleft_ref[c, 0] - 8.0 * xleft_ref[c, 1] for c in range(3)]
        elif place == 1:
            ghost = [xleft_ref[c, 1] for c in range(3)]
        elif place == 2:
            ghost = [-xright_ref[c, 0] for c in range(3)]
        else:
            ghost = [8.0 * xright_ref[c, 0] - xright_ref[c, 1] for c in range(3)]
        depth = kept_ref[place, 2] + on_border(first_ref[...], x)
        more = ghost[0] * (0.5 * ghost[0] + kept_ref[place, 0]) + ghost[1] * kept_ref[place, 1] + ghost[2] * depth
        raws.append(raw_ref[x] + on_border(fix_ref[...], x) + more * scale_ref[x // SUB])
    gather(density, raws, level_ref, sums_ref, sum_ref)
    for place, x in enumerate(edge_rows(nx)):
        blend(level_ref, sums_ref, place, put(image_ref, x))


def edged(density, middle, raw, *rest):
    nx, ny, nz = raw.shape
    return pl.pallas_call(
        functools.partial(edge_kernel, density),
        out_shape=jax.ShapeDtypeStruct(middle.shape, jnp.float32),
        in_specs=[VMEM] * 8,
        out_specs=VMEM,
        scratch_shapes=row_tables(4, ny, nz, 1),
        compiler_params=PARAMS,
        cost_estimate=COST,
    )(middle, raw, *rest)


def turn(block, axis, by):
    count = lax.axis_size(axis)
    return lax.ppermute(block, axis, [(i, (i + by) % count) for i in range(count)])


def both_sides(tail_head, axis):
    if lax.axis_size(axis) == 2:
        other = turn(tail_head, axis, 1)
        return other[0], other[1]
    return turn(tail_head[0], axis, 1), turn(tail_head[1], axis, -1)


def exchanged(blocks, axis):
    count = lax.axis_size(axis)
    me = lax.axis_index(axis)
    paired = count & (count - 1) == 0
    found = [(me, lax.dynamic_index_in_dim(blocks, me, 0, keepdims=False))]
    for step in range(count - 1, 0, -1):
        if paired:
            to = source = me ^ step
            route = [(i, i ^ step) for i in range(count)]
        else:
            to, source = (me + step) % count, (me - step) % count
            route = [(i, (i + step) % count) for i in range(count)]
        sent = lax.dynamic_index_in_dim(blocks, to, 0, keepdims=False)
        found.append((source, lax.ppermute(sent, axis, route)))
    return found


def local(velocity, occupied, q_floor, q_span):
    comps, nx, ny, nz = velocity.shape
    views = lax.axis_size("view")
    density = 5.0 / (nz * views)
    xtail, xhead, yface = ends(velocity)
    xleft = turn(xtail, "gx", 1)
    xright = turn(xhead, "gx", -1)
    u, parts, ztail, zhead = faces(velocity)
    zleft = turn(ztail, "view", 1)
    zright = turn(zhead, "view", -1)
    yleft, yright = both_sides(yface, "gy")
    raw, pack, kept, scale = shaded(u, parts, yleft, yright, occupied[:, :, 0], q_floor, q_span)
    middle, fix, first = blended(density, views, raw, pack, scale, zleft, zright)
    blocks = edged(density, middle, raw, kept, scale, fix, first, xleft, xright)
    images = exchanged(blocks, "view")
    colour = jnp.zeros((3, nx // views, ny), jnp.float32)
    through = jnp.ones((nx // views, ny), jnp.float32)
    for source, image in images:
        passing = jnp.ones((nx // views, ny), jnp.float32)
        for other, front in images:
            passing = passing * jnp.where(other < source, front[3], 1.0)
        colour = colour + passing * image[:3]
        through = through * image[3]
    finished = jnp.concatenate([colour, 1.0 - through[None]], axis=0)
    return finished.reshape(1, 1, 4, nx // views, ny)


def solution(mesh):
    placed = (P(None, "gx", "gy", "view"), P("gx", "gy", "view"), P(), P())
    return jax.shard_map(
        local,
        mesh=mesh,
        in_specs=placed,
        out_specs=P("gx", "gy", None, "view", None),
        check_vma=False,
    )
```

```python
import functools
import math

import jax
import jax.numpy as jnp
from jax import lax
from jax.experimental import pallas as pl
from jax.experimental.pallas import tpu as pltpu
from jax.sharding import PartitionSpec as P

SUB = 8
ROWS = 32
VMEM = pl.BlockSpec(memory_space=pltpu.VMEM)
HBM = pl.BlockSpec(memory_space=pltpu.HBM)
COST = pl.CostEstimate(flops=1 << 20, bytes_accessed=1 << 20, transcendentals=0)
PARAMS = pltpu.CompilerParams(vmem_limit_bytes=16 << 20)


def split(values):
    high = values.astype(jnp.bfloat16)
    low = (values - high.astype(jnp.float32)).astype(jnp.bfloat16)
    return high, low


def iota(shape, dim):
    return lax.broadcasted_iota(jnp.int32, shape, dim)


def ends_kernel(u_hbm, xtail_ref, xhead_ref, yface_ref, sems):
    _, nx, ny, _ = u_hbm.shape
    pieces = (
        (u_hbm.at[:, pl.ds(nx - 2, 2)], xtail_ref),
        (u_hbm.at[:, pl.ds(0, 2)], xhead_ref),
        (u_hbm.at[:, :, pl.ds(ny - 8, 8)], yface_ref.at[0]),
        (u_hbm.at[:, :, pl.ds(0, 8)], yface_ref.at[1]),
    )
    copies = [pltpu.make_async_copy(source, target, sems.at[k]) for k, (source, target) in enumerate(pieces)]
    for copy in copies:
        copy.start()
    for copy in copies:
        copy.wait()


def ends(u):
    comps, nx, ny, nz = u.shape
    layers = jax.ShapeDtypeStruct((comps, 2, ny, nz), jnp.float32)
    return pl.pallas_call(
        ends_kernel,
        out_shape=(layers, layers, jax.ShapeDtypeStruct((2, comps, nx, 8, nz), jnp.float32)),
        in_specs=[HBM],
        out_specs=(VMEM,) * 3,
        scratch_shapes=[pltpu.SemaphoreType.DMA((4,))],
        compiler_params=pltpu.CompilerParams(vmem_limit_bytes=50 << 20),
        cost_estimate=COST,
    )(u)


def faces_kernel(u_hbm, u_ref, parts_ref, tail_ref, head_ref, packed_ref, sems):
    comps, nx, ny, nz = u_ref.shape
    quarters = sems.shape[1]
    rows = ny // quarters

    def fetch(c, k):
        span = pl.ds(k * rows if isinstance(k, int) else pl.multiple_of(k * rows, rows), rows)
        return pltpu.make_async_copy(u_hbm.at[c, :, span], u_ref.at[c, :, span], sems.at[c, k])

    for c in range(comps):
        for k in range(quarters):
            fetch(c, k).start()
    slot = iota((8, nz), 1) // 4
    for c in range(comps):

        def quarter(k, carry):
            fetch(c, k).wait()
            start = pl.multiple_of(k * rows, rows)
            packed = [jnp.zeros((8, nz), jnp.float32)] * (rows // 8)
            for x in range(nx):
                cells = u_ref[c, x, pl.ds(start, rows), :]
                high, low = split(cells)
                parts_ref[c, x, pl.ds(start, rows), pl.ds(0, nz)] = high
                parts_ref[c, x, pl.ds(start, rows), pl.ds(nz, nz)] = low
                mine = slot == x
                for n in range(rows // 8):
                    packed[n] = jnp.where(mine, pltpu.roll(cells[8 * n : 8 * n + 8], (4 * x + 2) % nz, 1), packed[n])
            for n in range(rows // 8):
                packed_ref[c, pl.ds(pl.multiple_of(start + 8 * n, 8), 8), :] = packed[n]
            return carry

        lax.fori_loop(0, quarters, quarter, 0)
    tails, heads = fold([packed_ref[c] for c in range(comps)], ny, nz)
    tail_ref[...] = tails
    head_ref[...] = heads


def fold(packed, ny, nz):
    early = iota((ny, nz), 1) % 4 < 2
    early2 = early[: ny // 2]
    third, fourth = packed[2][: ny // 2], packed[2][ny // 2 :]
    tails = jnp.where(early, packed[0], pltpu.roll(packed[1], 2, 1))
    tails2 = jnp.where(early2, third, pltpu.roll(fourth, 2, 1))
    heads = jnp.where(early, pltpu.roll(packed[0], nz - 2, 1), packed[1])
    heads2 = jnp.where(early2, pltpu.roll(third, nz - 2, 1), fourth)
    return jnp.concatenate([tails, tails2], axis=0), jnp.concatenate([heads, heads2], axis=0)


def unfold(left, right, ny, nz):
    early = iota((ny, nz), 1) % 4 < 2
    early2 = early[: ny // 2]
    left2, right2 = left[ny:], right[ny:]
    left, right = left[:ny], right[:ny]
    first = jnp.where(early, left, pltpu.roll(right, 2, 1))
    second = jnp.where(early, pltpu.roll(left, nz - 2, 1), right)
    third = jnp.where(early2, left2, pltpu.roll(right2, 2, 1))
    fourth = jnp.where(early2, pltpu.roll(left2, nz - 2, 1), right2)
    return first, second, jnp.concatenate([third, fourth], axis=0)


def faces(u):
    comps, nx, ny, nz = u.shape
    message = jax.ShapeDtypeStruct((ny + ny // 2, nz), jnp.float32)
    return pl.pallas_call(
        faces_kernel,
        out_shape=(
            jax.ShapeDtypeStruct(u.shape, jnp.float32),
            jax.ShapeDtypeStruct((comps, nx, ny, 2 * nz), jnp.bfloat16),
            message,
            message,
        ),
        in_specs=[HBM],
        out_specs=(VMEM,) * 4,
        scratch_shapes=[pltpu.VMEM((comps, ny, nz), jnp.float32), pltpu.SemaphoreType.DMA((comps, 4))],
        compiler_params=pltpu.CompilerParams(vmem_limit_bytes=37 << 20),
        cost_estimate=COST,
    )(u)


def stencil(far):
    one = jnp.where(far == 1, 8.0, 0.0) - jnp.where(far == -1, 8.0, 0.0)
    return (one - jnp.where(far == 2, 1.0, 0.0) + jnp.where(far == -2, 1.0, 0.0)).astype(jnp.bfloat16)


def shading(occupied_ref, floor, span, scale_ref, offset_ref):
    blocks, ny, nz = scale_ref.shape
    groups = ny // SUB
    mine = iota((ny, groups), 0) // SUB == iota((ny, groups), 1)
    shrink = 1.0 / span
    for block in range(blocks):
        row = occupied_ref[block : block + 1, :].astype(jnp.float32)
        column = jnp.sum(jnp.where(mine, row, 0.0), axis=1, keepdims=True)
        scale_ref[block] = jnp.broadcast_to(column * (shrink * (-1.0 / 144.0)), (ny, nz))
        offset_ref[block] = jnp.broadcast_to(column * (shrink * -floor), (ny, nz))


def lane_shift(x, nz, back):
    if isinstance(x, int):
        return (4 * x + 2 if back else 2 * nz - 2 - 4 * x) % nz
    return lax.rem(4 * x + 2 if back else 2 * nz - 2 - 4 * x, nz)


def slopes(parts_ref, x, tables, slope_ref):
    yleft_ref, yright_ref, dz_ref, dy_ref = tables
    comps, ny, nz = slope_ref.shape[2:]
    sub = iota((8, nz), 0)

    def top(left):
        return jnp.where(sub < 2, pltpu.roll(left, 2, 0) - jnp.where(sub == 0, 8.0 * pltpu.roll(left, 1, 0), 0.0), 0.0)

    def low(right):
        far = pltpu.roll(right, 6, 0)
        return jnp.where(sub >= 6, jnp.where(sub == 7, 8.0 * pltpu.roll(right, 7, 0), 0.0) - far, 0.0)

    parts = [[parts_ref[c, x + k] for k in range(2)] for c in range(comps)]
    depth = jnp.dot(
        jnp.concatenate([part for pair in parts for part in pair], axis=0),
        dz_ref[...],
        preferred_element_type=jnp.float32,
    )
    for c in range(comps):
        both = jnp.concatenate(
            [jnp.concatenate([part[:, half : half + nz] for part in parts[c]], axis=1) for half in (0, nz)], axis=0
        )
        down = jnp.dot(dy_ref[...], both, preferred_element_type=jnp.float32)
        for k in range(2):
            slope_ref[1, k, c] = depth[(2 * c + k) * ny : (2 * c + k + 1) * ny]
            mine = down[:, k * nz : (k + 1) * nz]
            slope_ref[0, k, c, pl.ds(0, 8), :] = mine[:8] + top(yleft_ref[c, x + k])
            slope_ref[0, k, c, pl.ds(8, ny - 16), :] = mine[8 : ny - 8]
            slope_ref[0, k, c, pl.ds(ny - 8, 8), :] = mine[ny - 8 :] + low(yright_ref[c, x + k])


def shade(u_ref, x, slope_ref, scale_ref, offset_ref, raw_ref, pack_ref, kept_ref=None, place=None):
    comps, nx, ny, nz = u_ref.shape
    block = x // SUB

    def difference(high, low):
        if high is None:
            return 0.0 if low is None else -low
        return high if low is None else high - low

    for y in range(0, ny, ROWS):
        rows = pl.ds(y, ROWS)
        slots = iota((ROWS, nz), 1) // 4
        across = []
        for c in range(comps):
            near = [
                u_ref[c, x + d, rows, :] if not isinstance(x, int) or 0 <= x + d < nx else None for d in range(-2, 4)
            ]
            across.append(
                [8.0 * difference(near[k + 3], near[k + 1]) - difference(near[k + 4], near[k]) for k in range(2)]
            )
        packs = [pack_ref[k, rows, :] for k in range(3)]
        for k in range(2):
            side = [across[c][k] for c in range(comps)]
            down = [slope_ref[0, k, c, rows, :] for c in range(comps)]
            depth = [slope_ref[1, k, c, rows, :] for c in range(comps)]
            total = 0.5 * (side[0] * side[0] + down[1] * down[1] + depth[2] * depth[2])
            total = total + side[1] * down[0] + side[2] * depth[0] + down[2] * depth[1]
            raw_ref[x + k, rows, :] = total * scale_ref[block, rows, :] + offset_ref[block, rows, :]
            back = lane_shift(x + k, nz, True)
            packs = [
                jnp.where(slots == x + k, pltpu.roll(values, back, 1), pack)
                for values, pack in zip((side[2], down[2], depth[2]), packs)
            ]
            if kept_ref is not None:
                for n, values in enumerate((side[0], down[0], depth[0])):
                    kept_ref[place + k, n, rows, :] = values
        for k in range(3):
            pack_ref[k, rows, :] = packs[k]


def edge_rows(nx):
    return (0, 1, nx - 2, nx - 1)


def shade_kernel(
    u_ref, parts_ref, yleft_ref, yright_ref, occupied_ref, floor_ref, span_ref,
    raw_ref, pack_ref, kept_ref, scale_ref, offset_ref, dz_ref, dy_ref, slope0_ref, slope1_ref,
):
    comps, nx, ny, nz = u_ref.shape
    dz_ref[...] = stencil(iota((2 * nz, nz), 0) % nz - iota((2 * nz, nz), 1))
    dy_ref[...] = stencil(iota((ny, 2 * ny), 1) % ny - iota((ny, 2 * ny), 0))
    shading(occupied_ref, floor_ref[...].reshape(1, 1), span_ref[...].reshape(1, 1), scale_ref, offset_ref)
    pack_ref[...] = jnp.zeros(pack_ref.shape, jnp.float32)
    tables = (yleft_ref, yright_ref, dz_ref, dy_ref)
    outs = (scale_ref, offset_ref, raw_ref, pack_ref)
    slopes(parts_ref, 0, tables, slope0_ref)
    slopes(parts_ref, 2, tables, slope1_ref)
    shade(u_ref, 0, slope0_ref, *outs, kept_ref, 0)

    def pairs(i, carry):
        x = 4 * i + 2
        slopes(parts_ref, x + 2, tables, slope0_ref)
        shade(u_ref, x, slope1_ref, *outs)
        slopes(parts_ref, x + 4, tables, slope1_ref)
        shade(u_ref, x + 2, slope0_ref, *outs)
        return carry

    lax.fori_loop(0, (nx - 4) // 4, pairs, 0)
    shade(u_ref, nx - 2, slope1_ref, *outs, kept_ref, 2)


def shaded(u, *rest):
    comps, nx, ny, nz = u.shape
    return pl.pallas_call(
        shade_kernel,
        out_shape=(
            jax.ShapeDtypeStruct((nx, ny, nz), jnp.float32),
            jax.ShapeDtypeStruct((comps, ny, nz), jnp.float32),
            jax.ShapeDtypeStruct((4, comps, ny, nz), jnp.float32),
            jax.ShapeDtypeStruct((nx // SUB, ny, nz), jnp.float32),
        ),
        in_specs=[VMEM] * 7,
        out_specs=(VMEM,) * 4,
        scratch_shapes=[
            pltpu.VMEM((nx // SUB, ny, nz), jnp.float32),
            pltpu.VMEM((2 * nz, nz), jnp.bfloat16),
            pltpu.VMEM((ny, 2 * ny), jnp.bfloat16),
            pltpu.VMEM((2, 2, comps, ny, nz), jnp.float32),
            pltpu.VMEM((2, 2, comps, ny, nz), jnp.float32),
        ],
        compiler_params=PARAMS,
        cost_estimate=COST,
    )(u, *rest)


def sides_deep(nx, ny, nz, zleft_ref, zright_ref):
    source, target = iota((2 * nz, nz), 0) % nz, iota((2 * nz, nz), 1)
    where = jnp.where(source // 4 == target // 4, source % 4 + 10 * (target % 4), -1)
    weights = jnp.zeros((2 * nz, nz), jnp.float32)
    for value, m, t in ((1.0, 0, 2), (-8.0, 1, 2), (1.0, 1, 3), (-1.0, 2, 0), (8.0, 2, 1), (-1.0, 3, 1)):
        weights = jnp.where(where == m + 10 * t, value, weights)
    weights = weights.astype(jnp.bfloat16)
    return [
        jnp.dot(jnp.concatenate(split(ghost), axis=1), weights, preferred_element_type=jnp.float32)
        for ghost in unfold(zleft_ref[...], zright_ref[...], ny, nz)
    ]


def on_border(packed, x, rows=None):
    ny, nz = packed.shape
    lane = iota((ny, nz), 1)
    return jnp.where((lane >= nz - 2) | (lane < 2), pltpu.roll(packed, lane_shift(x, nz, False), 1), 0.0)


def gather(density, raws, level_ref, sums_ref, sum_ref):
    parts = []
    for k, raw in enumerate(raws):
        level = jnp.clip(raw, 0.0, 1.0)
        level_ref[k] = level
        parts.append(jnp.concatenate(split((density / math.log(2.0)) * level), axis=1))
    ny, nz = level_ref.shape[1:]
    sums = jnp.dot(jnp.concatenate(parts, axis=0), sum_ref[...], preferred_element_type=jnp.float32)
    for k in range(len(raws)):
        sums_ref[k] = sums[k * ny : (k + 1) * ny]


def blend(level_ref, sums_ref, k, store):
    ny, nz = level_ref.shape[1:]
    lane_group = iota((8, ny), 1) // 8
    eye = iota((8, ny), 1) % 8 == iota((8, ny), 0)
    totals = [jnp.zeros((8, ny), jnp.float32)] * 3
    for group in range(ny // 8):
        rows = pl.ds(8 * group, 8)
        level = level_ref[k, rows, :]
        passing = jnp.exp2(sums_ref[k, rows, pl.ds(0, nz)])
        first = (passing - jnp.exp2(sums_ref[k, rows, pl.ds(nz, nz)])) * level
        red = jnp.sum(first, axis=1, keepdims=True)
        square = jnp.sum(first * level, axis=1, keepdims=True)
        whole = sums_ref[k, rows, pl.ds(2 * nz, ny)]
        totals = [jnp.where(lane_group == group, part, total) for part, total in zip((red, square, whole), totals)]
    red, square, whole = [jnp.sum(jnp.where(eye, total, 0.0), axis=0, keepdims=True) for total in totals]
    through = jnp.exp2(whole)
    store(red, 4.0 * (red - square), 1.0 - through - red, through)


def put(image_ref, x, slot=lambda view: view):
    per_view = image_ref.shape[2]
    view, row = (x // per_view, x % per_view) if isinstance(x, int) else (lax.div(x, per_view), lax.rem(x, per_view))

    def store(*channels):
        for k, values in enumerate(channels):
            image_ref[slot(view), k, pl.ds(row, 1), :] = values

    return store


def summing(sum_ref):
    nz = sum_ref.shape[0] // 2
    row = iota(sum_ref.shape, 0) % nz
    col = iota(sum_ref.shape, 1)
    sum_ref[...] = jnp.where((row < col) & (col < nz) | (row <= col - nz), -1.0, 0.0).astype(jnp.bfloat16)


def blend_kernel(
    density, raw_ref, pack_ref, scale_ref, zleft_ref, zright_ref,
    image_ref, fix_ref, first_ref, sum_ref, level0_ref, level1_ref, sums0_ref, sums1_ref,
):
    nx, ny, nz = raw_ref.shape
    summing(sum_ref)
    ghosts = sides_deep(nx, ny, nz, zleft_ref, zright_ref)
    first_ref[...] = ghosts[0]
    fix = ghosts[2] * (0.5 * ghosts[2] + pack_ref[2]) + ghosts[0] * pack_ref[0] + ghosts[1] * pack_ref[1]
    per_block = 4 * SUB
    lane_block = iota((ny, nz), 1) // per_block
    scale = scale_ref[0]
    for block in range(1, nx // SUB):
        scale = jnp.where(lane_block == block, scale_ref[block], scale)
    fix_ref[...] = fix * scale
    image_ref[...] = jnp.zeros(image_ref.shape, jnp.float32)
    batch = level0_ref.shape[0]

    def load(x, level_ref, sums_ref):
        raws = [raw_ref[x + k] + on_border(fix_ref[...], x + k) for k in range(batch)]
        gather(density, raws, level_ref, sums_ref, sum_ref)

    def mix(x, level_ref, sums_ref):
        for k in range(batch):
            blend(level_ref, sums_ref, k, put(image_ref, x + k))

    load(2, level0_ref, sums0_ref)

    def batches(i, carry):
        x = 2 * batch * i + 2
        load(x + batch, level1_ref, sums1_ref)
        mix(x, level0_ref, sums0_ref)
        load(x + 2 * batch, level0_ref, sums0_ref)
        mix(x + batch, level1_ref, sums1_ref)
        return carry

    count = (nx - 4) // batch
    lax.fori_loop(0, (count - 1) // 2, batches, 0)
    if count % 2 == 0:
        load(nx - 2 - batch, level1_ref, sums1_ref)
        mix(nx - 2 - 2 * batch, level0_ref, sums0_ref)
        mix(nx - 2 - batch, level1_ref, sums1_ref)
    else:
        mix(nx - 2 - batch, level0_ref, sums0_ref)


def row_tables(batch, ny, nz, buffers):
    return (
        [pltpu.VMEM((2 * nz, 2 * nz + ny), jnp.bfloat16)]
        + [pltpu.VMEM((batch, ny, nz), jnp.float32)] * buffers
        + [pltpu.VMEM((batch, ny, 2 * nz + ny), jnp.float32)] * buffers
    )


def blended(density, views, raw, *rest):
    nx, ny, nz = raw.shape
    return pl.pallas_call(
        functools.partial(blend_kernel, density),
        out_shape=(
            jax.ShapeDtypeStruct((views, 4, nx // views, ny), jnp.float32),
            jax.ShapeDtypeStruct((ny, nz), jnp.float32),
            jax.ShapeDtypeStruct((ny, nz), jnp.float32),
        ),
        in_specs=[VMEM] * 5,
        out_specs=(VMEM,) * 3,
        scratch_shapes=row_tables(4, ny, nz, 2),
        compiler_params=PARAMS,
        cost_estimate=COST,
    )(raw, *rest)


def edge_kernel(
    density, middle_ref, raw_ref, kept_ref, scale_ref, fix_ref, first_ref, xleft_ref, xright_ref,
    image_ref, sum_ref, level_ref, sums_ref,
):
    nx, ny, nz = raw_ref.shape
    summing(sum_ref)
    views = image_ref.shape[0]
    me = lax.axis_index("view")

    def slot(view):
        return step_to(me, view, views)

    for view in range(views):
        image_ref[slot(view)] = middle_ref[view]
    raws = []
    for place, x in enumerate(edge_rows(nx)):
        if place == 0:
            ghost = [xleft_ref[c, 0] - 8.0 * xleft_ref[c, 1] for c in range(3)]
        elif place == 1:
            ghost = [xleft_ref[c, 1] for c in range(3)]
        elif place == 2:
            ghost = [-xright_ref[c, 0] for c in range(3)]
        else:
            ghost = [8.0 * xright_ref[c, 0] - xright_ref[c, 1] for c in range(3)]
        depth = kept_ref[place, 2] + on_border(first_ref[...], x)
        more = ghost[0] * (0.5 * ghost[0] + kept_ref[place, 0]) + ghost[1] * kept_ref[place, 1] + ghost[2] * depth
        raws.append(raw_ref[x] + on_border(fix_ref[...], x) + more * scale_ref[x // SUB])
    gather(density, raws, level_ref, sums_ref, sum_ref)
    for place, x in enumerate(edge_rows(nx)):
        blend(level_ref, sums_ref, place, put(image_ref, x, slot))


def edged(density, middle, raw, *rest):
    nx, ny, nz = raw.shape
    return pl.pallas_call(
        functools.partial(edge_kernel, density),
        out_shape=jax.ShapeDtypeStruct(middle.shape, jnp.float32),
        in_specs=[VMEM] * 8,
        out_specs=VMEM,
        scratch_shapes=row_tables(4, ny, nz, 1),
        compiler_params=PARAMS,
        cost_estimate=COST,
    )(middle, raw, *rest)


def turn(block, axis, by):
    count = lax.axis_size(axis)
    return lax.ppermute(block, axis, [(i, (i + by) % count) for i in range(count)])


def both_sides(tail_head, axis):
    if lax.axis_size(axis) == 2:
        other = turn(tail_head, axis, 1)
        return other[0], other[1]
    return turn(tail_head[0], axis, 1), turn(tail_head[1], axis, -1)


def step_to(me, other, count):
    return me ^ other if count & (count - 1) == 0 else lax.rem(other - me + count, count)


def exchanged(blocks, axis):
    count = lax.axis_size(axis)
    paired = count & (count - 1) == 0
    found = [blocks[0]]
    for step in range(count - 1, 0, -1):
        route = [(i, i ^ step if paired else (i + step) % count) for i in range(count)]
        found.insert(1, lax.ppermute(blocks[step], axis, route))
    return found


def composite_kernel(*refs):
    *image_refs, out_ref = refs
    count = len(image_refs)
    me = lax.axis_index("view")
    if count & (count - 1) == 0:
        sources = [me ^ step for step in range(count)]
    else:
        sources = [lax.rem(me - step + count, count) for step in range(count)]
    colour = [0.0] * 3
    through = 1.0
    for source, image_ref in zip(sources, image_refs):
        passing = 1.0
        for other, front_ref in zip(sources, image_refs):
            passing = passing * jnp.where(other < source, front_ref[3], 1.0)
        colour = [total + passing * image_ref[k] for k, total in enumerate(colour)]
        through = through * image_ref[3]
    for k in range(3):
        out_ref[0, 0, k] = colour[k]
    out_ref[0, 0, 3] = 1.0 - through


def composited(images):
    return pl.pallas_call(
        composite_kernel,
        out_shape=jax.ShapeDtypeStruct((1, 1) + images[0].shape, jnp.float32),
        in_specs=[VMEM] * len(images),
        out_specs=VMEM,
        compiler_params=PARAMS,
        cost_estimate=COST,
    )(*images)


def local(velocity, occupied, q_floor, q_span):
    comps, nx, ny, nz = velocity.shape
    views = lax.axis_size("view")
    density = 5.0 / (nz * views)
    xtail, xhead, yface = ends(velocity)
    xleft = turn(xtail, "gx", 1)
    xright = turn(xhead, "gx", -1)
    u, parts, ztail, zhead = faces(velocity)
    zleft = turn(ztail, "view", 1)
    zright = turn(zhead, "view", -1)
    yleft, yright = both_sides(yface, "gy")
    raw, pack, kept, scale = shaded(u, parts, yleft, yright, occupied[:, :, 0], q_floor, q_span)
    middle, fix, first = blended(density, views, raw, pack, scale, zleft, zright)
    blocks = edged(density, middle, raw, kept, scale, fix, first, xleft, xright)
    return composited(exchanged(blocks, "view"))


def solution(mesh):
    placed = (P(None, "gx", "gy", "view"), P("gx", "gy", "view"), P(), P())
    return jax.shard_map(
        local,
        mesh=mesh,
        in_specs=placed,
        out_specs=P("gx", "gy", None, "view", None),
        check_vma=False,
    )
```

```python
import functools
import math

import jax
import jax.numpy as jnp
from jax import lax
from jax.experimental import pallas as pl
from jax.experimental.pallas import tpu as pltpu
from jax.sharding import PartitionSpec as P

SUB = 8
ROWS = 32
VMEM = pl.BlockSpec(memory_space=pltpu.VMEM)
HBM = pl.BlockSpec(memory_space=pltpu.HBM)
COST = pl.CostEstimate(flops=1 << 20, bytes_accessed=1 << 20, transcendentals=0)
PARAMS = pltpu.CompilerParams(vmem_limit_bytes=16 << 20)


def split(values):
    high = values.astype(jnp.bfloat16)
    low = (values - high.astype(jnp.float32)).astype(jnp.bfloat16)
    return high, low


def iota(shape, dim):
    return lax.broadcasted_iota(jnp.int32, shape, dim)


def ends_kernel(u_hbm, xtail_ref, xhead_ref, yface_ref, sems):
    _, nx, ny, _ = u_hbm.shape
    pieces = (
        (u_hbm.at[:, pl.ds(nx - 2, 2)], xtail_ref),
        (u_hbm.at[:, pl.ds(0, 2)], xhead_ref),
        (u_hbm.at[:, :, pl.ds(ny - 8, 8)], yface_ref.at[0]),
        (u_hbm.at[:, :, pl.ds(0, 8)], yface_ref.at[1]),
    )
    copies = [pltpu.make_async_copy(source, target, sems.at[k]) for k, (source, target) in enumerate(pieces)]
    for copy in copies:
        copy.start()
    for copy in copies:
        copy.wait()


def ends(u):
    comps, nx, ny, nz = u.shape
    layers = jax.ShapeDtypeStruct((comps, 2, ny, nz), jnp.float32)
    return pl.pallas_call(
        ends_kernel,
        out_shape=(layers, layers, jax.ShapeDtypeStruct((2, comps, nx, 8, nz), jnp.float32)),
        in_specs=[HBM],
        out_specs=(VMEM,) * 3,
        scratch_shapes=[pltpu.SemaphoreType.DMA((4,))],
        compiler_params=pltpu.CompilerParams(vmem_limit_bytes=50 << 20),
        cost_estimate=COST,
    )(u)


def faces_kernel(u_hbm, u_ref, parts_ref, tail_ref, head_ref, packed_ref, sems):
    comps, nx, ny, nz = u_ref.shape
    quarters = sems.shape[1]
    rows = ny // quarters

    def fetch(c, k):
        span = pl.ds(k * rows if isinstance(k, int) else pl.multiple_of(k * rows, rows), rows)
        return pltpu.make_async_copy(u_hbm.at[c, :, span], u_ref.at[c, :, span], sems.at[c, k])

    for c in range(comps):
        for k in range(quarters):
            fetch(c, k).start()
    slot = iota((8, nz), 1) // 4
    for c in range(comps):

        def quarter(k, carry):
            fetch(c, k).wait()
            start = pl.multiple_of(k * rows, rows)
            packed = [jnp.zeros((8, nz), jnp.float32)] * (rows // 8)
            for x in range(nx):
                cells = u_ref[c, x, pl.ds(start, rows), :]
                high, low = split(cells)
                parts_ref[c, x, pl.ds(start, rows), pl.ds(0, nz)] = high
                parts_ref[c, x, pl.ds(start, rows), pl.ds(nz, nz)] = low
                mine = slot == x
                for n in range(rows // 8):
                    packed[n] = jnp.where(mine, pltpu.roll(cells[8 * n : 8 * n + 8], (4 * x + 2) % nz, 1), packed[n])
            for n in range(rows // 8):
                packed_ref[c, pl.ds(pl.multiple_of(start + 8 * n, 8), 8), :] = packed[n]
            return carry

        lax.fori_loop(0, quarters, quarter, 0)
    tails, heads = fold([packed_ref[c] for c in range(comps)], ny, nz)
    tail_ref[...] = tails
    head_ref[...] = heads


def fold(packed, ny, nz):
    early = iota((ny, nz), 1) % 4 < 2
    early2 = early[: ny // 2]
    third, fourth = packed[2][: ny // 2], packed[2][ny // 2 :]
    tails = jnp.where(early, packed[0], pltpu.roll(packed[1], 2, 1))
    tails2 = jnp.where(early2, third, pltpu.roll(fourth, 2, 1))
    heads = jnp.where(early, pltpu.roll(packed[0], nz - 2, 1), packed[1])
    heads2 = jnp.where(early2, pltpu.roll(third, nz - 2, 1), fourth)
    return jnp.concatenate([tails, tails2], axis=0), jnp.concatenate([heads, heads2], axis=0)


def unfold(left, right, ny, nz):
    early = iota((ny, nz), 1) % 4 < 2
    early2 = early[: ny // 2]
    left2, right2 = left[ny:], right[ny:]
    left, right = left[:ny], right[:ny]
    first = jnp.where(early, left, pltpu.roll(right, 2, 1))
    second = jnp.where(early, pltpu.roll(left, nz - 2, 1), right)
    third = jnp.where(early2, left2, pltpu.roll(right2, 2, 1))
    fourth = jnp.where(early2, pltpu.roll(left2, nz - 2, 1), right2)
    return first, second, jnp.concatenate([third, fourth], axis=0)


def faces(u):
    comps, nx, ny, nz = u.shape
    message = jax.ShapeDtypeStruct((ny + ny // 2, nz), jnp.float32)
    return pl.pallas_call(
        faces_kernel,
        out_shape=(
            jax.ShapeDtypeStruct(u.shape, jnp.float32),
            jax.ShapeDtypeStruct((comps, nx, ny, 2 * nz), jnp.bfloat16),
            message,
            message,
        ),
        in_specs=[HBM],
        out_specs=(VMEM,) * 4,
        scratch_shapes=[pltpu.VMEM((comps, ny, nz), jnp.float32), pltpu.SemaphoreType.DMA((comps, 4))],
        compiler_params=pltpu.CompilerParams(vmem_limit_bytes=37 << 20),
        cost_estimate=COST,
    )(u)


def stencil(far):
    one = jnp.where(far == 1, 8.0, 0.0) - jnp.where(far == -1, 8.0, 0.0)
    return (one - jnp.where(far == 2, 1.0, 0.0) + jnp.where(far == -2, 1.0, 0.0)).astype(jnp.bfloat16)


def shading(occupied_ref, floor, span, scale_ref, offset_ref):
    blocks, ny, nz = scale_ref.shape
    groups = ny // SUB
    mine = iota((ny, groups), 0) // SUB == iota((ny, groups), 1)
    shrink = 1.0 / span
    for block in range(blocks):
        row = occupied_ref[block : block + 1, :].astype(jnp.float32)
        column = jnp.sum(jnp.where(mine, row, 0.0), axis=1, keepdims=True)
        scale_ref[block] = jnp.broadcast_to(column * (shrink * (-1.0 / 144.0)), (ny, nz))
        offset_ref[block] = jnp.broadcast_to(column * (shrink * -floor), (ny, nz))


def lane_shift(x, nz, back):
    if isinstance(x, int):
        return (4 * x + 2 if back else 2 * nz - 2 - 4 * x) % nz
    return lax.rem(4 * x + 2 if back else 2 * nz - 2 - 4 * x, nz)


def slopes(parts_ref, x, tables, slope_ref):
    yleft_ref, yright_ref, dz_ref, dy_ref = tables
    comps, ny, nz = slope_ref.shape[2:]
    sub = iota((8, nz), 0)

    def top(left):
        return jnp.where(sub < 2, pltpu.roll(left, 2, 0) - jnp.where(sub == 0, 8.0 * pltpu.roll(left, 1, 0), 0.0), 0.0)

    def low(right):
        far = pltpu.roll(right, 6, 0)
        return jnp.where(sub >= 6, jnp.where(sub == 7, 8.0 * pltpu.roll(right, 7, 0), 0.0) - far, 0.0)

    parts = [[parts_ref[c, x + k] for k in range(2)] for c in range(comps)]
    depth = jnp.dot(
        jnp.concatenate([part for pair in parts for part in pair], axis=0),
        dz_ref[...],
        preferred_element_type=jnp.float32,
    )
    for c in range(comps):
        both = jnp.concatenate(
            [jnp.concatenate([part[:, half : half + nz] for part in parts[c]], axis=1) for half in (0, nz)], axis=0
        )
        down = jnp.dot(dy_ref[...], both, preferred_element_type=jnp.float32)
        for k in range(2):
            slope_ref[1, k, c] = depth[(2 * c + k) * ny : (2 * c + k + 1) * ny]
            mine = down[:, k * nz : (k + 1) * nz]
            slope_ref[0, k, c, pl.ds(0, 8), :] = mine[:8] + top(yleft_ref[c, x + k])
            slope_ref[0, k, c, pl.ds(8, ny - 16), :] = mine[8 : ny - 8]
            slope_ref[0, k, c, pl.ds(ny - 8, 8), :] = mine[ny - 8 :] + low(yright_ref[c, x + k])


def shade(u_ref, x, slope_ref, scale_ref, offset_ref, raw_ref, pack_ref, kept_ref=None, place=None):
    comps, nx, ny, nz = u_ref.shape
    block = x // SUB

    def difference(high, low):
        if high is None:
            return 0.0 if low is None else -low
        return high if low is None else high - low

    for y in range(0, ny, ROWS):
        rows = pl.ds(y, ROWS)
        slots = iota((ROWS, nz), 1) // 4
        across = []
        for c in range(comps):
            near = [
                u_ref[c, x + d, rows, :] if not isinstance(x, int) or 0 <= x + d < nx else None for d in range(-2, 4)
            ]
            across.append(
                [8.0 * difference(near[k + 3], near[k + 1]) - difference(near[k + 4], near[k]) for k in range(2)]
            )
        packs = [pack_ref[k, rows, :] for k in range(3)]
        for k in range(2):
            side = [across[c][k] for c in range(comps)]
            down = [slope_ref[0, k, c, rows, :] for c in range(comps)]
            depth = [slope_ref[1, k, c, rows, :] for c in range(comps)]
            total = 0.5 * (side[0] * side[0] + down[1] * down[1] + depth[2] * depth[2])
            total = total + side[1] * down[0] + side[2] * depth[0] + down[2] * depth[1]
            raw_ref[x + k, rows, :] = total * scale_ref[block, rows, :] + offset_ref[block, rows, :]
            back = lane_shift(x + k, nz, True)
            packs = [
                jnp.where(slots == x + k, pltpu.roll(values, back, 1), pack)
                for values, pack in zip((side[2], down[2], depth[2]), packs)
            ]
            if kept_ref is not None:
                for n, values in enumerate((side[0], down[0], depth[0])):
                    kept_ref[place + k, n, rows, :] = values
        for k in range(3):
            pack_ref[k, rows, :] = packs[k]


def edge_rows(nx):
    return (0, 1, nx - 2, nx - 1)


def shade_kernel(
    u_ref, parts_ref, yleft_ref, yright_ref, occupied_ref, floor_ref, span_ref,
    raw_ref, pack_ref, kept_ref, scale_ref, offset_ref, dz_ref, dy_ref, slope0_ref, slope1_ref,
):
    comps, nx, ny, nz = u_ref.shape
    dz_ref[...] = stencil(iota((2 * nz, nz), 0) % nz - iota((2 * nz, nz), 1))
    dy_ref[...] = stencil(iota((ny, 2 * ny), 1) % ny - iota((ny, 2 * ny), 0))
    shading(occupied_ref, floor_ref[...].reshape(1, 1), span_ref[...].reshape(1, 1), scale_ref, offset_ref)
    pack_ref[...] = jnp.zeros(pack_ref.shape, jnp.float32)
    tables = (yleft_ref, yright_ref, dz_ref, dy_ref)
    outs = (scale_ref, offset_ref, raw_ref, pack_ref)
    slopes(parts_ref, 0, tables, slope0_ref)
    slopes(parts_ref, 2, tables, slope1_ref)
    shade(u_ref, 0, slope0_ref, *outs, kept_ref, 0)

    def pairs(i, carry):
        x = 4 * i + 2
        slopes(parts_ref, x + 2, tables, slope0_ref)
        shade(u_ref, x, slope1_ref, *outs)
        slopes(parts_ref, x + 4, tables, slope1_ref)
        shade(u_ref, x + 2, slope0_ref, *outs)
        return carry

    lax.fori_loop(0, (nx - 4) // 4, pairs, 0)
    shade(u_ref, nx - 2, slope1_ref, *outs, kept_ref, 2)


def shaded(u, *rest):
    comps, nx, ny, nz = u.shape
    return pl.pallas_call(
        shade_kernel,
        out_shape=(
            jax.ShapeDtypeStruct((nx, ny, nz), jnp.float32),
            jax.ShapeDtypeStruct((comps, ny, nz), jnp.float32),
            jax.ShapeDtypeStruct((4, comps, ny, nz), jnp.float32),
            jax.ShapeDtypeStruct((nx // SUB, ny, nz), jnp.float32),
        ),
        in_specs=[VMEM] * 7,
        out_specs=(VMEM,) * 4,
        scratch_shapes=[
            pltpu.VMEM((nx // SUB, ny, nz), jnp.float32),
            pltpu.VMEM((2 * nz, nz), jnp.bfloat16),
            pltpu.VMEM((ny, 2 * ny), jnp.bfloat16),
            pltpu.VMEM((2, 2, comps, ny, nz), jnp.float32),
            pltpu.VMEM((2, 2, comps, ny, nz), jnp.float32),
        ],
        compiler_params=PARAMS,
        cost_estimate=COST,
    )(u, *rest)


def sides_deep(nx, ny, nz, zleft_ref, zright_ref):
    source, target = iota((2 * nz, nz), 0) % nz, iota((2 * nz, nz), 1)
    where = jnp.where(source // 4 == target // 4, source % 4 + 10 * (target % 4), -1)
    weights = jnp.zeros((2 * nz, nz), jnp.float32)
    for value, m, t in ((1.0, 0, 2), (-8.0, 1, 2), (1.0, 1, 3), (-1.0, 2, 0), (8.0, 2, 1), (-1.0, 3, 1)):
        weights = jnp.where(where == m + 10 * t, value, weights)
    weights = weights.astype(jnp.bfloat16)
    return [
        jnp.dot(jnp.concatenate(split(ghost), axis=1), weights, preferred_element_type=jnp.float32)
        for ghost in unfold(zleft_ref[...], zright_ref[...], ny, nz)
    ]


def on_border(packed, x, rows=None):
    ny, nz = packed.shape
    lane = iota((ny, nz), 1)
    return jnp.where((lane >= nz - 2) | (lane < 2), pltpu.roll(packed, lane_shift(x, nz, False), 1), 0.0)


def gather(density, raws, level_ref, sums_ref, sum_ref):
    parts = []
    for k, raw in enumerate(raws):
        level = jnp.clip(raw, 0.0, 1.0)
        level_ref[k] = level
        parts.append(jnp.concatenate(split((density / math.log(2.0)) * level), axis=1))
    ny, nz = level_ref.shape[1:]
    sums = jnp.dot(jnp.concatenate(parts, axis=0), sum_ref[...], preferred_element_type=jnp.float32)
    for k in range(len(raws)):
        sums_ref[k] = sums[k * ny : (k + 1) * ny]


def blend(level_ref, sums_ref, k, store):
    ny, nz = level_ref.shape[1:]
    lane_group = iota((8, ny), 1) // 8
    eye = iota((8, ny), 1) % 8 == iota((8, ny), 0)
    totals = [jnp.zeros((8, ny), jnp.float32)] * 3
    for group in range(ny // 8):
        rows = pl.ds(8 * group, 8)
        level = level_ref[k, rows, :]
        passing = jnp.exp2(sums_ref[k, rows, pl.ds(0, nz)])
        first = (passing - jnp.exp2(sums_ref[k, rows, pl.ds(nz, nz)])) * level
        red = jnp.sum(first, axis=1, keepdims=True)
        square = jnp.sum(first * level, axis=1, keepdims=True)
        whole = sums_ref[k, rows, pl.ds(2 * nz, ny)]
        totals = [jnp.where(lane_group == group, part, total) for part, total in zip((red, square, whole), totals)]
    red, square, whole = [jnp.sum(jnp.where(eye, total, 0.0), axis=0, keepdims=True) for total in totals]
    through = jnp.exp2(whole)
    store(red, 4.0 * (red - square), 1.0 - through - red, through)


def put(image_ref, x, slot=lambda view: view):
    per_view = image_ref.shape[2]
    view, row = (x // per_view, x % per_view) if isinstance(x, int) else (lax.div(x, per_view), lax.rem(x, per_view))

    def store(*channels):
        for k, values in enumerate(channels):
            image_ref[slot(view), k, pl.ds(row, 1), :] = values

    return store


def summing(sum_ref):
    nz = sum_ref.shape[0] // 2
    row = iota(sum_ref.shape, 0) % nz
    col = iota(sum_ref.shape, 1)
    sum_ref[...] = jnp.where((row < col) & (col < nz) | (row <= col - nz), -1.0, 0.0).astype(jnp.bfloat16)


def blend_kernel(
    density, raw_ref, pack_ref, scale_ref, zleft_ref, zright_ref,
    image_ref, fix_ref, first_ref, sum_ref, level0_ref, level1_ref, sums0_ref, sums1_ref,
):
    nx, ny, nz = raw_ref.shape
    summing(sum_ref)
    ghosts = sides_deep(nx, ny, nz, zleft_ref, zright_ref)
    first_ref[...] = ghosts[0]
    fix = ghosts[2] * (0.5 * ghosts[2] + pack_ref[2]) + ghosts[0] * pack_ref[0] + ghosts[1] * pack_ref[1]
    per_block = 4 * SUB
    lane_block = iota((ny, nz), 1) // per_block
    scale = scale_ref[0]
    for block in range(1, nx // SUB):
        scale = jnp.where(lane_block == block, scale_ref[block], scale)
    fix_ref[...] = fix * scale
    image_ref[...] = jnp.zeros(image_ref.shape, jnp.float32)
    batch = level0_ref.shape[0]

    def load(x, level_ref, sums_ref):
        raws = [raw_ref[x + k] + on_border(fix_ref[...], x + k) for k in range(batch)]
        gather(density, raws, level_ref, sums_ref, sum_ref)

    def mix(x, level_ref, sums_ref):
        for k in range(batch):
            blend(level_ref, sums_ref, k, put(image_ref, x + k))

    load(2, level0_ref, sums0_ref)

    def batches(i, carry):
        x = 2 * batch * i + 2
        load(x + batch, level1_ref, sums1_ref)
        mix(x, level0_ref, sums0_ref)
        load(x + 2 * batch, level0_ref, sums0_ref)
        mix(x + batch, level1_ref, sums1_ref)
        return carry

    count = (nx - 4) // batch
    lax.fori_loop(0, (count - 1) // 2, batches, 0)
    if count % 2 == 0:
        load(nx - 2 - batch, level1_ref, sums1_ref)
        mix(nx - 2 - 2 * batch, level0_ref, sums0_ref)
        mix(nx - 2 - batch, level1_ref, sums1_ref)
    else:
        mix(nx - 2 - batch, level0_ref, sums0_ref)


def row_tables(batch, ny, nz, buffers):
    return (
        [pltpu.VMEM((2 * nz, 2 * nz + ny), jnp.bfloat16)]
        + [pltpu.VMEM((batch, ny, nz), jnp.float32)] * buffers
        + [pltpu.VMEM((batch, ny, 2 * nz + ny), jnp.float32)] * buffers
    )


def blended(density, views, raw, *rest):
    nx, ny, nz = raw.shape
    return pl.pallas_call(
        functools.partial(blend_kernel, density),
        out_shape=(
            jax.ShapeDtypeStruct((views, 4, nx // views, ny), jnp.float32),
            jax.ShapeDtypeStruct((ny, nz), jnp.float32),
            jax.ShapeDtypeStruct((ny, nz), jnp.float32),
        ),
        in_specs=[VMEM] * 5,
        out_specs=(VMEM,) * 3,
        scratch_shapes=row_tables(4, ny, nz, 2),
        compiler_params=PARAMS,
        cost_estimate=COST,
    )(raw, *rest)


def edge_kernel(
    density, raw_ref, kept_ref, scale_ref, fix_ref, first_ref, xleft_ref, xright_ref,
    own_ref, *refs,
):
    *sent_refs, sum_ref, level_ref, sums_ref = refs
    nx, ny, nz = raw_ref.shape
    summing(sum_ref)
    raws = []
    for place, x in enumerate(edge_rows(nx)):
        if place == 0:
            ghost = [xleft_ref[c, 0] - 8.0 * xleft_ref[c, 1] for c in range(3)]
        elif place == 1:
            ghost = [xleft_ref[c, 1] for c in range(3)]
        elif place == 2:
            ghost = [-xright_ref[c, 0] for c in range(3)]
        else:
            ghost = [8.0 * xright_ref[c, 0] - xright_ref[c, 1] for c in range(3)]
        depth = kept_ref[place, 2] + on_border(first_ref[...], x)
        more = ghost[0] * (0.5 * ghost[0] + kept_ref[place, 0]) + ghost[1] * kept_ref[place, 1] + ghost[2] * depth
        raws.append(raw_ref[x] + on_border(fix_ref[...], x) + more * scale_ref[x // SUB])
    gather(density, raws, level_ref, sums_ref, sum_ref)

    def put_edge(place):
        def store(*channels):
            for k, values in enumerate(channels):
                own_ref[place // 2, pl.ds(2 * k + place % 2, 1), :] = values

        return store

    for place in range(4):
        blend(level_ref, sums_ref, place, put_edge(place))
    me = lax.axis_index("view")
    for step, sent_ref in enumerate(sent_refs, 1):
        sent_ref[...] = jnp.where(me == step, own_ref[0], own_ref[1])


def edged(density, raw, *rest, views):
    nx, ny, nz = raw.shape
    rows = jax.ShapeDtypeStruct((8, ny), jnp.float32)
    return pl.pallas_call(
        functools.partial(edge_kernel, density),
        out_shape=(jax.ShapeDtypeStruct((2, 8, ny), jnp.float32),) + (rows,) * (views - 1),
        in_specs=[VMEM] * 7,
        out_specs=(VMEM,) * views,
        scratch_shapes=row_tables(4, ny, nz, 1),
        compiler_params=PARAMS,
        cost_estimate=COST,
    )(raw, *rest)


def turn(block, axis, by):
    count = lax.axis_size(axis)
    return lax.ppermute(block, axis, [(i, (i + by) % count) for i in range(count)])


def both_sides(tail_head, axis):
    if lax.axis_size(axis) == 2:
        other = turn(tail_head, axis, 1)
        return other[0], other[1]
    return turn(tail_head[0], axis, 1), turn(tail_head[1], axis, -1)


def owners_edges(sent, views):
    found = []
    for step, rows in enumerate(sent, 1):
        mirror = views - 1 - step
        if mirror == step:
            received = [lax.ppermute(rows, "view", [(step, owner)]) for owner in (0, views - 1)]
            found.append(jnp.where(lax.axis_index("view") == 0, *received))
        else:
            found.append(lax.ppermute(rows, "view", [(step, 0), (mirror, views - 1)]))
    return found


def composite(images):
    colour, through = images[0][:3], images[0][3]
    for image in images[1:]:
        colour = [front + through * behind for front, behind in zip(colour, image[:3])]
        through = through * image[3]
    return [*colour, 1.0 - through]


def inside_kernel(gathered_hbm, out_ref, images_ref, sem):
    copy = pltpu.make_async_copy(gathered_hbm.at[:, lax.axis_index("view")], images_ref, sem)
    copy.start()
    copy.wait()
    block = composite([[images_ref[view, k] for k in range(4)] for view in range(images_ref.shape[0])])
    for k in range(4):
        out_ref[k] = block[k]


def inside(gathered):
    views, _, channels, rows, ny = gathered.shape
    return pl.pallas_call(
        inside_kernel,
        out_shape=jax.ShapeDtypeStruct((channels, rows, ny), jnp.float32),
        in_specs=[HBM],
        out_specs=VMEM,
        scratch_shapes=[pltpu.VMEM((views, channels, rows, ny), jnp.float32), pltpu.SemaphoreType.DMA],
        compiler_params=pltpu.CompilerParams(vmem_limit_bytes=54 << 20),
        cost_estimate=COST,
    )(gathered)


def finish_kernel(block_ref, own_ref, *refs):
    *edge_refs, out_ref = refs
    _, rows, ny = block_ref.shape
    views = len(edge_refs) + 1
    me = lax.axis_index("view")
    out_ref[0, 0] = block_ref[...]

    def channels(values):
        return [values[2 * k : 2 * k + 2] for k in range(4)]

    for owner, order, place in (
        (0, [own_ref[0]] + [ref[...] for ref in edge_refs], 0),
        (views - 1, [ref[...] for ref in edge_refs[::-1]] + [own_ref[1]], rows - 2),
    ):

        @pl.when(me == owner)
        def _():
            for k, values in enumerate(composite([channels(values) for values in order])):
                out_ref[0, 0, k, pl.ds(place, 2), :] = values


def finished(block, own, edges):
    return pl.pallas_call(
        finish_kernel,
        out_shape=jax.ShapeDtypeStruct((1, 1) + block.shape, jnp.float32),
        in_specs=[VMEM] * (2 + len(edges)),
        out_specs=VMEM,
        compiler_params=PARAMS,
        cost_estimate=COST,
    )(block, own, *edges)


def local(velocity, occupied, q_floor, q_span):
    comps, nx, ny, nz = velocity.shape
    views = lax.axis_size("view")
    density = 5.0 / (nz * views)
    xtail, xhead, yface = ends(velocity)
    xleft = turn(xtail, "gx", 1)
    xright = turn(xhead, "gx", -1)
    u, parts, ztail, zhead = faces(velocity)
    zleft = turn(ztail, "view", 1)
    zright = turn(zhead, "view", -1)
    yleft, yright = both_sides(yface, "gy")
    raw, pack, kept, scale = shaded(u, parts, yleft, yright, occupied[:, :, 0], q_floor, q_span)
    middle, fix, first = blended(density, views, raw, pack, scale, zleft, zright)
    gathered = lax.all_gather(middle, "view")
    own, *sent = edged(density, raw, kept, scale, fix, first, xleft, xright, views=views)
    return finished(inside(gathered), own, owners_edges(sent, views))


def solution(mesh):
    placed = (P(None, "gx", "gy", "view"), P("gx", "gy", "view"), P(), P())
    return jax.shard_map(
        local,
        mesh=mesh,
        in_specs=placed,
        out_specs=P("gx", "gy", None, "view", None),
        check_vma=False,
    )
```

```python
import functools
import math

import jax
import jax.numpy as jnp
from jax import lax
from jax.experimental import pallas as pl
from jax.experimental.pallas import tpu as pltpu
from jax.sharding import PartitionSpec as P

SUB = 8
ROWS = 32
VMEM = pl.BlockSpec(memory_space=pltpu.VMEM)
HBM = pl.BlockSpec(memory_space=pltpu.HBM)
COST = pl.CostEstimate(flops=1 << 20, bytes_accessed=1 << 20, transcendentals=0)
PARAMS = pltpu.CompilerParams(vmem_limit_bytes=16 << 20)


def split(values):
    high = values.astype(jnp.bfloat16)
    low = (values - high.astype(jnp.float32)).astype(jnp.bfloat16)
    return high, low


def iota(shape, dim):
    return lax.broadcasted_iota(jnp.int32, shape, dim)


def ends_kernel(u_hbm, xtail_ref, xhead_ref, yface_ref, sems):
    _, nx, ny, _ = u_hbm.shape
    pieces = (
        (u_hbm.at[:, pl.ds(nx - 2, 2)], xtail_ref),
        (u_hbm.at[:, pl.ds(0, 2)], xhead_ref),
        (u_hbm.at[:, :, pl.ds(ny - 2, 2)], yface_ref.at[:, :, pl.ds(6, 2)]),
        (u_hbm.at[:, :, pl.ds(0, 2)], yface_ref.at[:, :, pl.ds(0, 2)]),
    )
    copies = [pltpu.make_async_copy(source, target, sems.at[k]) for k, (source, target) in enumerate(pieces)]
    for copy in copies:
        copy.start()
    for copy in copies:
        copy.wait()


def ends(u):
    comps, nx, ny, nz = u.shape
    layers = jax.ShapeDtypeStruct((comps, 2, ny, nz), jnp.float32)
    return pl.pallas_call(
        ends_kernel,
        out_shape=(layers, layers, jax.ShapeDtypeStruct((comps, nx, 8, nz), jnp.float32)),
        in_specs=[HBM],
        out_specs=(VMEM,) * 3,
        scratch_shapes=[pltpu.SemaphoreType.DMA((4,))],
        compiler_params=pltpu.CompilerParams(vmem_limit_bytes=50 << 20),
        cost_estimate=COST,
    )(u)


def faces_kernel(u_hbm, u_ref, parts_ref, tail_ref, head_ref, packed_ref, sems):
    comps, nx, ny, nz = u_ref.shape
    quarters = sems.shape[1]
    rows = ny // quarters

    def fetch(c, k):
        span = pl.ds(k * rows if isinstance(k, int) else pl.multiple_of(k * rows, rows), rows)
        return pltpu.make_async_copy(u_hbm.at[c, :, span], u_ref.at[c, :, span], sems.at[c, k])

    for c in range(comps):
        for k in range(quarters):
            fetch(c, k).start()
    slot = iota((8, nz), 1) // 4
    for c in range(comps):

        def quarter(k, carry):
            fetch(c, k).wait()
            start = pl.multiple_of(k * rows, rows)
            packed = [jnp.zeros((8, nz), jnp.float32)] * (rows // 8)
            for x in range(nx):
                cells = u_ref[c, x, pl.ds(start, rows), :]
                high, low = split(cells)
                parts_ref[c, x, pl.ds(start, rows), pl.ds(0, nz)] = high
                parts_ref[c, x, pl.ds(start, rows), pl.ds(nz, nz)] = low
                mine = slot == x
                for n in range(rows // 8):
                    packed[n] = jnp.where(mine, pltpu.roll(cells[8 * n : 8 * n + 8], (4 * x + 2) % nz, 1), packed[n])
            for n in range(rows // 8):
                packed_ref[c, pl.ds(pl.multiple_of(start + 8 * n, 8), 8), :] = packed[n]
            return carry

        lax.fori_loop(0, quarters, quarter, 0)
    tails, heads = fold([packed_ref[c] for c in range(comps)], ny, nz)
    tail_ref[...] = tails
    head_ref[...] = heads


def fold(packed, ny, nz):
    early = iota((ny, nz), 1) % 4 < 2
    early2 = early[: ny // 2]
    third, fourth = packed[2][: ny // 2], packed[2][ny // 2 :]
    tails = jnp.where(early, packed[0], pltpu.roll(packed[1], 2, 1))
    tails2 = jnp.where(early2, third, pltpu.roll(fourth, 2, 1))
    heads = jnp.where(early, pltpu.roll(packed[0], nz - 2, 1), packed[1])
    heads2 = jnp.where(early2, pltpu.roll(third, nz - 2, 1), fourth)
    return jnp.concatenate([tails, tails2], axis=0), jnp.concatenate([heads, heads2], axis=0)


def unfold(left, right, ny, nz):
    early = iota((ny, nz), 1) % 4 < 2
    early2 = early[: ny // 2]
    left2, right2 = left[ny:], right[ny:]
    left, right = left[:ny], right[:ny]
    first = jnp.where(early, left, pltpu.roll(right, 2, 1))
    second = jnp.where(early, pltpu.roll(left, nz - 2, 1), right)
    third = jnp.where(early2, left2, pltpu.roll(right2, 2, 1))
    fourth = jnp.where(early2, pltpu.roll(left2, nz - 2, 1), right2)
    return first, second, jnp.concatenate([third, fourth], axis=0)


def faces(u):
    comps, nx, ny, nz = u.shape
    message = jax.ShapeDtypeStruct((ny + ny // 2, nz), jnp.float32)
    return pl.pallas_call(
        faces_kernel,
        out_shape=(
            jax.ShapeDtypeStruct(u.shape, jnp.float32),
            jax.ShapeDtypeStruct((comps, nx, ny, 2 * nz), jnp.bfloat16),
            message,
            message,
        ),
        in_specs=[HBM],
        out_specs=(VMEM,) * 4,
        scratch_shapes=[pltpu.VMEM((comps, ny, nz), jnp.float32), pltpu.SemaphoreType.DMA((comps, 4))],
        compiler_params=pltpu.CompilerParams(vmem_limit_bytes=37 << 20),
        cost_estimate=COST,
    )(u)


def stencil(far):
    one = jnp.where(far == 1, 8.0, 0.0) - jnp.where(far == -1, 8.0, 0.0)
    return (one - jnp.where(far == 2, 1.0, 0.0) + jnp.where(far == -2, 1.0, 0.0)).astype(jnp.bfloat16)


def shading(occupied_ref, floor, span, scale_ref, offset_ref):
    blocks, ny, nz = scale_ref.shape
    groups = ny // SUB
    mine = iota((ny, groups), 0) // SUB == iota((ny, groups), 1)
    shrink = 1.0 / span
    for block in range(blocks):
        row = occupied_ref[block : block + 1, :].astype(jnp.float32)
        column = jnp.sum(jnp.where(mine, row, 0.0), axis=1, keepdims=True)
        scale_ref[block] = jnp.broadcast_to(column * (shrink * (-1.0 / 144.0)), (ny, nz))
        offset_ref[block] = jnp.broadcast_to(column * (shrink * -floor), (ny, nz))


def lane_shift(x, nz, back):
    if isinstance(x, int):
        return (4 * x + 2 if back else 2 * nz - 2 - 4 * x) % nz
    return lax.rem(4 * x + 2 if back else 2 * nz - 2 - 4 * x, nz)


def slopes(parts_ref, x, tables, slope_ref):
    yleft_ref, yright_ref, dz_ref, dy_ref = tables
    comps, ny, nz = slope_ref.shape[2:]
    sub = iota((8, nz), 0)

    def top(left):
        return jnp.where(sub < 2, pltpu.roll(left, 2, 0) - jnp.where(sub == 0, 8.0 * pltpu.roll(left, 1, 0), 0.0), 0.0)

    def low(right):
        far = pltpu.roll(right, 6, 0)
        return jnp.where(sub >= 6, jnp.where(sub == 7, 8.0 * pltpu.roll(right, 7, 0), 0.0) - far, 0.0)

    parts = [[parts_ref[c, x + k] for k in range(2)] for c in range(comps)]
    depth = jnp.dot(
        jnp.concatenate([part for pair in parts for part in pair], axis=0),
        dz_ref[...],
        preferred_element_type=jnp.float32,
    )
    for c in range(comps):
        both = jnp.concatenate(
            [jnp.concatenate([part[:, half : half + nz] for part in parts[c]], axis=1) for half in (0, nz)], axis=0
        )
        down = jnp.dot(dy_ref[...], both, preferred_element_type=jnp.float32)
        for k in range(2):
            slope_ref[1, k, c] = depth[(2 * c + k) * ny : (2 * c + k + 1) * ny]
            mine = down[:, k * nz : (k + 1) * nz]
            slope_ref[0, k, c, pl.ds(0, 8), :] = mine[:8] + top(yleft_ref[c, x + k])
            slope_ref[0, k, c, pl.ds(8, ny - 16), :] = mine[8 : ny - 8]
            slope_ref[0, k, c, pl.ds(ny - 8, 8), :] = mine[ny - 8 :] + low(yright_ref[c, x + k])


def shade(u_ref, x, slope_ref, scale_ref, offset_ref, raw_ref, pack_ref, kept_ref=None, place=None):
    comps, nx, ny, nz = u_ref.shape
    block = x // SUB

    def difference(high, low):
        if high is None:
            return 0.0 if low is None else -low
        return high if low is None else high - low

    for y in range(0, ny, ROWS):
        rows = pl.ds(y, ROWS)
        slots = iota((ROWS, nz), 1) // 4
        across = []
        for c in range(comps):
            near = [
                u_ref[c, x + d, rows, :] if not isinstance(x, int) or 0 <= x + d < nx else None for d in range(-2, 4)
            ]
            across.append(
                [8.0 * difference(near[k + 3], near[k + 1]) - difference(near[k + 4], near[k]) for k in range(2)]
            )
        packs = [pack_ref[k, rows, :] for k in range(3)]
        for k in range(2):
            side = [across[c][k] for c in range(comps)]
            down = [slope_ref[0, k, c, rows, :] for c in range(comps)]
            depth = [slope_ref[1, k, c, rows, :] for c in range(comps)]
            total = 0.5 * (side[0] * side[0] + down[1] * down[1] + depth[2] * depth[2])
            total = total + side[1] * down[0] + side[2] * depth[0] + down[2] * depth[1]
            raw_ref[x + k, rows, :] = total * scale_ref[block, rows, :] + offset_ref[block, rows, :]
            back = lane_shift(x + k, nz, True)
            packs = [
                jnp.where(slots == x + k, pltpu.roll(values, back, 1), pack)
                for values, pack in zip((side[2], down[2], depth[2]), packs)
            ]
            if kept_ref is not None:
                for n, values in enumerate((side[0], down[0], depth[0])):
                    kept_ref[place + k, n, rows, :] = values
        for k in range(3):
            pack_ref[k, rows, :] = packs[k]


def shade_kernel(
    u_ref, parts_ref, yleft_ref, yright_ref, occupied_ref, floor_ref, span_ref,
    raw_ref, pack_ref, kept_ref, scale_ref, offset_ref, dz_ref, dy_ref, slope0_ref, slope1_ref,
):
    comps, nx, ny, nz = u_ref.shape
    dz_ref[...] = stencil(iota((2 * nz, nz), 0) % nz - iota((2 * nz, nz), 1))
    dy_ref[...] = stencil(iota((ny, 2 * ny), 1) % ny - iota((ny, 2 * ny), 0))
    shading(occupied_ref, floor_ref[...].reshape(1, 1), span_ref[...].reshape(1, 1), scale_ref, offset_ref)
    pack_ref[...] = jnp.zeros(pack_ref.shape, jnp.float32)
    tables = (yleft_ref, yright_ref, dz_ref, dy_ref)
    outs = (scale_ref, offset_ref, raw_ref, pack_ref)
    slopes(parts_ref, 0, tables, slope0_ref)
    slopes(parts_ref, 2, tables, slope1_ref)
    shade(u_ref, 0, slope0_ref, *outs, kept_ref, 0)

    def pairs(i, carry):
        x = 4 * i + 2
        slopes(parts_ref, x + 2, tables, slope0_ref)
        shade(u_ref, x, slope1_ref, *outs)
        slopes(parts_ref, x + 4, tables, slope1_ref)
        shade(u_ref, x + 2, slope0_ref, *outs)
        return carry

    lax.fori_loop(0, (nx - 4) // 4, pairs, 0)
    shade(u_ref, nx - 2, slope1_ref, *outs, kept_ref, 2)


def shaded(u, *rest):
    comps, nx, ny, nz = u.shape
    return pl.pallas_call(
        shade_kernel,
        out_shape=(
            jax.ShapeDtypeStruct((nx, ny, nz), jnp.float32),
            jax.ShapeDtypeStruct((comps, ny, nz), jnp.float32),
            jax.ShapeDtypeStruct((4, comps, ny, nz), jnp.float32),
            jax.ShapeDtypeStruct((nx // SUB, ny, nz), jnp.float32),
        ),
        in_specs=[VMEM] * 7,
        out_specs=(VMEM,) * 4,
        scratch_shapes=[
            pltpu.VMEM((nx // SUB, ny, nz), jnp.float32),
            pltpu.VMEM((2 * nz, nz), jnp.bfloat16),
            pltpu.VMEM((ny, 2 * ny), jnp.bfloat16),
            pltpu.VMEM((2, 2, comps, ny, nz), jnp.float32),
            pltpu.VMEM((2, 2, comps, ny, nz), jnp.float32),
        ],
        compiler_params=PARAMS,
        cost_estimate=COST,
    )(u, *rest)


def sides_deep(nx, ny, nz, zleft_ref, zright_ref):
    source, target = iota((2 * nz, nz), 0) % nz, iota((2 * nz, nz), 1)
    where = jnp.where(source // 4 == target // 4, source % 4 + 10 * (target % 4), -1)
    weights = jnp.zeros((2 * nz, nz), jnp.float32)
    for value, m, t in ((1.0, 0, 2), (-8.0, 1, 2), (1.0, 1, 3), (-1.0, 2, 0), (8.0, 2, 1), (-1.0, 3, 1)):
        weights = jnp.where(where == m + 10 * t, value, weights)
    weights = weights.astype(jnp.bfloat16)
    return [
        jnp.dot(jnp.concatenate(split(ghost), axis=1), weights, preferred_element_type=jnp.float32)
        for ghost in unfold(zleft_ref[...], zright_ref[...], ny, nz)
    ]


def on_border(packed, x, rows=None):
    ny, nz = packed.shape
    lane = iota((ny, nz), 1)
    return jnp.where((lane >= nz - 2) | (lane < 2), pltpu.roll(packed, lane_shift(x, nz, False), 1), 0.0)


def gather(density, raws, level_ref, sums_ref, sum_ref):
    parts = []
    for k, raw in enumerate(raws):
        level = jnp.clip(raw, 0.0, 1.0)
        level_ref[k] = level
        parts.append(jnp.concatenate(split((density / math.log(2.0)) * level), axis=1))
    ny, nz = level_ref.shape[1:]
    sums = jnp.dot(jnp.concatenate(parts, axis=0), sum_ref[...], preferred_element_type=jnp.float32)
    for k in range(len(raws)):
        sums_ref[k] = sums[k * ny : (k + 1) * ny]


def blend(level_ref, sums_ref, k, store):
    ny, nz = level_ref.shape[1:]
    lane_group = iota((8, ny), 1) // 8
    eye = iota((8, ny), 1) % 8 == iota((8, ny), 0)
    totals = [jnp.zeros((8, ny), jnp.float32)] * 3
    for group in range(ny // 8):
        rows = pl.ds(8 * group, 8)
        level = level_ref[k, rows, :]
        passing = jnp.exp2(sums_ref[k, rows, pl.ds(0, nz)])
        first = (passing - jnp.exp2(sums_ref[k, rows, pl.ds(nz, nz)])) * level
        red = jnp.sum(first, axis=1, keepdims=True)
        square = jnp.sum(first * level, axis=1, keepdims=True)
        whole = sums_ref[k, rows, pl.ds(2 * nz, ny)]
        totals = [jnp.where(lane_group == group, part, total) for part, total in zip((red, square, whole), totals)]
    red, square, whole = [jnp.sum(jnp.where(eye, total, 0.0), axis=0, keepdims=True) for total in totals]
    through = jnp.exp2(whole)
    store(red, 4.0 * (red - square), 1.0 - through - red, through)


def put(image_ref, x, slot=lambda view: view):
    per_view = image_ref.shape[2]
    view, row = (x // per_view, x % per_view) if isinstance(x, int) else (lax.div(x, per_view), lax.rem(x, per_view))

    def store(*channels):
        for k, values in enumerate(channels):
            image_ref[slot(view), k, pl.ds(row, 1), :] = values

    return store


def summing(sum_ref):
    nz = sum_ref.shape[0] // 2
    row = iota(sum_ref.shape, 0) % nz
    col = iota(sum_ref.shape, 1)
    sum_ref[...] = jnp.where((row < col) & (col < nz) | (row <= col - nz), -1.0, 0.0).astype(jnp.bfloat16)


def blend_kernel(
    density, raw_ref, pack_ref, scale_ref, zleft_ref, zright_ref,
    image_ref, fix_ref, first_ref, sum_ref, level0_ref, level1_ref, sums0_ref, sums1_ref,
):
    nx, ny, nz = raw_ref.shape
    summing(sum_ref)
    ghosts = sides_deep(nx, ny, nz, zleft_ref, zright_ref)
    first_ref[...] = ghosts[0]
    fix = ghosts[2] * (0.5 * ghosts[2] + pack_ref[2]) + ghosts[0] * pack_ref[0] + ghosts[1] * pack_ref[1]
    per_block = 4 * SUB
    lane_block = iota((ny, nz), 1) // per_block
    scale = scale_ref[0]
    for block in range(1, nx // SUB):
        scale = jnp.where(lane_block == block, scale_ref[block], scale)
    fix_ref[...] = fix * scale
    image_ref[...] = jnp.zeros(image_ref.shape, jnp.float32)
    batch = level0_ref.shape[0]

    def load(x, level_ref, sums_ref):
        raws = [raw_ref[x + k] + on_border(fix_ref[...], x + k) for k in range(batch)]
        gather(density, raws, level_ref, sums_ref, sum_ref)

    def mix(x, level_ref, sums_ref):
        for k in range(batch):
            blend(level_ref, sums_ref, k, put(image_ref, x + k))

    load(2, level0_ref, sums0_ref)

    def batches(i, carry):
        x = 2 * batch * i + 2
        load(x + batch, level1_ref, sums1_ref)
        mix(x, level0_ref, sums0_ref)
        load(x + 2 * batch, level0_ref, sums0_ref)
        mix(x + batch, level1_ref, sums1_ref)
        return carry

    count = (nx - 4) // batch
    lax.fori_loop(0, (count - 1) // 2, batches, 0)
    if count % 2 == 0:
        load(nx - 2 - batch, level1_ref, sums1_ref)
        mix(nx - 2 - 2 * batch, level0_ref, sums0_ref)
        mix(nx - 2 - batch, level1_ref, sums1_ref)
    else:
        mix(nx - 2 - batch, level0_ref, sums0_ref)


def row_tables(batch, ny, nz, buffers):
    return (
        [pltpu.VMEM((batch, ny, nz), jnp.float32)] * buffers
        + [pltpu.VMEM((batch, ny, 2 * nz + ny), jnp.float32)] * buffers
    )


def blended(density, views, raw, *rest):
    nx, ny, nz = raw.shape
    return pl.pallas_call(
        functools.partial(blend_kernel, density),
        out_shape=(
            jax.ShapeDtypeStruct((views, 4, nx // views, ny), jnp.float32),
            jax.ShapeDtypeStruct((ny, nz), jnp.float32),
            jax.ShapeDtypeStruct((ny, nz), jnp.float32),
            jax.ShapeDtypeStruct((2 * nz, 2 * nz + ny), jnp.bfloat16),
        ),
        in_specs=[VMEM] * 5,
        out_specs=(VMEM,) * 4,
        scratch_shapes=row_tables(4, ny, nz, 2),
        compiler_params=PARAMS,
        cost_estimate=COST,
    )(raw, *rest)


def edge_raw(x, place, ghost, raw_ref, kept_ref, scale_ref, fix_ref, first_ref):
    depth = kept_ref[place, 2] + on_border(first_ref[...], x)
    more = ghost[0] * (0.5 * ghost[0] + kept_ref[place, 0]) + ghost[1] * kept_ref[place, 1] + ghost[2] * depth
    return raw_ref[x] + on_border(fix_ref[...], x) + more * scale_ref[x // SUB]


def first_kernel(
    density, image_in_ref, raw_ref, kept_ref, scale_ref, fix_ref, first_ref, sum_ref, xleft_ref,
    image_ref, level_ref, sums_ref,
):
    image_ref[...] = image_in_ref[...]
    near = [xleft_ref[c, 1] for c in range(3)]
    far = [xleft_ref[c, 0] - 8.0 * cells for c, cells in enumerate(near)]
    edge_refs = (raw_ref, kept_ref, scale_ref, fix_ref, first_ref)
    gather(density, [edge_raw(0, 0, far, *edge_refs), edge_raw(1, 1, near, *edge_refs)], level_ref, sums_ref, sum_ref)
    for x in range(2):
        blend(level_ref, sums_ref, x, put(image_ref, x))


def last_kernel(
    density, image_in_ref, raw_ref, kept_ref, scale_ref, fix_ref, first_ref, sum_ref, xright_ref,
    image_ref, level_ref, sums_ref,
):
    nx = raw_ref.shape[0]
    views = image_ref.shape[0]
    me = lax.axis_index("view")

    def slot(view):
        return step_to(me, view, views)

    for view in range(views):
        image_ref[slot(view)] = image_in_ref[view]
    near = [-xright_ref[c, 0] for c in range(3)]
    far = [-8.0 * cells - xright_ref[c, 1] for c, cells in enumerate(near)]
    edge_refs = (raw_ref, kept_ref, scale_ref, fix_ref, first_ref)
    raws = [edge_raw(nx - 2, 2, near, *edge_refs), edge_raw(nx - 1, 3, far, *edge_refs)]
    gather(density, raws, level_ref, sums_ref, sum_ref)
    for k in range(2):
        blend(level_ref, sums_ref, k, put(image_ref, nx - 2 + k, slot))


def edged(kernel, density, image, raw, *rest):
    nx, ny, nz = raw.shape
    return pl.pallas_call(
        functools.partial(kernel, density),
        out_shape=jax.ShapeDtypeStruct(image.shape, jnp.float32),
        in_specs=[VMEM] * 8,
        out_specs=VMEM,
        scratch_shapes=row_tables(2, ny, nz, 1),
        compiler_params=PARAMS,
        cost_estimate=COST,
    )(image, raw, *rest)


def turn(block, axis, by):
    count = lax.axis_size(axis)
    return lax.ppermute(block, axis, [(i, (i + by) % count) for i in range(count)])


def both_sides(block, axis):
    before = turn(block, axis, 1)
    return before, before if lax.axis_size(axis) == 2 else turn(block, axis, -1)


def step_to(me, other, count):
    return me ^ other if count & (count - 1) == 0 else lax.rem(other - me + count, count)


def exchanged(blocks, axis):
    count = lax.axis_size(axis)
    paired = count & (count - 1) == 0
    found = [blocks[0]]
    for step in range(count - 1, 0, -1):
        route = [(i, i ^ step if paired else (i + step) % count) for i in range(count)]
        found.insert(1, lax.ppermute(blocks[step], axis, route))
    return found


def composite_kernel(*refs):
    *image_refs, out_ref = refs
    count = len(image_refs)
    me = lax.axis_index("view")
    if count & (count - 1) == 0:
        sources = [me ^ step for step in range(count)]
    else:
        sources = [lax.rem(me - step + count, count) for step in range(count)]
    colour = [0.0] * 3
    through = 1.0
    for source, image_ref in zip(sources, image_refs):
        passing = 1.0
        for other, front_ref in zip(sources, image_refs):
            passing = passing * jnp.where(other < source, front_ref[3], 1.0)
        colour = [total + passing * image_ref[k] for k, total in enumerate(colour)]
        through = through * image_ref[3]
    for k in range(3):
        out_ref[0, 0, k] = colour[k]
    out_ref[0, 0, 3] = 1.0 - through


def composited(images):
    return pl.pallas_call(
        composite_kernel,
        out_shape=jax.ShapeDtypeStruct((1, 1) + images[0].shape, jnp.float32),
        in_specs=[VMEM] * len(images),
        out_specs=VMEM,
        compiler_params=PARAMS,
        cost_estimate=COST,
    )(*images)


def local(velocity, occupied, q_floor, q_span):
    comps, nx, ny, nz = velocity.shape
    views = lax.axis_size("view")
    density = 5.0 / (nz * views)
    xtail, xhead, yface = ends(velocity)
    xleft = turn(xtail, "gx", 1)
    xright = turn(xhead, "gx", -1)
    u, parts, ztail, zhead = faces(velocity)
    zleft = turn(ztail, "view", 1)
    zright = turn(zhead, "view", -1)
    yleft, yright = both_sides(yface, "gy")
    raw, pack, kept, scale = shaded(u, parts, yleft, yright, occupied[:, :, 0], q_floor, q_span)
    image, fix, first, summer = blended(density, views, raw, pack, scale, zleft, zright)
    shared = (raw, kept, scale, fix, first, summer)
    image = edged(first_kernel, density, image, *shared, xleft)
    blocks = edged(last_kernel, density, image, *shared, xright)
    return composited(exchanged(blocks, "view"))


def solution(mesh):
    placed = (P(None, "gx", "gy", "view"), P("gx", "gy", "view"), P(), P())
    return jax.shard_map(
        local,
        mesh=mesh,
        in_specs=placed,
        out_specs=P("gx", "gy", None, "view", None),
        check_vma=False,
    )
```

```python
import functools
import math

import jax
import jax.numpy as jnp
from jax import lax
from jax.experimental import pallas as pl
from jax.experimental.pallas import tpu as pltpu
from jax.sharding import PartitionSpec as P

SUB = 8
ROWS = 32
VMEM = pl.BlockSpec(memory_space=pltpu.VMEM)
HBM = pl.BlockSpec(memory_space=pltpu.HBM)
COST = pl.CostEstimate(flops=1 << 20, bytes_accessed=1 << 20, transcendentals=0)
PARAMS = pltpu.CompilerParams(vmem_limit_bytes=16 << 20)


def split(values):
    high = values.astype(jnp.bfloat16)
    low = (values - high.astype(jnp.float32)).astype(jnp.bfloat16)
    return high, low


def iota(shape, dim):
    return lax.broadcasted_iota(jnp.int32, shape, dim)


def layers_kernel(start, u_hbm, out_ref, sem):
    copy = pltpu.make_async_copy(u_hbm.at[:, pl.ds(start, 2)], out_ref, sem)
    copy.start()
    copy.wait()


def layers(u, start):
    comps, _, ny, nz = u.shape
    return pl.pallas_call(
        functools.partial(layers_kernel, start),
        out_shape=jax.ShapeDtypeStruct((comps, 2, ny, nz), jnp.float32),
        in_specs=[HBM],
        out_specs=VMEM,
        scratch_shapes=[pltpu.SemaphoreType.DMA],
        compiler_params=pltpu.CompilerParams(vmem_limit_bytes=50 << 20),
        cost_estimate=COST,
    )(u)


def faces_kernel(u_hbm, u_ref, parts_ref, yface_ref, tail_ref, head_ref, packed_ref, sems):
    comps, nx, ny, nz = u_ref.shape
    quarters = sems.shape[1]
    rows = ny // quarters

    def fetch(c, k):
        span = pl.ds(k * rows if isinstance(k, int) else pl.multiple_of(k * rows, rows), rows)
        return pltpu.make_async_copy(u_hbm.at[c, :, span], u_ref.at[c, :, span], sems.at[c, k])

    for c in range(comps):
        for k in range(quarters):
            fetch(c, k).start()
    slot = iota((8, nz), 1) // 4
    for c in range(comps):

        def quarter(k, carry):
            fetch(c, k).wait()
            start = pl.multiple_of(k * rows, rows)
            packed = [jnp.zeros((8, nz), jnp.float32)] * (rows // 8)
            for x in range(nx):
                cells = u_ref[c, x, pl.ds(start, rows), :]
                high, low = split(cells)
                parts_ref[c, x, pl.ds(start, rows), pl.ds(0, nz)] = high
                parts_ref[c, x, pl.ds(start, rows), pl.ds(nz, nz)] = low
                mine = slot == x
                for n in range(rows // 8):
                    packed[n] = jnp.where(mine, pltpu.roll(cells[8 * n : 8 * n + 8], (4 * x + 2) % nz, 1), packed[n])
            for n in range(rows // 8):
                packed_ref[c, pl.ds(pl.multiple_of(start + 8 * n, 8), 8), :] = packed[n]
            return carry

        lax.fori_loop(0, quarters, quarter, 0)
    sub = iota((8, nz), 0)
    for c in range(comps):
        for x in range(nx):
            lines = jnp.where(sub >= 6, u_ref[c, x, pl.ds(ny - 8, 8), :], u_ref[c, x, pl.ds(0, 8), :])
            yface_ref[c, x] = pltpu.roll(lines, 2, 0)[:4]
    tails, heads = fold([packed_ref[c] for c in range(comps)], ny, nz)
    tail_ref[...] = tails
    head_ref[...] = heads


def fold(packed, ny, nz):
    early = iota((ny, nz), 1) % 4 < 2
    early2 = early[: ny // 2]
    third, fourth = packed[2][: ny // 2], packed[2][ny // 2 :]
    tails = jnp.where(early, packed[0], pltpu.roll(packed[1], 2, 1))
    tails2 = jnp.where(early2, third, pltpu.roll(fourth, 2, 1))
    heads = jnp.where(early, pltpu.roll(packed[0], nz - 2, 1), packed[1])
    heads2 = jnp.where(early2, pltpu.roll(third, nz - 2, 1), fourth)
    return jnp.concatenate([tails, tails2], axis=0), jnp.concatenate([heads, heads2], axis=0)


def unfold(left, right, ny, nz):
    early = iota((ny, nz), 1) % 4 < 2
    early2 = early[: ny // 2]
    left2, right2 = left[ny:], right[ny:]
    left, right = left[:ny], right[:ny]
    first = jnp.where(early, left, pltpu.roll(right, 2, 1))
    second = jnp.where(early, pltpu.roll(left, nz - 2, 1), right)
    third = jnp.where(early2, left2, pltpu.roll(right2, 2, 1))
    fourth = jnp.where(early2, pltpu.roll(left2, nz - 2, 1), right2)
    return first, second, jnp.concatenate([third, fourth], axis=0)


def faces(u):
    comps, nx, ny, nz = u.shape
    message = jax.ShapeDtypeStruct((ny + ny // 2, nz), jnp.float32)
    return pl.pallas_call(
        faces_kernel,
        out_shape=(
            jax.ShapeDtypeStruct(u.shape, jnp.float32),
            jax.ShapeDtypeStruct((comps, nx, ny, 2 * nz), jnp.bfloat16),
            jax.ShapeDtypeStruct((comps, nx, 4, nz), jnp.float32),
            message,
            message,
        ),
        in_specs=[HBM],
        out_specs=(VMEM,) * 5,
        scratch_shapes=[pltpu.VMEM((comps, ny, nz), jnp.float32), pltpu.SemaphoreType.DMA((comps, 4))],
        compiler_params=pltpu.CompilerParams(vmem_limit_bytes=37 << 20),
        cost_estimate=COST,
    )(u)


def stencil(far):
    one = jnp.where(far == 1, 8.0, 0.0) - jnp.where(far == -1, 8.0, 0.0)
    return (one - jnp.where(far == 2, 1.0, 0.0) + jnp.where(far == -2, 1.0, 0.0)).astype(jnp.bfloat16)


def shading(occupied_ref, floor, span, scale_ref, offset_ref):
    blocks, ny, nz = scale_ref.shape
    groups = ny // SUB
    mine = iota((ny, groups), 0) // SUB == iota((ny, groups), 1)
    shrink = 1.0 / span
    for block in range(blocks):
        row = occupied_ref[block : block + 1, :].astype(jnp.float32)
        column = jnp.sum(jnp.where(mine, row, 0.0), axis=1, keepdims=True)
        scale_ref[block] = jnp.broadcast_to(column * (shrink * (-1.0 / 144.0)), (ny, nz))
        offset_ref[block] = jnp.broadcast_to(column * (shrink * -floor), (ny, nz))


def lane_shift(x, nz, back):
    if isinstance(x, int):
        return (4 * x + 2 if back else 2 * nz - 2 - 4 * x) % nz
    return lax.rem(4 * x + 2 if back else 2 * nz - 2 - 4 * x, nz)


def slopes(parts_ref, x, tables, slope_ref):
    yleft_ref, yright_ref, dz_ref, dy_ref = tables
    comps, ny, nz = slope_ref.shape[2:]
    sub = iota((8, nz), 0)

    def top(left):
        lines = jnp.concatenate([left, left], axis=0)
        return jnp.where(sub < 2, lines - jnp.where(sub == 0, 8.0 * pltpu.roll(lines, 7, 0), 0.0), 0.0)

    def low(right):
        lines = jnp.concatenate([right, right], axis=0)
        return jnp.where(sub >= 6, jnp.where(sub == 7, 8.0 * pltpu.roll(lines, 1, 0), 0.0) - lines, 0.0)

    parts = [[parts_ref[c, x + k] for k in range(2)] for c in range(comps)]
    depth = jnp.dot(
        jnp.concatenate([part for pair in parts for part in pair], axis=0),
        dz_ref[...],
        preferred_element_type=jnp.float32,
    )
    for c in range(comps):
        both = jnp.concatenate(
            [jnp.concatenate([part[:, half : half + nz] for part in parts[c]], axis=1) for half in (0, nz)], axis=0
        )
        down = jnp.dot(dy_ref[...], both, preferred_element_type=jnp.float32)
        for k in range(2):
            slope_ref[1, k, c] = depth[(2 * c + k) * ny : (2 * c + k + 1) * ny]
            mine = down[:, k * nz : (k + 1) * nz]
            slope_ref[0, k, c, pl.ds(0, 8), :] = mine[:8] + top(yleft_ref[c, x + k])
            slope_ref[0, k, c, pl.ds(8, ny - 16), :] = mine[8 : ny - 8]
            slope_ref[0, k, c, pl.ds(ny - 8, 8), :] = mine[ny - 8 :] + low(yright_ref[c, x + k])


def shade(u_ref, x, slope_ref, scale_ref, offset_ref, raw_ref, pack_ref, kept_ref=None, place=None):
    comps, nx, ny, nz = u_ref.shape
    block = x // SUB

    def difference(high, low):
        if high is None:
            return 0.0 if low is None else -low
        return high if low is None else high - low

    for y in range(0, ny, ROWS):
        rows = pl.ds(y, ROWS)
        slots = iota((ROWS, nz), 1) // 4
        across = []
        for c in range(comps):
            near = [
                u_ref[c, x + d, rows, :] if not isinstance(x, int) or 0 <= x + d < nx else None for d in range(-2, 4)
            ]
            across.append(
                [8.0 * difference(near[k + 3], near[k + 1]) - difference(near[k + 4], near[k]) for k in range(2)]
            )
        packs = [pack_ref[k, rows, :] for k in range(3)]
        for k in range(2):
            side = [across[c][k] for c in range(comps)]
            down = [slope_ref[0, k, c, rows, :] for c in range(comps)]
            depth = [slope_ref[1, k, c, rows, :] for c in range(comps)]
            total = 0.5 * (side[0] * side[0] + down[1] * down[1] + depth[2] * depth[2])
            total = total + side[1] * down[0] + side[2] * depth[0] + down[2] * depth[1]
            raw_ref[x + k, rows, :] = total * scale_ref[block, rows, :] + offset_ref[block, rows, :]
            back = lane_shift(x + k, nz, True)
            packs = [
                jnp.where(slots == x + k, pltpu.roll(values, back, 1), pack)
                for values, pack in zip((side[2], down[2], depth[2]), packs)
            ]
            if kept_ref is not None:
                for n, values in enumerate((side[0], down[0], depth[0])):
                    kept_ref[place + k, n, rows, :] = values
        for k in range(3):
            pack_ref[k, rows, :] = packs[k]


def shade_kernel(
    u_ref, parts_ref, yleft_ref, yright_ref, occupied_ref, floor_ref, span_ref,
    raw_ref, pack_ref, kept_ref, scale_ref, offset_ref, dz_ref, dy_ref, slope0_ref, slope1_ref,
):
    comps, nx, ny, nz = u_ref.shape
    dz_ref[...] = stencil(iota((2 * nz, nz), 0) % nz - iota((2 * nz, nz), 1))
    dy_ref[...] = stencil(iota((ny, 2 * ny), 1) % ny - iota((ny, 2 * ny), 0))
    shading(occupied_ref, floor_ref[...].reshape(1, 1), span_ref[...].reshape(1, 1), scale_ref, offset_ref)
    pack_ref[...] = jnp.zeros(pack_ref.shape, jnp.float32)
    tables = (yleft_ref, yright_ref, dz_ref, dy_ref)
    outs = (scale_ref, offset_ref, raw_ref, pack_ref)
    slopes(parts_ref, 0, tables, slope0_ref)
    slopes(parts_ref, 2, tables, slope1_ref)
    shade(u_ref, 0, slope0_ref, *outs, kept_ref, 0)

    def pairs(i, carry):
        x = 4 * i + 2
        slopes(parts_ref, x + 2, tables, slope0_ref)
        shade(u_ref, x, slope1_ref, *outs)
        slopes(parts_ref, x + 4, tables, slope1_ref)
        shade(u_ref, x + 2, slope0_ref, *outs)
        return carry

    lax.fori_loop(0, (nx - 4) // 4, pairs, 0)
    shade(u_ref, nx - 2, slope1_ref, *outs, kept_ref, 2)


def shaded(u, *rest):
    comps, nx, ny, nz = u.shape
    return pl.pallas_call(
        shade_kernel,
        out_shape=(
            jax.ShapeDtypeStruct((nx, ny, nz), jnp.float32),
            jax.ShapeDtypeStruct((comps, ny, nz), jnp.float32),
            jax.ShapeDtypeStruct((4, comps, ny, nz), jnp.float32),
            jax.ShapeDtypeStruct((nx // SUB, ny, nz), jnp.float32),
        ),
        in_specs=[VMEM] * 7,
        out_specs=(VMEM,) * 4,
        scratch_shapes=[
            pltpu.VMEM((nx // SUB, ny, nz), jnp.float32),
            pltpu.VMEM((2 * nz, nz), jnp.bfloat16),
            pltpu.VMEM((ny, 2 * ny), jnp.bfloat16),
            pltpu.VMEM((2, 2, comps, ny, nz), jnp.float32),
            pltpu.VMEM((2, 2, comps, ny, nz), jnp.float32),
        ],
        compiler_params=PARAMS,
        cost_estimate=COST,
    )(u, *rest)


def sides_deep(nx, ny, nz, zleft_ref, zright_ref):
    source, target = iota((2 * nz, nz), 0) % nz, iota((2 * nz, nz), 1)
    where = jnp.where(source // 4 == target // 4, source % 4 + 10 * (target % 4), -1)
    weights = jnp.zeros((2 * nz, nz), jnp.float32)
    for value, m, t in ((1.0, 0, 2), (-8.0, 1, 2), (1.0, 1, 3), (-1.0, 2, 0), (8.0, 2, 1), (-1.0, 3, 1)):
        weights = jnp.where(where == m + 10 * t, value, weights)
    weights = weights.astype(jnp.bfloat16)
    return [
        jnp.dot(jnp.concatenate(split(ghost), axis=1), weights, preferred_element_type=jnp.float32)
        for ghost in unfold(zleft_ref[...], zright_ref[...], ny, nz)
    ]


def on_border(packed, x, rows=None):
    ny, nz = packed.shape
    lane = iota((ny, nz), 1)
    return jnp.where((lane >= nz - 2) | (lane < 2), pltpu.roll(packed, lane_shift(x, nz, False), 1), 0.0)


def gather(density, raws, level_ref, sums_ref, sum_ref):
    parts = []
    for k, raw in enumerate(raws):
        level = jnp.clip(raw, 0.0, 1.0)
        level_ref[k] = level
        parts.append(jnp.concatenate(split((density / math.log(2.0)) * level), axis=1))
    ny, nz = level_ref.shape[1:]
    sums = jnp.dot(jnp.concatenate(parts, axis=0), sum_ref[...], preferred_element_type=jnp.float32)
    for k in range(len(raws)):
        sums_ref[k] = sums[k * ny : (k + 1) * ny]


def blend(level_ref, sums_ref, k, store):
    ny, nz = level_ref.shape[1:]
    lane_group = iota((8, ny), 1) // 8
    eye = iota((8, ny), 1) % 8 == iota((8, ny), 0)
    totals = [jnp.zeros((8, ny), jnp.float32)] * 3
    for group in range(ny // 8):
        rows = pl.ds(8 * group, 8)
        level = level_ref[k, rows, :]
        passing = jnp.exp2(sums_ref[k, rows, pl.ds(0, nz)])
        first = (passing - jnp.exp2(sums_ref[k, rows, pl.ds(nz, nz)])) * level
        red = jnp.sum(first, axis=1, keepdims=True)
        square = jnp.sum(first * level, axis=1, keepdims=True)
        whole = sums_ref[k, rows, pl.ds(2 * nz, ny)]
        totals = [jnp.where(lane_group == group, part, total) for part, total in zip((red, square, whole), totals)]
    red, square, whole = [jnp.sum(jnp.where(eye, total, 0.0), axis=0, keepdims=True) for total in totals]
    through = jnp.exp2(whole)
    store(red, 4.0 * (red - square), 1.0 - through - red, through)


def put(image_ref, x, slot=lambda view: view):
    per_view = image_ref.shape[2]
    view, row = (x // per_view, x % per_view) if isinstance(x, int) else (lax.div(x, per_view), lax.rem(x, per_view))

    def store(*channels):
        for k, values in enumerate(channels):
            image_ref[slot(view), k, pl.ds(row, 1), :] = values

    return store


def summing(sum_ref):
    nz = sum_ref.shape[0] // 2
    row = iota(sum_ref.shape, 0) % nz
    col = iota(sum_ref.shape, 1)
    sum_ref[...] = jnp.where((row < col) & (col < nz) | (row <= col - nz), -1.0, 0.0).astype(jnp.bfloat16)


def blend_kernel(
    density, raw_ref, pack_ref, scale_ref, zleft_ref, zright_ref,
    image_ref, fix_ref, first_ref, sum_ref, level0_ref, level1_ref, sums0_ref, sums1_ref,
):
    nx, ny, nz = raw_ref.shape
    summing(sum_ref)
    ghosts = sides_deep(nx, ny, nz, zleft_ref, zright_ref)
    first_ref[...] = ghosts[0]
    fix = ghosts[2] * (0.5 * ghosts[2] + pack_ref[2]) + ghosts[0] * pack_ref[0] + ghosts[1] * pack_ref[1]
    per_block = 4 * SUB
    lane_block = iota((ny, nz), 1) // per_block
    scale = scale_ref[0]
    for block in range(1, nx // SUB):
        scale = jnp.where(lane_block == block, scale_ref[block], scale)
    fix_ref[...] = fix * scale
    image_ref[...] = jnp.zeros(image_ref.shape, jnp.float32)
    batch = level0_ref.shape[0]

    def load(x, level_ref, sums_ref):
        raws = [raw_ref[x + k] + on_border(fix_ref[...], x + k) for k in range(batch)]
        gather(density, raws, level_ref, sums_ref, sum_ref)

    def mix(x, level_ref, sums_ref):
        for k in range(batch):
            blend(level_ref, sums_ref, k, put(image_ref, x + k))

    load(2, level0_ref, sums0_ref)

    def batches(i, carry):
        x = 2 * batch * i + 2
        load(x + batch, level1_ref, sums1_ref)
        mix(x, level0_ref, sums0_ref)
        load(x + 2 * batch, level0_ref, sums0_ref)
        mix(x + batch, level1_ref, sums1_ref)
        return carry

    count = (nx - 4) // batch
    lax.fori_loop(0, (count - 1) // 2, batches, 0)
    if count % 2 == 0:
        load(nx - 2 - batch, level1_ref, sums1_ref)
        mix(nx - 2 - 2 * batch, level0_ref, sums0_ref)
        mix(nx - 2 - batch, level1_ref, sums1_ref)
    else:
        mix(nx - 2 - batch, level0_ref, sums0_ref)


def row_tables(batch, ny, nz, buffers):
    return (
        [pltpu.VMEM((batch, ny, nz), jnp.float32)] * buffers
        + [pltpu.VMEM((batch, ny, 2 * nz + ny), jnp.float32)] * buffers
    )


def blended(density, views, raw, *rest):
    nx, ny, nz = raw.shape
    return pl.pallas_call(
        functools.partial(blend_kernel, density),
        out_shape=(
            jax.ShapeDtypeStruct((views, 4, nx // views, ny), jnp.float32),
            jax.ShapeDtypeStruct((ny, nz), jnp.float32),
            jax.ShapeDtypeStruct((ny, nz), jnp.float32),
            jax.ShapeDtypeStruct((2 * nz, 2 * nz + ny), jnp.bfloat16),
        ),
        in_specs=[VMEM] * 5,
        out_specs=(VMEM,) * 4,
        scratch_shapes=row_tables(4, ny, nz, 2),
        compiler_params=PARAMS,
        cost_estimate=COST,
    )(raw, *rest)


def edge_raw(x, place, ghost, raw_ref, kept_ref, scale_ref, fix_ref, first_ref):
    depth = kept_ref[place, 2] + on_border(first_ref[...], x)
    more = ghost[0] * (0.5 * ghost[0] + kept_ref[place, 0]) + ghost[1] * kept_ref[place, 1] + ghost[2] * depth
    return raw_ref[x] + on_border(fix_ref[...], x) + more * scale_ref[x // SUB]


def first_kernel(
    density, image_in_ref, raw_ref, kept_ref, scale_ref, fix_ref, first_ref, sum_ref, xleft_ref,
    image_ref, level_ref, sums_ref,
):
    image_ref[...] = image_in_ref[...]
    near = [xleft_ref[c, 1] for c in range(3)]
    far = [xleft_ref[c, 0] - 8.0 * cells for c, cells in enumerate(near)]
    edge_refs = (raw_ref, kept_ref, scale_ref, fix_ref, first_ref)
    gather(density, [edge_raw(0, 0, far, *edge_refs), edge_raw(1, 1, near, *edge_refs)], level_ref, sums_ref, sum_ref)
    for x in range(2):
        blend(level_ref, sums_ref, x, put(image_ref, x))


def last_kernel(
    density, image_in_ref, raw_ref, kept_ref, scale_ref, fix_ref, first_ref, sum_ref, xright_ref,
    image_ref, level_ref, sums_ref,
):
    nx = raw_ref.shape[0]
    views = image_ref.shape[0]
    me = lax.axis_index("view")

    def slot(view):
        return step_to(me, view, views)

    for view in range(views):
        image_ref[slot(view)] = image_in_ref[view]
    near = [-xright_ref[c, 0] for c in range(3)]
    far = [-8.0 * cells - xright_ref[c, 1] for c, cells in enumerate(near)]
    edge_refs = (raw_ref, kept_ref, scale_ref, fix_ref, first_ref)
    raws = [edge_raw(nx - 2, 2, near, *edge_refs), edge_raw(nx - 1, 3, far, *edge_refs)]
    gather(density, raws, level_ref, sums_ref, sum_ref)
    for k in range(2):
        blend(level_ref, sums_ref, k, put(image_ref, nx - 2 + k, slot))


def edged(kernel, density, image, raw, *rest):
    nx, ny, nz = raw.shape
    return pl.pallas_call(
        functools.partial(kernel, density),
        out_shape=jax.ShapeDtypeStruct(image.shape, jnp.float32),
        in_specs=[VMEM] * 8,
        out_specs=VMEM,
        scratch_shapes=row_tables(2, ny, nz, 1),
        compiler_params=PARAMS,
        cost_estimate=COST,
    )(image, raw, *rest)


def turn(block, axis, by):
    count = lax.axis_size(axis)
    return lax.ppermute(block, axis, [(i, (i + by) % count) for i in range(count)])


def both_sides(block, axis):
    before = turn(block, axis, 1)
    return before, before if lax.axis_size(axis) == 2 else turn(block, axis, -1)


def exchange(count):
    if count == 4:
        return [(1, 0, 3, 2), (3, 2, 0, 1), (2, 3, 1, 0)]
    if count & (count - 1) == 0:
        return [tuple(i ^ step for i in range(count)) for step in range(1, count)]
    return [tuple((i + step) % count for i in range(count)) for step in range(1, count)]


def looked_up(index, table):
    found = jnp.int32(table[0])
    for place, entry in enumerate(table[1:], 1):
        found = jnp.where(index == place, entry, found)
    return found


def step_to(me, other, count):
    steps = [(i,) + targets for i, targets in enumerate(zip(*exchange(count)))]
    return looked_up(me, [targets.index(other) for targets in steps])


def exchanged(blocks, axis):
    routes = exchange(lax.axis_size(axis))
    return [blocks[0]] + [lax.ppermute(blocks[k], axis, list(enumerate(route))) for k, route in enumerate(routes, 1)]


def composite_kernel(*refs):
    *image_refs, out_ref = refs
    count = len(image_refs)
    me = lax.axis_index("view")
    sources = [me] + [looked_up(me, [route.index(i) for i in range(count)]) for route in exchange(count)]
    colour = [0.0] * 3
    through = 1.0
    for source, image_ref in zip(sources, image_refs):
        passing = 1.0
        for other, front_ref in zip(sources, image_refs):
            passing = passing * jnp.where(other < source, front_ref[3], 1.0)
        colour = [total + passing * image_ref[k] for k, total in enumerate(colour)]
        through = through * image_ref[3]
    for k in range(3):
        out_ref[0, 0, k] = colour[k]
    out_ref[0, 0, 3] = 1.0 - through


def composited(images):
    return pl.pallas_call(
        composite_kernel,
        out_shape=jax.ShapeDtypeStruct((1, 1) + images[0].shape, jnp.float32),
        in_specs=[VMEM] * len(images),
        out_specs=VMEM,
        compiler_params=PARAMS,
        cost_estimate=COST,
    )(*images)


def local(velocity, occupied, q_floor, q_span):
    comps, nx, ny, nz = velocity.shape
    views = lax.axis_size("view")
    density = 5.0 / (nz * views)
    xleft = turn(layers(velocity, nx - 2), "gx", 1)
    xright = turn(layers(velocity, 0), "gx", -1)
    u, parts, yface, ztail, zhead = faces(velocity)
    zleft = turn(ztail, "view", 1)
    zright = turn(zhead, "view", -1)
    yleft, yright = both_sides(yface, "gy")
    raw, pack, kept, scale = shaded(u, parts, yleft, yright, occupied[:, :, 0], q_floor, q_span)
    image, fix, first, summer = blended(density, views, raw, pack, scale, zleft, zright)
    shared = (raw, kept, scale, fix, first, summer)
    image = edged(first_kernel, density, image, *shared, xleft)
    blocks = edged(last_kernel, density, image, *shared, xright)
    return composited(exchanged(blocks, "view"))


def solution(mesh):
    placed = (P(None, "gx", "gy", "view"), P("gx", "gy", "view"), P(), P())
    return jax.shard_map(
        local,
        mesh=mesh,
        in_specs=placed,
        out_specs=P("gx", "gy", None, "view", None),
        check_vma=False,
    )
```

```python
import functools
import math

import jax
import jax.numpy as jnp
from jax import lax
from jax.experimental import pallas as pl
from jax.experimental.pallas import tpu as pltpu
from jax.sharding import PartitionSpec as P

SUB = 8
ROWS = 32
VMEM = pl.BlockSpec(memory_space=pltpu.VMEM)
HBM = pl.BlockSpec(memory_space=pltpu.HBM)
COST = pl.CostEstimate(flops=1 << 20, bytes_accessed=1 << 20, transcendentals=0)
PARAMS = pltpu.CompilerParams(vmem_limit_bytes=16 << 20)


def split(values):
    high = values.astype(jnp.bfloat16)
    low = (values - high.astype(jnp.float32)).astype(jnp.bfloat16)
    return high, low


def iota(shape, dim):
    return lax.broadcasted_iota(jnp.int32, shape, dim)


def layers_kernel(start, u_hbm, out_ref, sem):
    copy = pltpu.make_async_copy(u_hbm.at[:, pl.ds(start, 2)], out_ref, sem)
    copy.start()
    copy.wait()


def layers(u, start):
    comps, _, ny, nz = u.shape
    return pl.pallas_call(
        functools.partial(layers_kernel, start),
        out_shape=jax.ShapeDtypeStruct((comps, 2, ny, nz), jnp.float32),
        in_specs=[HBM],
        out_specs=VMEM,
        scratch_shapes=[pltpu.SemaphoreType.DMA],
        compiler_params=pltpu.CompilerParams(vmem_limit_bytes=50 << 20),
        cost_estimate=COST,
    )(u)


def faces_kernel(u_hbm, u_ref, parts_ref, yface_ref, tail_ref, head_ref, packed_ref, sems):
    comps, nx, ny, nz = u_ref.shape
    quarters = sems.shape[1]
    rows = ny // quarters

    def fetch(c, k):
        span = pl.ds(k * rows if isinstance(k, int) else pl.multiple_of(k * rows, rows), rows)
        return pltpu.make_async_copy(u_hbm.at[c, :, span], u_ref.at[c, :, span], sems.at[c, k])

    for c in range(comps):
        for k in range(quarters):
            fetch(c, k).start()
    slot = iota((8, nz), 1) // 4
    for c in range(comps):

        def quarter(k, carry):
            fetch(c, k).wait()
            start = pl.multiple_of(k * rows, rows)
            packed = [jnp.zeros((8, nz), jnp.float32)] * (rows // 8)
            for x in range(nx):
                cells = u_ref[c, x, pl.ds(start, rows), :]
                high, low = split(cells)
                parts_ref[c, x, pl.ds(start, rows), pl.ds(0, nz)] = high
                parts_ref[c, x, pl.ds(start, rows), pl.ds(nz, nz)] = low
                mine = slot == x
                for n in range(rows // 8):
                    packed[n] = jnp.where(mine, pltpu.roll(cells[8 * n : 8 * n + 8], (4 * x + 2) % nz, 1), packed[n])
            for n in range(rows // 8):
                packed_ref[c, pl.ds(pl.multiple_of(start + 8 * n, 8), 8), :] = packed[n]
            return carry

        lax.fori_loop(0, quarters, quarter, 0)
    sub = iota((8, nz), 0)
    for c in range(comps):
        for x in range(nx):
            lines = jnp.where(sub >= 6, u_ref[c, x, pl.ds(ny - 8, 8), :], u_ref[c, x, pl.ds(0, 8), :])
            yface_ref[c, x] = pltpu.roll(lines, 2, 0)[:4]
    tails, heads = fold([packed_ref[c] for c in range(comps)], ny, nz)
    tail_ref[...] = tails
    head_ref[...] = heads


def fold(packed, ny, nz):
    early = iota((ny, nz), 1) % 4 < 2
    early2 = early[: ny // 2]
    third, fourth = packed[2][: ny // 2], packed[2][ny // 2 :]
    tails = jnp.where(early, packed[0], pltpu.roll(packed[1], 2, 1))
    tails2 = jnp.where(early2, third, pltpu.roll(fourth, 2, 1))
    heads = jnp.where(early, pltpu.roll(packed[0], nz - 2, 1), packed[1])
    heads2 = jnp.where(early2, pltpu.roll(third, nz - 2, 1), fourth)
    return jnp.concatenate([tails, tails2], axis=0), jnp.concatenate([heads, heads2], axis=0)


def unfold(left, right, ny, nz):
    early = iota((ny, nz), 1) % 4 < 2
    early2 = early[: ny // 2]
    left2, right2 = left[ny:], right[ny:]
    left, right = left[:ny], right[:ny]
    first = jnp.where(early, left, pltpu.roll(right, 2, 1))
    second = jnp.where(early, pltpu.roll(left, nz - 2, 1), right)
    third = jnp.where(early2, left2, pltpu.roll(right2, 2, 1))
    fourth = jnp.where(early2, pltpu.roll(left2, nz - 2, 1), right2)
    return first, second, jnp.concatenate([third, fourth], axis=0)


def faces(u):
    comps, nx, ny, nz = u.shape
    message = jax.ShapeDtypeStruct((ny + ny // 2, nz), jnp.float32)
    return pl.pallas_call(
        faces_kernel,
        out_shape=(
            jax.ShapeDtypeStruct(u.shape, jnp.float32),
            jax.ShapeDtypeStruct((comps, nx, ny, 2 * nz), jnp.bfloat16),
            jax.ShapeDtypeStruct((comps, nx, 4, nz), jnp.float32),
            message,
            message,
        ),
        in_specs=[HBM],
        out_specs=(VMEM,) * 5,
        scratch_shapes=[pltpu.VMEM((comps, ny, nz), jnp.float32), pltpu.SemaphoreType.DMA((comps, 4))],
        compiler_params=pltpu.CompilerParams(vmem_limit_bytes=37 << 20),
        cost_estimate=COST,
    )(u)


def stencil(far):
    one = jnp.where(far == 1, 8.0, 0.0) - jnp.where(far == -1, 8.0, 0.0)
    return (one - jnp.where(far == 2, 1.0, 0.0) + jnp.where(far == -2, 1.0, 0.0)).astype(jnp.bfloat16)


def shading(occupied_ref, floor, span, scale_ref, offset_ref):
    blocks, ny, nz = scale_ref.shape
    groups = ny // SUB
    mine = iota((ny, groups), 0) // SUB == iota((ny, groups), 1)
    shrink = 1.0 / span
    for block in range(blocks):
        row = occupied_ref[block : block + 1, :].astype(jnp.float32)
        column = jnp.sum(jnp.where(mine, row, 0.0), axis=1, keepdims=True)
        scale_ref[block] = jnp.broadcast_to(column * (shrink * (-1.0 / 144.0)), (ny, nz))
        offset_ref[block] = jnp.broadcast_to(column * (shrink * -floor), (ny, nz))


def lane_shift(x, nz, back):
    if isinstance(x, int):
        return (4 * x + 2 if back else 2 * nz - 2 - 4 * x) % nz
    return lax.rem(4 * x + 2 if back else 2 * nz - 2 - 4 * x, nz)


def slopes(parts_ref, x, tables, slope_ref):
    yleft_ref, yright_ref, dz_ref, dy_ref = tables
    comps, ny, nz = slope_ref.shape[2:]
    sub = iota((8, nz), 0)

    def top(left):
        lines = jnp.concatenate([left, left], axis=0)
        return jnp.where(sub < 2, lines - jnp.where(sub == 0, 8.0 * pltpu.roll(lines, 7, 0), 0.0), 0.0)

    def low(right):
        lines = jnp.concatenate([right, right], axis=0)
        return jnp.where(sub >= 6, jnp.where(sub == 7, 8.0 * pltpu.roll(lines, 1, 0), 0.0) - lines, 0.0)

    parts = [[parts_ref[c, x + k] for k in range(2)] for c in range(comps)]
    depth = jnp.dot(
        jnp.concatenate([part for pair in parts for part in pair], axis=0),
        dz_ref[...],
        preferred_element_type=jnp.float32,
    )
    for c in range(comps):
        both = jnp.concatenate(
            [jnp.concatenate([part[:, half : half + nz] for part in parts[c]], axis=1) for half in (0, nz)], axis=0
        )
        down = jnp.dot(dy_ref[...], both, preferred_element_type=jnp.float32)
        for k in range(2):
            slope_ref[1, k, c] = depth[(2 * c + k) * ny : (2 * c + k + 1) * ny]
            mine = down[:, k * nz : (k + 1) * nz]
            slope_ref[0, k, c, pl.ds(0, 8), :] = mine[:8] + top(yleft_ref[c, x + k])
            slope_ref[0, k, c, pl.ds(8, ny - 16), :] = mine[8 : ny - 8]
            slope_ref[0, k, c, pl.ds(ny - 8, 8), :] = mine[ny - 8 :] + low(yright_ref[c, x + k])


def shade(u_ref, x, slope_ref, scale_ref, offset_ref, raw_ref, pack_ref, kept_ref=None, place=None):
    comps, nx, ny, nz = u_ref.shape
    block = x // SUB

    def difference(high, low):
        if high is None:
            return 0.0 if low is None else -low
        return high if low is None else high - low

    for y in range(0, ny, ROWS):
        rows = pl.ds(y, ROWS)
        slots = iota((ROWS, nz), 1) // 4
        across = []
        for c in range(comps):
            near = [
                u_ref[c, x + d, rows, :] if not isinstance(x, int) or 0 <= x + d < nx else None for d in range(-2, 4)
            ]
            across.append(
                [8.0 * difference(near[k + 3], near[k + 1]) - difference(near[k + 4], near[k]) for k in range(2)]
            )
        packs = [pack_ref[k, rows, :] for k in range(3)]
        for k in range(2):
            side = [across[c][k] for c in range(comps)]
            down = [slope_ref[0, k, c, rows, :] for c in range(comps)]
            depth = [slope_ref[1, k, c, rows, :] for c in range(comps)]
            total = 0.5 * (side[0] * side[0] + down[1] * down[1] + depth[2] * depth[2])
            total = total + side[1] * down[0] + side[2] * depth[0] + down[2] * depth[1]
            raw_ref[x + k, rows, :] = total * scale_ref[block, rows, :] + offset_ref[block, rows, :]
            back = lane_shift(x + k, nz, True)
            packs = [
                jnp.where(slots == x + k, pltpu.roll(values, back, 1), pack)
                for values, pack in zip((side[2], down[2], depth[2]), packs)
            ]
            if kept_ref is not None:
                for n, values in enumerate((side[0], down[0], depth[0])):
                    kept_ref[place + k, n, rows, :] = values
        for k in range(3):
            pack_ref[k, rows, :] = packs[k]


def shade_kernel(
    u_ref, parts_ref, yleft_ref, yright_ref, occupied_ref, floor_ref, span_ref,
    raw_ref, pack_ref, kept_ref, scale_ref, offset_ref, dz_ref, dy_ref, slope0_ref, slope1_ref,
):
    comps, nx, ny, nz = u_ref.shape
    dz_ref[...] = stencil(iota((2 * nz, nz), 0) % nz - iota((2 * nz, nz), 1))
    dy_ref[...] = stencil(iota((ny, 2 * ny), 1) % ny - iota((ny, 2 * ny), 0))
    shading(occupied_ref, floor_ref[...].reshape(1, 1), span_ref[...].reshape(1, 1), scale_ref, offset_ref)
    pack_ref[...] = jnp.zeros(pack_ref.shape, jnp.float32)
    tables = (yleft_ref, yright_ref, dz_ref, dy_ref)
    outs = (scale_ref, offset_ref, raw_ref, pack_ref)
    slopes(parts_ref, 0, tables, slope0_ref)
    slopes(parts_ref, 2, tables, slope1_ref)
    shade(u_ref, 0, slope0_ref, *outs, kept_ref, 0)

    def pairs(i, carry):
        x = 4 * i + 2
        slopes(parts_ref, x + 2, tables, slope0_ref)
        shade(u_ref, x, slope1_ref, *outs)
        slopes(parts_ref, x + 4, tables, slope1_ref)
        shade(u_ref, x + 2, slope0_ref, *outs)
        return carry

    lax.fori_loop(0, (nx - 4) // 4, pairs, 0)
    shade(u_ref, nx - 2, slope1_ref, *outs, kept_ref, 2)


def shaded(u, *rest):
    comps, nx, ny, nz = u.shape
    return pl.pallas_call(
        shade_kernel,
        out_shape=(
            jax.ShapeDtypeStruct((nx, ny, nz), jnp.float32),
            jax.ShapeDtypeStruct((comps, ny, nz), jnp.float32),
            jax.ShapeDtypeStruct((4, comps, ny, nz), jnp.float32),
            jax.ShapeDtypeStruct((nx // SUB, ny, nz), jnp.float32),
        ),
        in_specs=[VMEM] * 7,
        out_specs=(VMEM,) * 4,
        scratch_shapes=[
            pltpu.VMEM((nx // SUB, ny, nz), jnp.float32),
            pltpu.VMEM((2 * nz, nz), jnp.bfloat16),
            pltpu.VMEM((ny, 2 * ny), jnp.bfloat16),
            pltpu.VMEM((2, 2, comps, ny, nz), jnp.float32),
            pltpu.VMEM((2, 2, comps, ny, nz), jnp.float32),
        ],
        compiler_params=PARAMS,
        cost_estimate=COST,
    )(u, *rest)


def sides_deep(nx, ny, nz, zleft_ref, zright_ref):
    source, target = iota((2 * nz, nz), 0) % nz, iota((2 * nz, nz), 1)
    where = jnp.where(source // 4 == target // 4, source % 4 + 10 * (target % 4), -1)
    weights = jnp.zeros((2 * nz, nz), jnp.float32)
    for value, m, t in ((1.0, 0, 2), (-8.0, 1, 2), (1.0, 1, 3), (-1.0, 2, 0), (8.0, 2, 1), (-1.0, 3, 1)):
        weights = jnp.where(where == m + 10 * t, value, weights)
    weights = weights.astype(jnp.bfloat16)
    return [
        jnp.dot(jnp.concatenate(split(ghost), axis=1), weights, preferred_element_type=jnp.float32)
        for ghost in unfold(zleft_ref[...], zright_ref[...], ny, nz)
    ]


def on_border(packed, x, rows=None):
    ny, nz = packed.shape
    lane = iota((ny, nz), 1)
    return jnp.where((lane >= nz - 2) | (lane < 2), pltpu.roll(packed, lane_shift(x, nz, False), 1), 0.0)


def gather(density, raws, level_ref, sums_ref, sum_ref):
    parts = []
    for k, raw in enumerate(raws):
        level = jnp.clip(raw, 0.0, 1.0)
        level_ref[k] = level
        parts.append(jnp.concatenate(split((density / math.log(2.0)) * level), axis=1))
    ny, nz = level_ref.shape[1:]
    sums = jnp.dot(jnp.concatenate(parts, axis=0), sum_ref[...], preferred_element_type=jnp.float32)
    for k in range(len(raws)):
        sums_ref[k] = sums[k * ny : (k + 1) * ny]


def blend(level_ref, sums_ref, k, store):
    ny, nz = level_ref.shape[1:]
    lane_group = iota((8, ny), 1) // 8
    eye = iota((8, ny), 1) % 8 == iota((8, ny), 0)
    totals = [jnp.zeros((8, ny), jnp.float32)] * 3
    for group in range(ny // 8):
        rows = pl.ds(8 * group, 8)
        level = level_ref[k, rows, :]
        passing = jnp.exp2(sums_ref[k, rows, pl.ds(0, nz)])
        first = (passing - jnp.exp2(sums_ref[k, rows, pl.ds(nz, nz)])) * level
        red = jnp.sum(first, axis=1, keepdims=True)
        square = jnp.sum(first * level, axis=1, keepdims=True)
        whole = sums_ref[k, rows, pl.ds(2 * nz, ny)]
        totals = [jnp.where(lane_group == group, part, total) for part, total in zip((red, square, whole), totals)]
    red, square, whole = [jnp.sum(jnp.where(eye, total, 0.0), axis=0, keepdims=True) for total in totals]
    through = jnp.exp2(whole)
    store(red, 4.0 * (red - square), 1.0 - through - red, through)


def put(image_ref, x, slot=lambda view: view):
    per_view = image_ref.shape[2]
    view, row = (x // per_view, x % per_view) if isinstance(x, int) else (lax.div(x, per_view), lax.rem(x, per_view))

    def store(*channels):
        for k, values in enumerate(channels):
            image_ref[slot(view), k, pl.ds(row, 1), :] = values

    return store


def summing(sum_ref):
    nz = sum_ref.shape[0] // 2
    row = iota(sum_ref.shape, 0) % nz
    col = iota(sum_ref.shape, 1)
    sum_ref[...] = jnp.where((row < col) & (col < nz) | (row <= col - nz), -1.0, 0.0).astype(jnp.bfloat16)


def blend_kernel(
    density, raw_ref, pack_ref, scale_ref, zleft_ref, zright_ref,
    image_ref, fix_ref, first_ref, sum_ref, level0_ref, level1_ref, sums0_ref, sums1_ref,
):
    nx, ny, nz = raw_ref.shape
    summing(sum_ref)
    ghosts = sides_deep(nx, ny, nz, zleft_ref, zright_ref)
    first_ref[...] = ghosts[0]
    fix = ghosts[2] * (0.5 * ghosts[2] + pack_ref[2]) + ghosts[0] * pack_ref[0] + ghosts[1] * pack_ref[1]
    per_block = 4 * SUB
    lane_block = iota((ny, nz), 1) // per_block
    scale = scale_ref[0]
    for block in range(1, nx // SUB):
        scale = jnp.where(lane_block == block, scale_ref[block], scale)
    fix_ref[...] = fix * scale
    image_ref[...] = jnp.zeros(image_ref.shape, jnp.float32)
    batch = level0_ref.shape[0]

    def load(x, level_ref, sums_ref):
        raws = [raw_ref[x + k] + on_border(fix_ref[...], x + k) for k in range(batch)]
        gather(density, raws, level_ref, sums_ref, sum_ref)

    def mix(x, level_ref, sums_ref):
        for k in range(batch):
            blend(level_ref, sums_ref, k, put(image_ref, x + k))

    load(2, level0_ref, sums0_ref)

    def batches(i, carry):
        x = 2 * batch * i + 2
        load(x + batch, level1_ref, sums1_ref)
        mix(x, level0_ref, sums0_ref)
        load(x + 2 * batch, level0_ref, sums0_ref)
        mix(x + batch, level1_ref, sums1_ref)
        return carry

    count = (nx - 4) // batch
    lax.fori_loop(0, (count - 1) // 2, batches, 0)
    if count % 2 == 0:
        load(nx - 2 - batch, level1_ref, sums1_ref)
        mix(nx - 2 - 2 * batch, level0_ref, sums0_ref)
        mix(nx - 2 - batch, level1_ref, sums1_ref)
    else:
        mix(nx - 2 - batch, level0_ref, sums0_ref)


def row_tables(batch, ny, nz, buffers):
    return (
        [pltpu.VMEM((batch, ny, nz), jnp.float32)] * buffers
        + [pltpu.VMEM((batch, ny, 2 * nz + ny), jnp.float32)] * buffers
    )


def blended(density, views, raw, *rest):
    nx, ny, nz = raw.shape
    return pl.pallas_call(
        functools.partial(blend_kernel, density),
        out_shape=(
            jax.ShapeDtypeStruct((views, 4, nx // views, ny), jnp.float32),
            jax.ShapeDtypeStruct((ny, nz), jnp.float32),
            jax.ShapeDtypeStruct((ny, nz), jnp.float32),
            jax.ShapeDtypeStruct((2 * nz, 2 * nz + ny), jnp.bfloat16),
        ),
        in_specs=[VMEM] * 5,
        out_specs=(VMEM,) * 4,
        scratch_shapes=row_tables(4, ny, nz, 2),
        compiler_params=PARAMS,
        cost_estimate=COST,
    )(raw, *rest)


def edge_raw(x, place, ghost, raw_ref, kept_ref, scale_ref, fix_ref, first_ref):
    depth = kept_ref[place, 2] + on_border(first_ref[...], x)
    more = ghost[0] * (0.5 * ghost[0] + kept_ref[place, 0]) + ghost[1] * kept_ref[place, 1] + ghost[2] * depth
    return raw_ref[x] + on_border(fix_ref[...], x) + more * scale_ref[x // SUB]


def first_kernel(
    density, image_in_ref, raw_ref, kept_ref, scale_ref, fix_ref, first_ref, sum_ref, xleft_ref,
    image_ref, level_ref, sums_ref,
):
    image_ref[...] = image_in_ref[...]
    near = [xleft_ref[c, 1] for c in range(3)]
    far = [xleft_ref[c, 0] - 8.0 * cells for c, cells in enumerate(near)]
    edge_refs = (raw_ref, kept_ref, scale_ref, fix_ref, first_ref)
    gather(density, [edge_raw(0, 0, far, *edge_refs), edge_raw(1, 1, near, *edge_refs)], level_ref, sums_ref, sum_ref)
    for x in range(2):
        blend(level_ref, sums_ref, x, put(image_ref, x))


def last_kernel(
    density, image_in_ref, raw_ref, kept_ref, scale_ref, fix_ref, first_ref, sum_ref, xright_ref,
    image_ref, level_ref, sums_ref,
):
    nx = raw_ref.shape[0]
    views = image_ref.shape[0]
    me = lax.axis_index("view")

    def slot(view):
        return step_to(me, view, views)

    for view in range(views):
        image_ref[slot(view)] = image_in_ref[view]
    near = [-xright_ref[c, 0] for c in range(3)]
    far = [-8.0 * cells - xright_ref[c, 1] for c, cells in enumerate(near)]
    edge_refs = (raw_ref, kept_ref, scale_ref, fix_ref, first_ref)
    raws = [edge_raw(nx - 2, 2, near, *edge_refs), edge_raw(nx - 1, 3, far, *edge_refs)]
    gather(density, raws, level_ref, sums_ref, sum_ref)
    for k in range(2):
        blend(level_ref, sums_ref, k, put(image_ref, nx - 2 + k, slot))


def edged(kernel, density, image, raw, *rest):
    nx, ny, nz = raw.shape
    return pl.pallas_call(
        functools.partial(kernel, density),
        out_shape=jax.ShapeDtypeStruct(image.shape, jnp.float32),
        in_specs=[VMEM] * 8,
        out_specs=VMEM,
        scratch_shapes=row_tables(2, ny, nz, 1),
        compiler_params=PARAMS,
        cost_estimate=COST,
    )(image, raw, *rest)


def turn(block, axis, by):
    count = lax.axis_size(axis)
    return lax.ppermute(block, axis, [(i, (i + by) % count) for i in range(count)])


def both_sides(block, axis):
    before = turn(block, axis, 1)
    return before, before if lax.axis_size(axis) == 2 else turn(block, axis, -1)


def exchange(count):
    if count == 4:
        return [(2, 3, 1, 0), (3, 2, 0, 1), (1, 0, 3, 2)]
    if count & (count - 1) == 0:
        return [tuple(i ^ step for i in range(count)) for step in range(count - 1, 0, -1)]
    return [tuple((i + step) % count for i in range(count)) for step in range(1, count)]


def looked_up(index, table):
    found = jnp.int32(table[0])
    for place, entry in enumerate(table[1:], 1):
        found = jnp.where(index == place, entry, found)
    return found


def step_to(me, other, count):
    steps = [(i,) + targets for i, targets in enumerate(zip(*exchange(count)))]
    return looked_up(me, [targets.index(other) for targets in steps])


def exchanged(blocks, axis):
    routes = exchange(lax.axis_size(axis))
    return [blocks[0]] + [lax.ppermute(blocks[k], axis, list(enumerate(route))) for k, route in enumerate(routes, 1)]


def composite_kernel(*refs):
    *image_refs, out_ref = refs
    count = len(image_refs)
    me = lax.axis_index("view")
    sources = [me] + [looked_up(me, [route.index(i) for i in range(count)]) for route in exchange(count)]
    colour = [0.0] * 3
    through = 1.0
    for source, image_ref in zip(sources, image_refs):
        passing = 1.0
        for other, front_ref in zip(sources, image_refs):
            passing = passing * jnp.where(other < source, front_ref[3], 1.0)
        colour = [total + passing * image_ref[k] for k, total in enumerate(colour)]
        through = through * image_ref[3]
    for k in range(3):
        out_ref[0, 0, k] = colour[k]
    out_ref[0, 0, 3] = 1.0 - through


def composited(images):
    return pl.pallas_call(
        composite_kernel,
        out_shape=jax.ShapeDtypeStruct((1, 1) + images[0].shape, jnp.float32),
        in_specs=[VMEM] * len(images),
        out_specs=VMEM,
        compiler_params=PARAMS,
        cost_estimate=COST,
    )(*images)


def local(velocity, occupied, q_floor, q_span):
    comps, nx, ny, nz = velocity.shape
    views = lax.axis_size("view")
    density = 5.0 / (nz * views)
    xleft = turn(layers(velocity, nx - 2), "gx", 1)
    xright = turn(layers(velocity, 0), "gx", -1)
    u, parts, yface, ztail, zhead = faces(velocity)
    zleft = turn(ztail, "view", 1)
    zright = turn(zhead, "view", -1)
    yleft, yright = both_sides(yface, "gy")
    raw, pack, kept, scale = shaded(u, parts, yleft, yright, occupied[:, :, 0], q_floor, q_span)
    image, fix, first, summer = blended(density, views, raw, pack, scale, zleft, zright)
    shared = (raw, kept, scale, fix, first, summer)
    image = edged(first_kernel, density, image, *shared, xleft)
    blocks = edged(last_kernel, density, image, *shared, xright)
    return composited(exchanged(blocks, "view"))


def solution(mesh):
    placed = (P(None, "gx", "gy", "view"), P("gx", "gy", "view"), P(), P())
    return jax.shard_map(
        local,
        mesh=mesh,
        in_specs=placed,
        out_specs=P("gx", "gy", None, "view", None),
        check_vma=False,
    )
```

```python
import functools
import math

import jax
import jax.numpy as jnp
from jax import lax
from jax.experimental import pallas as pl
from jax.experimental.pallas import tpu as pltpu
from jax.sharding import PartitionSpec as P

SUB = 8
ROWS = 32
VMEM = pl.BlockSpec(memory_space=pltpu.VMEM)
HBM = pl.BlockSpec(memory_space=pltpu.HBM)
COST = pl.CostEstimate(flops=1 << 20, bytes_accessed=1 << 20, transcendentals=0)
PARAMS = pltpu.CompilerParams(vmem_limit_bytes=16 << 20)


def split(values):
    high = values.astype(jnp.bfloat16)
    low = (values - high.astype(jnp.float32)).astype(jnp.bfloat16)
    return high, low


def iota(shape, dim):
    return lax.broadcasted_iota(jnp.int32, shape, dim)


def faces_kernel(u_hbm, u_ref, parts_ref, yface_ref, tail_ref, head_ref, packed_ref, sems):
    comps, nx, ny, nz = u_ref.shape
    quarters = sems.shape[1]
    rows = ny // quarters

    def fetch(c, k):
        span = pl.ds(k * rows if isinstance(k, int) else pl.multiple_of(k * rows, rows), rows)
        return pltpu.make_async_copy(u_hbm.at[c, :, span], u_ref.at[c, :, span], sems.at[c, k])

    for c in range(comps):
        for k in range(quarters):
            fetch(c, k).start()
    slot = iota((8, nz), 1) // 4
    for c in range(comps):

        def quarter(k, carry):
            fetch(c, k).wait()
            start = pl.multiple_of(k * rows, rows)
            packed = [jnp.zeros((8, nz), jnp.float32)] * (rows // 8)
            for x in range(nx):
                cells = u_ref[c, x, pl.ds(start, rows), :]
                high, low = split(cells)
                parts_ref[c, x, pl.ds(start, rows), pl.ds(0, nz)] = high
                parts_ref[c, x, pl.ds(start, rows), pl.ds(nz, nz)] = low
                mine = slot == x
                for n in range(rows // 8):
                    packed[n] = jnp.where(mine, pltpu.roll(cells[8 * n : 8 * n + 8], (4 * x + 2) % nz, 1), packed[n])
            for n in range(rows // 8):
                packed_ref[c, pl.ds(pl.multiple_of(start + 8 * n, 8), 8), :] = packed[n]
            return carry

        lax.fori_loop(0, quarters, quarter, 0)
    sub = iota((8, nz), 0)
    for c in range(comps):
        for x in range(nx):
            lines = jnp.where(sub >= 6, u_ref[c, x, pl.ds(ny - 8, 8), :], u_ref[c, x, pl.ds(0, 8), :])
            yface_ref[c, x] = pltpu.roll(lines, 2, 0)[:4]
    tails, heads = fold([packed_ref[c] for c in range(comps)], ny, nz)
    tail_ref[...] = tails
    head_ref[...] = heads


def fold(packed, ny, nz):
    early = iota((ny, nz), 1) % 4 < 2
    early2 = early[: ny // 2]
    third, fourth = packed[2][: ny // 2], packed[2][ny // 2 :]
    tails = jnp.where(early, packed[0], pltpu.roll(packed[1], 2, 1))
    tails2 = jnp.where(early2, third, pltpu.roll(fourth, 2, 1))
    heads = jnp.where(early, pltpu.roll(packed[0], nz - 2, 1), packed[1])
    heads2 = jnp.where(early2, pltpu.roll(third, nz - 2, 1), fourth)
    return jnp.concatenate([tails, tails2], axis=0), jnp.concatenate([heads, heads2], axis=0)


def unfold(left, right, ny, nz):
    early = iota((ny, nz), 1) % 4 < 2
    early2 = early[: ny // 2]
    left2, right2 = left[ny:], right[ny:]
    left, right = left[:ny], right[:ny]
    first = jnp.where(early, left, pltpu.roll(right, 2, 1))
    second = jnp.where(early, pltpu.roll(left, nz - 2, 1), right)
    third = jnp.where(early2, left2, pltpu.roll(right2, 2, 1))
    fourth = jnp.where(early2, pltpu.roll(left2, nz - 2, 1), right2)
    return first, second, jnp.concatenate([third, fourth], axis=0)


def faces(u):
    comps, nx, ny, nz = u.shape
    message = jax.ShapeDtypeStruct((ny + ny // 2, nz), jnp.float32)
    return pl.pallas_call(
        faces_kernel,
        out_shape=(
            jax.ShapeDtypeStruct(u.shape, jnp.float32),
            jax.ShapeDtypeStruct((comps, nx, ny, 2 * nz), jnp.bfloat16),
            jax.ShapeDtypeStruct((comps, nx, 4, nz), jnp.float32),
            message,
            message,
        ),
        in_specs=[HBM],
        out_specs=(VMEM,) * 5,
        scratch_shapes=[pltpu.VMEM((comps, ny, nz), jnp.float32), pltpu.SemaphoreType.DMA((comps, 4))],
        compiler_params=pltpu.CompilerParams(vmem_limit_bytes=37 << 20),
        cost_estimate=COST,
    )(u)


def stencil(far):
    one = jnp.where(far == 1, 8.0, 0.0) - jnp.where(far == -1, 8.0, 0.0)
    return (one - jnp.where(far == 2, 1.0, 0.0) + jnp.where(far == -2, 1.0, 0.0)).astype(jnp.bfloat16)


def shading(occupied_ref, floor, span, scale_ref, offset_ref):
    blocks, ny, nz = scale_ref.shape
    groups = ny // SUB
    mine = iota((ny, groups), 0) // SUB == iota((ny, groups), 1)
    shrink = 1.0 / span
    for block in range(blocks):
        row = occupied_ref[block : block + 1, :].astype(jnp.float32)
        column = jnp.sum(jnp.where(mine, row, 0.0), axis=1, keepdims=True)
        scale_ref[block] = jnp.broadcast_to(column * (shrink * (-1.0 / 144.0)), (ny, nz))
        offset_ref[block] = jnp.broadcast_to(column * (shrink * -floor), (ny, nz))


def lane_shift(x, nz, back):
    if isinstance(x, int):
        return (4 * x + 2 if back else 2 * nz - 2 - 4 * x) % nz
    return lax.rem(4 * x + 2 if back else 2 * nz - 2 - 4 * x, nz)


def slopes(parts_ref, x, tables, slope_ref):
    yleft_ref, yright_ref, dz_ref, dy_ref = tables
    comps, ny, nz = slope_ref.shape[2:]
    sub = iota((8, nz), 0)

    def top(left):
        lines = jnp.concatenate([left, left], axis=0)
        return jnp.where(sub < 2, lines - jnp.where(sub == 0, 8.0 * pltpu.roll(lines, 7, 0), 0.0), 0.0)

    def low(right):
        lines = jnp.concatenate([right, right], axis=0)
        return jnp.where(sub >= 6, jnp.where(sub == 7, 8.0 * pltpu.roll(lines, 1, 0), 0.0) - lines, 0.0)

    parts = [[parts_ref[c, x + k] for k in range(2)] for c in range(comps)]
    depth = jnp.dot(
        jnp.concatenate([part for pair in parts for part in pair], axis=0),
        dz_ref[...],
        preferred_element_type=jnp.float32,
    )
    for c in range(comps):
        both = jnp.concatenate(
            [jnp.concatenate([part[:, half : half + nz] for part in parts[c]], axis=1) for half in (0, nz)], axis=0
        )
        down = jnp.dot(dy_ref[...], both, preferred_element_type=jnp.float32)
        for k in range(2):
            slope_ref[1, k, c] = depth[(2 * c + k) * ny : (2 * c + k + 1) * ny]
            mine = down[:, k * nz : (k + 1) * nz]
            slope_ref[0, k, c, pl.ds(0, 8), :] = mine[:8] + top(yleft_ref[c, x + k])
            slope_ref[0, k, c, pl.ds(8, ny - 16), :] = mine[8 : ny - 8]
            slope_ref[0, k, c, pl.ds(ny - 8, 8), :] = mine[ny - 8 :] + low(yright_ref[c, x + k])


def shade(u_ref, x, slope_ref, scale_ref, offset_ref, raw_ref, pack_ref, kept_ref=None, place=None):
    comps, nx, ny, nz = u_ref.shape
    block = x // SUB

    def difference(high, low):
        if high is None:
            return 0.0 if low is None else -low
        return high if low is None else high - low

    for y in range(0, ny, ROWS):
        rows = pl.ds(y, ROWS)
        slots = iota((ROWS, nz), 1) // 4
        across = []
        for c in range(comps):
            near = [
                u_ref[c, x + d, rows, :] if not isinstance(x, int) or 0 <= x + d < nx else None for d in range(-2, 4)
            ]
            across.append(
                [8.0 * difference(near[k + 3], near[k + 1]) - difference(near[k + 4], near[k]) for k in range(2)]
            )
        packs = [pack_ref[k, rows, :] for k in range(3)]
        for k in range(2):
            side = [across[c][k] for c in range(comps)]
            down = [slope_ref[0, k, c, rows, :] for c in range(comps)]
            depth = [slope_ref[1, k, c, rows, :] for c in range(comps)]
            total = 0.5 * (side[0] * side[0] + down[1] * down[1] + depth[2] * depth[2])
            total = total + side[1] * down[0] + side[2] * depth[0] + down[2] * depth[1]
            raw_ref[x + k, rows, :] = total * scale_ref[block, rows, :] + offset_ref[block, rows, :]
            back = lane_shift(x + k, nz, True)
            packs = [
                jnp.where(slots == x + k, pltpu.roll(values, back, 1), pack)
                for values, pack in zip((side[2], down[2], depth[2]), packs)
            ]
            if kept_ref is not None:
                for n, values in enumerate((side[0], down[0], depth[0])):
                    kept_ref[place + k, n, rows, :] = values
        for k in range(3):
            pack_ref[k, rows, :] = packs[k]


def shade_kernel(
    u_ref, parts_ref, yleft_ref, yright_ref, occupied_ref, floor_ref, span_ref,
    raw_ref, pack_ref, kept_ref, scale_ref, offset_ref, dz_ref, dy_ref, slope0_ref, slope1_ref,
):
    comps, nx, ny, nz = u_ref.shape
    dz_ref[...] = stencil(iota((2 * nz, nz), 0) % nz - iota((2 * nz, nz), 1))
    dy_ref[...] = stencil(iota((ny, 2 * ny), 1) % ny - iota((ny, 2 * ny), 0))
    shading(occupied_ref, floor_ref[...].reshape(1, 1), span_ref[...].reshape(1, 1), scale_ref, offset_ref)
    pack_ref[...] = jnp.zeros(pack_ref.shape, jnp.float32)
    tables = (yleft_ref, yright_ref, dz_ref, dy_ref)
    outs = (scale_ref, offset_ref, raw_ref, pack_ref)
    slopes(parts_ref, 0, tables, slope0_ref)
    slopes(parts_ref, 2, tables, slope1_ref)
    shade(u_ref, 0, slope0_ref, *outs, kept_ref, 0)

    def pairs(i, carry):
        x = 4 * i + 2
        slopes(parts_ref, x + 2, tables, slope0_ref)
        shade(u_ref, x, slope1_ref, *outs)
        slopes(parts_ref, x + 4, tables, slope1_ref)
        shade(u_ref, x + 2, slope0_ref, *outs)
        return carry

    lax.fori_loop(0, (nx - 4) // 4, pairs, 0)
    shade(u_ref, nx - 2, slope1_ref, *outs, kept_ref, 2)


def shaded(u, *rest):
    comps, nx, ny, nz = u.shape
    return pl.pallas_call(
        shade_kernel,
        out_shape=(
            jax.ShapeDtypeStruct((nx, ny, nz), jnp.float32),
            jax.ShapeDtypeStruct((comps, ny, nz), jnp.float32),
            jax.ShapeDtypeStruct((4, comps, ny, nz), jnp.float32),
            jax.ShapeDtypeStruct((nx // SUB, ny, nz), jnp.float32),
        ),
        in_specs=[VMEM] * 7,
        out_specs=(VMEM,) * 4,
        scratch_shapes=[
            pltpu.VMEM((nx // SUB, ny, nz), jnp.float32),
            pltpu.VMEM((2 * nz, nz), jnp.bfloat16),
            pltpu.VMEM((ny, 2 * ny), jnp.bfloat16),
            pltpu.VMEM((2, 2, comps, ny, nz), jnp.float32),
            pltpu.VMEM((2, 2, comps, ny, nz), jnp.float32),
        ],
        compiler_params=PARAMS,
        cost_estimate=COST,
    )(u, *rest)


def sides_deep(nx, ny, nz, zleft_ref, zright_ref):
    source, target = iota((2 * nz, nz), 0) % nz, iota((2 * nz, nz), 1)
    where = jnp.where(source // 4 == target // 4, source % 4 + 10 * (target % 4), -1)
    weights = jnp.zeros((2 * nz, nz), jnp.float32)
    for value, m, t in ((1.0, 0, 2), (-8.0, 1, 2), (1.0, 1, 3), (-1.0, 2, 0), (8.0, 2, 1), (-1.0, 3, 1)):
        weights = jnp.where(where == m + 10 * t, value, weights)
    weights = weights.astype(jnp.bfloat16)
    return [
        jnp.dot(jnp.concatenate(split(ghost), axis=1), weights, preferred_element_type=jnp.float32)
        for ghost in unfold(zleft_ref[...], zright_ref[...], ny, nz)
    ]


def on_border(packed, x, rows=None):
    ny, nz = packed.shape
    lane = iota((ny, nz), 1)
    return jnp.where((lane >= nz - 2) | (lane < 2), pltpu.roll(packed, lane_shift(x, nz, False), 1), 0.0)


def gather(density, raws, level_ref, sums_ref, sum_ref):
    parts = []
    for k, raw in enumerate(raws):
        level = jnp.clip(raw, 0.0, 1.0)
        level_ref[k] = level
        parts.append(jnp.concatenate(split((density / math.log(2.0)) * level), axis=1))
    ny, nz = level_ref.shape[1:]
    sums = jnp.dot(jnp.concatenate(parts, axis=0), sum_ref[...], preferred_element_type=jnp.float32)
    for k in range(len(raws)):
        sums_ref[k] = sums[k * ny : (k + 1) * ny]


def blend(level_ref, sums_ref, k, store):
    ny, nz = level_ref.shape[1:]
    lane_group = iota((8, ny), 1) // 8
    eye = iota((8, ny), 1) % 8 == iota((8, ny), 0)
    totals = [jnp.zeros((8, ny), jnp.float32)] * 3
    for group in range(ny // 8):
        rows = pl.ds(8 * group, 8)
        level = level_ref[k, rows, :]
        passing = jnp.exp2(sums_ref[k, rows, pl.ds(0, nz)])
        first = (passing - jnp.exp2(sums_ref[k, rows, pl.ds(nz, nz)])) * level
        red = jnp.sum(first, axis=1, keepdims=True)
        square = jnp.sum(first * level, axis=1, keepdims=True)
        whole = sums_ref[k, rows, pl.ds(2 * nz, ny)]
        totals = [jnp.where(lane_group == group, part, total) for part, total in zip((red, square, whole), totals)]
    red, square, whole = [jnp.sum(jnp.where(eye, total, 0.0), axis=0, keepdims=True) for total in totals]
    through = jnp.exp2(whole)
    store(red, 4.0 * (red - square), 1.0 - through - red, through)


def put(image_ref, x, slot=lambda view: view):
    per_view = image_ref.shape[2]
    view, row = (x // per_view, x % per_view) if isinstance(x, int) else (lax.div(x, per_view), lax.rem(x, per_view))

    def store(*channels):
        for k, values in enumerate(channels):
            image_ref[slot(view), k, pl.ds(row, 1), :] = values

    return store


def summing(sum_ref):
    nz = sum_ref.shape[0] // 2
    row = iota(sum_ref.shape, 0) % nz
    col = iota(sum_ref.shape, 1)
    sum_ref[...] = jnp.where((row < col) & (col < nz) | (row <= col - nz), -1.0, 0.0).astype(jnp.bfloat16)


def blend_kernel(
    density, raw_ref, pack_ref, scale_ref, zleft_ref, zright_ref,
    image_ref, fix_ref, first_ref, sum_ref, level0_ref, level1_ref, sums0_ref, sums1_ref,
):
    nx, ny, nz = raw_ref.shape
    summing(sum_ref)
    ghosts = sides_deep(nx, ny, nz, zleft_ref, zright_ref)
    first_ref[...] = ghosts[0]
    fix = ghosts[2] * (0.5 * ghosts[2] + pack_ref[2]) + ghosts[0] * pack_ref[0] + ghosts[1] * pack_ref[1]
    per_block = 4 * SUB
    lane_block = iota((ny, nz), 1) // per_block
    scale = scale_ref[0]
    for block in range(1, nx // SUB):
        scale = jnp.where(lane_block == block, scale_ref[block], scale)
    fix_ref[...] = fix * scale
    image_ref[...] = jnp.zeros(image_ref.shape, jnp.float32)
    batch = level0_ref.shape[0]

    def load(x, level_ref, sums_ref):
        raws = [raw_ref[x + k] + on_border(fix_ref[...], x + k) for k in range(batch)]
        gather(density, raws, level_ref, sums_ref, sum_ref)

    def mix(x, level_ref, sums_ref):
        for k in range(batch):
            blend(level_ref, sums_ref, k, put(image_ref, x + k))

    load(2, level0_ref, sums0_ref)

    def batches(i, carry):
        x = 2 * batch * i + 2
        load(x + batch, level1_ref, sums1_ref)
        mix(x, level0_ref, sums0_ref)
        load(x + 2 * batch, level0_ref, sums0_ref)
        mix(x + batch, level1_ref, sums1_ref)
        return carry

    count = (nx - 4) // batch
    lax.fori_loop(0, (count - 1) // 2, batches, 0)
    if count % 2 == 0:
        load(nx - 2 - batch, level1_ref, sums1_ref)
        mix(nx - 2 - 2 * batch, level0_ref, sums0_ref)
        mix(nx - 2 - batch, level1_ref, sums1_ref)
    else:
        mix(nx - 2 - batch, level0_ref, sums0_ref)


def row_tables(batch, ny, nz, buffers):
    return (
        [pltpu.VMEM((batch, ny, nz), jnp.float32)] * buffers
        + [pltpu.VMEM((batch, ny, 2 * nz + ny), jnp.float32)] * buffers
    )


def blended(density, views, raw, *rest):
    nx, ny, nz = raw.shape
    return pl.pallas_call(
        functools.partial(blend_kernel, density),
        out_shape=(
            jax.ShapeDtypeStruct((views, 4, nx // views, ny), jnp.float32),
            jax.ShapeDtypeStruct((ny, nz), jnp.float32),
            jax.ShapeDtypeStruct((ny, nz), jnp.float32),
            jax.ShapeDtypeStruct((2 * nz, 2 * nz + ny), jnp.bfloat16),
        ),
        in_specs=[VMEM] * 5,
        out_specs=(VMEM,) * 4,
        scratch_shapes=row_tables(4, ny, nz, 2),
        compiler_params=PARAMS,
        cost_estimate=COST,
    )(raw, *rest)


def edge_raw(x, place, ghost, raw_ref, kept_ref, scale_ref, fix_ref, first_ref):
    depth = kept_ref[place, 2] + on_border(first_ref[...], x)
    more = ghost[0] * (0.5 * ghost[0] + kept_ref[place, 0]) + ghost[1] * kept_ref[place, 1] + ghost[2] * depth
    return raw_ref[x] + on_border(fix_ref[...], x) + more * scale_ref[x // SUB]


def first_kernel(
    density, image_in_ref, raw_ref, kept_ref, scale_ref, fix_ref, first_ref, sum_ref, xleft_ref,
    image_ref, level_ref, sums_ref,
):
    image_ref[...] = image_in_ref[...]
    near = [xleft_ref[c, 1] for c in range(3)]
    far = [xleft_ref[c, 0] - 8.0 * cells for c, cells in enumerate(near)]
    edge_refs = (raw_ref, kept_ref, scale_ref, fix_ref, first_ref)
    gather(density, [edge_raw(0, 0, far, *edge_refs), edge_raw(1, 1, near, *edge_refs)], level_ref, sums_ref, sum_ref)
    for x in range(2):
        blend(level_ref, sums_ref, x, put(image_ref, x))


def last_kernel(
    density, image_in_ref, raw_ref, kept_ref, scale_ref, fix_ref, first_ref, sum_ref, xright_ref,
    image_ref, level_ref, sums_ref,
):
    nx = raw_ref.shape[0]
    views = image_ref.shape[0]
    me = lax.axis_index("view")

    def slot(view):
        return step_to(me, view, views)

    for view in range(views):
        image_ref[slot(view)] = image_in_ref[view]
    near = [-xright_ref[c, 0] for c in range(3)]
    far = [-8.0 * cells - xright_ref[c, 1] for c, cells in enumerate(near)]
    edge_refs = (raw_ref, kept_ref, scale_ref, fix_ref, first_ref)
    raws = [edge_raw(nx - 2, 2, near, *edge_refs), edge_raw(nx - 1, 3, far, *edge_refs)]
    gather(density, raws, level_ref, sums_ref, sum_ref)
    for k in range(2):
        blend(level_ref, sums_ref, k, put(image_ref, nx - 2 + k, slot))


def edged(kernel, density, image, raw, *rest):
    nx, ny, nz = raw.shape
    return pl.pallas_call(
        functools.partial(kernel, density),
        out_shape=jax.ShapeDtypeStruct(image.shape, jnp.float32),
        in_specs=[VMEM] * 8,
        out_specs=VMEM,
        scratch_shapes=row_tables(2, ny, nz, 1),
        compiler_params=PARAMS,
        cost_estimate=COST,
    )(image, raw, *rest)


def turn(block, axis, by):
    count = lax.axis_size(axis)
    return lax.ppermute(block, axis, [(i, (i + by) % count) for i in range(count)])


def both_sides(block, axis):
    before = turn(block, axis, 1)
    return before, before if lax.axis_size(axis) == 2 else turn(block, axis, -1)


def exchange(count):
    if count == 4:
        return [(2, 3, 1, 0), (3, 2, 0, 1), (1, 0, 3, 2)]
    if count & (count - 1) == 0:
        return [tuple(i ^ step for i in range(count)) for step in range(count - 1, 0, -1)]
    return [tuple((i + step) % count for i in range(count)) for step in range(1, count)]


def looked_up(index, table):
    found = jnp.int32(table[0])
    for place, entry in enumerate(table[1:], 1):
        found = jnp.where(index == place, entry, found)
    return found


def step_to(me, other, count):
    steps = [(i,) + targets for i, targets in enumerate(zip(*exchange(count)))]
    return looked_up(me, [targets.index(other) for targets in steps])


def exchanged(blocks, axis):
    routes = exchange(lax.axis_size(axis))
    return [blocks[0]] + [lax.ppermute(blocks[k], axis, list(enumerate(route))) for k, route in enumerate(routes, 1)]


def composite_kernel(*refs):
    *image_refs, out_ref = refs
    count = len(image_refs)
    me = lax.axis_index("view")
    sources = [me] + [looked_up(me, [route.index(i) for i in range(count)]) for route in exchange(count)]
    colour = [0.0] * 3
    through = 1.0
    for source, image_ref in zip(sources, image_refs):
        passing = 1.0
        for other, front_ref in zip(sources, image_refs):
            passing = passing * jnp.where(other < source, front_ref[3], 1.0)
        colour = [total + passing * image_ref[k] for k, total in enumerate(colour)]
        through = through * image_ref[3]
    for k in range(3):
        out_ref[0, 0, k] = colour[k]
    out_ref[0, 0, 3] = 1.0 - through


def composited(images):
    return pl.pallas_call(
        composite_kernel,
        out_shape=jax.ShapeDtypeStruct((1, 1) + images[0].shape, jnp.float32),
        in_specs=[VMEM] * len(images),
        out_specs=VMEM,
        compiler_params=PARAMS,
        cost_estimate=COST,
    )(*images)


def local(velocity, occupied, q_floor, q_span):
    comps, nx, ny, nz = velocity.shape
    views = lax.axis_size("view")
    density = 5.0 / (nz * views)
    xtail, later = lax.optimization_barrier((velocity[:, nx - 2 :], velocity))
    xleft = turn(xtail, "gx", 1)
    xright = turn(later[:, :2], "gx", -1)
    u, parts, yface, ztail, zhead = faces(velocity)
    zleft = turn(ztail, "view", 1)
    zright = turn(zhead, "view", -1)
    yleft, yright = both_sides(yface, "gy")
    raw, pack, kept, scale = shaded(u, parts, yleft, yright, occupied[:, :, 0], q_floor, q_span)
    image, fix, first, summer = blended(density, views, raw, pack, scale, zleft, zright)
    shared = (raw, kept, scale, fix, first, summer)
    image = edged(first_kernel, density, image, *shared, xleft)
    blocks = edged(last_kernel, density, image, *shared, xright)
    return composited(exchanged(blocks, "view"))


def solution(mesh):
    placed = (P(None, "gx", "gy", "view"), P("gx", "gy", "view"), P(), P())
    return jax.shard_map(
        local,
        mesh=mesh,
        in_specs=placed,
        out_specs=P("gx", "gy", None, "view", None),
        check_vma=False,
    )
```

```python
import functools
import math

import jax
import jax.numpy as jnp
from jax import lax
from jax.experimental import pallas as pl
from jax.experimental.pallas import tpu as pltpu
from jax.sharding import PartitionSpec as P

SUB = 8
ROWS = 32
VMEM = pl.BlockSpec(memory_space=pltpu.VMEM)
HBM = pl.BlockSpec(memory_space=pltpu.HBM)
COST = pl.CostEstimate(flops=1 << 20, bytes_accessed=1 << 20, transcendentals=0)
PARAMS = pltpu.CompilerParams(vmem_limit_bytes=16 << 20)


def split(values):
    high = values.astype(jnp.bfloat16)
    low = (values - high.astype(jnp.float32)).astype(jnp.bfloat16)
    return high, low


def iota(shape, dim):
    return lax.broadcasted_iota(jnp.int32, shape, dim)


def faces_kernel(u_hbm, u_ref, parts_ref, yface_ref, tail_ref, head_ref, packed_ref, sems):
    comps, nx, ny, nz = u_ref.shape
    quarters = sems.shape[1]
    rows = ny // quarters

    def fetch(c, k):
        span = pl.ds(k * rows if isinstance(k, int) else pl.multiple_of(k * rows, rows), rows)
        return pltpu.make_async_copy(u_hbm.at[c, :, span], u_ref.at[c, :, span], sems.at[c, k])

    for c in range(comps):
        for k in range(quarters):
            fetch(c, k).start()
    slot = iota((8, nz), 1) // 4
    for c in range(comps):

        def quarter(k, carry):
            fetch(c, k).wait()
            start = pl.multiple_of(k * rows, rows)
            packed = [jnp.zeros((8, nz), jnp.float32)] * (rows // 8)
            for x in range(nx):
                cells = u_ref[c, x, pl.ds(start, rows), :]
                high, low = split(cells)
                parts_ref[c, x, pl.ds(start, rows), pl.ds(0, nz)] = high
                parts_ref[c, x, pl.ds(start, rows), pl.ds(nz, nz)] = low
                mine = slot == x
                for n in range(rows // 8):
                    packed[n] = jnp.where(mine, pltpu.roll(cells[8 * n : 8 * n + 8], (4 * x + 2) % nz, 1), packed[n])
            for n in range(rows // 8):
                packed_ref[c, pl.ds(pl.multiple_of(start + 8 * n, 8), 8), :] = packed[n]
            return carry

        lax.fori_loop(0, quarters, quarter, 0)
    sub = iota((8, nz), 0)
    for c in range(comps):
        for x in range(nx):
            lines = jnp.where(sub >= 6, u_ref[c, x, pl.ds(ny - 8, 8), :], u_ref[c, x, pl.ds(0, 8), :])
            yface_ref[c, x] = pltpu.roll(lines, 2, 0)[:4]
    tails, heads = fold([packed_ref[c] for c in range(comps)], ny, nz)
    tail_ref[...] = tails
    head_ref[...] = heads


def fold(packed, ny, nz):
    early = iota((ny, nz), 1) % 4 < 2
    early2 = early[: ny // 2]
    third, fourth = packed[2][: ny // 2], packed[2][ny // 2 :]
    tails = jnp.where(early, packed[0], pltpu.roll(packed[1], 2, 1))
    tails2 = jnp.where(early2, third, pltpu.roll(fourth, 2, 1))
    heads = jnp.where(early, pltpu.roll(packed[0], nz - 2, 1), packed[1])
    heads2 = jnp.where(early2, pltpu.roll(third, nz - 2, 1), fourth)
    return jnp.concatenate([tails, tails2], axis=0), jnp.concatenate([heads, heads2], axis=0)


def unfold(left, right, ny, nz):
    early = iota((ny, nz), 1) % 4 < 2
    early2 = early[: ny // 2]
    left2, right2 = left[ny:], right[ny:]
    left, right = left[:ny], right[:ny]
    first = jnp.where(early, left, pltpu.roll(right, 2, 1))
    second = jnp.where(early, pltpu.roll(left, nz - 2, 1), right)
    third = jnp.where(early2, left2, pltpu.roll(right2, 2, 1))
    fourth = jnp.where(early2, pltpu.roll(left2, nz - 2, 1), right2)
    return first, second, jnp.concatenate([third, fourth], axis=0)


def faces(u):
    comps, nx, ny, nz = u.shape
    message = jax.ShapeDtypeStruct((ny + ny // 2, nz), jnp.float32)
    return pl.pallas_call(
        faces_kernel,
        out_shape=(
            jax.ShapeDtypeStruct(u.shape, jnp.float32),
            jax.ShapeDtypeStruct((comps, nx, ny, 2 * nz), jnp.bfloat16),
            jax.ShapeDtypeStruct((comps, nx, 4, nz), jnp.float32),
            message,
            message,
        ),
        in_specs=[HBM],
        out_specs=(VMEM,) * 5,
        scratch_shapes=[pltpu.VMEM((comps, ny, nz), jnp.float32), pltpu.SemaphoreType.DMA((comps, 4))],
        compiler_params=pltpu.CompilerParams(vmem_limit_bytes=37 << 20),
        cost_estimate=COST,
    )(u)


def stencil(far):
    one = jnp.where(far == 1, 8.0, 0.0) - jnp.where(far == -1, 8.0, 0.0)
    return (one - jnp.where(far == 2, 1.0, 0.0) + jnp.where(far == -2, 1.0, 0.0)).astype(jnp.bfloat16)


def shading(occupied_ref, floor, span, scale_ref, offset_ref):
    blocks, ny, nz = scale_ref.shape
    groups = ny // SUB
    mine = iota((ny, groups), 0) // SUB == iota((ny, groups), 1)
    shrink = 1.0 / span
    for block in range(blocks):
        row = occupied_ref[block : block + 1, :].astype(jnp.float32)
        column = jnp.sum(jnp.where(mine, row, 0.0), axis=1, keepdims=True)
        scale_ref[block] = jnp.broadcast_to(column * (shrink * (-1.0 / 144.0)), (ny, nz))
        offset_ref[block] = jnp.broadcast_to(column * (shrink * -floor), (ny, nz))


def lane_shift(x, nz, back):
    if isinstance(x, int):
        return (4 * x + 2 if back else 2 * nz - 2 - 4 * x) % nz
    return lax.rem(4 * x + 2 if back else 2 * nz - 2 - 4 * x, nz)


def slopes(parts_ref, x, tables, slope_ref):
    yleft_ref, yright_ref, dz_ref, dy_ref = tables
    comps, ny, nz = slope_ref.shape[2:]
    sub = iota((8, nz), 0)

    def top(left):
        lines = jnp.concatenate([left, left], axis=0)
        return jnp.where(sub < 2, lines - jnp.where(sub == 0, 8.0 * pltpu.roll(lines, 7, 0), 0.0), 0.0)

    def low(right):
        lines = jnp.concatenate([right, right], axis=0)
        return jnp.where(sub >= 6, jnp.where(sub == 7, 8.0 * pltpu.roll(lines, 1, 0), 0.0) - lines, 0.0)

    parts = [[parts_ref[c, x + k] for k in range(2)] for c in range(comps)]
    depth = jnp.dot(
        jnp.concatenate([part for pair in parts for part in pair], axis=0),
        dz_ref[...],
        preferred_element_type=jnp.float32,
    )
    for c in range(comps):
        both = jnp.concatenate(
            [jnp.concatenate([part[:, half : half + nz] for part in parts[c]], axis=1) for half in (0, nz)], axis=0
        )
        down = jnp.dot(dy_ref[...], both, preferred_element_type=jnp.float32)
        for k in range(2):
            slope_ref[1, k, c] = depth[(2 * c + k) * ny : (2 * c + k + 1) * ny]
            mine = down[:, k * nz : (k + 1) * nz]
            slope_ref[0, k, c, pl.ds(0, 8), :] = mine[:8] + top(yleft_ref[c, x + k])
            slope_ref[0, k, c, pl.ds(8, ny - 16), :] = mine[8 : ny - 8]
            slope_ref[0, k, c, pl.ds(ny - 8, 8), :] = mine[ny - 8 :] + low(yright_ref[c, x + k])


def shade(u_ref, x, slope_ref, scale_ref, offset_ref, raw_ref, pack_ref, kept_ref=None, place=None):
    comps, nx, ny, nz = u_ref.shape
    block = x // SUB

    def difference(high, low):
        if high is None:
            return 0.0 if low is None else -low
        return high if low is None else high - low

    for y in range(0, ny, ROWS):
        rows = pl.ds(y, ROWS)
        slots = iota((ROWS, nz), 1) // 4
        across = []
        for c in range(comps):
            near = [
                u_ref[c, x + d, rows, :] if not isinstance(x, int) or 0 <= x + d < nx else None for d in range(-2, 4)
            ]
            across.append(
                [8.0 * difference(near[k + 3], near[k + 1]) - difference(near[k + 4], near[k]) for k in range(2)]
            )
        packs = [pack_ref[k, rows, :] for k in range(3)]
        for k in range(2):
            side = [across[c][k] for c in range(comps)]
            down = [slope_ref[0, k, c, rows, :] for c in range(comps)]
            depth = [slope_ref[1, k, c, rows, :] for c in range(comps)]
            total = 0.5 * (side[0] * side[0] + down[1] * down[1] + depth[2] * depth[2])
            total = total + side[1] * down[0] + side[2] * depth[0] + down[2] * depth[1]
            raw_ref[x + k, rows, :] = total * scale_ref[block, rows, :] + offset_ref[block, rows, :]
            back = lane_shift(x + k, nz, True)
            packs = [
                jnp.where(slots == x + k, pltpu.roll(values, back, 1), pack)
                for values, pack in zip((side[2], down[2], depth[2]), packs)
            ]
            if kept_ref is not None:
                for n, values in enumerate((side[0], down[0], depth[0])):
                    kept_ref[place + k, n, rows, :] = values
        for k in range(3):
            pack_ref[k, rows, :] = packs[k]


def shade_kernel(
    u_ref, parts_ref, yleft_ref, yright_ref, occupied_ref, floor_ref, span_ref,
    raw_ref, pack_ref, kept_ref, scale_ref, offset_ref, dz_ref, dy_ref, slope0_ref, slope1_ref,
):
    comps, nx, ny, nz = u_ref.shape
    dz_ref[...] = stencil(iota((2 * nz, nz), 0) % nz - iota((2 * nz, nz), 1))
    dy_ref[...] = stencil(iota((ny, 2 * ny), 1) % ny - iota((ny, 2 * ny), 0))
    shading(occupied_ref, floor_ref[...].reshape(1, 1), span_ref[...].reshape(1, 1), scale_ref, offset_ref)
    pack_ref[...] = jnp.zeros(pack_ref.shape, jnp.float32)
    tables = (yleft_ref, yright_ref, dz_ref, dy_ref)
    outs = (scale_ref, offset_ref, raw_ref, pack_ref)
    slopes(parts_ref, 0, tables, slope0_ref)
    slopes(parts_ref, 2, tables, slope1_ref)
    shade(u_ref, 0, slope0_ref, *outs, kept_ref, 0)

    def pairs(i, carry):
        x = 4 * i + 2
        slopes(parts_ref, x + 2, tables, slope0_ref)
        shade(u_ref, x, slope1_ref, *outs)
        slopes(parts_ref, x + 4, tables, slope1_ref)
        shade(u_ref, x + 2, slope0_ref, *outs)
        return carry

    lax.fori_loop(0, (nx - 4) // 4, pairs, 0)
    shade(u_ref, nx - 2, slope1_ref, *outs, kept_ref, 2)


def shaded(u, *rest):
    comps, nx, ny, nz = u.shape
    return pl.pallas_call(
        shade_kernel,
        out_shape=(
            jax.ShapeDtypeStruct((nx, ny, nz), jnp.float32),
            jax.ShapeDtypeStruct((comps, ny, nz), jnp.float32),
            jax.ShapeDtypeStruct((4, comps, ny, nz), jnp.float32),
            jax.ShapeDtypeStruct((nx // SUB, ny, nz), jnp.float32),
        ),
        in_specs=[VMEM] * 7,
        out_specs=(VMEM,) * 4,
        scratch_shapes=[
            pltpu.VMEM((nx // SUB, ny, nz), jnp.float32),
            pltpu.VMEM((2 * nz, nz), jnp.bfloat16),
            pltpu.VMEM((ny, 2 * ny), jnp.bfloat16),
            pltpu.VMEM((2, 2, comps, ny, nz), jnp.float32),
            pltpu.VMEM((2, 2, comps, ny, nz), jnp.float32),
        ],
        compiler_params=PARAMS,
        cost_estimate=COST,
    )(u, *rest)


def sides_deep(nx, ny, nz, zleft_ref, zright_ref):
    source, target = iota((2 * nz, nz), 0) % nz, iota((2 * nz, nz), 1)
    where = jnp.where(source // 4 == target // 4, source % 4 + 10 * (target % 4), -1)
    weights = jnp.zeros((2 * nz, nz), jnp.float32)
    for value, m, t in ((1.0, 0, 2), (-8.0, 1, 2), (1.0, 1, 3), (-1.0, 2, 0), (8.0, 2, 1), (-1.0, 3, 1)):
        weights = jnp.where(where == m + 10 * t, value, weights)
    weights = weights.astype(jnp.bfloat16)
    return [
        jnp.dot(jnp.concatenate(split(ghost), axis=1), weights, preferred_element_type=jnp.float32)
        for ghost in unfold(zleft_ref[...], zright_ref[...], ny, nz)
    ]


def on_border(packed, x, rows=None):
    ny, nz = packed.shape
    lane = iota((ny, nz), 1)
    return jnp.where((lane >= nz - 2) | (lane < 2), pltpu.roll(packed, lane_shift(x, nz, False), 1), 0.0)


def gather(density, raws, level_ref, sums_ref, sum_ref):
    parts = []
    for k, raw in enumerate(raws):
        level = jnp.clip(raw, 0.0, 1.0)
        level_ref[k] = level
        parts.append(jnp.concatenate(split((density / math.log(2.0)) * level), axis=1))
    ny, nz = level_ref.shape[1:]
    sums = jnp.dot(jnp.concatenate(parts, axis=0), sum_ref[...], preferred_element_type=jnp.float32)
    for k in range(len(raws)):
        sums_ref[k] = sums[k * ny : (k + 1) * ny]


def blend(level_ref, sums_ref, k, store):
    ny, nz = level_ref.shape[1:]
    lane_group = iota((8, ny), 1) // 8
    eye = iota((8, ny), 1) % 8 == iota((8, ny), 0)
    totals = [jnp.zeros((8, ny), jnp.float32)] * 3
    for group in range(ny // 8):
        rows = pl.ds(8 * group, 8)
        level = level_ref[k, rows, :]
        passing = jnp.exp2(sums_ref[k, rows, pl.ds(0, nz)])
        first = (passing - jnp.exp2(sums_ref[k, rows, pl.ds(nz, nz)])) * level
        red = jnp.sum(first, axis=1, keepdims=True)
        square = jnp.sum(first * level, axis=1, keepdims=True)
        whole = sums_ref[k, rows, pl.ds(2 * nz, ny)]
        totals = [jnp.where(lane_group == group, part, total) for part, total in zip((red, square, whole), totals)]
    red, square, whole = [jnp.sum(jnp.where(eye, total, 0.0), axis=0, keepdims=True) for total in totals]
    through = jnp.exp2(whole)
    store(red, square, through)


def put(image_ref, x, slot=lambda view: view):
    per_view = image_ref.shape[2]
    view, row = (x // per_view, x % per_view) if isinstance(x, int) else (lax.div(x, per_view), lax.rem(x, per_view))

    def store(*channels):
        for k, values in enumerate(channels):
            image_ref[slot(view), k, pl.ds(row, 1), :] = values

    return store


def summing(sum_ref):
    nz = sum_ref.shape[0] // 2
    row = iota(sum_ref.shape, 0) % nz
    col = iota(sum_ref.shape, 1)
    sum_ref[...] = jnp.where((row < col) & (col < nz) | (row <= col - nz), -1.0, 0.0).astype(jnp.bfloat16)


def blend_kernel(
    density, raw_ref, pack_ref, scale_ref, zleft_ref, zright_ref,
    image_ref, fix_ref, first_ref, sum_ref, level0_ref, level1_ref, sums0_ref, sums1_ref,
):
    nx, ny, nz = raw_ref.shape
    summing(sum_ref)
    ghosts = sides_deep(nx, ny, nz, zleft_ref, zright_ref)
    first_ref[...] = ghosts[0]
    fix = ghosts[2] * (0.5 * ghosts[2] + pack_ref[2]) + ghosts[0] * pack_ref[0] + ghosts[1] * pack_ref[1]
    per_block = 4 * SUB
    lane_block = iota((ny, nz), 1) // per_block
    scale = scale_ref[0]
    for block in range(1, nx // SUB):
        scale = jnp.where(lane_block == block, scale_ref[block], scale)
    fix_ref[...] = fix * scale
    image_ref[...] = jnp.zeros(image_ref.shape, jnp.float32)
    batch = level0_ref.shape[0]

    def load(x, level_ref, sums_ref):
        raws = [raw_ref[x + k] + on_border(fix_ref[...], x + k) for k in range(batch)]
        gather(density, raws, level_ref, sums_ref, sum_ref)

    def mix(x, level_ref, sums_ref):
        for k in range(batch):
            blend(level_ref, sums_ref, k, put(image_ref, x + k))

    load(2, level0_ref, sums0_ref)

    def batches(i, carry):
        x = 2 * batch * i + 2
        load(x + batch, level1_ref, sums1_ref)
        mix(x, level0_ref, sums0_ref)
        load(x + 2 * batch, level0_ref, sums0_ref)
        mix(x + batch, level1_ref, sums1_ref)
        return carry

    count = (nx - 4) // batch
    lax.fori_loop(0, (count - 1) // 2, batches, 0)
    if count % 2 == 0:
        load(nx - 2 - batch, level1_ref, sums1_ref)
        mix(nx - 2 - 2 * batch, level0_ref, sums0_ref)
        mix(nx - 2 - batch, level1_ref, sums1_ref)
    else:
        mix(nx - 2 - batch, level0_ref, sums0_ref)


def row_tables(batch, ny, nz, buffers):
    return (
        [pltpu.VMEM((batch, ny, nz), jnp.float32)] * buffers
        + [pltpu.VMEM((batch, ny, 2 * nz + ny), jnp.float32)] * buffers
    )


def blended(density, views, raw, *rest):
    nx, ny, nz = raw.shape
    return pl.pallas_call(
        functools.partial(blend_kernel, density),
        out_shape=(
            jax.ShapeDtypeStruct((views, 3, nx // views, ny), jnp.float32),
            jax.ShapeDtypeStruct((ny, nz), jnp.float32),
            jax.ShapeDtypeStruct((ny, nz), jnp.float32),
            jax.ShapeDtypeStruct((2 * nz, 2 * nz + ny), jnp.bfloat16),
        ),
        in_specs=[VMEM] * 5,
        out_specs=(VMEM,) * 4,
        scratch_shapes=row_tables(4, ny, nz, 2),
        compiler_params=PARAMS,
        cost_estimate=COST,
    )(raw, *rest)


def edge_raw(x, place, ghost, raw_ref, kept_ref, scale_ref, fix_ref, first_ref):
    depth = kept_ref[place, 2] + on_border(first_ref[...], x)
    more = ghost[0] * (0.5 * ghost[0] + kept_ref[place, 0]) + ghost[1] * kept_ref[place, 1] + ghost[2] * depth
    return raw_ref[x] + on_border(fix_ref[...], x) + more * scale_ref[x // SUB]


def first_kernel(
    density, image_in_ref, raw_ref, kept_ref, scale_ref, fix_ref, first_ref, sum_ref, xleft_ref,
    image_ref, level_ref, sums_ref,
):
    image_ref[...] = image_in_ref[...]
    near = [xleft_ref[c, 1] for c in range(3)]
    far = [xleft_ref[c, 0] - 8.0 * cells for c, cells in enumerate(near)]
    edge_refs = (raw_ref, kept_ref, scale_ref, fix_ref, first_ref)
    gather(density, [edge_raw(0, 0, far, *edge_refs), edge_raw(1, 1, near, *edge_refs)], level_ref, sums_ref, sum_ref)
    for x in range(2):
        blend(level_ref, sums_ref, x, put(image_ref, x))


def last_kernel(
    density, image_in_ref, raw_ref, kept_ref, scale_ref, fix_ref, first_ref, sum_ref, xright_ref,
    image_ref, level_ref, sums_ref,
):
    nx = raw_ref.shape[0]
    views = image_ref.shape[0]
    me = lax.axis_index("view")

    def slot(view):
        return step_to(me, view, views)

    for view in range(views):
        image_ref[slot(view)] = image_in_ref[view]
    near = [-xright_ref[c, 0] for c in range(3)]
    far = [-8.0 * cells - xright_ref[c, 1] for c, cells in enumerate(near)]
    edge_refs = (raw_ref, kept_ref, scale_ref, fix_ref, first_ref)
    raws = [edge_raw(nx - 2, 2, near, *edge_refs), edge_raw(nx - 1, 3, far, *edge_refs)]
    gather(density, raws, level_ref, sums_ref, sum_ref)
    for k in range(2):
        blend(level_ref, sums_ref, k, put(image_ref, nx - 2 + k, slot))


def edged(kernel, density, image, raw, *rest):
    nx, ny, nz = raw.shape
    return pl.pallas_call(
        functools.partial(kernel, density),
        out_shape=jax.ShapeDtypeStruct(image.shape, jnp.float32),
        in_specs=[VMEM] * 8,
        out_specs=VMEM,
        scratch_shapes=row_tables(2, ny, nz, 1),
        compiler_params=PARAMS,
        cost_estimate=COST,
    )(image, raw, *rest)


def turn(block, axis, by):
    count = lax.axis_size(axis)
    return lax.ppermute(block, axis, [(i, (i + by) % count) for i in range(count)])


def both_sides(block, axis):
    before = turn(block, axis, 1)
    return before, before if lax.axis_size(axis) == 2 else turn(block, axis, -1)


def exchange(count):
    if count == 4:
        return [(2, 3, 1, 0), (3, 2, 0, 1), (1, 0, 3, 2)]
    if count & (count - 1) == 0:
        return [tuple(i ^ step for i in range(count)) for step in range(count - 1, 0, -1)]
    return [tuple((i + step) % count for i in range(count)) for step in range(1, count)]


def looked_up(index, table):
    found = jnp.int32(table[0])
    for place, entry in enumerate(table[1:], 1):
        found = jnp.where(index == place, entry, found)
    return found


def step_to(me, other, count):
    steps = [(i,) + targets for i, targets in enumerate(zip(*exchange(count)))]
    return looked_up(me, [targets.index(other) for targets in steps])


def exchanged(blocks, axis):
    routes = exchange(lax.axis_size(axis))
    return [blocks[0]] + [lax.ppermute(blocks[k], axis, list(enumerate(route))) for k, route in enumerate(routes, 1)]


def composite_kernel(*refs):
    *image_refs, out_ref = refs
    count = len(image_refs)
    me = lax.axis_index("view")
    sources = [me] + [looked_up(me, [route.index(i) for i in range(count)]) for route in exchange(count)]
    red = square = 0.0
    through = 1.0
    for source, image_ref in zip(sources, image_refs):
        passing = 1.0
        for other, front_ref in zip(sources, image_refs):
            passing = passing * jnp.where(other < source, front_ref[2], 1.0)
        red = red + passing * image_ref[0]
        square = square + passing * image_ref[1]
        through = through * image_ref[2]
    for k, values in enumerate((red, 4.0 * (red - square), 1.0 - through - red, 1.0 - through)):
        out_ref[0, 0, k] = values


def composited(images):
    return pl.pallas_call(
        composite_kernel,
        out_shape=jax.ShapeDtypeStruct((1, 1, 4) + images[0].shape[1:], jnp.float32),
        in_specs=[VMEM] * len(images),
        out_specs=VMEM,
        compiler_params=PARAMS,
        cost_estimate=COST,
    )(*images)


def local(velocity, occupied, q_floor, q_span):
    comps, nx, ny, nz = velocity.shape
    views = lax.axis_size("view")
    density = 5.0 / (nz * views)
    xleft = turn(velocity[:, nx - 2 :], "gx", 1)
    xright = turn(velocity[:, :2], "gx", -1)
    u, parts, yface, ztail, zhead = faces(velocity)
    zleft = turn(ztail, "view", 1)
    zright = turn(zhead, "view", -1)
    yleft, yright = both_sides(yface, "gy")
    raw, pack, kept, scale = shaded(u, parts, yleft, yright, occupied[:, :, 0], q_floor, q_span)
    image, fix, first, summer = blended(density, views, raw, pack, scale, zleft, zright)
    shared = (raw, kept, scale, fix, first, summer)
    image = edged(first_kernel, density, image, *shared, xleft)
    blocks = edged(last_kernel, density, image, *shared, xright)
    return composited(exchanged(blocks, "view"))


def solution(mesh):
    placed = (P(None, "gx", "gy", "view"), P("gx", "gy", "view"), P(), P())
    return jax.shard_map(
        local,
        mesh=mesh,
        in_specs=placed,
        out_specs=P("gx", "gy", None, "view", None),
        check_vma=False,
    )
```

```python
import functools
import math

import jax
import jax.numpy as jnp
from jax import lax
from jax.experimental import pallas as pl
from jax.experimental.pallas import tpu as pltpu
from jax.sharding import PartitionSpec as P

SUB = 8
ROWS = 32
VMEM = pl.BlockSpec(memory_space=pltpu.VMEM)
HBM = pl.BlockSpec(memory_space=pltpu.HBM)
COST = pl.CostEstimate(flops=1 << 20, bytes_accessed=1 << 20, transcendentals=0)
PARAMS = pltpu.CompilerParams(vmem_limit_bytes=16 << 20)


def split(values):
    high = values.astype(jnp.bfloat16)
    low = (values - high.astype(jnp.float32)).astype(jnp.bfloat16)
    return high, low


def iota(shape, dim):
    return lax.broadcasted_iota(jnp.int32, shape, dim)


def faces_kernel(u_hbm, u_ref, parts_ref, yface_ref, tail_ref, head_ref, packed_ref, sems):
    comps, nx, ny, nz = u_ref.shape
    quarters = sems.shape[1]
    rows = ny // quarters

    def fetch(c, k):
        span = pl.ds(k * rows if isinstance(k, int) else pl.multiple_of(k * rows, rows), rows)
        return pltpu.make_async_copy(u_hbm.at[c, :, span], u_ref.at[c, :, span], sems.at[c, k])

    for c in range(comps):
        for k in range(quarters):
            fetch(c, k).start()
    slot = iota((8, nz), 1) // 4
    for c in range(comps):

        def quarter(k, carry):
            fetch(c, k).wait()
            start = pl.multiple_of(k * rows, rows)
            packed = [jnp.zeros((8, nz), jnp.float32)] * (rows // 8)
            for x in range(nx):
                cells = u_ref[c, x, pl.ds(start, rows), :]
                high, low = split(cells)
                parts_ref[c, x, pl.ds(start, rows), pl.ds(0, nz)] = high
                parts_ref[c, x, pl.ds(start, rows), pl.ds(nz, nz)] = low
                mine = slot == x
                for n in range(rows // 8):
                    packed[n] = jnp.where(mine, pltpu.roll(cells[8 * n : 8 * n + 8], (4 * x + 2) % nz, 1), packed[n])
            for n in range(rows // 8):
                packed_ref[c, pl.ds(pl.multiple_of(start + 8 * n, 8), 8), :] = packed[n]
            return carry

        lax.fori_loop(0, quarters, quarter, 0)
    sub = iota((8, nz), 0)
    for c in range(comps):
        for x in range(nx):
            lines = jnp.where(sub >= 6, u_ref[c, x, pl.ds(ny - 8, 8), :], u_ref[c, x, pl.ds(0, 8), :])
            yface_ref[c, x] = pltpu.roll(lines, 2, 0)[:4]
    tails, heads = fold([packed_ref[c] for c in range(comps)], ny, nz)
    tail_ref[...] = tails
    head_ref[...] = heads


def fold(packed, ny, nz):
    early = iota((ny, nz), 1) % 4 < 2
    early2 = early[: ny // 2]
    third, fourth = packed[2][: ny // 2], packed[2][ny // 2 :]
    tails = jnp.where(early, packed[0], pltpu.roll(packed[1], 2, 1))
    tails2 = jnp.where(early2, third, pltpu.roll(fourth, 2, 1))
    heads = jnp.where(early, pltpu.roll(packed[0], nz - 2, 1), packed[1])
    heads2 = jnp.where(early2, pltpu.roll(third, nz - 2, 1), fourth)
    return jnp.concatenate([tails, tails2], axis=0), jnp.concatenate([heads, heads2], axis=0)


def unfold(left, right, ny, nz):
    early = iota((ny, nz), 1) % 4 < 2
    early2 = early[: ny // 2]
    left2, right2 = left[ny:], right[ny:]
    left, right = left[:ny], right[:ny]
    first = jnp.where(early, left, pltpu.roll(right, 2, 1))
    second = jnp.where(early, pltpu.roll(left, nz - 2, 1), right)
    third = jnp.where(early2, left2, pltpu.roll(right2, 2, 1))
    fourth = jnp.where(early2, pltpu.roll(left2, nz - 2, 1), right2)
    return first, second, jnp.concatenate([third, fourth], axis=0)


def faces(u):
    comps, nx, ny, nz = u.shape
    message = jax.ShapeDtypeStruct((ny + ny // 2, nz), jnp.float32)
    return pl.pallas_call(
        faces_kernel,
        out_shape=(
            jax.ShapeDtypeStruct(u.shape, jnp.float32),
            jax.ShapeDtypeStruct((comps, nx, ny, 2 * nz), jnp.bfloat16),
            jax.ShapeDtypeStruct((comps, nx, 4, nz), jnp.float32),
            message,
            message,
        ),
        in_specs=[HBM],
        out_specs=(VMEM,) * 5,
        scratch_shapes=[pltpu.VMEM((comps, ny, nz), jnp.float32), pltpu.SemaphoreType.DMA((comps, 4))],
        compiler_params=pltpu.CompilerParams(vmem_limit_bytes=37 << 20),
        cost_estimate=COST,
    )(u)


def stencil(far):
    one = jnp.where(far == 1, 8.0, 0.0) - jnp.where(far == -1, 8.0, 0.0)
    return (one - jnp.where(far == 2, 1.0, 0.0) + jnp.where(far == -2, 1.0, 0.0)).astype(jnp.bfloat16)


def shading(occupied_ref, floor, span, scale_ref, offset_ref):
    blocks, ny, nz = scale_ref.shape
    groups = ny // SUB
    mine = iota((ny, groups), 0) // SUB == iota((ny, groups), 1)
    shrink = 1.0 / span
    for block in range(blocks):
        row = occupied_ref[block : block + 1, :].astype(jnp.float32)
        column = jnp.sum(jnp.where(mine, row, 0.0), axis=1, keepdims=True)
        scale_ref[block] = jnp.broadcast_to(column * (shrink * (-1.0 / 144.0)), (ny, nz))
        offset_ref[block] = jnp.broadcast_to(column * (shrink * -floor), (ny, nz))


def lane_shift(x, nz, back):
    if isinstance(x, int):
        return (4 * x + 2 if back else 2 * nz - 2 - 4 * x) % nz
    return lax.rem(4 * x + 2 if back else 2 * nz - 2 - 4 * x, nz)


def slopes(parts_ref, x, tables, slope_ref):
    yleft_ref, yright_ref, dz_ref, dy_ref = tables
    comps, ny, nz = slope_ref.shape[2:]
    sub = iota((8, nz), 0)

    def top(left):
        lines = jnp.concatenate([left, left], axis=0)
        return jnp.where(sub < 2, lines - jnp.where(sub == 0, 8.0 * pltpu.roll(lines, 7, 0), 0.0), 0.0)

    def low(right):
        lines = jnp.concatenate([right, right], axis=0)
        return jnp.where(sub >= 6, jnp.where(sub == 7, 8.0 * pltpu.roll(lines, 1, 0), 0.0) - lines, 0.0)

    parts = [[parts_ref[c, x + k] for k in range(2)] for c in range(comps)]
    depth = jnp.dot(
        jnp.concatenate([part for pair in parts for part in pair], axis=0),
        dz_ref[...],
        preferred_element_type=jnp.float32,
    )
    for c in range(comps):
        both = jnp.concatenate(
            [jnp.concatenate([part[:, half : half + nz] for part in parts[c]], axis=1) for half in (0, nz)], axis=0
        )
        down = jnp.dot(dy_ref[...], both, preferred_element_type=jnp.float32)
        for k in range(2):
            slope_ref[1, k, c] = depth[(2 * c + k) * ny : (2 * c + k + 1) * ny]
            mine = down[:, k * nz : (k + 1) * nz]
            slope_ref[0, k, c, pl.ds(0, 8), :] = mine[:8] + top(yleft_ref[c, x + k])
            slope_ref[0, k, c, pl.ds(8, ny - 16), :] = mine[8 : ny - 8]
            slope_ref[0, k, c, pl.ds(ny - 8, 8), :] = mine[ny - 8 :] + low(yright_ref[c, x + k])


def shade(u_ref, x, slope_ref, scale_ref, offset_ref, raw_ref, pack_ref, kept_ref=None, place=None):
    comps, nx, ny, nz = u_ref.shape
    block = x // SUB

    def difference(high, low):
        if high is None:
            return 0.0 if low is None else -low
        return high if low is None else high - low

    for y in range(0, ny, ROWS):
        rows = pl.ds(y, ROWS)
        slots = iota((ROWS, nz), 1) // 4
        across = []
        for c in range(comps):
            near = [
                u_ref[c, x + d, rows, :] if not isinstance(x, int) or 0 <= x + d < nx else None for d in range(-2, 4)
            ]
            across.append(
                [8.0 * difference(near[k + 3], near[k + 1]) - difference(near[k + 4], near[k]) for k in range(2)]
            )
        packs = [pack_ref[k, rows, :] for k in range(3)]
        for k in range(2):
            side = [across[c][k] for c in range(comps)]
            down = [slope_ref[0, k, c, rows, :] for c in range(comps)]
            depth = [slope_ref[1, k, c, rows, :] for c in range(comps)]
            total = 0.5 * (side[0] * side[0] + down[1] * down[1] + depth[2] * depth[2])
            total = total + side[1] * down[0] + side[2] * depth[0] + down[2] * depth[1]
            raw_ref[x + k, rows, :] = total * scale_ref[block, rows, :] + offset_ref[block, rows, :]
            back = lane_shift(x + k, nz, True)
            packs = [
                jnp.where(slots == x + k, pltpu.roll(values, back, 1), pack)
                for values, pack in zip((side[2], down[2], depth[2]), packs)
            ]
            if kept_ref is not None:
                for n, values in enumerate((side[0], down[0], depth[0])):
                    kept_ref[place + k, n, rows, :] = values
        for k in range(3):
            pack_ref[k, rows, :] = packs[k]


def shade_kernel(
    u_ref, parts_ref, yleft_ref, yright_ref, occupied_ref, floor_ref, span_ref,
    raw_ref, pack_ref, kept_ref, scale_ref, offset_ref, dz_ref, dy_ref, slope0_ref, slope1_ref,
):
    comps, nx, ny, nz = u_ref.shape
    dz_ref[...] = stencil(iota((2 * nz, nz), 0) % nz - iota((2 * nz, nz), 1))
    dy_ref[...] = stencil(iota((ny, 2 * ny), 1) % ny - iota((ny, 2 * ny), 0))
    shading(occupied_ref, floor_ref[...].reshape(1, 1), span_ref[...].reshape(1, 1), scale_ref, offset_ref)
    pack_ref[...] = jnp.zeros(pack_ref.shape, jnp.float32)
    tables = (yleft_ref, yright_ref, dz_ref, dy_ref)
    outs = (scale_ref, offset_ref, raw_ref, pack_ref)
    slopes(parts_ref, 0, tables, slope0_ref)
    slopes(parts_ref, 2, tables, slope1_ref)
    shade(u_ref, 0, slope0_ref, *outs, kept_ref, 0)

    def pairs(i, carry):
        x = 4 * i + 2
        slopes(parts_ref, x + 2, tables, slope0_ref)
        shade(u_ref, x, slope1_ref, *outs)
        slopes(parts_ref, x + 4, tables, slope1_ref)
        shade(u_ref, x + 2, slope0_ref, *outs)
        return carry

    lax.fori_loop(0, (nx - 4) // 4, pairs, 0)
    shade(u_ref, nx - 2, slope1_ref, *outs, kept_ref, 2)


def shaded(u, *rest):
    comps, nx, ny, nz = u.shape
    return pl.pallas_call(
        shade_kernel,
        out_shape=(
            jax.ShapeDtypeStruct((nx, ny, nz), jnp.float32),
            jax.ShapeDtypeStruct((comps, ny, nz), jnp.float32),
            jax.ShapeDtypeStruct((4, comps, ny, nz), jnp.float32),
            jax.ShapeDtypeStruct((nx // SUB, ny, nz), jnp.float32),
        ),
        in_specs=[VMEM] * 7,
        out_specs=(VMEM,) * 4,
        scratch_shapes=[
            pltpu.VMEM((nx // SUB, ny, nz), jnp.float32),
            pltpu.VMEM((2 * nz, nz), jnp.bfloat16),
            pltpu.VMEM((ny, 2 * ny), jnp.bfloat16),
            pltpu.VMEM((2, 2, comps, ny, nz), jnp.float32),
            pltpu.VMEM((2, 2, comps, ny, nz), jnp.float32),
        ],
        compiler_params=PARAMS,
        cost_estimate=COST,
    )(u, *rest)


def sides_deep(nx, ny, nz, zleft_ref, zright_ref):
    source, target = iota((2 * nz, nz), 0) % nz, iota((2 * nz, nz), 1)
    where = jnp.where(source // 4 == target // 4, source % 4 + 10 * (target % 4), -1)
    weights = jnp.zeros((2 * nz, nz), jnp.float32)
    for value, m, t in ((1.0, 0, 2), (-8.0, 1, 2), (1.0, 1, 3), (-1.0, 2, 0), (8.0, 2, 1), (-1.0, 3, 1)):
        weights = jnp.where(where == m + 10 * t, value, weights)
    weights = weights.astype(jnp.bfloat16)
    return [
        jnp.dot(jnp.concatenate(split(ghost), axis=1), weights, preferred_element_type=jnp.float32)
        for ghost in unfold(zleft_ref[...], zright_ref[...], ny, nz)
    ]


def on_border(packed, x, rows=None):
    ny, nz = packed.shape
    lane = iota((ny, nz), 1)
    return jnp.where((lane >= nz - 2) | (lane < 2), pltpu.roll(packed, lane_shift(x, nz, False), 1), 0.0)


def gather(density, raws, level_ref, sums_ref, sum_ref):
    parts = []
    for k, raw in enumerate(raws):
        level = jnp.clip(raw, 0.0, 1.0)
        level_ref[k] = level
        parts.append(jnp.concatenate(split((density / math.log(2.0)) * level), axis=1))
    ny, nz = level_ref.shape[1:]
    sums = jnp.dot(jnp.concatenate(parts, axis=0), sum_ref[...], preferred_element_type=jnp.float32)
    for k in range(len(raws)):
        sums_ref[k] = sums[k * ny : (k + 1) * ny]


def blend(level_ref, sums_ref, k, store):
    ny, nz = level_ref.shape[1:]
    lane_group = iota((8, ny), 1) // 8
    eye = iota((8, ny), 1) % 8 == iota((8, ny), 0)
    totals = [jnp.zeros((8, ny), jnp.float32)] * 3
    for group in range(ny // 8):
        rows = pl.ds(8 * group, 8)
        level = level_ref[k, rows, :]
        passing = jnp.exp2(sums_ref[k, rows, pl.ds(0, nz)])
        first = (passing - jnp.exp2(sums_ref[k, rows, pl.ds(nz, nz)])) * level
        red = jnp.sum(first, axis=1, keepdims=True)
        square = jnp.sum(first * level, axis=1, keepdims=True)
        whole = sums_ref[k, rows, pl.ds(2 * nz, ny)]
        totals = [jnp.where(lane_group == group, part, total) for part, total in zip((red, square, whole), totals)]
    red, square, whole = [jnp.sum(jnp.where(eye, total, 0.0), axis=0, keepdims=True) for total in totals]
    through = jnp.exp2(whole)
    store(red, square, through)


def put(image_ref, x, slot=lambda view: view):
    per_view = image_ref.shape[2]
    view, row = (x // per_view, x % per_view) if isinstance(x, int) else (lax.div(x, per_view), lax.rem(x, per_view))

    def store(*channels):
        for k, values in enumerate(channels):
            image_ref[slot(view), k, pl.ds(row, 1), :] = values

    return store


def summing(sum_ref):
    nz = sum_ref.shape[0] // 2
    row = iota(sum_ref.shape, 0) % nz
    col = iota(sum_ref.shape, 1)
    sum_ref[...] = jnp.where((row < col) & (col < nz) | (row <= col - nz), -1.0, 0.0).astype(jnp.bfloat16)


def blend_kernel(
    density, raw_ref, pack_ref, scale_ref, zleft_ref, zright_ref,
    image_ref, fix_ref, first_ref, sum_ref, level0_ref, level1_ref, sums0_ref, sums1_ref,
):
    nx, ny, nz = raw_ref.shape
    summing(sum_ref)
    ghosts = sides_deep(nx, ny, nz, zleft_ref, zright_ref)
    first_ref[...] = ghosts[0]
    fix = ghosts[2] * (0.5 * ghosts[2] + pack_ref[2]) + ghosts[0] * pack_ref[0] + ghosts[1] * pack_ref[1]
    per_block = 4 * SUB
    lane_block = iota((ny, nz), 1) // per_block
    scale = scale_ref[0]
    for block in range(1, nx // SUB):
        scale = jnp.where(lane_block == block, scale_ref[block], scale)
    fix_ref[...] = fix * scale
    image_ref[...] = jnp.zeros(image_ref.shape, jnp.float32)
    batch = level0_ref.shape[0]

    def load(x, level_ref, sums_ref):
        raws = [raw_ref[x + k] + on_border(fix_ref[...], x + k) for k in range(batch)]
        gather(density, raws, level_ref, sums_ref, sum_ref)

    def mix(x, level_ref, sums_ref):
        for k in range(batch):
            blend(level_ref, sums_ref, k, put(image_ref, x + k))

    load(2, level0_ref, sums0_ref)

    def batches(i, carry):
        x = 2 * batch * i + 2
        load(x + batch, level1_ref, sums1_ref)
        mix(x, level0_ref, sums0_ref)
        load(x + 2 * batch, level0_ref, sums0_ref)
        mix(x + batch, level1_ref, sums1_ref)
        return carry

    count = (nx - 4) // batch
    lax.fori_loop(0, (count - 1) // 2, batches, 0)
    if count % 2 == 0:
        load(nx - 2 - batch, level1_ref, sums1_ref)
        mix(nx - 2 - 2 * batch, level0_ref, sums0_ref)
        mix(nx - 2 - batch, level1_ref, sums1_ref)
    else:
        mix(nx - 2 - batch, level0_ref, sums0_ref)


def row_tables(batch, ny, nz, buffers):
    return (
        [pltpu.VMEM((batch, ny, nz), jnp.float32)] * buffers
        + [pltpu.VMEM((batch, ny, 2 * nz + ny), jnp.float32)] * buffers
    )


def blended(density, views, raw, *rest):
    nx, ny, nz = raw.shape
    return pl.pallas_call(
        functools.partial(blend_kernel, density),
        out_shape=(
            jax.ShapeDtypeStruct((views, 3, nx // views, ny), jnp.float32),
            jax.ShapeDtypeStruct((ny, nz), jnp.float32),
            jax.ShapeDtypeStruct((ny, nz), jnp.float32),
            jax.ShapeDtypeStruct((2 * nz, 2 * nz + ny), jnp.bfloat16),
        ),
        in_specs=[VMEM] * 5,
        out_specs=(VMEM,) * 4,
        scratch_shapes=row_tables(4, ny, nz, 2),
        compiler_params=PARAMS,
        cost_estimate=COST,
    )(raw, *rest)


def two_rows(density, raws, level_ref, sums_ref, sum_ref, stores):
    ny, nz = raws[0].shape
    binary = density / math.log(2.0)
    parts = []
    for k, raw in enumerate(raws):
        level = jnp.clip(raw, 0.0, 1.0)
        level_ref[k] = level
        parts.append(jnp.concatenate(split(binary * level), axis=1))
    sums = jnp.dot(
        jnp.concatenate(parts, axis=0), sum_ref[:, pl.ds(nz, nz)], preferred_element_type=jnp.float32
    )
    lane_group = iota((8, ny), 1) // 8
    eye = iota((8, ny), 1) % 8 == iota((8, ny), 0)
    last = iota((8, nz), 1) == nz - 1
    for k, store in enumerate(stores):
        sums_ref[k] = sums[k * ny : (k + 1) * ny]
        totals = [jnp.zeros((8, ny), jnp.float32)] * 3
        for group in range(ny // 8):
            rows = pl.ds(8 * group, 8)
            level, behind = level_ref[k, rows, :], sums_ref[k, rows, :]
            left = jnp.exp2(behind)
            first = (jnp.exp2(behind + binary * level) - left) * level
            found = [jnp.sum(cells, axis=1, keepdims=True) for cells in (first, first * level, jnp.where(last, left, 0.0))]
            totals = [jnp.where(lane_group == group, part, total) for part, total in zip(found, totals)]
        store(*[jnp.sum(jnp.where(eye, total, 0.0), axis=0, keepdims=True) for total in totals])


def ghost_terms(ghost, kept, deep):
    return ghost[0] * (0.5 * ghost[0] + kept[0]) + ghost[1] * kept[1] + ghost[2] * deep


def slots(views):
    me = lax.axis_index("view")
    return lambda view: step_to(me, view, views)


def first_kernel(
    density, image_in_ref, raw_ref, kept_ref, scale_ref, fix_ref, first_ref, sum_ref, xleft_ref,
    image_ref, base_ref, deep_ref, level_ref, sums_ref,
):
    nx = raw_ref.shape[0]
    views = image_ref.shape[0]
    slot = slots(views)
    for view in range(views):
        image_ref[slot(view)] = image_in_ref[view]
    near = [xleft_ref[c, 1] for c in range(3)]
    far = [xleft_ref[c, 0] - 8.0 * cells for c, cells in enumerate(near)]

    def prepared(x, place):
        return raw_ref[x] + on_border(fix_ref[...], x), kept_ref[place, 2] + on_border(first_ref[...], x)

    raws = []
    for x, ghost in enumerate((far, near)):
        base, deep = prepared(x, x)
        raws.append(base + ghost_terms(ghost, kept_ref[x], deep) * scale_ref[0])
    two_rows(density, raws, level_ref, sums_ref, sum_ref, [put(image_ref, x, slot) for x in range(2)])
    for k in range(2):
        base_ref[k], deep_ref[k] = prepared(nx - 2 + k, 2 + k)


def last_kernel(
    density, image_in_ref, base_ref, deep_ref, kept_ref, scale_ref, sum_ref, xright_ref,
    image_ref, level_ref, sums_ref,
):
    views, _, per_view, _ = image_ref.shape
    nx = views * per_view
    slot = slots(views)
    image_ref[...] = image_in_ref[...]
    near = [-xright_ref[c, 0] for c in range(3)]
    far = [-8.0 * cells - xright_ref[c, 1] for c, cells in enumerate(near)]
    raws = [
        base_ref[k] + ghost_terms(ghost, kept_ref[2 + k], deep_ref[k]) * scale_ref[scale_ref.shape[0] - 1]
        for k, ghost in enumerate((near, far))
    ]
    two_rows(density, raws, level_ref, sums_ref, sum_ref, [put(image_ref, nx - 2 + k, slot) for k in range(2)])


def edged(kernel, density, out_shape, image, *rest):
    ny = image.shape[3]
    nz = out_shape[-1].shape[-1] if len(out_shape) > 1 else rest[0].shape[-1]
    return pl.pallas_call(
        functools.partial(kernel, density),
        out_shape=out_shape,
        in_specs=[VMEM] * (1 + len(rest)),
        out_specs=(VMEM,) * len(out_shape),
        scratch_shapes=[pltpu.VMEM((2, ny, nz), jnp.float32), pltpu.VMEM((2, ny, nz), jnp.float32)],
        compiler_params=PARAMS,
        cost_estimate=COST,
    )(image, *rest)


def turn(block, axis, by):
    count = lax.axis_size(axis)
    return lax.ppermute(block, axis, [(i, (i + by) % count) for i in range(count)])


def both_sides(block, axis):
    before = turn(block, axis, 1)
    return before, before if lax.axis_size(axis) == 2 else turn(block, axis, -1)


def exchange(count):
    if count == 4:
        return [(2, 3, 1, 0), (3, 2, 0, 1), (1, 0, 3, 2)]
    if count & (count - 1) == 0:
        return [tuple(i ^ step for i in range(count)) for step in range(count - 1, 0, -1)]
    return [tuple((i + step) % count for i in range(count)) for step in range(1, count)]


def looked_up(index, table):
    found = jnp.int32(table[0])
    for place, entry in enumerate(table[1:], 1):
        found = jnp.where(index == place, entry, found)
    return found


def step_to(me, other, count):
    steps = [(i,) + targets for i, targets in enumerate(zip(*exchange(count)))]
    return looked_up(me, [targets.index(other) for targets in steps])


def exchanged(blocks, axis):
    routes = exchange(lax.axis_size(axis))
    return [blocks[0]] + [lax.ppermute(blocks[k], axis, list(enumerate(route))) for k, route in enumerate(routes, 1)]


def composite_kernel(*refs):
    *image_refs, out_ref = refs
    count = len(image_refs)
    me = lax.axis_index("view")
    sources = [me] + [looked_up(me, [route.index(i) for i in range(count)]) for route in exchange(count)]
    red = square = 0.0
    through = 1.0
    for source, image_ref in zip(sources, image_refs):
        passing = 1.0
        for other, front_ref in zip(sources, image_refs):
            passing = passing * jnp.where(other < source, front_ref[2], 1.0)
        red = red + passing * image_ref[0]
        square = square + passing * image_ref[1]
        through = through * image_ref[2]
    for k, values in enumerate((red, 4.0 * (red - square), 1.0 - through - red, 1.0 - through)):
        out_ref[0, 0, k] = values


def composited(images):
    return pl.pallas_call(
        composite_kernel,
        out_shape=jax.ShapeDtypeStruct((1, 1, 4) + images[0].shape[1:], jnp.float32),
        in_specs=[VMEM] * len(images),
        out_specs=VMEM,
        compiler_params=PARAMS,
        cost_estimate=COST,
    )(*images)


def local(velocity, occupied, q_floor, q_span):
    comps, nx, ny, nz = velocity.shape
    views = lax.axis_size("view")
    density = 5.0 / (nz * views)
    xleft = turn(velocity[:, nx - 2 :], "gx", 1)
    xright = turn(velocity[:, :2], "gx", -1)
    u, parts, yface, ztail, zhead = faces(velocity)
    zleft = turn(ztail, "view", 1)
    zright = turn(zhead, "view", -1)
    yleft, yright = both_sides(yface, "gy")
    raw, pack, kept, scale = shaded(u, parts, yleft, yright, occupied[:, :, 0], q_floor, q_span)
    image, fix, first, summer = blended(density, views, raw, pack, scale, zleft, zright)
    drawn = jax.ShapeDtypeStruct(image.shape, jnp.float32)
    two = jax.ShapeDtypeStruct((2, ny, nz), jnp.float32)
    image, base, deep = edged(
        first_kernel, density, (drawn, two, two), image, raw, kept, scale, fix, first, summer, xleft
    )
    (blocks,) = edged(last_kernel, density, (drawn,), image, base, deep, kept, scale, summer, xright)
    return composited(exchanged(blocks, "view"))


def solution(mesh):
    placed = (P(None, "gx", "gy", "view"), P("gx", "gy", "view"), P(), P())
    return jax.shard_map(
        local,
        mesh=mesh,
        in_specs=placed,
        out_specs=P("gx", "gy", None, "view", None),
        check_vma=False,
    )
```

```python
import functools
import math

import jax
import jax.numpy as jnp
from jax import lax
from jax.experimental import pallas as pl
from jax.experimental.pallas import tpu as pltpu
from jax.sharding import PartitionSpec as P

SUB = 8
ROWS = 32
VMEM = pl.BlockSpec(memory_space=pltpu.VMEM)
HBM = pl.BlockSpec(memory_space=pltpu.HBM)
COST = pl.CostEstimate(flops=1 << 20, bytes_accessed=1 << 20, transcendentals=0)
PARAMS = pltpu.CompilerParams(vmem_limit_bytes=16 << 20)


def split(values):
    high = values.astype(jnp.bfloat16)
    low = (values - high.astype(jnp.float32)).astype(jnp.bfloat16)
    return high, low


def iota(shape, dim):
    return lax.broadcasted_iota(jnp.int32, shape, dim)


def faces_kernel(u_hbm, u_ref, parts_ref, xhead_ref, yface_ref, tail_ref, head_ref, packed_ref, sems):
    comps, nx, ny, nz = u_ref.shape
    quarters = sems.shape[1]
    rows = ny // quarters

    def fetch(c, k):
        span = pl.ds(k * rows if isinstance(k, int) else pl.multiple_of(k * rows, rows), rows)
        return pltpu.make_async_copy(u_hbm.at[c, :, span], u_ref.at[c, :, span], sems.at[c, k])

    for c in range(comps):
        for k in range(quarters):
            fetch(c, k).start()
    slot = iota((8, nz), 1) // 4
    for c in range(comps):

        def quarter(k, carry):
            fetch(c, k).wait()
            start = pl.multiple_of(k * rows, rows)
            packed = [jnp.zeros((8, nz), jnp.float32)] * (rows // 8)
            for x in range(nx):
                cells = u_ref[c, x, pl.ds(start, rows), :]
                high, low = split(cells)
                parts_ref[c, x, pl.ds(start, rows), pl.ds(0, nz)] = high
                parts_ref[c, x, pl.ds(start, rows), pl.ds(nz, nz)] = low
                mine = slot == x
                for n in range(rows // 8):
                    packed[n] = jnp.where(mine, pltpu.roll(cells[8 * n : 8 * n + 8], (4 * x + 2) % nz, 1), packed[n])
            for n in range(rows // 8):
                packed_ref[c, pl.ds(pl.multiple_of(start + 8 * n, 8), 8), :] = packed[n]
            return carry

        lax.fori_loop(0, quarters, quarter, 0)
    sub = iota((8, nz), 0)
    for c in range(comps):
        xhead_ref[c] = u_ref[c, pl.ds(0, 2)]
        for x in range(nx):
            lines = jnp.where(sub >= 6, u_ref[c, x, pl.ds(ny - 8, 8), :], u_ref[c, x, pl.ds(0, 8), :])
            yface_ref[c, x] = pltpu.roll(lines, 2, 0)[:4]
    tails, heads = fold([packed_ref[c] for c in range(comps)], ny, nz)
    tail_ref[...] = tails
    head_ref[...] = heads


def fold(packed, ny, nz):
    early = iota((ny, nz), 1) % 4 < 2
    early2 = early[: ny // 2]
    third, fourth = packed[2][: ny // 2], packed[2][ny // 2 :]
    tails = jnp.where(early, packed[0], pltpu.roll(packed[1], 2, 1))
    tails2 = jnp.where(early2, third, pltpu.roll(fourth, 2, 1))
    heads = jnp.where(early, pltpu.roll(packed[0], nz - 2, 1), packed[1])
    heads2 = jnp.where(early2, pltpu.roll(third, nz - 2, 1), fourth)
    return jnp.concatenate([tails, tails2], axis=0), jnp.concatenate([heads, heads2], axis=0)


def unfold(left, right, ny, nz):
    early = iota((ny, nz), 1) % 4 < 2
    early2 = early[: ny // 2]
    left2, right2 = left[ny:], right[ny:]
    left, right = left[:ny], right[:ny]
    first = jnp.where(early, left, pltpu.roll(right, 2, 1))
    second = jnp.where(early, pltpu.roll(left, nz - 2, 1), right)
    third = jnp.where(early2, left2, pltpu.roll(right2, 2, 1))
    fourth = jnp.where(early2, pltpu.roll(left2, nz - 2, 1), right2)
    return first, second, jnp.concatenate([third, fourth], axis=0)


def faces(u):
    comps, nx, ny, nz = u.shape
    message = jax.ShapeDtypeStruct((ny + ny // 2, nz), jnp.float32)
    return pl.pallas_call(
        faces_kernel,
        out_shape=(
            jax.ShapeDtypeStruct(u.shape, jnp.float32),
            jax.ShapeDtypeStruct((comps, nx, ny, 2 * nz), jnp.bfloat16),
            jax.ShapeDtypeStruct((comps, 2, ny, nz), jnp.float32),
            jax.ShapeDtypeStruct((comps, nx, 4, nz), jnp.float32),
            message,
            message,
        ),
        in_specs=[HBM],
        out_specs=(VMEM,) * 6,
        scratch_shapes=[pltpu.VMEM((comps, ny, nz), jnp.float32), pltpu.SemaphoreType.DMA((comps, 4))],
        compiler_params=pltpu.CompilerParams(vmem_limit_bytes=37 << 20),
        cost_estimate=COST,
    )(u)


def stencil(far):
    one = jnp.where(far == 1, 8.0, 0.0) - jnp.where(far == -1, 8.0, 0.0)
    return (one - jnp.where(far == 2, 1.0, 0.0) + jnp.where(far == -2, 1.0, 0.0)).astype(jnp.bfloat16)


def shading(occupied_ref, floor, span, scale_ref, offset_ref):
    blocks, ny, nz = scale_ref.shape
    groups = ny // SUB
    mine = iota((ny, groups), 0) // SUB == iota((ny, groups), 1)
    shrink = 1.0 / span
    for block in range(blocks):
        row = occupied_ref[block : block + 1, :].astype(jnp.float32)
        column = jnp.sum(jnp.where(mine, row, 0.0), axis=1, keepdims=True)
        scale_ref[block] = jnp.broadcast_to(column * (shrink * (-1.0 / 144.0)), (ny, nz))
        offset_ref[block] = jnp.broadcast_to(column * (shrink * -floor), (ny, nz))


def lane_shift(x, nz, back):
    if isinstance(x, int):
        return (4 * x + 2 if back else 2 * nz - 2 - 4 * x) % nz
    return lax.rem(4 * x + 2 if back else 2 * nz - 2 - 4 * x, nz)


def slopes(parts_ref, x, tables, slope_ref):
    yleft_ref, yright_ref, dz_ref, dy_ref = tables
    comps, ny, nz = slope_ref.shape[2:]
    sub = iota((8, nz), 0)

    def top(left):
        lines = jnp.concatenate([left, left], axis=0)
        return jnp.where(sub < 2, lines - jnp.where(sub == 0, 8.0 * pltpu.roll(lines, 7, 0), 0.0), 0.0)

    def low(right):
        lines = jnp.concatenate([right, right], axis=0)
        return jnp.where(sub >= 6, jnp.where(sub == 7, 8.0 * pltpu.roll(lines, 1, 0), 0.0) - lines, 0.0)

    parts = [[parts_ref[c, x + k] for k in range(2)] for c in range(comps)]
    depth = jnp.dot(
        jnp.concatenate([part for pair in parts for part in pair], axis=0),
        dz_ref[...],
        preferred_element_type=jnp.float32,
    )
    for c in range(comps):
        both = jnp.concatenate(
            [jnp.concatenate([part[:, half : half + nz] for part in parts[c]], axis=1) for half in (0, nz)], axis=0
        )
        down = jnp.dot(dy_ref[...], both, preferred_element_type=jnp.float32)
        for k in range(2):
            slope_ref[1, k, c] = depth[(2 * c + k) * ny : (2 * c + k + 1) * ny]
            mine = down[:, k * nz : (k + 1) * nz]
            slope_ref[0, k, c, pl.ds(0, 8), :] = mine[:8] + top(yleft_ref[c, x + k])
            slope_ref[0, k, c, pl.ds(8, ny - 16), :] = mine[8 : ny - 8]
            slope_ref[0, k, c, pl.ds(ny - 8, 8), :] = mine[ny - 8 :] + low(yright_ref[c, x + k])


def shade(u_ref, x, slope_ref, scale_ref, offset_ref, raw_ref, pack_ref, kept_ref=None, place=None):
    comps, nx, ny, nz = u_ref.shape
    block = x // SUB

    def difference(high, low):
        if high is None:
            return 0.0 if low is None else -low
        return high if low is None else high - low

    for y in range(0, ny, ROWS):
        rows = pl.ds(y, ROWS)
        slots = iota((ROWS, nz), 1) // 4
        across = []
        for c in range(comps):
            near = [
                u_ref[c, x + d, rows, :] if not isinstance(x, int) or 0 <= x + d < nx else None for d in range(-2, 4)
            ]
            across.append(
                [8.0 * difference(near[k + 3], near[k + 1]) - difference(near[k + 4], near[k]) for k in range(2)]
            )
        packs = [pack_ref[k, rows, :] for k in range(3)]
        for k in range(2):
            side = [across[c][k] for c in range(comps)]
            down = [slope_ref[0, k, c, rows, :] for c in range(comps)]
            depth = [slope_ref[1, k, c, rows, :] for c in range(comps)]
            total = 0.5 * (side[0] * side[0] + down[1] * down[1] + depth[2] * depth[2])
            total = total + side[1] * down[0] + side[2] * depth[0] + down[2] * depth[1]
            raw_ref[x + k, rows, :] = total * scale_ref[block, rows, :] + offset_ref[block, rows, :]
            back = lane_shift(x + k, nz, True)
            packs = [
                jnp.where(slots == x + k, pltpu.roll(values, back, 1), pack)
                for values, pack in zip((side[2], down[2], depth[2]), packs)
            ]
            if kept_ref is not None:
                for n, values in enumerate((side[0], down[0], depth[0])):
                    kept_ref[place + k, n, rows, :] = values
        for k in range(3):
            pack_ref[k, rows, :] = packs[k]


def shade_kernel(
    u_ref, parts_ref, yleft_ref, yright_ref, occupied_ref, floor_ref, span_ref,
    raw_ref, pack_ref, kept_ref, scale_ref, offset_ref, dz_ref, dy_ref, slope0_ref, slope1_ref,
):
    comps, nx, ny, nz = u_ref.shape
    dz_ref[...] = stencil(iota((2 * nz, nz), 0) % nz - iota((2 * nz, nz), 1))
    dy_ref[...] = stencil(iota((ny, 2 * ny), 1) % ny - iota((ny, 2 * ny), 0))
    shading(occupied_ref, floor_ref[...].reshape(1, 1), span_ref[...].reshape(1, 1), scale_ref, offset_ref)
    pack_ref[...] = jnp.zeros(pack_ref.shape, jnp.float32)
    tables = (yleft_ref, yright_ref, dz_ref, dy_ref)
    outs = (scale_ref, offset_ref, raw_ref, pack_ref)
    slopes(parts_ref, 0, tables, slope0_ref)
    slopes(parts_ref, 2, tables, slope1_ref)
    shade(u_ref, 0, slope0_ref, *outs, kept_ref, 0)

    def pairs(i, carry):
        x = 4 * i + 2
        slopes(parts_ref, x + 2, tables, slope0_ref)
        shade(u_ref, x, slope1_ref, *outs)
        slopes(parts_ref, x + 4, tables, slope1_ref)
        shade(u_ref, x + 2, slope0_ref, *outs)
        return carry

    lax.fori_loop(0, (nx - 4) // 4, pairs, 0)
    shade(u_ref, nx - 2, slope1_ref, *outs, kept_ref, 2)


def shaded(u, *rest):
    comps, nx, ny, nz = u.shape
    return pl.pallas_call(
        shade_kernel,
        out_shape=(
            jax.ShapeDtypeStruct((nx, ny, nz), jnp.float32),
            jax.ShapeDtypeStruct((comps, ny, nz), jnp.float32),
            jax.ShapeDtypeStruct((4, comps, ny, nz), jnp.float32),
            jax.ShapeDtypeStruct((nx // SUB, ny, nz), jnp.float32),
        ),
        in_specs=[VMEM] * 7,
        out_specs=(VMEM,) * 4,
        scratch_shapes=[
            pltpu.VMEM((nx // SUB, ny, nz), jnp.float32),
            pltpu.VMEM((2 * nz, nz), jnp.bfloat16),
            pltpu.VMEM((ny, 2 * ny), jnp.bfloat16),
            pltpu.VMEM((2, 2, comps, ny, nz), jnp.float32),
            pltpu.VMEM((2, 2, comps, ny, nz), jnp.float32),
        ],
        compiler_params=PARAMS,
        cost_estimate=COST,
    )(u, *rest)


def sides_deep(nx, ny, nz, zleft_ref, zright_ref):
    source, target = iota((2 * nz, nz), 0) % nz, iota((2 * nz, nz), 1)
    where = jnp.where(source // 4 == target // 4, source % 4 + 10 * (target % 4), -1)
    weights = jnp.zeros((2 * nz, nz), jnp.float32)
    for value, m, t in ((1.0, 0, 2), (-8.0, 1, 2), (1.0, 1, 3), (-1.0, 2, 0), (8.0, 2, 1), (-1.0, 3, 1)):
        weights = jnp.where(where == m + 10 * t, value, weights)
    weights = weights.astype(jnp.bfloat16)
    return [
        jnp.dot(jnp.concatenate(split(ghost), axis=1), weights, preferred_element_type=jnp.float32)
        for ghost in unfold(zleft_ref[...], zright_ref[...], ny, nz)
    ]


def on_border(packed, x, rows=None):
    ny, nz = packed.shape
    lane = iota((ny, nz), 1)
    return jnp.where((lane >= nz - 2) | (lane < 2), pltpu.roll(packed, lane_shift(x, nz, False), 1), 0.0)


def gather(density, raws, level_ref, sums_ref, sum_ref):
    parts = []
    for k, raw in enumerate(raws):
        level = jnp.clip(raw, 0.0, 1.0)
        level_ref[k] = level
        parts.append(jnp.concatenate(split((density / math.log(2.0)) * level), axis=1))
    ny, nz = level_ref.shape[1:]
    sums = jnp.dot(jnp.concatenate(parts, axis=0), sum_ref[...], preferred_element_type=jnp.float32)
    for k in range(len(raws)):
        sums_ref[k] = sums[k * ny : (k + 1) * ny]


def blend(level_ref, sums_ref, k, store):
    ny, nz = level_ref.shape[1:]
    lane_group = iota((8, ny), 1) // 8
    eye = iota((8, ny), 1) % 8 == iota((8, ny), 0)
    totals = [jnp.zeros((8, ny), jnp.float32)] * 3
    for group in range(ny // 8):
        rows = pl.ds(8 * group, 8)
        level = level_ref[k, rows, :]
        passing = jnp.exp2(sums_ref[k, rows, pl.ds(0, nz)])
        first = (passing - jnp.exp2(sums_ref[k, rows, pl.ds(nz, nz)])) * level
        red = jnp.sum(first, axis=1, keepdims=True)
        square = jnp.sum(first * level, axis=1, keepdims=True)
        whole = sums_ref[k, rows, pl.ds(2 * nz, ny)]
        totals = [jnp.where(lane_group == group, part, total) for part, total in zip((red, square, whole), totals)]
    red, square, whole = [jnp.sum(jnp.where(eye, total, 0.0), axis=0, keepdims=True) for total in totals]
    through = jnp.exp2(whole)
    store(red, square, through)


def put(image_ref, x, slot=lambda view: view):
    per_view = image_ref.shape[2]
    view, row = (x // per_view, x % per_view) if isinstance(x, int) else (lax.div(x, per_view), lax.rem(x, per_view))

    def store(*channels):
        for k, values in enumerate(channels):
            image_ref[slot(view), k, pl.ds(row, 1), :] = values

    return store


def summing(sum_ref):
    nz = sum_ref.shape[0] // 2
    row = iota(sum_ref.shape, 0) % nz
    col = iota(sum_ref.shape, 1)
    sum_ref[...] = jnp.where((row < col) & (col < nz) | (row <= col - nz), -1.0, 0.0).astype(jnp.bfloat16)


def blend_kernel(
    density, raw_ref, pack_ref, scale_ref, zleft_ref, zright_ref,
    image_ref, fix_ref, first_ref, sum_ref, level0_ref, level1_ref, sums0_ref, sums1_ref,
):
    nx, ny, nz = raw_ref.shape
    summing(sum_ref)
    ghosts = sides_deep(nx, ny, nz, zleft_ref, zright_ref)
    first_ref[...] = ghosts[0]
    fix = ghosts[2] * (0.5 * ghosts[2] + pack_ref[2]) + ghosts[0] * pack_ref[0] + ghosts[1] * pack_ref[1]
    per_block = 4 * SUB
    lane_block = iota((ny, nz), 1) // per_block
    scale = scale_ref[0]
    for block in range(1, nx // SUB):
        scale = jnp.where(lane_block == block, scale_ref[block], scale)
    fix_ref[...] = fix * scale
    image_ref[...] = jnp.zeros(image_ref.shape, jnp.float32)
    batch = level0_ref.shape[0]

    def load(x, level_ref, sums_ref):
        raws = [raw_ref[x + k] + on_border(fix_ref[...], x + k) for k in range(batch)]
        gather(density, raws, level_ref, sums_ref, sum_ref)

    def mix(x, level_ref, sums_ref):
        for k in range(batch):
            blend(level_ref, sums_ref, k, put(image_ref, x + k))

    load(2, level0_ref, sums0_ref)

    def batches(i, carry):
        x = 2 * batch * i + 2
        load(x + batch, level1_ref, sums1_ref)
        mix(x, level0_ref, sums0_ref)
        load(x + 2 * batch, level0_ref, sums0_ref)
        mix(x + batch, level1_ref, sums1_ref)
        return carry

    count = (nx - 4) // batch
    lax.fori_loop(0, (count - 1) // 2, batches, 0)
    if count % 2 == 0:
        load(nx - 2 - batch, level1_ref, sums1_ref)
        mix(nx - 2 - 2 * batch, level0_ref, sums0_ref)
        mix(nx - 2 - batch, level1_ref, sums1_ref)
    else:
        mix(nx - 2 - batch, level0_ref, sums0_ref)


def row_tables(batch, ny, nz, buffers):
    return (
        [pltpu.VMEM((batch, ny, nz), jnp.float32)] * buffers
        + [pltpu.VMEM((batch, ny, 2 * nz + ny), jnp.float32)] * buffers
    )


def blended(density, views, raw, *rest):
    nx, ny, nz = raw.shape
    return pl.pallas_call(
        functools.partial(blend_kernel, density),
        out_shape=(
            jax.ShapeDtypeStruct((views, 3, nx // views, ny), jnp.float32),
            jax.ShapeDtypeStruct((ny, nz), jnp.float32),
            jax.ShapeDtypeStruct((ny, nz), jnp.float32),
            jax.ShapeDtypeStruct((2 * nz, 2 * nz + ny), jnp.bfloat16),
        ),
        in_specs=[VMEM] * 5,
        out_specs=(VMEM,) * 4,
        scratch_shapes=row_tables(4, ny, nz, 2),
        compiler_params=PARAMS,
        cost_estimate=COST,
    )(raw, *rest)


def two_rows(density, raws, level_ref, sums_ref, sum_ref, stores):
    ny, nz = raws[0].shape
    binary = density / math.log(2.0)
    parts = []
    for k, raw in enumerate(raws):
        level = jnp.clip(raw, 0.0, 1.0)
        level_ref[k] = level
        parts.append(jnp.concatenate(split(binary * level), axis=1))
    sums = jnp.dot(
        jnp.concatenate(parts, axis=0), sum_ref[:, pl.ds(nz, nz)], preferred_element_type=jnp.float32
    )
    lane_group = iota((8, ny), 1) // 8
    eye = iota((8, ny), 1) % 8 == iota((8, ny), 0)
    last = iota((8, nz), 1) == nz - 1
    for k, store in enumerate(stores):
        sums_ref[k] = sums[k * ny : (k + 1) * ny]
        totals = [jnp.zeros((8, ny), jnp.float32)] * 3
        for group in range(ny // 8):
            rows = pl.ds(8 * group, 8)
            level, behind = level_ref[k, rows, :], sums_ref[k, rows, :]
            left = jnp.exp2(behind)
            first = (jnp.exp2(behind + binary * level) - left) * level
            found = [jnp.sum(cells, axis=1, keepdims=True) for cells in (first, first * level, jnp.where(last, left, 0.0))]
            totals = [jnp.where(lane_group == group, part, total) for part, total in zip(found, totals)]
        store(*[jnp.sum(jnp.where(eye, total, 0.0), axis=0, keepdims=True) for total in totals])


def ghost_terms(ghost, kept, deep):
    return ghost[0] * (0.5 * ghost[0] + kept[0]) + ghost[1] * kept[1] + ghost[2] * deep


def slots(views):
    me = lax.axis_index("view")
    return lambda view: step_to(me, view, views)


def first_kernel(
    density, image_in_ref, raw_ref, kept_ref, scale_ref, fix_ref, first_ref, sum_ref, xleft_ref,
    image_ref, base_ref, deep_ref, level_ref, sums_ref,
):
    nx = raw_ref.shape[0]
    views = image_ref.shape[0]
    slot = slots(views)
    for view in range(views):
        image_ref[slot(view)] = image_in_ref[view]
    near = [xleft_ref[c, 1] for c in range(3)]
    far = [xleft_ref[c, 0] - 8.0 * cells for c, cells in enumerate(near)]

    def prepared(x, place):
        return raw_ref[x] + on_border(fix_ref[...], x), kept_ref[place, 2] + on_border(first_ref[...], x)

    raws = []
    for x, ghost in enumerate((far, near)):
        base, deep = prepared(x, x)
        raws.append(base + ghost_terms(ghost, kept_ref[x], deep) * scale_ref[0])
    two_rows(density, raws, level_ref, sums_ref, sum_ref, [put(image_ref, x, slot) for x in range(2)])
    for k in range(2):
        base_ref[k], deep_ref[k] = prepared(nx - 2 + k, 2 + k)


def last_kernel(
    density, image_in_ref, base_ref, deep_ref, kept_ref, scale_ref, sum_ref, xright_ref,
    image_ref, level_ref, sums_ref,
):
    views, _, per_view, _ = image_ref.shape
    nx = views * per_view
    slot = slots(views)
    image_ref[...] = image_in_ref[...]
    near = [-xright_ref[c, 0] for c in range(3)]
    far = [-8.0 * cells - xright_ref[c, 1] for c, cells in enumerate(near)]
    raws = [
        base_ref[k] + ghost_terms(ghost, kept_ref[2 + k], deep_ref[k]) * scale_ref[scale_ref.shape[0] - 1]
        for k, ghost in enumerate((near, far))
    ]
    two_rows(density, raws, level_ref, sums_ref, sum_ref, [put(image_ref, nx - 2 + k, slot) for k in range(2)])


def edged(kernel, density, out_shape, image, *rest):
    ny = image.shape[3]
    nz = out_shape[-1].shape[-1] if len(out_shape) > 1 else rest[0].shape[-1]
    return pl.pallas_call(
        functools.partial(kernel, density),
        out_shape=out_shape,
        in_specs=[VMEM] * (1 + len(rest)),
        out_specs=(VMEM,) * len(out_shape),
        scratch_shapes=[pltpu.VMEM((2, ny, nz), jnp.float32), pltpu.VMEM((2, ny, nz), jnp.float32)],
        compiler_params=PARAMS,
        cost_estimate=COST,
    )(image, *rest)


def turn(block, axis, by):
    count = lax.axis_size(axis)
    return lax.ppermute(block, axis, [(i, (i + by) % count) for i in range(count)])


def both_sides(block, axis):
    before = turn(block, axis, 1)
    return before, before if lax.axis_size(axis) == 2 else turn(block, axis, -1)


def exchange(count):
    if count == 4:
        return [(2, 3, 1, 0), (3, 2, 0, 1), (1, 0, 3, 2)]
    if count & (count - 1) == 0:
        return [tuple(i ^ step for i in range(count)) for step in range(count - 1, 0, -1)]
    return [tuple((i + step) % count for i in range(count)) for step in range(1, count)]


def looked_up(index, table):
    found = jnp.int32(table[0])
    for place, entry in enumerate(table[1:], 1):
        found = jnp.where(index == place, entry, found)
    return found


def step_to(me, other, count):
    steps = [(i,) + targets for i, targets in enumerate(zip(*exchange(count)))]
    return looked_up(me, [targets.index(other) for targets in steps])


def exchanged(blocks, axis):
    routes = exchange(lax.axis_size(axis))
    return [blocks[0]] + [lax.ppermute(blocks[k], axis, list(enumerate(route))) for k, route in enumerate(routes, 1)]


def composite_kernel(*refs):
    *image_refs, out_ref = refs
    count = len(image_refs)
    me = lax.axis_index("view")
    sources = [me] + [looked_up(me, [route.index(i) for i in range(count)]) for route in exchange(count)]
    red = square = 0.0
    through = 1.0
    for source, image_ref in zip(sources, image_refs):
        passing = 1.0
        for other, front_ref in zip(sources, image_refs):
            passing = passing * jnp.where(other < source, front_ref[2], 1.0)
        red = red + passing * image_ref[0]
        square = square + passing * image_ref[1]
        through = through * image_ref[2]
    for k, values in enumerate((red, 4.0 * (red - square), 1.0 - through - red, 1.0 - through)):
        out_ref[0, 0, k] = values


def composited(images):
    return pl.pallas_call(
        composite_kernel,
        out_shape=jax.ShapeDtypeStruct((1, 1, 4) + images[0].shape[1:], jnp.float32),
        in_specs=[VMEM] * len(images),
        out_specs=VMEM,
        compiler_params=PARAMS,
        cost_estimate=COST,
    )(*images)


def local(velocity, occupied, q_floor, q_span):
    comps, nx, ny, nz = velocity.shape
    views = lax.axis_size("view")
    density = 5.0 / (nz * views)
    xleft = turn(velocity[:, nx - 2 :], "gx", 1)
    u, parts, xhead, yface, ztail, zhead = faces(velocity)
    xright = turn(xhead, "gx", -1)
    zleft = turn(ztail, "view", 1)
    zright = turn(zhead, "view", -1)
    yleft, yright = both_sides(yface, "gy")
    raw, pack, kept, scale = shaded(u, parts, yleft, yright, occupied[:, :, 0], q_floor, q_span)
    image, fix, first, summer = blended(density, views, raw, pack, scale, zleft, zright)
    drawn = jax.ShapeDtypeStruct(image.shape, jnp.float32)
    two = jax.ShapeDtypeStruct((2, ny, nz), jnp.float32)
    image, base, deep = edged(
        first_kernel, density, (drawn, two, two), image, raw, kept, scale, fix, first, summer, xleft
    )
    (blocks,) = edged(last_kernel, density, (drawn,), image, base, deep, kept, scale, summer, xright)
    return composited(exchanged(blocks, "view"))


def solution(mesh):
    placed = (P(None, "gx", "gy", "view"), P("gx", "gy", "view"), P(), P())
    return jax.shard_map(
        local,
        mesh=mesh,
        in_specs=placed,
        out_specs=P("gx", "gy", None, "view", None),
        check_vma=False,
    )
```

```python
import functools
import math

import jax
import jax.numpy as jnp
from jax import lax
from jax.experimental import pallas as pl
from jax.experimental.pallas import tpu as pltpu
from jax.sharding import PartitionSpec as P

SUB = 8
ROWS = 32
VMEM = pl.BlockSpec(memory_space=pltpu.VMEM)
HBM = pl.BlockSpec(memory_space=pltpu.HBM)
COST = pl.CostEstimate(flops=1 << 20, bytes_accessed=1 << 20, transcendentals=0)
PARAMS = pltpu.CompilerParams(vmem_limit_bytes=16 << 20)


def split(values):
    high = values.astype(jnp.bfloat16)
    low = (values - high.astype(jnp.float32)).astype(jnp.bfloat16)
    return high, low


def iota(shape, dim):
    return lax.broadcasted_iota(jnp.int32, shape, dim)


def faces_kernel(u_hbm, u_ref, parts_ref, xhead_ref, yface_ref, tail_ref, head_ref, packed_ref, sems):
    comps, nx, ny, nz = u_ref.shape
    quarters = sems.shape[1]
    rows = ny // quarters

    def fetch(c, k):
        span = pl.ds(k * rows if isinstance(k, int) else pl.multiple_of(k * rows, rows), rows)
        return pltpu.make_async_copy(u_hbm.at[c, :, span], u_ref.at[c, :, span], sems.at[c, k])

    for c in range(comps):
        for k in range(quarters):
            fetch(c, k).start()
    slot = iota((8, nz), 1) // 4
    for c in range(comps):

        def quarter(k, carry):
            fetch(c, k).wait()
            start = pl.multiple_of(k * rows, rows)
            packed = [jnp.zeros((8, nz), jnp.float32)] * (rows // 8)
            for x in range(nx):
                cells = u_ref[c, x, pl.ds(start, rows), :]
                high, low = split(cells)
                parts_ref[c, x, pl.ds(start, rows), pl.ds(0, nz)] = high
                parts_ref[c, x, pl.ds(start, rows), pl.ds(nz, nz)] = low
                mine = slot == x
                for n in range(rows // 8):
                    packed[n] = jnp.where(mine, pltpu.roll(cells[8 * n : 8 * n + 8], (4 * x + 2) % nz, 1), packed[n])
            for n in range(rows // 8):
                packed_ref[c, pl.ds(pl.multiple_of(start + 8 * n, 8), 8), :] = packed[n]
            return carry

        lax.fori_loop(0, quarters, quarter, 0)
    sub = iota((8, nz), 0)
    for c in range(comps):
        xhead_ref[c] = u_ref[c, pl.ds(0, 2)]
        for x in range(nx):
            lines = jnp.where(sub >= 6, u_ref[c, x, pl.ds(ny - 8, 8), :], u_ref[c, x, pl.ds(0, 8), :])
            yface_ref[c, x] = pltpu.roll(lines, 2, 0)[:4]
    tails, heads = fold([packed_ref[c] for c in range(comps)], ny, nz)
    tail_ref[...] = tails
    head_ref[...] = heads


def fold(packed, ny, nz):
    early = iota((ny, nz), 1) % 4 < 2
    early2 = early[: ny // 2]
    third, fourth = packed[2][: ny // 2], packed[2][ny // 2 :]
    tails = jnp.where(early, packed[0], pltpu.roll(packed[1], 2, 1))
    tails2 = jnp.where(early2, third, pltpu.roll(fourth, 2, 1))
    heads = jnp.where(early, pltpu.roll(packed[0], nz - 2, 1), packed[1])
    heads2 = jnp.where(early2, pltpu.roll(third, nz - 2, 1), fourth)
    return jnp.concatenate([tails, tails2], axis=0), jnp.concatenate([heads, heads2], axis=0)


def unfold(left, right, ny, nz):
    early = iota((ny, nz), 1) % 4 < 2
    early2 = early[: ny // 2]
    left2, right2 = left[ny:], right[ny:]
    left, right = left[:ny], right[:ny]
    first = jnp.where(early, left, pltpu.roll(right, 2, 1))
    second = jnp.where(early, pltpu.roll(left, nz - 2, 1), right)
    third = jnp.where(early2, left2, pltpu.roll(right2, 2, 1))
    fourth = jnp.where(early2, pltpu.roll(left2, nz - 2, 1), right2)
    return first, second, jnp.concatenate([third, fourth], axis=0)


def faces(u):
    comps, nx, ny, nz = u.shape
    message = jax.ShapeDtypeStruct((ny + ny // 2, nz), jnp.float32)
    return pl.pallas_call(
        faces_kernel,
        out_shape=(
            jax.ShapeDtypeStruct(u.shape, jnp.float32),
            jax.ShapeDtypeStruct((comps, nx, ny, 2 * nz), jnp.bfloat16),
            jax.ShapeDtypeStruct((comps, 2, ny, nz), jnp.float32),
            jax.ShapeDtypeStruct((comps, nx, 4, nz), jnp.float32),
            message,
            message,
        ),
        in_specs=[HBM],
        out_specs=(VMEM,) * 6,
        scratch_shapes=[pltpu.VMEM((comps, ny, nz), jnp.float32), pltpu.SemaphoreType.DMA((comps, 4))],
        compiler_params=pltpu.CompilerParams(vmem_limit_bytes=37 << 20),
        cost_estimate=COST,
    )(u)


def stencil(far):
    one = jnp.where(far == 1, 8.0, 0.0) - jnp.where(far == -1, 8.0, 0.0)
    return (one - jnp.where(far == 2, 1.0, 0.0) + jnp.where(far == -2, 1.0, 0.0)).astype(jnp.bfloat16)


def shading(occupied_ref, floor, span, scale_ref, offset_ref):
    blocks, ny, nz = scale_ref.shape
    groups = ny // SUB
    mine = iota((ny, groups), 0) // SUB == iota((ny, groups), 1)
    shrink = 1.0 / span
    for block in range(blocks):
        row = occupied_ref[block : block + 1, :].astype(jnp.float32)
        column = jnp.sum(jnp.where(mine, row, 0.0), axis=1, keepdims=True)
        scale_ref[block] = jnp.broadcast_to(column * (shrink * (-1.0 / 144.0)), (ny, nz))
        offset_ref[block] = jnp.broadcast_to(column * (shrink * -floor), (ny, nz))


def lane_shift(x, nz, back):
    if isinstance(x, int):
        return (4 * x + 2 if back else 2 * nz - 2 - 4 * x) % nz
    return lax.rem(4 * x + 2 if back else 2 * nz - 2 - 4 * x, nz)


def slopes(parts_ref, x, tables, slope_ref):
    yleft_ref, yright_ref, dz_ref, dy_ref = tables
    comps, ny, nz = slope_ref.shape[2:]
    sub = iota((8, nz), 0)

    def top(left):
        lines = jnp.concatenate([left, left], axis=0)
        return jnp.where(sub < 2, lines - jnp.where(sub == 0, 8.0 * pltpu.roll(lines, 7, 0), 0.0), 0.0)

    def low(right):
        lines = jnp.concatenate([right, right], axis=0)
        return jnp.where(sub >= 6, jnp.where(sub == 7, 8.0 * pltpu.roll(lines, 1, 0), 0.0) - lines, 0.0)

    parts = [[parts_ref[c, x + k] for k in range(2)] for c in range(comps)]
    depth = jnp.dot(
        jnp.concatenate([part for pair in parts for part in pair], axis=0),
        dz_ref[...],
        preferred_element_type=jnp.float32,
    )
    for c in range(comps):
        both = jnp.concatenate(
            [jnp.concatenate([part[:, half : half + nz] for part in parts[c]], axis=1) for half in (0, nz)], axis=0
        )
        down = jnp.dot(dy_ref[...], both, preferred_element_type=jnp.float32)
        for k in range(2):
            slope_ref[1, k, c] = depth[(2 * c + k) * ny : (2 * c + k + 1) * ny]
            mine = down[:, k * nz : (k + 1) * nz]
            slope_ref[0, k, c, pl.ds(0, 8), :] = mine[:8] + top(yleft_ref[c, x + k])
            slope_ref[0, k, c, pl.ds(8, ny - 16), :] = mine[8 : ny - 8]
            slope_ref[0, k, c, pl.ds(ny - 8, 8), :] = mine[ny - 8 :] + low(yright_ref[c, x + k])


def shade(u_ref, x, slope_ref, scale_ref, offset_ref, raw_ref, pack_ref, kept_ref=None, place=None):
    comps, nx, ny, nz = u_ref.shape
    block = x // SUB

    def difference(high, low):
        if high is None:
            return 0.0 if low is None else -low
        return high if low is None else high - low

    for y in range(0, ny, ROWS):
        rows = pl.ds(y, ROWS)
        slots = iota((ROWS, nz), 1) // 4
        across = []
        for c in range(comps):
            near = [
                u_ref[c, x + d, rows, :] if not isinstance(x, int) or 0 <= x + d < nx else None for d in range(-2, 4)
            ]
            across.append(
                [8.0 * difference(near[k + 3], near[k + 1]) - difference(near[k + 4], near[k]) for k in range(2)]
            )
        packs = [pack_ref[k, rows, :] for k in range(3)]
        for k in range(2):
            side = [across[c][k] for c in range(comps)]
            down = [slope_ref[0, k, c, rows, :] for c in range(comps)]
            depth = [slope_ref[1, k, c, rows, :] for c in range(comps)]
            total = 0.5 * (side[0] * side[0] + down[1] * down[1] + depth[2] * depth[2])
            total = total + side[1] * down[0] + side[2] * depth[0] + down[2] * depth[1]
            raw_ref[x + k, rows, :] = total * scale_ref[block, rows, :] + offset_ref[block, rows, :]
            back = lane_shift(x + k, nz, True)
            packs = [
                jnp.where(slots == x + k, pltpu.roll(values, back, 1), pack)
                for values, pack in zip((side[2], down[2], depth[2]), packs)
            ]
            if kept_ref is not None:
                for n, values in enumerate((side[0], down[0], depth[0])):
                    kept_ref[place + k, n, rows, :] = values
        for k in range(3):
            pack_ref[k, rows, :] = packs[k]


def shade_kernel(
    u_ref, parts_ref, yleft_ref, yright_ref, occupied_ref, floor_ref, span_ref,
    raw_ref, pack_ref, kept_ref, scale_ref, offset_ref, dz_ref, dy_ref, slope0_ref, slope1_ref,
):
    comps, nx, ny, nz = u_ref.shape
    dz_ref[...] = stencil(iota((2 * nz, nz), 0) % nz - iota((2 * nz, nz), 1))
    dy_ref[...] = stencil(iota((ny, 2 * ny), 1) % ny - iota((ny, 2 * ny), 0))
    shading(occupied_ref, floor_ref[...].reshape(1, 1), span_ref[...].reshape(1, 1), scale_ref, offset_ref)
    pack_ref[...] = jnp.zeros(pack_ref.shape, jnp.float32)
    tables = (yleft_ref, yright_ref, dz_ref, dy_ref)
    outs = (scale_ref, offset_ref, raw_ref, pack_ref)
    slopes(parts_ref, 0, tables, slope0_ref)
    slopes(parts_ref, 2, tables, slope1_ref)
    shade(u_ref, 0, slope0_ref, *outs, kept_ref, 0)

    def pairs(i, carry):
        x = 4 * i + 2
        slopes(parts_ref, x + 2, tables, slope0_ref)
        shade(u_ref, x, slope1_ref, *outs)
        slopes(parts_ref, x + 4, tables, slope1_ref)
        shade(u_ref, x + 2, slope0_ref, *outs)
        return carry

    lax.fori_loop(0, (nx - 4) // 4, pairs, 0)
    shade(u_ref, nx - 2, slope1_ref, *outs, kept_ref, 2)


def shaded(u, *rest):
    comps, nx, ny, nz = u.shape
    return pl.pallas_call(
        shade_kernel,
        out_shape=(
            jax.ShapeDtypeStruct((nx, ny, nz), jnp.float32),
            jax.ShapeDtypeStruct((comps, ny, nz), jnp.float32),
            jax.ShapeDtypeStruct((4, comps, ny, nz), jnp.float32),
            jax.ShapeDtypeStruct((nx // SUB, ny, nz), jnp.float32),
        ),
        in_specs=[VMEM] * 7,
        out_specs=(VMEM,) * 4,
        scratch_shapes=[
            pltpu.VMEM((nx // SUB, ny, nz), jnp.float32),
            pltpu.VMEM((2 * nz, nz), jnp.bfloat16),
            pltpu.VMEM((ny, 2 * ny), jnp.bfloat16),
            pltpu.VMEM((2, 2, comps, ny, nz), jnp.float32),
            pltpu.VMEM((2, 2, comps, ny, nz), jnp.float32),
        ],
        compiler_params=PARAMS,
        cost_estimate=COST,
    )(u, *rest)


def sides_deep(nx, ny, nz, zleft_ref, zright_ref):
    source, target = iota((2 * nz, nz), 0) % nz, iota((2 * nz, nz), 1)
    where = jnp.where(source // 4 == target // 4, source % 4 + 10 * (target % 4), -1)
    weights = jnp.zeros((2 * nz, nz), jnp.float32)
    for value, m, t in ((1.0, 0, 2), (-8.0, 1, 2), (1.0, 1, 3), (-1.0, 2, 0), (8.0, 2, 1), (-1.0, 3, 1)):
        weights = jnp.where(where == m + 10 * t, value, weights)
    weights = weights.astype(jnp.bfloat16)
    return [
        jnp.dot(jnp.concatenate(split(ghost), axis=1), weights, preferred_element_type=jnp.float32)
        for ghost in unfold(zleft_ref[...], zright_ref[...], ny, nz)
    ]


def on_border(packed, x, rows=None):
    ny, nz = packed.shape
    lane = iota((ny, nz), 1)
    return jnp.where((lane >= nz - 2) | (lane < 2), pltpu.roll(packed, lane_shift(x, nz, False), 1), 0.0)


def gather(density, raws, level_ref, sums_ref, sum_ref):
    parts = []
    for k, raw in enumerate(raws):
        level = jnp.clip(raw, 0.0, 1.0)
        level_ref[k] = level
        parts.append(jnp.concatenate(split((density / math.log(2.0)) * level), axis=1))
    ny, nz = level_ref.shape[1:]
    sums = jnp.dot(jnp.concatenate(parts, axis=0), sum_ref[...], preferred_element_type=jnp.float32)
    for k in range(len(raws)):
        sums_ref[k] = sums[k * ny : (k + 1) * ny]


def blend(level_ref, sums_ref, k, store):
    ny, nz = level_ref.shape[1:]
    lane_group = iota((8, ny), 1) // 8
    eye = iota((8, ny), 1) % 8 == iota((8, ny), 0)
    totals = [jnp.zeros((8, ny), jnp.float32)] * 3
    for group in range(ny // 8):
        rows = pl.ds(8 * group, 8)
        level = level_ref[k, rows, :]
        passing = jnp.exp2(sums_ref[k, rows, pl.ds(0, nz)])
        first = (passing - jnp.exp2(sums_ref[k, rows, pl.ds(nz, nz)])) * level
        red = jnp.sum(first, axis=1, keepdims=True)
        square = jnp.sum(first * level, axis=1, keepdims=True)
        whole = sums_ref[k, rows, pl.ds(2 * nz, ny)]
        totals = [jnp.where(lane_group == group, part, total) for part, total in zip((red, square, whole), totals)]
    red, square, whole = [jnp.sum(jnp.where(eye, total, 0.0), axis=0, keepdims=True) for total in totals]
    through = jnp.exp2(whole)
    store(red, square, through)


def put(image_ref, x, slot=lambda view: view):
    per_view = image_ref.shape[2]
    view, row = (x // per_view, x % per_view) if isinstance(x, int) else (lax.div(x, per_view), lax.rem(x, per_view))

    def store(*channels):
        for k, values in enumerate(channels):
            image_ref[slot(view), k, pl.ds(row, 1), :] = values

    return store


def summing(sum_ref):
    nz = sum_ref.shape[0] // 2
    row = iota(sum_ref.shape, 0) % nz
    col = iota(sum_ref.shape, 1)
    sum_ref[...] = jnp.where((row < col) & (col < nz) | (row <= col - nz), -1.0, 0.0).astype(jnp.bfloat16)


def blend_kernel(
    density, raw_ref, pack_ref, scale_ref, zleft_ref, zright_ref,
    image_ref, fix_ref, first_ref, sum_ref, level0_ref, level1_ref, sums0_ref, sums1_ref,
):
    nx, ny, nz = raw_ref.shape
    summing(sum_ref)
    ghosts = sides_deep(nx, ny, nz, zleft_ref, zright_ref)
    first_ref[...] = ghosts[0]
    fix = ghosts[2] * (0.5 * ghosts[2] + pack_ref[2]) + ghosts[0] * pack_ref[0] + ghosts[1] * pack_ref[1]
    per_block = 4 * SUB
    lane_block = iota((ny, nz), 1) // per_block
    scale = scale_ref[0]
    for block in range(1, nx // SUB):
        scale = jnp.where(lane_block == block, scale_ref[block], scale)
    fix_ref[...] = fix * scale
    image_ref[...] = jnp.zeros(image_ref.shape, jnp.float32)
    batch = level0_ref.shape[0]

    def load(x, level_ref, sums_ref):
        raws = [raw_ref[x + k] + on_border(fix_ref[...], x + k) for k in range(batch)]
        gather(density, raws, level_ref, sums_ref, sum_ref)

    def mix(x, level_ref, sums_ref):
        for k in range(batch):
            blend(level_ref, sums_ref, k, put(image_ref, x + k))

    load(2, level0_ref, sums0_ref)

    def batches(i, carry):
        x = 2 * batch * i + 2
        load(x + batch, level1_ref, sums1_ref)
        mix(x, level0_ref, sums0_ref)
        load(x + 2 * batch, level0_ref, sums0_ref)
        mix(x + batch, level1_ref, sums1_ref)
        return carry

    count = (nx - 4) // batch
    lax.fori_loop(0, (count - 1) // 2, batches, 0)
    if count % 2 == 0:
        load(nx - 2 - batch, level1_ref, sums1_ref)
        mix(nx - 2 - 2 * batch, level0_ref, sums0_ref)
        mix(nx - 2 - batch, level1_ref, sums1_ref)
    else:
        mix(nx - 2 - batch, level0_ref, sums0_ref)


def row_tables(batch, ny, nz, buffers):
    return (
        [pltpu.VMEM((batch, ny, nz), jnp.float32)] * buffers
        + [pltpu.VMEM((batch, ny, 2 * nz + ny), jnp.float32)] * buffers
    )


def blended(density, views, raw, *rest):
    nx, ny, nz = raw.shape
    return pl.pallas_call(
        functools.partial(blend_kernel, density),
        out_shape=(
            jax.ShapeDtypeStruct((views, 3, nx // views, ny), jnp.float32),
            jax.ShapeDtypeStruct((ny, nz), jnp.float32),
            jax.ShapeDtypeStruct((ny, nz), jnp.float32),
            jax.ShapeDtypeStruct((2 * nz, 2 * nz + ny), jnp.bfloat16),
        ),
        in_specs=[VMEM] * 5,
        out_specs=(VMEM,) * 4,
        scratch_shapes=row_tables(4, ny, nz, 2),
        compiler_params=PARAMS,
        cost_estimate=COST,
    )(raw, *rest)


def two_rows(density, raws, level_ref, sums_ref, sum_ref, stores):
    ny, nz = raws[0].shape
    binary = density / math.log(2.0)
    parts = []
    for k, raw in enumerate(raws):
        level = jnp.clip(raw, 0.0, 1.0)
        level_ref[k] = level
        parts.append(jnp.concatenate(split(binary * level), axis=1))
    sums = jnp.dot(
        jnp.concatenate(parts, axis=0), sum_ref[:, pl.ds(nz, nz)], preferred_element_type=jnp.float32
    )
    lane_group = iota((8, ny), 1) // 8
    eye = iota((8, ny), 1) % 8 == iota((8, ny), 0)
    last = iota((8, nz), 1) == nz - 1
    for k, store in enumerate(stores):
        sums_ref[k] = sums[k * ny : (k + 1) * ny]
        totals = [jnp.zeros((8, ny), jnp.float32)] * 3
        for group in range(ny // 8):
            rows = pl.ds(8 * group, 8)
            level, behind = level_ref[k, rows, :], sums_ref[k, rows, :]
            left = jnp.exp2(behind)
            first = (jnp.exp2(behind + binary * level) - left) * level
            found = [jnp.sum(cells, axis=1, keepdims=True) for cells in (first, first * level, jnp.where(last, left, 0.0))]
            totals = [jnp.where(lane_group == group, part, total) for part, total in zip(found, totals)]
        store(*[jnp.sum(jnp.where(eye, total, 0.0), axis=0, keepdims=True) for total in totals])


def ghost_terms(ghost, kept, deep):
    return ghost[0] * (0.5 * ghost[0] + kept[0]) + ghost[1] * kept[1] + ghost[2] * deep


def slots(views):
    me = lax.axis_index("view")
    return lambda view: step_to(me, view, views)


def first_kernel(
    density, image_in_ref, raw_ref, kept_ref, scale_ref, fix_ref, first_ref, sum_ref, xleft_ref,
    image_ref, base_ref, deep_ref, level_ref, sums_ref,
):
    nx = raw_ref.shape[0]
    views = image_in_ref.shape[0]
    slot = slots(views)
    for view in range(views):
        image_ref[slot(view)] = image_in_ref[view]
    near = [xleft_ref[c, 1] for c in range(3)]
    far = [xleft_ref[c, 0] - 8.0 * cells for c, cells in enumerate(near)]

    def prepared(x, place):
        return raw_ref[x] + on_border(fix_ref[...], x), kept_ref[place, 2] + on_border(first_ref[...], x)

    raws = []
    for x, ghost in enumerate((far, near)):
        base, deep = prepared(x, x)
        raws.append(base + ghost_terms(ghost, kept_ref[x], deep) * scale_ref[0])
    two_rows(density, raws, level_ref, sums_ref, sum_ref, [put(image_ref, x, slot) for x in range(2)])
    for k in range(2):
        base_ref[k], deep_ref[k] = prepared(nx - 2 + k, 2 + k)


def last_kernel(
    views, density, image_in_ref, base_ref, deep_ref, kept_ref, scale_ref, sum_ref, xright_ref,
    image_ref, level_ref, sums_ref,
):
    nx = views * image_ref.shape[2]
    slot = slots(views)
    image_ref[...] = image_in_ref[...]
    near = [-xright_ref[c, 0] for c in range(3)]
    far = [-8.0 * cells - xright_ref[c, 1] for c, cells in enumerate(near)]
    raws = [
        base_ref[k] + ghost_terms(ghost, kept_ref[2 + k], deep_ref[k]) * scale_ref[scale_ref.shape[0] - 1]
        for k, ghost in enumerate((near, far))
    ]
    two_rows(density, raws, level_ref, sums_ref, sum_ref, [put(image_ref, nx - 2 + k, slot) for k in range(2)])


def edged(kernel, density, out_shape, image, *rest):
    ny = image.shape[3]
    nz = out_shape[-1].shape[-1] if len(out_shape) > 1 else rest[0].shape[-1]
    return pl.pallas_call(
        functools.partial(kernel, density),
        out_shape=out_shape,
        in_specs=[VMEM] * (1 + len(rest)),
        out_specs=(VMEM,) * len(out_shape),
        scratch_shapes=[pltpu.VMEM((2, ny, nz), jnp.float32), pltpu.VMEM((2, ny, nz), jnp.float32)],
        compiler_params=PARAMS,
        cost_estimate=COST,
    )(image, *rest)


def turn(block, axis, by):
    count = lax.axis_size(axis)
    return lax.ppermute(block, axis, [(i, (i + by) % count) for i in range(count)])


def both_sides(block, axis):
    before = turn(block, axis, 1)
    return before, before if lax.axis_size(axis) == 2 else turn(block, axis, -1)


def exchange(count):
    if count == 4:
        return [(1, 2, 0, 3), (2, 1, 3, 0), (3, 0, 2, 1), (0, 3, 1, 2)]
    if count & (count - 1) == 0:
        return [tuple(i ^ step for i in range(count)) for step in range(count - 1, 0, -1)]
    return [tuple((i + step) % count for i in range(count)) for step in range(1, count)]


def looked_up(index, table):
    found = jnp.int32(table[0])
    for place, entry in enumerate(table[1:], 1):
        found = jnp.where(index == place, entry, found)
    return found


def step_to(me, other, count):
    steps = [(i,) + targets for i, targets in enumerate(zip(*exchange(count)))]
    return looked_up(me, [targets.index(other) for targets in steps])


def exchanged(blocks, axis):
    routes = exchange(lax.axis_size(axis))
    return [blocks[0]] + [lax.ppermute(blocks[k], axis, list(enumerate(route))) for k, route in enumerate(routes, 1)]


def composite_kernel(count, *refs):
    *image_refs, out_ref = refs
    me = lax.axis_index("view")
    sources = [me] + [looked_up(me, [route.index(i) for i in range(count)]) for route in exchange(count)]
    idle = [False] + [source == me for source in sources[1:]]
    images = [
        [image_ref[k] if sits is False else jnp.where(sits, float(k == 2), image_ref[k]) for k in range(3)]
        for image_ref, sits in zip(image_refs, idle)
    ]
    red = square = 0.0
    through = 1.0
    for source, image in zip(sources, images):
        passing = 1.0
        for other, front in zip(sources, images):
            passing = passing * jnp.where(other < source, front[2], 1.0)
        red = red + passing * image[0]
        square = square + passing * image[1]
        through = through * image[2]
    for k, values in enumerate((red, 4.0 * (red - square), 1.0 - through - red, 1.0 - through)):
        out_ref[0, 0, k] = values


def composited(count, images):
    return pl.pallas_call(
        functools.partial(composite_kernel, count),
        out_shape=jax.ShapeDtypeStruct((1, 1, 4) + images[0].shape[1:], jnp.float32),
        in_specs=[VMEM] * len(images),
        out_specs=VMEM,
        compiler_params=PARAMS,
        cost_estimate=COST,
    )(*images)


def local(velocity, occupied, q_floor, q_span):
    comps, nx, ny, nz = velocity.shape
    views = lax.axis_size("view")
    density = 5.0 / (nz * views)
    xleft = turn(velocity[:, nx - 2 :], "gx", 1)
    u, parts, xhead, yface, ztail, zhead = faces(velocity)
    xright = turn(xhead, "gx", -1)
    zleft = turn(ztail, "view", 1)
    zright = turn(zhead, "view", -1)
    yleft, yright = both_sides(yface, "gy")
    raw, pack, kept, scale = shaded(u, parts, yleft, yright, occupied[:, :, 0], q_floor, q_span)
    image, fix, first, summer = blended(density, views, raw, pack, scale, zleft, zright)
    drawn = jax.ShapeDtypeStruct((1 + len(exchange(views)),) + image.shape[1:], jnp.float32)
    two = jax.ShapeDtypeStruct((2, ny, nz), jnp.float32)
    image, base, deep = edged(
        first_kernel, density, (drawn, two, two), image, raw, kept, scale, fix, first, summer, xleft
    )
    (blocks,) = edged(functools.partial(last_kernel, views), density, (drawn,), image, base, deep, kept, scale, summer, xright)
    return composited(views, exchanged(blocks, "view"))


def solution(mesh):
    placed = (P(None, "gx", "gy", "view"), P("gx", "gy", "view"), P(), P())
    return jax.shard_map(
        local,
        mesh=mesh,
        in_specs=placed,
        out_specs=P("gx", "gy", None, "view", None),
        check_vma=False,
    )
```

```python
import functools
import math

import jax
import jax.numpy as jnp
from jax import lax
from jax.experimental import pallas as pl
from jax.experimental.pallas import tpu as pltpu
from jax.sharding import PartitionSpec as P

SUB = 8
ROWS = 32
VMEM = pl.BlockSpec(memory_space=pltpu.VMEM)
HBM = pl.BlockSpec(memory_space=pltpu.HBM)
COST = pl.CostEstimate(flops=1 << 20, bytes_accessed=1 << 20, transcendentals=0)
PARAMS = pltpu.CompilerParams(vmem_limit_bytes=16 << 20)


def split(values):
    high = values.astype(jnp.bfloat16)
    low = (values - high.astype(jnp.float32)).astype(jnp.bfloat16)
    return high, low


def iota(shape, dim):
    return lax.broadcasted_iota(jnp.int32, shape, dim)


def tail_kernel(u_hbm, out_ref, sems):
    comps, nx, ny, _ = u_hbm.shape
    half = ny // 2
    copies = [
        pltpu.make_async_copy(
            u_hbm.at[c, nx - 2 + layer, pl.ds(part * half, half)],
            out_ref.at[c, layer, pl.ds(part * half, half)],
            sems.at[c, layer, part],
        )
        for c in range(comps)
        for layer in range(2)
        for part in range(2)
    ]
    for copy in copies:
        copy.start()
    for copy in copies:
        copy.wait()


def tail(u):
    comps, _, ny, nz = u.shape
    return pl.pallas_call(
        tail_kernel,
        out_shape=jax.ShapeDtypeStruct((comps, 2, ny, nz), jnp.float32),
        in_specs=[HBM],
        out_specs=VMEM,
        scratch_shapes=[pltpu.SemaphoreType.DMA((comps, 2, 2))],
        compiler_params=pltpu.CompilerParams(vmem_limit_bytes=50 << 20),
        cost_estimate=COST,
    )(u)


def faces_kernel(u_hbm, u_ref, parts_ref, xhead_ref, yface_ref, tail_ref, head_ref, packed_ref, sems):
    comps, nx, ny, nz = u_ref.shape
    quarters = sems.shape[1]
    rows = ny // quarters

    def fetch(c, k):
        span = pl.ds(k * rows if isinstance(k, int) else pl.multiple_of(k * rows, rows), rows)
        return pltpu.make_async_copy(u_hbm.at[c, :, span], u_ref.at[c, :, span], sems.at[c, k])

    for c in range(comps):
        for k in range(quarters):
            fetch(c, k).start()
    slot = iota((8, nz), 1) // 4
    for c in range(comps):

        def quarter(k, carry):
            fetch(c, k).wait()
            start = pl.multiple_of(k * rows, rows)
            packed = [jnp.zeros((8, nz), jnp.float32)] * (rows // 8)
            for x in range(nx):
                cells = u_ref[c, x, pl.ds(start, rows), :]
                high, low = split(cells)
                parts_ref[c, x, pl.ds(start, rows), pl.ds(0, nz)] = high
                parts_ref[c, x, pl.ds(start, rows), pl.ds(nz, nz)] = low
                mine = slot == x
                for n in range(rows // 8):
                    packed[n] = jnp.where(mine, pltpu.roll(cells[8 * n : 8 * n + 8], (4 * x + 2) % nz, 1), packed[n])
            for n in range(rows // 8):
                packed_ref[c, pl.ds(pl.multiple_of(start + 8 * n, 8), 8), :] = packed[n]
            return carry

        lax.fori_loop(0, quarters, quarter, 0)
    sub = iota((8, nz), 0)
    for c in range(comps):
        xhead_ref[c] = u_ref[c, pl.ds(0, 2)]
        for x in range(nx):
            lines = jnp.where(sub >= 6, u_ref[c, x, pl.ds(ny - 8, 8), :], u_ref[c, x, pl.ds(0, 8), :])
            yface_ref[c, x] = pltpu.roll(lines, 2, 0)[:4]
    tails, heads = fold([packed_ref[c] for c in range(comps)], ny, nz)
    tail_ref[...] = tails
    head_ref[...] = heads


def fold(packed, ny, nz):
    early = iota((ny, nz), 1) % 4 < 2
    early2 = early[: ny // 2]
    third, fourth = packed[2][: ny // 2], packed[2][ny // 2 :]
    tails = jnp.where(early, packed[0], pltpu.roll(packed[1], 2, 1))
    tails2 = jnp.where(early2, third, pltpu.roll(fourth, 2, 1))
    heads = jnp.where(early, pltpu.roll(packed[0], nz - 2, 1), packed[1])
    heads2 = jnp.where(early2, pltpu.roll(third, nz - 2, 1), fourth)
    return jnp.concatenate([tails, tails2], axis=0), jnp.concatenate([heads, heads2], axis=0)


def unfold(left, right, ny, nz):
    early = iota((ny, nz), 1) % 4 < 2
    early2 = early[: ny // 2]
    left2, right2 = left[ny:], right[ny:]
    left, right = left[:ny], right[:ny]
    first = jnp.where(early, left, pltpu.roll(right, 2, 1))
    second = jnp.where(early, pltpu.roll(left, nz - 2, 1), right)
    third = jnp.where(early2, left2, pltpu.roll(right2, 2, 1))
    fourth = jnp.where(early2, pltpu.roll(left2, nz - 2, 1), right2)
    return first, second, jnp.concatenate([third, fourth], axis=0)


def faces(u):
    comps, nx, ny, nz = u.shape
    message = jax.ShapeDtypeStruct((ny + ny // 2, nz), jnp.float32)
    return pl.pallas_call(
        faces_kernel,
        out_shape=(
            jax.ShapeDtypeStruct(u.shape, jnp.float32),
            jax.ShapeDtypeStruct((comps, nx, ny, 2 * nz), jnp.bfloat16),
            jax.ShapeDtypeStruct((comps, 2, ny, nz), jnp.float32),
            jax.ShapeDtypeStruct((comps, nx, 4, nz), jnp.float32),
            message,
            message,
        ),
        in_specs=[HBM],
        out_specs=(VMEM,) * 6,
        scratch_shapes=[pltpu.VMEM((comps, ny, nz), jnp.float32), pltpu.SemaphoreType.DMA((comps, 4))],
        compiler_params=pltpu.CompilerParams(vmem_limit_bytes=37 << 20),
        cost_estimate=COST,
    )(u)


def stencil(far):
    one = jnp.where(far == 1, 8.0, 0.0) - jnp.where(far == -1, 8.0, 0.0)
    return (one - jnp.where(far == 2, 1.0, 0.0) + jnp.where(far == -2, 1.0, 0.0)).astype(jnp.bfloat16)


def shading(occupied_ref, floor, span, scale_ref, offset_ref):
    blocks, ny, nz = scale_ref.shape
    groups = ny // SUB
    mine = iota((ny, groups), 0) // SUB == iota((ny, groups), 1)
    shrink = 1.0 / span
    for block in range(blocks):
        row = occupied_ref[block : block + 1, :].astype(jnp.float32)
        column = jnp.sum(jnp.where(mine, row, 0.0), axis=1, keepdims=True)
        scale_ref[block] = jnp.broadcast_to(column * (shrink * (-1.0 / 144.0)), (ny, nz))
        offset_ref[block] = jnp.broadcast_to(column * (shrink * -floor), (ny, nz))


def lane_shift(x, nz, back):
    if isinstance(x, int):
        return (4 * x + 2 if back else 2 * nz - 2 - 4 * x) % nz
    return lax.rem(4 * x + 2 if back else 2 * nz - 2 - 4 * x, nz)


def slopes(parts_ref, x, tables, slope_ref):
    yleft_ref, yright_ref, dz_ref, dy_ref = tables
    comps, ny, nz = slope_ref.shape[2:]
    sub = iota((8, nz), 0)

    def top(left):
        lines = jnp.concatenate([left, left], axis=0)
        return jnp.where(sub < 2, lines - jnp.where(sub == 0, 8.0 * pltpu.roll(lines, 7, 0), 0.0), 0.0)

    def low(right):
        lines = jnp.concatenate([right, right], axis=0)
        return jnp.where(sub >= 6, jnp.where(sub == 7, 8.0 * pltpu.roll(lines, 1, 0), 0.0) - lines, 0.0)

    parts = [[parts_ref[c, x + k] for k in range(2)] for c in range(comps)]
    depth = jnp.dot(
        jnp.concatenate([part for pair in parts for part in pair], axis=0),
        dz_ref[...],
        preferred_element_type=jnp.float32,
    )
    for c in range(comps):
        both = jnp.concatenate(
            [jnp.concatenate([part[:, half : half + nz] for part in parts[c]], axis=1) for half in (0, nz)], axis=0
        )
        down = jnp.dot(dy_ref[...], both, preferred_element_type=jnp.float32)
        for k in range(2):
            slope_ref[1, k, c] = depth[(2 * c + k) * ny : (2 * c + k + 1) * ny]
            mine = down[:, k * nz : (k + 1) * nz]
            slope_ref[0, k, c, pl.ds(0, 8), :] = mine[:8] + top(yleft_ref[c, x + k])
            slope_ref[0, k, c, pl.ds(8, ny - 16), :] = mine[8 : ny - 8]
            slope_ref[0, k, c, pl.ds(ny - 8, 8), :] = mine[ny - 8 :] + low(yright_ref[c, x + k])


def shade(u_ref, x, slope_ref, scale_ref, offset_ref, raw_ref, pack_ref, kept_ref=None, place=None):
    comps, nx, ny, nz = u_ref.shape
    block = x // SUB

    def difference(high, low):
        if high is None:
            return 0.0 if low is None else -low
        return high if low is None else high - low

    for y in range(0, ny, ROWS):
        rows = pl.ds(y, ROWS)
        slots = iota((ROWS, nz), 1) // 4
        across = []
        for c in range(comps):
            near = [
                u_ref[c, x + d, rows, :] if not isinstance(x, int) or 0 <= x + d < nx else None for d in range(-2, 4)
            ]
            across.append(
                [8.0 * difference(near[k + 3], near[k + 1]) - difference(near[k + 4], near[k]) for k in range(2)]
            )
        packs = [pack_ref[k, rows, :] for k in range(3)]
        for k in range(2):
            side = [across[c][k] for c in range(comps)]
            down = [slope_ref[0, k, c, rows, :] for c in range(comps)]
            depth = [slope_ref[1, k, c, rows, :] for c in range(comps)]
            total = 0.5 * (side[0] * side[0] + down[1] * down[1] + depth[2] * depth[2])
            total = total + side[1] * down[0] + side[2] * depth[0] + down[2] * depth[1]
            raw_ref[x + k, rows, :] = total * scale_ref[block, rows, :] + offset_ref[block, rows, :]
            back = lane_shift(x + k, nz, True)
            packs = [
                jnp.where(slots == x + k, pltpu.roll(values, back, 1), pack)
                for values, pack in zip((side[2], down[2], depth[2]), packs)
            ]
            if kept_ref is not None:
                for n, values in enumerate((side[0], down[0], depth[0])):
                    kept_ref[place + k, n, rows, :] = values
        for k in range(3):
            pack_ref[k, rows, :] = packs[k]


def shade_kernel(
    u_ref, parts_ref, yleft_ref, yright_ref, occupied_ref, floor_ref, span_ref,
    raw_ref, pack_ref, kept_ref, scale_ref, offset_ref, dz_ref, dy_ref, slope0_ref, slope1_ref,
):
    comps, nx, ny, nz = u_ref.shape
    dz_ref[...] = stencil(iota((2 * nz, nz), 0) % nz - iota((2 * nz, nz), 1))
    dy_ref[...] = stencil(iota((ny, 2 * ny), 1) % ny - iota((ny, 2 * ny), 0))
    shading(occupied_ref, floor_ref[...].reshape(1, 1), span_ref[...].reshape(1, 1), scale_ref, offset_ref)
    pack_ref[...] = jnp.zeros(pack_ref.shape, jnp.float32)
    tables = (yleft_ref, yright_ref, dz_ref, dy_ref)
    outs = (scale_ref, offset_ref, raw_ref, pack_ref)
    slopes(parts_ref, 0, tables, slope0_ref)
    slopes(parts_ref, 2, tables, slope1_ref)
    shade(u_ref, 0, slope0_ref, *outs, kept_ref, 0)

    def pairs(i, carry):
        x = 4 * i + 2
        slopes(parts_ref, x + 2, tables, slope0_ref)
        shade(u_ref, x, slope1_ref, *outs)
        slopes(parts_ref, x + 4, tables, slope1_ref)
        shade(u_ref, x + 2, slope0_ref, *outs)
        return carry

    lax.fori_loop(0, (nx - 4) // 4, pairs, 0)
    shade(u_ref, nx - 2, slope1_ref, *outs, kept_ref, 2)


def shaded(u, *rest):
    comps, nx, ny, nz = u.shape
    return pl.pallas_call(
        shade_kernel,
        out_shape=(
            jax.ShapeDtypeStruct((nx, ny, nz), jnp.float32),
            jax.ShapeDtypeStruct((comps, ny, nz), jnp.float32),
            jax.ShapeDtypeStruct((4, comps, ny, nz), jnp.float32),
            jax.ShapeDtypeStruct((nx // SUB, ny, nz), jnp.float32),
        ),
        in_specs=[VMEM] * 7,
        out_specs=(VMEM,) * 4,
        scratch_shapes=[
            pltpu.VMEM((nx // SUB, ny, nz), jnp.float32),
            pltpu.VMEM((2 * nz, nz), jnp.bfloat16),
            pltpu.VMEM((ny, 2 * ny), jnp.bfloat16),
            pltpu.VMEM((2, 2, comps, ny, nz), jnp.float32),
            pltpu.VMEM((2, 2, comps, ny, nz), jnp.float32),
        ],
        compiler_params=PARAMS,
        cost_estimate=COST,
    )(u, *rest)


def sides_deep(nx, ny, nz, zleft_ref, zright_ref):
    source, target = iota((2 * nz, nz), 0) % nz, iota((2 * nz, nz), 1)
    where = jnp.where(source // 4 == target // 4, source % 4 + 10 * (target % 4), -1)
    weights = jnp.zeros((2 * nz, nz), jnp.float32)
    for value, m, t in ((1.0, 0, 2), (-8.0, 1, 2), (1.0, 1, 3), (-1.0, 2, 0), (8.0, 2, 1), (-1.0, 3, 1)):
        weights = jnp.where(where == m + 10 * t, value, weights)
    weights = weights.astype(jnp.bfloat16)
    return [
        jnp.dot(jnp.concatenate(split(ghost), axis=1), weights, preferred_element_type=jnp.float32)
        for ghost in unfold(zleft_ref[...], zright_ref[...], ny, nz)
    ]


def on_border(packed, x, rows=None):
    ny, nz = packed.shape
    lane = iota((ny, nz), 1)
    return jnp.where((lane >= nz - 2) | (lane < 2), pltpu.roll(packed, lane_shift(x, nz, False), 1), 0.0)


def gather(density, raws, level_ref, sums_ref, sum_ref):
    parts = []
    for k, raw in enumerate(raws):
        level = jnp.clip(raw, 0.0, 1.0)
        level_ref[k] = level
        parts.append(jnp.concatenate(split((density / math.log(2.0)) * level), axis=1))
    ny, nz = level_ref.shape[1:]
    sums = jnp.dot(jnp.concatenate(parts, axis=0), sum_ref[...], preferred_element_type=jnp.float32)
    for k in range(len(raws)):
        sums_ref[k] = sums[k * ny : (k + 1) * ny]


def blend(level_ref, sums_ref, k, store):
    ny, nz = level_ref.shape[1:]
    lane_group = iota((8, ny), 1) // 8
    eye = iota((8, ny), 1) % 8 == iota((8, ny), 0)
    totals = [jnp.zeros((8, ny), jnp.float32)] * 3
    for group in range(ny // 8):
        rows = pl.ds(8 * group, 8)
        level = level_ref[k, rows, :]
        passing = jnp.exp2(sums_ref[k, rows, pl.ds(0, nz)])
        first = (passing - jnp.exp2(sums_ref[k, rows, pl.ds(nz, nz)])) * level
        red = jnp.sum(first, axis=1, keepdims=True)
        square = jnp.sum(first * level, axis=1, keepdims=True)
        whole = sums_ref[k, rows, pl.ds(2 * nz, ny)]
        totals = [jnp.where(lane_group == group, part, total) for part, total in zip((red, square, whole), totals)]
    red, square, whole = [jnp.sum(jnp.where(eye, total, 0.0), axis=0, keepdims=True) for total in totals]
    through = jnp.exp2(whole)
    store(red, square, through)


def put(image_ref, x, slot=lambda view: view):
    per_view = image_ref.shape[2]
    view, row = (x // per_view, x % per_view) if isinstance(x, int) else (lax.div(x, per_view), lax.rem(x, per_view))

    def store(*channels):
        for k, values in enumerate(channels):
            image_ref[slot(view), k, pl.ds(row, 1), :] = values

    return store


def summing(sum_ref):
    nz = sum_ref.shape[0] // 2
    row = iota(sum_ref.shape, 0) % nz
    col = iota(sum_ref.shape, 1)
    sum_ref[...] = jnp.where((row < col) & (col < nz) | (row <= col - nz), -1.0, 0.0).astype(jnp.bfloat16)


def blend_kernel(
    density, raw_ref, pack_ref, scale_ref, zleft_ref, zright_ref,
    image_ref, fix_ref, first_ref, sum_ref, level0_ref, level1_ref, sums0_ref, sums1_ref,
):
    nx, ny, nz = raw_ref.shape
    summing(sum_ref)
    ghosts = sides_deep(nx, ny, nz, zleft_ref, zright_ref)
    first_ref[...] = ghosts[0]
    fix = ghosts[2] * (0.5 * ghosts[2] + pack_ref[2]) + ghosts[0] * pack_ref[0] + ghosts[1] * pack_ref[1]
    per_block = 4 * SUB
    lane_block = iota((ny, nz), 1) // per_block
    scale = scale_ref[0]
    for block in range(1, nx // SUB):
        scale = jnp.where(lane_block == block, scale_ref[block], scale)
    fix_ref[...] = fix * scale
    image_ref[...] = jnp.zeros(image_ref.shape, jnp.float32)
    batch = level0_ref.shape[0]

    def load(x, level_ref, sums_ref):
        raws = [raw_ref[x + k] + on_border(fix_ref[...], x + k) for k in range(batch)]
        gather(density, raws, level_ref, sums_ref, sum_ref)

    def mix(x, level_ref, sums_ref):
        for k in range(batch):
            blend(level_ref, sums_ref, k, put(image_ref, x + k))

    load(2, level0_ref, sums0_ref)

    def batches(i, carry):
        x = 2 * batch * i + 2
        load(x + batch, level1_ref, sums1_ref)
        mix(x, level0_ref, sums0_ref)
        load(x + 2 * batch, level0_ref, sums0_ref)
        mix(x + batch, level1_ref, sums1_ref)
        return carry

    count = (nx - 4) // batch
    lax.fori_loop(0, (count - 1) // 2, batches, 0)
    if count % 2 == 0:
        load(nx - 2 - batch, level1_ref, sums1_ref)
        mix(nx - 2 - 2 * batch, level0_ref, sums0_ref)
        mix(nx - 2 - batch, level1_ref, sums1_ref)
    else:
        mix(nx - 2 - batch, level0_ref, sums0_ref)


def row_tables(batch, ny, nz, buffers):
    return (
        [pltpu.VMEM((batch, ny, nz), jnp.float32)] * buffers
        + [pltpu.VMEM((batch, ny, 2 * nz + ny), jnp.float32)] * buffers
    )


def blended(density, views, raw, *rest):
    nx, ny, nz = raw.shape
    return pl.pallas_call(
        functools.partial(blend_kernel, density),
        out_shape=(
            jax.ShapeDtypeStruct((views, 3, nx // views, ny), jnp.float32),
            jax.ShapeDtypeStruct((ny, nz), jnp.float32),
            jax.ShapeDtypeStruct((ny, nz), jnp.float32),
            jax.ShapeDtypeStruct((2 * nz, 2 * nz + ny), jnp.bfloat16),
        ),
        in_specs=[VMEM] * 5,
        out_specs=(VMEM,) * 4,
        scratch_shapes=row_tables(4, ny, nz, 2),
        compiler_params=PARAMS,
        cost_estimate=COST,
    )(raw, *rest)


def two_rows(density, raws, level_ref, sums_ref, sum_ref, stores):
    ny, nz = raws[0].shape
    binary = density / math.log(2.0)
    parts = []
    for k, raw in enumerate(raws):
        level = jnp.clip(raw, 0.0, 1.0)
        level_ref[k] = level
        parts.append(jnp.concatenate(split(binary * level), axis=1))
    sums = jnp.dot(
        jnp.concatenate(parts, axis=0), sum_ref[:, pl.ds(nz, nz)], preferred_element_type=jnp.float32
    )
    lane_group = iota((8, ny), 1) // 8
    eye = iota((8, ny), 1) % 8 == iota((8, ny), 0)
    last = iota((8, nz), 1) == nz - 1
    for k, store in enumerate(stores):
        sums_ref[k] = sums[k * ny : (k + 1) * ny]
        totals = [jnp.zeros((8, ny), jnp.float32)] * 3
        for group in range(ny // 8):
            rows = pl.ds(8 * group, 8)
            level, behind = level_ref[k, rows, :], sums_ref[k, rows, :]
            left = jnp.exp2(behind)
            first = (jnp.exp2(behind + binary * level) - left) * level
            found = [jnp.sum(cells, axis=1, keepdims=True) for cells in (first, first * level, jnp.where(last, left, 0.0))]
            totals = [jnp.where(lane_group == group, part, total) for part, total in zip(found, totals)]
        store(*[jnp.sum(jnp.where(eye, total, 0.0), axis=0, keepdims=True) for total in totals])


def ghost_terms(ghost, kept, deep):
    return ghost[0] * (0.5 * ghost[0] + kept[0]) + ghost[1] * kept[1] + ghost[2] * deep


def slots(views):
    me = lax.axis_index("view")
    return lambda view: step_to(me, view, views)


def first_kernel(
    density, image_in_ref, raw_ref, kept_ref, scale_ref, fix_ref, first_ref, sum_ref, xleft_ref,
    image_ref, base_ref, deep_ref, level_ref, sums_ref,
):
    nx = raw_ref.shape[0]
    views = image_ref.shape[0]
    slot = slots(views)
    for view in range(views):
        image_ref[slot(view)] = image_in_ref[view]
    near = [xleft_ref[c, 1] for c in range(3)]
    far = [xleft_ref[c, 0] - 8.0 * cells for c, cells in enumerate(near)]

    def prepared(x, place):
        return raw_ref[x] + on_border(fix_ref[...], x), kept_ref[place, 2] + on_border(first_ref[...], x)

    raws = []
    for x, ghost in enumerate((far, near)):
        base, deep = prepared(x, x)
        raws.append(base + ghost_terms(ghost, kept_ref[x], deep) * scale_ref[0])
    two_rows(density, raws, level_ref, sums_ref, sum_ref, [put(image_ref, x, slot) for x in range(2)])
    for k in range(2):
        base_ref[k], deep_ref[k] = prepared(nx - 2 + k, 2 + k)


def last_kernel(
    density, image_in_ref, base_ref, deep_ref, kept_ref, scale_ref, sum_ref, xright_ref,
    image_ref, level_ref, sums_ref,
):
    views, _, per_view, _ = image_ref.shape
    nx = views * per_view
    slot = slots(views)
    image_ref[...] = image_in_ref[...]
    near = [-xright_ref[c, 0] for c in range(3)]
    far = [-8.0 * cells - xright_ref[c, 1] for c, cells in enumerate(near)]
    raws = [
        base_ref[k] + ghost_terms(ghost, kept_ref[2 + k], deep_ref[k]) * scale_ref[scale_ref.shape[0] - 1]
        for k, ghost in enumerate((near, far))
    ]
    two_rows(density, raws, level_ref, sums_ref, sum_ref, [put(image_ref, nx - 2 + k, slot) for k in range(2)])


def edged(kernel, density, out_shape, image, *rest):
    ny = image.shape[3]
    nz = out_shape[-1].shape[-1] if len(out_shape) > 1 else rest[0].shape[-1]
    return pl.pallas_call(
        functools.partial(kernel, density),
        out_shape=out_shape,
        in_specs=[VMEM] * (1 + len(rest)),
        out_specs=(VMEM,) * len(out_shape),
        scratch_shapes=[pltpu.VMEM((2, ny, nz), jnp.float32), pltpu.VMEM((2, ny, nz), jnp.float32)],
        compiler_params=PARAMS,
        cost_estimate=COST,
    )(image, *rest)


def turn(block, axis, by):
    count = lax.axis_size(axis)
    return lax.ppermute(block, axis, [(i, (i + by) % count) for i in range(count)])


def both_sides(block, axis):
    before = turn(block, axis, 1)
    return before, before if lax.axis_size(axis) == 2 else turn(block, axis, -1)


def exchange(count):
    if count == 4:
        return [(2, 3, 1, 0), (3, 2, 0, 1), (1, 0, 3, 2)]
    if count & (count - 1) == 0:
        return [tuple(i ^ step for i in range(count)) for step in range(count - 1, 0, -1)]
    return [tuple((i + step) % count for i in range(count)) for step in range(1, count)]


def looked_up(index, table):
    found = jnp.int32(table[0])
    for place, entry in enumerate(table[1:], 1):
        found = jnp.where(index == place, entry, found)
    return found


def step_to(me, other, count):
    steps = [(i,) + targets for i, targets in enumerate(zip(*exchange(count)))]
    return looked_up(me, [targets.index(other) for targets in steps])


def exchanged(blocks, axis):
    routes = exchange(lax.axis_size(axis))
    return [blocks[0]] + [lax.ppermute(blocks[k], axis, list(enumerate(route))) for k, route in enumerate(routes, 1)]


def composite_kernel(*refs):
    *image_refs, out_ref = refs
    count = len(image_refs)
    me = lax.axis_index("view")
    sources = [me] + [looked_up(me, [route.index(i) for i in range(count)]) for route in exchange(count)]
    red = square = 0.0
    through = 1.0
    for source, image_ref in zip(sources, image_refs):
        passing = 1.0
        for other, front_ref in zip(sources, image_refs):
            passing = passing * jnp.where(other < source, front_ref[2], 1.0)
        red = red + passing * image_ref[0]
        square = square + passing * image_ref[1]
        through = through * image_ref[2]
    for k, values in enumerate((red, 4.0 * (red - square), 1.0 - through - red, 1.0 - through)):
        out_ref[0, 0, k] = values


def composited(images):
    return pl.pallas_call(
        composite_kernel,
        out_shape=jax.ShapeDtypeStruct((1, 1, 4) + images[0].shape[1:], jnp.float32),
        in_specs=[VMEM] * len(images),
        out_specs=VMEM,
        compiler_params=PARAMS,
        cost_estimate=COST,
    )(*images)


def local(velocity, occupied, q_floor, q_span):
    comps, nx, ny, nz = velocity.shape
    views = lax.axis_size("view")
    density = 5.0 / (nz * views)
    xleft = turn(tail(velocity), "gx", 1)
    u, parts, xhead, yface, ztail, zhead = faces(velocity)
    xright = turn(xhead, "gx", -1)
    zleft = turn(ztail, "view", 1)
    zright = turn(zhead, "view", -1)
    yleft, yright = both_sides(yface, "gy")
    raw, pack, kept, scale = shaded(u, parts, yleft, yright, occupied[:, :, 0], q_floor, q_span)
    image, fix, first, summer = blended(density, views, raw, pack, scale, zleft, zright)
    drawn = jax.ShapeDtypeStruct(image.shape, jnp.float32)
    two = jax.ShapeDtypeStruct((2, ny, nz), jnp.float32)
    image, base, deep = edged(
        first_kernel, density, (drawn, two, two), image, raw, kept, scale, fix, first, summer, xleft
    )
    (blocks,) = edged(last_kernel, density, (drawn,), image, base, deep, kept, scale, summer, xright)
    return composited(exchanged(blocks, "view"))


def solution(mesh):
    placed = (P(None, "gx", "gy", "view"), P("gx", "gy", "view"), P(), P())
    return jax.shard_map(
        local,
        mesh=mesh,
        in_specs=placed,
        out_specs=P("gx", "gy", None, "view", None),
        check_vma=False,
    )
```

```python
import functools
import math

import jax
import jax.numpy as jnp
from jax import lax
from jax.experimental import pallas as pl
from jax.experimental.pallas import tpu as pltpu
from jax.sharding import PartitionSpec as P

SUB = 8
ROWS = 32
VMEM = pl.BlockSpec(memory_space=pltpu.VMEM)
HBM = pl.BlockSpec(memory_space=pltpu.HBM)
COST = pl.CostEstimate(flops=1 << 20, bytes_accessed=1 << 20, transcendentals=0)
PARAMS = pltpu.CompilerParams(vmem_limit_bytes=16 << 20)


def split(values):
    high = values.astype(jnp.bfloat16)
    low = (values - high.astype(jnp.float32)).astype(jnp.bfloat16)
    return high, low


def iota(shape, dim):
    return lax.broadcasted_iota(jnp.int32, shape, dim)


def faces_kernel(u_hbm, u_ref, parts_ref, xhead_ref, yface_ref, tail_ref, head_ref, packed_ref, sems):
    comps, nx, ny, nz = u_ref.shape
    quarters = sems.shape[1]
    rows = ny // quarters

    def fetch(c, k):
        span = pl.ds(k * rows if isinstance(k, int) else pl.multiple_of(k * rows, rows), rows)
        return pltpu.make_async_copy(u_hbm.at[c, :, span], u_ref.at[c, :, span], sems.at[c, k])

    for c in range(comps):
        for k in range(quarters):
            fetch(c, k).start()
    slot = iota((8, nz), 1) // 4
    for c in range(comps):

        def quarter(k, carry):
            fetch(c, k).wait()
            start = pl.multiple_of(k * rows, rows)
            packed = [jnp.zeros((8, nz), jnp.float32)] * (rows // 8)
            for x in range(nx):
                cells = u_ref[c, x, pl.ds(start, rows), :]
                high, low = split(cells)
                parts_ref[c, x, pl.ds(start, rows), pl.ds(0, nz)] = high
                parts_ref[c, x, pl.ds(start, rows), pl.ds(nz, nz)] = low
                mine = slot == x
                for n in range(rows // 8):
                    packed[n] = jnp.where(mine, pltpu.roll(cells[8 * n : 8 * n + 8], (4 * x + 2) % nz, 1), packed[n])
            for n in range(rows // 8):
                packed_ref[c, pl.ds(pl.multiple_of(start + 8 * n, 8), 8), :] = packed[n]
            return carry

        lax.fori_loop(0, quarters, quarter, 0)
    sub = iota((8, nz), 0)
    for c in range(comps):
        xhead_ref[c] = u_ref[c, pl.ds(0, 2)]
        for x in range(nx):
            lines = jnp.where(sub >= 6, u_ref[c, x, pl.ds(ny - 8, 8), :], u_ref[c, x, pl.ds(0, 8), :])
            yface_ref[c, x] = pltpu.roll(lines, 2, 0)[:4]
    tails, heads = fold([packed_ref[c] for c in range(comps)], ny, nz)
    tail_ref[...] = tails
    head_ref[...] = heads


def fold(packed, ny, nz):
    early = iota((ny, nz), 1) % 4 < 2
    early2 = early[: ny // 2]
    third, fourth = packed[2][: ny // 2], packed[2][ny // 2 :]
    tails = jnp.where(early, packed[0], pltpu.roll(packed[1], 2, 1))
    tails2 = jnp.where(early2, third, pltpu.roll(fourth, 2, 1))
    heads = jnp.where(early, pltpu.roll(packed[0], nz - 2, 1), packed[1])
    heads2 = jnp.where(early2, pltpu.roll(third, nz - 2, 1), fourth)
    return jnp.concatenate([tails, tails2], axis=0), jnp.concatenate([heads, heads2], axis=0)


def unfold(left, right, ny, nz):
    early = iota((ny, nz), 1) % 4 < 2
    early2 = early[: ny // 2]
    left2, right2 = left[ny:], right[ny:]
    left, right = left[:ny], right[:ny]
    first = jnp.where(early, left, pltpu.roll(right, 2, 1))
    second = jnp.where(early, pltpu.roll(left, nz - 2, 1), right)
    third = jnp.where(early2, left2, pltpu.roll(right2, 2, 1))
    fourth = jnp.where(early2, pltpu.roll(left2, nz - 2, 1), right2)
    return first, second, jnp.concatenate([third, fourth], axis=0)


def faces(u):
    comps, nx, ny, nz = u.shape
    message = jax.ShapeDtypeStruct((ny + ny // 2, nz), jnp.float32)
    return pl.pallas_call(
        faces_kernel,
        out_shape=(
            jax.ShapeDtypeStruct(u.shape, jnp.float32),
            jax.ShapeDtypeStruct((comps, nx, ny, 2 * nz), jnp.bfloat16),
            jax.ShapeDtypeStruct((comps, 2, ny, nz), jnp.float32),
            jax.ShapeDtypeStruct((comps, nx, 4, nz), jnp.float32),
            message,
            message,
        ),
        in_specs=[HBM],
        out_specs=(VMEM,) * 6,
        scratch_shapes=[pltpu.VMEM((comps, ny, nz), jnp.float32), pltpu.SemaphoreType.DMA((comps, 4))],
        compiler_params=pltpu.CompilerParams(vmem_limit_bytes=37 << 20),
        cost_estimate=COST,
    )(u)


def stencil(far):
    one = jnp.where(far == 1, 8.0, 0.0) - jnp.where(far == -1, 8.0, 0.0)
    return (one - jnp.where(far == 2, 1.0, 0.0) + jnp.where(far == -2, 1.0, 0.0)).astype(jnp.bfloat16)


def shading(occupied_ref, floor, span, scale_ref, offset_ref):
    blocks, ny, nz = scale_ref.shape
    groups = ny // SUB
    mine = iota((ny, groups), 0) // SUB == iota((ny, groups), 1)
    shrink = 1.0 / span
    for block in range(blocks):
        row = occupied_ref[block : block + 1, :].astype(jnp.float32)
        column = jnp.sum(jnp.where(mine, row, 0.0), axis=1, keepdims=True)
        scale_ref[block] = jnp.broadcast_to(column * (shrink * (-1.0 / 144.0)), (ny, nz))
        offset_ref[block] = jnp.broadcast_to(column * (shrink * -floor), (ny, nz))


def lane_shift(x, nz, back):
    if isinstance(x, int):
        return (4 * x + 2 if back else 2 * nz - 2 - 4 * x) % nz
    return lax.rem(4 * x + 2 if back else 2 * nz - 2 - 4 * x, nz)


def slopes(parts_ref, x, tables, slope_ref):
    yleft_ref, yright_ref, dz_ref, dy_ref = tables
    comps, ny, nz = slope_ref.shape[2:]
    sub = iota((8, nz), 0)

    def top(left):
        lines = jnp.concatenate([left, left], axis=0)
        return jnp.where(sub < 2, lines - jnp.where(sub == 0, 8.0 * pltpu.roll(lines, 7, 0), 0.0), 0.0)

    def low(right):
        lines = jnp.concatenate([right, right], axis=0)
        return jnp.where(sub >= 6, jnp.where(sub == 7, 8.0 * pltpu.roll(lines, 1, 0), 0.0) - lines, 0.0)

    parts = [[parts_ref[c, x + k] for k in range(2)] for c in range(comps)]
    depth = jnp.dot(
        jnp.concatenate([part for pair in parts for part in pair], axis=0),
        dz_ref[...],
        preferred_element_type=jnp.float32,
    )
    for c in range(comps):
        both = jnp.concatenate(
            [jnp.concatenate([part[:, half : half + nz] for part in parts[c]], axis=1) for half in (0, nz)], axis=0
        )
        down = jnp.dot(dy_ref[...], both, preferred_element_type=jnp.float32)
        for k in range(2):
            slope_ref[1, k, c] = depth[(2 * c + k) * ny : (2 * c + k + 1) * ny]
            mine = down[:, k * nz : (k + 1) * nz]
            slope_ref[0, k, c, pl.ds(0, 8), :] = mine[:8] + top(yleft_ref[c, x + k])
            slope_ref[0, k, c, pl.ds(8, ny - 16), :] = mine[8 : ny - 8]
            slope_ref[0, k, c, pl.ds(ny - 8, 8), :] = mine[ny - 8 :] + low(yright_ref[c, x + k])


def shade(u_ref, x, slope_ref, scale_ref, offset_ref, raw_ref, pack_ref, kept_ref=None, place=None):
    comps, nx, ny, nz = u_ref.shape
    block = x // SUB

    def difference(high, low):
        if high is None:
            return 0.0 if low is None else -low
        return high if low is None else high - low

    for y in range(0, ny, ROWS):
        rows = pl.ds(y, ROWS)
        slots = iota((ROWS, nz), 1) // 4
        across = []
        for c in range(comps):
            near = [
                u_ref[c, x + d, rows, :] if not isinstance(x, int) or 0 <= x + d < nx else None for d in range(-2, 4)
            ]
            across.append(
                [8.0 * difference(near[k + 3], near[k + 1]) - difference(near[k + 4], near[k]) for k in range(2)]
            )
        packs = [pack_ref[k, rows, :] for k in range(3)]
        for k in range(2):
            side = [across[c][k] for c in range(comps)]
            down = [slope_ref[0, k, c, rows, :] for c in range(comps)]
            depth = [slope_ref[1, k, c, rows, :] for c in range(comps)]
            total = 0.5 * (side[0] * side[0] + down[1] * down[1] + depth[2] * depth[2])
            total = total + side[1] * down[0] + side[2] * depth[0] + down[2] * depth[1]
            raw_ref[x + k, rows, :] = total * scale_ref[block, rows, :] + offset_ref[block, rows, :]
            back = lane_shift(x + k, nz, True)
            packs = [
                jnp.where(slots == x + k, pltpu.roll(values, back, 1), pack)
                for values, pack in zip((side[2], down[2], depth[2]), packs)
            ]
            if kept_ref is not None:
                for n, values in enumerate((side[0], down[0], depth[0])):
                    kept_ref[place + k, n, rows, :] = values
        for k in range(3):
            pack_ref[k, rows, :] = packs[k]


def shade_kernel(
    u_ref, parts_ref, yleft_ref, yright_ref, occupied_ref, floor_ref, span_ref,
    raw_ref, pack_ref, kept_ref, scale_ref, offset_ref, dz_ref, dy_ref, slope0_ref, slope1_ref,
):
    comps, nx, ny, nz = u_ref.shape
    dz_ref[...] = stencil(iota((2 * nz, nz), 0) % nz - iota((2 * nz, nz), 1))
    dy_ref[...] = stencil(iota((ny, 2 * ny), 1) % ny - iota((ny, 2 * ny), 0))
    shading(occupied_ref, floor_ref[...].reshape(1, 1), span_ref[...].reshape(1, 1), scale_ref, offset_ref)
    pack_ref[...] = jnp.zeros(pack_ref.shape, jnp.float32)
    tables = (yleft_ref, yright_ref, dz_ref, dy_ref)
    outs = (scale_ref, offset_ref, raw_ref, pack_ref)
    slopes(parts_ref, 0, tables, slope0_ref)
    slopes(parts_ref, 2, tables, slope1_ref)
    shade(u_ref, 0, slope0_ref, *outs, kept_ref, 0)

    def pairs(i, carry):
        x = 4 * i + 2
        slopes(parts_ref, x + 2, tables, slope0_ref)
        shade(u_ref, x, slope1_ref, *outs)
        slopes(parts_ref, x + 4, tables, slope1_ref)
        shade(u_ref, x + 2, slope0_ref, *outs)
        return carry

    lax.fori_loop(0, (nx - 4) // 4, pairs, 0)
    shade(u_ref, nx - 2, slope1_ref, *outs, kept_ref, 2)


def shaded(u, *rest):
    comps, nx, ny, nz = u.shape
    return pl.pallas_call(
        shade_kernel,
        out_shape=(
            jax.ShapeDtypeStruct((nx, ny, nz), jnp.float32),
            jax.ShapeDtypeStruct((comps, ny, nz), jnp.float32),
            jax.ShapeDtypeStruct((4, comps, ny, nz), jnp.float32),
            jax.ShapeDtypeStruct((nx // SUB, ny, nz), jnp.float32),
        ),
        in_specs=[VMEM] * 7,
        out_specs=(VMEM,) * 4,
        scratch_shapes=[
            pltpu.VMEM((nx // SUB, ny, nz), jnp.float32),
            pltpu.VMEM((2 * nz, nz), jnp.bfloat16),
            pltpu.VMEM((ny, 2 * ny), jnp.bfloat16),
            pltpu.VMEM((2, 2, comps, ny, nz), jnp.float32),
            pltpu.VMEM((2, 2, comps, ny, nz), jnp.float32),
        ],
        compiler_params=PARAMS,
        cost_estimate=COST,
    )(u, *rest)


def sides_deep(nx, ny, nz, zleft_ref, zright_ref):
    source, target = iota((2 * nz, nz), 0) % nz, iota((2 * nz, nz), 1)
    where = jnp.where(source // 4 == target // 4, source % 4 + 10 * (target % 4), -1)
    weights = jnp.zeros((2 * nz, nz), jnp.float32)
    for value, m, t in ((1.0, 0, 2), (-8.0, 1, 2), (1.0, 1, 3), (-1.0, 2, 0), (8.0, 2, 1), (-1.0, 3, 1)):
        weights = jnp.where(where == m + 10 * t, value, weights)
    weights = weights.astype(jnp.bfloat16)
    return [
        jnp.dot(jnp.concatenate(split(ghost), axis=1), weights, preferred_element_type=jnp.float32)
        for ghost in unfold(zleft_ref[...], zright_ref[...], ny, nz)
    ]


def on_border(packed, x, rows=None):
    ny, nz = packed.shape
    lane = iota((ny, nz), 1)
    return jnp.where((lane >= nz - 2) | (lane < 2), pltpu.roll(packed, lane_shift(x, nz, False), 1), 0.0)


def gather(density, raws, level_ref, sums_ref, sum_ref):
    parts = []
    for k, raw in enumerate(raws):
        level = jnp.clip(raw, 0.0, 1.0)
        level_ref[k] = level
        parts.append(jnp.concatenate(split((density / math.log(2.0)) * level), axis=1))
    ny, nz = level_ref.shape[1:]
    sums = jnp.dot(jnp.concatenate(parts, axis=0), sum_ref[...], preferred_element_type=jnp.float32)
    for k in range(len(raws)):
        sums_ref[k] = sums[k * ny : (k + 1) * ny]


def blend(level_ref, sums_ref, k, store):
    ny, nz = level_ref.shape[1:]
    lane_group = iota((8, ny), 1) // 8
    eye = iota((8, ny), 1) % 8 == iota((8, ny), 0)
    totals = [jnp.zeros((8, ny), jnp.float32)] * 3
    for group in range(ny // 8):
        rows = pl.ds(8 * group, 8)
        level = level_ref[k, rows, :]
        passing = jnp.exp2(sums_ref[k, rows, pl.ds(0, nz)])
        first = (passing - jnp.exp2(sums_ref[k, rows, pl.ds(nz, nz)])) * level
        red = jnp.sum(first, axis=1, keepdims=True)
        square = jnp.sum(first * level, axis=1, keepdims=True)
        whole = sums_ref[k, rows, pl.ds(2 * nz, ny)]
        totals = [jnp.where(lane_group == group, part, total) for part, total in zip((red, square, whole), totals)]
    red, square, whole = [jnp.sum(jnp.where(eye, total, 0.0), axis=0, keepdims=True) for total in totals]
    through = jnp.exp2(whole)
    store(red, square, through)


def put(image_ref, x, slot=lambda view: view):
    per_view = image_ref.shape[2]
    view, row = (x // per_view, x % per_view) if isinstance(x, int) else (lax.div(x, per_view), lax.rem(x, per_view))

    def store(*channels):
        for k, values in enumerate(channels):
            image_ref[slot(view), k, pl.ds(row, 1), :] = values

    return store


def summing(sum_ref):
    nz = sum_ref.shape[0] // 2
    row = iota(sum_ref.shape, 0) % nz
    col = iota(sum_ref.shape, 1)
    sum_ref[...] = jnp.where((row < col) & (col < nz) | (row <= col - nz), -1.0, 0.0).astype(jnp.bfloat16)


def blend_kernel(
    density, raw_ref, pack_ref, kept_ref, scale_ref, zleft_ref, zright_ref, xleft_ref,
    image_ref, base_ref, deep_ref, sum_ref, level0_ref, level1_ref, sums0_ref, sums1_ref,
    fix_ref, first_ref, edge_level_ref, edge_sums_ref,
):
    nx, ny, nz = raw_ref.shape
    summing(sum_ref)
    ghosts = sides_deep(nx, ny, nz, zleft_ref, zright_ref)
    first_ref[...] = ghosts[0]
    fix = ghosts[2] * (0.5 * ghosts[2] + pack_ref[2]) + ghosts[0] * pack_ref[0] + ghosts[1] * pack_ref[1]
    per_block = 4 * SUB
    lane_block = iota((ny, nz), 1) // per_block
    scale = scale_ref[0]
    for block in range(1, nx // SUB):
        scale = jnp.where(lane_block == block, scale_ref[block], scale)
    fix_ref[...] = fix * scale
    image_ref[...] = jnp.zeros(image_ref.shape, jnp.float32)
    batch = level0_ref.shape[0]

    near = [xleft_ref[c, 1] for c in range(3)]
    far = [xleft_ref[c, 0] - 8.0 * cells for c, cells in enumerate(near)]

    def prepared(x, place):
        return raw_ref[x] + on_border(fix_ref[...], x), kept_ref[place, 2] + on_border(first_ref[...], x)

    raws = []
    for x, ghost in enumerate((far, near)):
        base, deep = prepared(x, x)
        raws.append(base + ghost_terms(ghost, kept_ref[x], deep) * scale_ref[0])
    for k in range(2):
        base_ref[k], deep_ref[k] = prepared(nx - 2 + k, 2 + k)

    def load(x, level_ref, sums_ref):
        raws = [raw_ref[x + k] + on_border(fix_ref[...], x + k) for k in range(batch)]
        gather(density, raws, level_ref, sums_ref, sum_ref)

    def mix(x, level_ref, sums_ref):
        for k in range(batch):
            blend(level_ref, sums_ref, k, put(image_ref, x + k))

    load(2, level0_ref, sums0_ref)
    two_rows(density, raws, edge_level_ref, edge_sums_ref, sum_ref, [put(image_ref, x) for x in range(2)])

    def batches(i, carry):
        x = 2 * batch * i + 2
        load(x + batch, level1_ref, sums1_ref)
        mix(x, level0_ref, sums0_ref)
        load(x + 2 * batch, level0_ref, sums0_ref)
        mix(x + batch, level1_ref, sums1_ref)
        return carry

    count = (nx - 4) // batch
    lax.fori_loop(0, (count - 1) // 2, batches, 0)
    if count % 2 == 0:
        load(nx - 2 - batch, level1_ref, sums1_ref)
        mix(nx - 2 - 2 * batch, level0_ref, sums0_ref)
        mix(nx - 2 - batch, level1_ref, sums1_ref)
    else:
        mix(nx - 2 - batch, level0_ref, sums0_ref)


def row_tables(batch, ny, nz, buffers):
    return (
        [pltpu.VMEM((batch, ny, nz), jnp.float32)] * buffers
        + [pltpu.VMEM((batch, ny, 2 * nz + ny), jnp.float32)] * buffers
    )


def blended(density, views, raw, *rest):
    nx, ny, nz = raw.shape
    return pl.pallas_call(
        functools.partial(blend_kernel, density),
        out_shape=(
            jax.ShapeDtypeStruct((views, 3, nx // views, ny), jnp.float32),
            jax.ShapeDtypeStruct((2, ny, nz), jnp.float32),
            jax.ShapeDtypeStruct((2, ny, nz), jnp.float32),
            jax.ShapeDtypeStruct((2 * nz, 2 * nz + ny), jnp.bfloat16),
        ),
        in_specs=[VMEM] * 7,
        out_specs=(VMEM,) * 4,
        scratch_shapes=row_tables(4, ny, nz, 2)
        + [pltpu.VMEM((ny, nz), jnp.float32)] * 2
        + [pltpu.VMEM((2, ny, nz), jnp.float32)] * 2,
        compiler_params=PARAMS,
        cost_estimate=COST,
    )(raw, *rest)


def two_rows(density, raws, level_ref, sums_ref, sum_ref, stores):
    ny, nz = raws[0].shape
    binary = density / math.log(2.0)
    parts = []
    for k, raw in enumerate(raws):
        level = jnp.clip(raw, 0.0, 1.0)
        level_ref[k] = level
        parts.append(jnp.concatenate(split(binary * level), axis=1))
    sums = jnp.dot(
        jnp.concatenate(parts, axis=0), sum_ref[:, pl.ds(nz, nz)], preferred_element_type=jnp.float32
    )
    lane_group = iota((8, ny), 1) // 8
    eye = iota((8, ny), 1) % 8 == iota((8, ny), 0)
    last = iota((8, nz), 1) == nz - 1
    for k, store in enumerate(stores):
        sums_ref[k] = sums[k * ny : (k + 1) * ny]
        totals = [jnp.zeros((8, ny), jnp.float32)] * 3
        for group in range(ny // 8):
            rows = pl.ds(8 * group, 8)
            level, behind = level_ref[k, rows, :], sums_ref[k, rows, :]
            left = jnp.exp2(behind)
            first = (jnp.exp2(behind + binary * level) - left) * level
            found = [jnp.sum(cells, axis=1, keepdims=True) for cells in (first, first * level, jnp.where(last, left, 0.0))]
            totals = [jnp.where(lane_group == group, part, total) for part, total in zip(found, totals)]
        store(*[jnp.sum(jnp.where(eye, total, 0.0), axis=0, keepdims=True) for total in totals])


def ghost_terms(ghost, kept, deep):
    return ghost[0] * (0.5 * ghost[0] + kept[0]) + ghost[1] * kept[1] + ghost[2] * deep


def slots(views):
    me = lax.axis_index("view")
    return lambda view: step_to(me, view, views)


def last_kernel(
    density, image_in_ref, base_ref, deep_ref, kept_ref, scale_ref, sum_ref, xright_ref,
    image_ref, level_ref, sums_ref,
):
    views, _, per_view, _ = image_ref.shape
    nx = views * per_view
    slot = slots(views)
    for view in range(views):
        image_ref[slot(view)] = image_in_ref[view]
    near = [-xright_ref[c, 0] for c in range(3)]
    far = [-8.0 * cells - xright_ref[c, 1] for c, cells in enumerate(near)]
    raws = [
        base_ref[k] + ghost_terms(ghost, kept_ref[2 + k], deep_ref[k]) * scale_ref[scale_ref.shape[0] - 1]
        for k, ghost in enumerate((near, far))
    ]
    two_rows(density, raws, level_ref, sums_ref, sum_ref, [put(image_ref, nx - 2 + k, slot) for k in range(2)])


def edged(density, image, base, *rest):
    return pl.pallas_call(
        functools.partial(last_kernel, density),
        out_shape=jax.ShapeDtypeStruct(image.shape, jnp.float32),
        in_specs=[VMEM] * (2 + len(rest)),
        out_specs=VMEM,
        scratch_shapes=[pltpu.VMEM(base.shape, jnp.float32)] * 2,
        compiler_params=PARAMS,
        cost_estimate=COST,
    )(image, base, *rest)


def turn(block, axis, by):
    count = lax.axis_size(axis)
    return lax.ppermute(block, axis, [(i, (i + by) % count) for i in range(count)])


def both_sides(block, axis):
    before = turn(block, axis, 1)
    return before, before if lax.axis_size(axis) == 2 else turn(block, axis, -1)


def exchange(count):
    if count == 4:
        return [(2, 3, 1, 0), (3, 2, 0, 1), (1, 0, 3, 2)]
    if count & (count - 1) == 0:
        return [tuple(i ^ step for i in range(count)) for step in range(count - 1, 0, -1)]
    return [tuple((i + step) % count for i in range(count)) for step in range(1, count)]


def looked_up(index, table):
    found = jnp.int32(table[0])
    for place, entry in enumerate(table[1:], 1):
        found = jnp.where(index == place, entry, found)
    return found


def step_to(me, other, count):
    steps = [(i,) + targets for i, targets in enumerate(zip(*exchange(count)))]
    return looked_up(me, [targets.index(other) for targets in steps])


def exchanged(blocks, axis):
    routes = exchange(lax.axis_size(axis))
    return [blocks[0]] + [lax.ppermute(blocks[k], axis, list(enumerate(route))) for k, route in enumerate(routes, 1)]


def composite_kernel(*refs):
    *image_refs, out_ref = refs
    count = len(image_refs)
    me = lax.axis_index("view")
    sources = [me] + [looked_up(me, [route.index(i) for i in range(count)]) for route in exchange(count)]
    red = square = 0.0
    through = 1.0
    for source, image_ref in zip(sources, image_refs):
        passing = 1.0
        for other, front_ref in zip(sources, image_refs):
            passing = passing * jnp.where(other < source, front_ref[2], 1.0)
        red = red + passing * image_ref[0]
        square = square + passing * image_ref[1]
        through = through * image_ref[2]
    for k, values in enumerate((red, 4.0 * (red - square), 1.0 - through - red, 1.0 - through)):
        out_ref[0, 0, k] = values


def composited(images):
    return pl.pallas_call(
        composite_kernel,
        out_shape=jax.ShapeDtypeStruct((1, 1, 4) + images[0].shape[1:], jnp.float32),
        in_specs=[VMEM] * len(images),
        out_specs=VMEM,
        compiler_params=PARAMS,
        cost_estimate=COST,
    )(*images)


def local(velocity, occupied, q_floor, q_span):
    comps, nx, ny, nz = velocity.shape
    views = lax.axis_size("view")
    density = 5.0 / (nz * views)
    xleft = turn(velocity[:, nx - 2 :], "gx", 1)
    u, parts, xhead, yface, ztail, zhead = faces(velocity)
    xright = turn(xhead, "gx", -1)
    zleft = turn(ztail, "view", 1)
    zright = turn(zhead, "view", -1)
    yleft, yright = both_sides(yface, "gy")
    raw, pack, kept, scale = shaded(u, parts, yleft, yright, occupied[:, :, 0], q_floor, q_span)
    image, base, deep, summer = blended(density, views, raw, pack, kept, scale, zleft, zright, xleft)
    blocks = edged(density, image, base, deep, kept, scale, summer, xright)
    return composited(exchanged(blocks, "view"))


def solution(mesh):
    placed = (P(None, "gx", "gy", "view"), P("gx", "gy", "view"), P(), P())
    return jax.shard_map(
        local,
        mesh=mesh,
        in_specs=placed,
        out_specs=P("gx", "gy", None, "view", None),
        check_vma=False,
    )
```

```python
import functools
import math

import jax
import jax.numpy as jnp
from jax import lax
from jax.experimental import pallas as pl
from jax.experimental.pallas import tpu as pltpu
from jax.sharding import PartitionSpec as P

SUB = 8
ROWS = 32
VMEM = pl.BlockSpec(memory_space=pltpu.VMEM)
HBM = pl.BlockSpec(memory_space=pltpu.HBM)
COST = pl.CostEstimate(flops=1 << 20, bytes_accessed=1 << 20, transcendentals=0)
PARAMS = pltpu.CompilerParams(vmem_limit_bytes=16 << 20)


def split(values):
    high = values.astype(jnp.bfloat16)
    low = (values - high.astype(jnp.float32)).astype(jnp.bfloat16)
    return high, low


def iota(shape, dim):
    return lax.broadcasted_iota(jnp.int32, shape, dim)


def tail_kernel(u_hbm, out_ref, sems):
    comps, nx, ny, _ = u_hbm.shape
    copies = [
        pltpu.make_async_copy(
            u_hbm.at[c, nx - 2 + layer], out_ref.at[pl.ds((2 * c + layer) * ny, ny)], sems.at[c, layer]
        )
        for c in range(comps)
        for layer in range(2)
    ]
    for copy in copies:
        copy.start()
    for copy in copies:
        copy.wait()


def tail(u):
    comps, _, ny, nz = u.shape
    return pl.pallas_call(
        tail_kernel,
        out_shape=jax.ShapeDtypeStruct((2 * comps * ny + 2 * SUB, nz), jnp.float32),
        in_specs=[HBM],
        out_specs=VMEM,
        scratch_shapes=[pltpu.SemaphoreType.DMA((comps, 2))],
        compiler_params=pltpu.CompilerParams(vmem_limit_bytes=50 << 20),
        cost_estimate=COST,
    )(u)


def faces_kernel(u_hbm, u_ref, parts_ref, xhead_ref, yface_ref, tail_ref, head_ref, packed_ref, sems):
    comps, nx, ny, nz = u_ref.shape
    quarters = sems.shape[1]
    rows = ny // quarters

    def fetch(c, k):
        span = pl.ds(k * rows if isinstance(k, int) else pl.multiple_of(k * rows, rows), rows)
        return pltpu.make_async_copy(u_hbm.at[c, :, span], u_ref.at[c, :, span], sems.at[c, k])

    for c in range(comps):
        for k in range(quarters):
            fetch(c, k).start()
    slot = iota((8, nz), 1) // 4
    for c in range(comps):

        def quarter(k, carry):
            fetch(c, k).wait()
            start = pl.multiple_of(k * rows, rows)
            packed = [jnp.zeros((8, nz), jnp.float32)] * (rows // 8)
            for x in range(nx):
                cells = u_ref[c, x, pl.ds(start, rows), :]
                high, low = split(cells)
                parts_ref[c, x, pl.ds(start, rows), pl.ds(0, nz)] = high
                parts_ref[c, x, pl.ds(start, rows), pl.ds(nz, nz)] = low
                mine = slot == x
                for n in range(rows // 8):
                    packed[n] = jnp.where(mine, pltpu.roll(cells[8 * n : 8 * n + 8], (4 * x + 2) % nz, 1), packed[n])
            for n in range(rows // 8):
                packed_ref[c, pl.ds(pl.multiple_of(start + 8 * n, 8), 8), :] = packed[n]
            return carry

        lax.fori_loop(0, quarters, quarter, 0)
    sub = iota((8, nz), 0)
    for c in range(comps):
        xhead_ref[c] = u_ref[c, pl.ds(0, 2)]
        for x in range(nx):
            lines = jnp.where(sub >= 6, u_ref[c, x, pl.ds(ny - 8, 8), :], u_ref[c, x, pl.ds(0, 8), :])
            yface_ref[c * nx + x] = lines
    tails, heads = fold([packed_ref[c] for c in range(comps)], ny, nz)
    tail_ref[...] = tails
    head_ref[...] = heads


def fold(packed, ny, nz):
    early = iota((ny, nz), 1) % 4 < 2
    early2 = early[: ny // 2]
    third, fourth = packed[2][: ny // 2], packed[2][ny // 2 :]
    tails = jnp.where(early, packed[0], pltpu.roll(packed[1], 2, 1))
    tails2 = jnp.where(early2, third, pltpu.roll(fourth, 2, 1))
    heads = jnp.where(early, pltpu.roll(packed[0], nz - 2, 1), packed[1])
    heads2 = jnp.where(early2, pltpu.roll(third, nz - 2, 1), fourth)
    return jnp.concatenate([tails, tails2], axis=0), jnp.concatenate([heads, heads2], axis=0)


def unfold(left, right, ny, nz):
    early = iota((ny, nz), 1) % 4 < 2
    early2 = early[: ny // 2]
    left2, right2 = left[ny:], right[ny:]
    left, right = left[:ny], right[:ny]
    first = jnp.where(early, left, pltpu.roll(right, 2, 1))
    second = jnp.where(early, pltpu.roll(left, nz - 2, 1), right)
    third = jnp.where(early2, left2, pltpu.roll(right2, 2, 1))
    fourth = jnp.where(early2, pltpu.roll(left2, nz - 2, 1), right2)
    return first, second, jnp.concatenate([third, fourth], axis=0)


def faces(u):
    comps, nx, ny, nz = u.shape
    message = jax.ShapeDtypeStruct((ny + ny // 2, nz), jnp.float32)
    return pl.pallas_call(
        faces_kernel,
        out_shape=(
            jax.ShapeDtypeStruct(u.shape, jnp.float32),
            jax.ShapeDtypeStruct((comps, nx, ny, 2 * nz), jnp.bfloat16),
            jax.ShapeDtypeStruct((comps, 2, ny, nz), jnp.float32),
            jax.ShapeDtypeStruct((comps * nx + 1, 8, nz), jnp.float32),
            message,
            message,
        ),
        in_specs=[HBM],
        out_specs=(VMEM,) * 6,
        scratch_shapes=[pltpu.VMEM((comps, ny, nz), jnp.float32), pltpu.SemaphoreType.DMA((comps, 4))],
        compiler_params=pltpu.CompilerParams(vmem_limit_bytes=37 << 20),
        cost_estimate=COST,
    )(u)


def stencil(far):
    one = jnp.where(far == 1, 8.0, 0.0) - jnp.where(far == -1, 8.0, 0.0)
    return (one - jnp.where(far == 2, 1.0, 0.0) + jnp.where(far == -2, 1.0, 0.0)).astype(jnp.bfloat16)


def shading(occupied_ref, floor, span, scale_ref, offset_ref):
    blocks, ny, nz = scale_ref.shape
    groups = ny // SUB
    mine = iota((ny, groups), 0) // SUB == iota((ny, groups), 1)
    shrink = 1.0 / span
    for block in range(blocks):
        row = occupied_ref[block : block + 1, :].astype(jnp.float32)
        column = jnp.sum(jnp.where(mine, row, 0.0), axis=1, keepdims=True)
        scale_ref[block] = jnp.broadcast_to(column * (shrink * (-1.0 / 144.0)), (ny, nz))
        offset_ref[block] = jnp.broadcast_to(column * (shrink * -floor), (ny, nz))


def lane_shift(x, nz, back):
    if isinstance(x, int):
        return (4 * x + 2 if back else 2 * nz - 2 - 4 * x) % nz
    return lax.rem(4 * x + 2 if back else 2 * nz - 2 - 4 * x, nz)


def slopes(parts_ref, x, tables, slope_ref):
    yleft_ref, yright_ref, dz_ref, dy_ref = tables
    comps, ny, nz = slope_ref.shape[2:]
    rows = parts_ref.shape[1]
    sub = iota((8, nz), 0)

    def top(left):
        lines = pltpu.roll(left, 2, 0)
        return jnp.where(sub < 2, lines - jnp.where(sub == 0, 8.0 * pltpu.roll(left, 1, 0), 0.0), 0.0)

    def low(right):
        lines = pltpu.roll(right, 6, 0)
        return jnp.where(sub >= 6, jnp.where(sub == 7, 8.0 * pltpu.roll(right, 7, 0), 0.0) - lines, 0.0)

    parts = [[parts_ref[c, x + k] for k in range(2)] for c in range(comps)]
    depth = jnp.dot(
        jnp.concatenate([part for pair in parts for part in pair], axis=0),
        dz_ref[...],
        preferred_element_type=jnp.float32,
    )
    for c in range(comps):
        both = jnp.concatenate(
            [jnp.concatenate([part[:, half : half + nz] for part in parts[c]], axis=1) for half in (0, nz)], axis=0
        )
        down = jnp.dot(dy_ref[...], both, preferred_element_type=jnp.float32)
        for k in range(2):
            slope_ref[1, k, c] = depth[(2 * c + k) * ny : (2 * c + k + 1) * ny]
            mine = down[:, k * nz : (k + 1) * nz]
            slope_ref[0, k, c, pl.ds(0, 8), :] = mine[:8] + top(yleft_ref[c * rows + x + k])
            slope_ref[0, k, c, pl.ds(8, ny - 16), :] = mine[8 : ny - 8]
            slope_ref[0, k, c, pl.ds(ny - 8, 8), :] = mine[ny - 8 :] + low(yright_ref[c * rows + x + k])


def shade(u_ref, x, slope_ref, scale_ref, offset_ref, raw_ref, pack_ref, kept_ref=None, place=None):
    comps, nx, ny, nz = u_ref.shape
    block = x // SUB

    def difference(high, low):
        if high is None:
            return 0.0 if low is None else -low
        return high if low is None else high - low

    for y in range(0, ny, ROWS):
        rows = pl.ds(y, ROWS)
        slots = iota((ROWS, nz), 1) // 4
        across = []
        for c in range(comps):
            near = [
                u_ref[c, x + d, rows, :] if not isinstance(x, int) or 0 <= x + d < nx else None for d in range(-2, 4)
            ]
            across.append(
                [8.0 * difference(near[k + 3], near[k + 1]) - difference(near[k + 4], near[k]) for k in range(2)]
            )
        packs = [pack_ref[k, rows, :] for k in range(3)]
        for k in range(2):
            side = [across[c][k] for c in range(comps)]
            down = [slope_ref[0, k, c, rows, :] for c in range(comps)]
            depth = [slope_ref[1, k, c, rows, :] for c in range(comps)]
            total = 0.5 * (side[0] * side[0] + down[1] * down[1] + depth[2] * depth[2])
            total = total + side[1] * down[0] + side[2] * depth[0] + down[2] * depth[1]
            raw_ref[x + k, rows, :] = total * scale_ref[block, rows, :] + offset_ref[block, rows, :]
            back = lane_shift(x + k, nz, True)
            packs = [
                jnp.where(slots == x + k, pltpu.roll(values, back, 1), pack)
                for values, pack in zip((side[2], down[2], depth[2]), packs)
            ]
            if kept_ref is not None:
                for n, values in enumerate((side[0], down[0], depth[0])):
                    kept_ref[place + k, n, rows, :] = values
        for k in range(3):
            pack_ref[k, rows, :] = packs[k]


def shade_kernel(
    u_ref, parts_ref, yleft_ref, yright_ref, occupied_ref, floor_ref, span_ref,
    raw_ref, pack_ref, kept_ref, scale_ref, offset_ref, dz_ref, dy_ref, slope0_ref, slope1_ref,
):
    comps, nx, ny, nz = u_ref.shape
    dz_ref[...] = stencil(iota((2 * nz, nz), 0) % nz - iota((2 * nz, nz), 1))
    dy_ref[...] = stencil(iota((ny, 2 * ny), 1) % ny - iota((ny, 2 * ny), 0))
    shading(occupied_ref, floor_ref[...].reshape(1, 1), span_ref[...].reshape(1, 1), scale_ref, offset_ref)
    pack_ref[...] = jnp.zeros(pack_ref.shape, jnp.float32)
    tables = (yleft_ref, yright_ref, dz_ref, dy_ref)
    outs = (scale_ref, offset_ref, raw_ref, pack_ref)
    slopes(parts_ref, 0, tables, slope0_ref)
    slopes(parts_ref, 2, tables, slope1_ref)
    shade(u_ref, 0, slope0_ref, *outs, kept_ref, 0)

    def pairs(i, carry):
        x = 4 * i + 2
        slopes(parts_ref, x + 2, tables, slope0_ref)
        shade(u_ref, x, slope1_ref, *outs)
        slopes(parts_ref, x + 4, tables, slope1_ref)
        shade(u_ref, x + 2, slope0_ref, *outs)
        return carry

    lax.fori_loop(0, (nx - 4) // 4, pairs, 0)
    shade(u_ref, nx - 2, slope1_ref, *outs, kept_ref, 2)


def shaded(u, *rest):
    comps, nx, ny, nz = u.shape
    return pl.pallas_call(
        shade_kernel,
        out_shape=(
            jax.ShapeDtypeStruct((nx, ny, nz), jnp.float32),
            jax.ShapeDtypeStruct((comps, ny, nz), jnp.float32),
            jax.ShapeDtypeStruct((4, comps, ny, nz), jnp.float32),
            jax.ShapeDtypeStruct((nx // SUB, ny, nz), jnp.float32),
        ),
        in_specs=[VMEM] * 7,
        out_specs=(VMEM,) * 4,
        scratch_shapes=[
            pltpu.VMEM((nx // SUB, ny, nz), jnp.float32),
            pltpu.VMEM((2 * nz, nz), jnp.bfloat16),
            pltpu.VMEM((ny, 2 * ny), jnp.bfloat16),
            pltpu.VMEM((2, 2, comps, ny, nz), jnp.float32),
            pltpu.VMEM((2, 2, comps, ny, nz), jnp.float32),
        ],
        compiler_params=PARAMS,
        cost_estimate=COST,
    )(u, *rest)


def sides_deep(nx, ny, nz, zleft_ref, zright_ref):
    source, target = iota((2 * nz, nz), 0) % nz, iota((2 * nz, nz), 1)
    where = jnp.where(source // 4 == target // 4, source % 4 + 10 * (target % 4), -1)
    weights = jnp.zeros((2 * nz, nz), jnp.float32)
    for value, m, t in ((1.0, 0, 2), (-8.0, 1, 2), (1.0, 1, 3), (-1.0, 2, 0), (8.0, 2, 1), (-1.0, 3, 1)):
        weights = jnp.where(where == m + 10 * t, value, weights)
    weights = weights.astype(jnp.bfloat16)
    return [
        jnp.dot(jnp.concatenate(split(ghost), axis=1), weights, preferred_element_type=jnp.float32)
        for ghost in unfold(zleft_ref[...], zright_ref[...], ny, nz)
    ]


def on_border(packed, x, rows=None):
    ny, nz = packed.shape
    lane = iota((ny, nz), 1)
    return jnp.where((lane >= nz - 2) | (lane < 2), pltpu.roll(packed, lane_shift(x, nz, False), 1), 0.0)


def gather(density, raws, level_ref, sums_ref, sum_ref):
    parts = []
    for k, raw in enumerate(raws):
        level = jnp.clip(raw, 0.0, 1.0)
        level_ref[k] = level
        parts.append(jnp.concatenate(split((density / math.log(2.0)) * level), axis=1))
    ny, nz = level_ref.shape[1:]
    sums = jnp.dot(jnp.concatenate(parts, axis=0), sum_ref[...], preferred_element_type=jnp.float32)
    for k in range(len(raws)):
        sums_ref[k] = sums[k * ny : (k + 1) * ny]


def blend(level_ref, sums_ref, k, store):
    ny, nz = level_ref.shape[1:]
    lane_group = iota((8, ny), 1) // 8
    eye = iota((8, ny), 1) % 8 == iota((8, ny), 0)
    totals = [jnp.zeros((8, ny), jnp.float32)] * 3
    for group in range(ny // 8):
        rows = pl.ds(8 * group, 8)
        level = level_ref[k, rows, :]
        passing = jnp.exp2(sums_ref[k, rows, pl.ds(0, nz)])
        first = (passing - jnp.exp2(sums_ref[k, rows, pl.ds(nz, nz)])) * level
        red = jnp.sum(first, axis=1, keepdims=True)
        square = jnp.sum(first * level, axis=1, keepdims=True)
        whole = sums_ref[k, rows, pl.ds(2 * nz, ny)]
        totals = [jnp.where(lane_group == group, part, total) for part, total in zip((red, square, whole), totals)]
    red, square, whole = [jnp.sum(jnp.where(eye, total, 0.0), axis=0, keepdims=True) for total in totals]
    through = jnp.exp2(whole)
    store(red, square, through)


def put(image_ref, x, slot=lambda view: view):
    per_view = image_ref.shape[2]
    view, row = (x // per_view, x % per_view) if isinstance(x, int) else (lax.div(x, per_view), lax.rem(x, per_view))

    def store(*channels):
        for k, values in enumerate(channels):
            image_ref[slot(view), k, pl.ds(row, 1), :] = values

    return store


def summing(sum_ref):
    nz = sum_ref.shape[0] // 2
    row = iota(sum_ref.shape, 0) % nz
    col = iota(sum_ref.shape, 1)
    sum_ref[...] = jnp.where((row < col) & (col < nz) | (row <= col - nz), -1.0, 0.0).astype(jnp.bfloat16)


def blend_kernel(
    density, raw_ref, pack_ref, kept_ref, scale_ref, zleft_ref, zright_ref, xleft_ref,
    image_ref, base_ref, deep_ref, sum_ref, level0_ref, level1_ref, sums0_ref, sums1_ref,
    fix_ref, first_ref, edge_level_ref, edge_sums_ref,
):
    nx, ny, nz = raw_ref.shape
    summing(sum_ref)
    ghosts = sides_deep(nx, ny, nz, zleft_ref, zright_ref)
    first_ref[...] = ghosts[0]
    fix = ghosts[2] * (0.5 * ghosts[2] + pack_ref[2]) + ghosts[0] * pack_ref[0] + ghosts[1] * pack_ref[1]
    per_block = 4 * SUB
    lane_block = iota((ny, nz), 1) // per_block
    scale = scale_ref[0]
    for block in range(1, nx // SUB):
        scale = jnp.where(lane_block == block, scale_ref[block], scale)
    fix_ref[...] = fix * scale
    image_ref[...] = jnp.zeros(image_ref.shape, jnp.float32)
    batch = level0_ref.shape[0]

    near = [xleft_ref[pl.ds((2 * c + 1) * ny, ny), :] for c in range(3)]
    far = [xleft_ref[pl.ds(2 * c * ny, ny), :] - 8.0 * cells for c, cells in enumerate(near)]

    def prepared(x, place):
        return raw_ref[x] + on_border(fix_ref[...], x), kept_ref[place, 2] + on_border(first_ref[...], x)

    raws = []
    for x, ghost in enumerate((far, near)):
        base, deep = prepared(x, x)
        raws.append(base + ghost_terms(ghost, kept_ref[x], deep) * scale_ref[0])
    for k in range(2):
        base_ref[k], deep_ref[k] = prepared(nx - 2 + k, 2 + k)

    def load(x, level_ref, sums_ref):
        raws = [raw_ref[x + k] + on_border(fix_ref[...], x + k) for k in range(batch)]
        gather(density, raws, level_ref, sums_ref, sum_ref)

    def mix(x, level_ref, sums_ref):
        for k in range(batch):
            blend(level_ref, sums_ref, k, put(image_ref, x + k))

    load(2, level0_ref, sums0_ref)
    two_rows(density, raws, edge_level_ref, edge_sums_ref, sum_ref, [put(image_ref, x) for x in range(2)])

    def batches(i, carry):
        x = 2 * batch * i + 2
        load(x + batch, level1_ref, sums1_ref)
        mix(x, level0_ref, sums0_ref)
        load(x + 2 * batch, level0_ref, sums0_ref)
        mix(x + batch, level1_ref, sums1_ref)
        return carry

    count = (nx - 4) // batch
    lax.fori_loop(0, (count - 1) // 2, batches, 0)
    if count % 2 == 0:
        load(nx - 2 - batch, level1_ref, sums1_ref)
        mix(nx - 2 - 2 * batch, level0_ref, sums0_ref)
        mix(nx - 2 - batch, level1_ref, sums1_ref)
    else:
        mix(nx - 2 - batch, level0_ref, sums0_ref)


def row_tables(batch, ny, nz, buffers):
    return (
        [pltpu.VMEM((batch, ny, nz), jnp.float32)] * buffers
        + [pltpu.VMEM((batch, ny, 2 * nz + ny), jnp.float32)] * buffers
    )


def blended(density, views, raw, *rest):
    nx, ny, nz = raw.shape
    return pl.pallas_call(
        functools.partial(blend_kernel, density),
        out_shape=(
            jax.ShapeDtypeStruct((views, 3, nx // views, ny), jnp.float32),
            jax.ShapeDtypeStruct((2, ny, nz), jnp.float32),
            jax.ShapeDtypeStruct((2, ny, nz), jnp.float32),
            jax.ShapeDtypeStruct((2 * nz, 2 * nz + ny), jnp.bfloat16),
        ),
        in_specs=[VMEM] * 7,
        out_specs=(VMEM,) * 4,
        scratch_shapes=row_tables(4, ny, nz, 2)
        + [pltpu.VMEM((ny, nz), jnp.float32)] * 2
        + [pltpu.VMEM((2, ny, nz), jnp.float32)] * 2,
        compiler_params=PARAMS,
        cost_estimate=COST,
    )(raw, *rest)


def two_rows(density, raws, level_ref, sums_ref, sum_ref, stores):
    ny, nz = raws[0].shape
    binary = density / math.log(2.0)
    parts = []
    for k, raw in enumerate(raws):
        level = jnp.clip(raw, 0.0, 1.0)
        level_ref[k] = level
        parts.append(jnp.concatenate(split(binary * level), axis=1))
    sums = jnp.dot(
        jnp.concatenate(parts, axis=0), sum_ref[:, pl.ds(nz, nz)], preferred_element_type=jnp.float32
    )
    lane_group = iota((8, ny), 1) // 8
    eye = iota((8, ny), 1) % 8 == iota((8, ny), 0)
    last = iota((8, nz), 1) == nz - 1
    for k, store in enumerate(stores):
        sums_ref[k] = sums[k * ny : (k + 1) * ny]
        totals = [jnp.zeros((8, ny), jnp.float32)] * 3
        for group in range(ny // 8):
            rows = pl.ds(8 * group, 8)
            level, behind = level_ref[k, rows, :], sums_ref[k, rows, :]
            left = jnp.exp2(behind)
            first = (jnp.exp2(behind + binary * level) - left) * level
            found = [jnp.sum(cells, axis=1, keepdims=True) for cells in (first, first * level, jnp.where(last, left, 0.0))]
            totals = [jnp.where(lane_group == group, part, total) for part, total in zip(found, totals)]
        store(*[jnp.sum(jnp.where(eye, total, 0.0), axis=0, keepdims=True) for total in totals])


def ghost_terms(ghost, kept, deep):
    return ghost[0] * (0.5 * ghost[0] + kept[0]) + ghost[1] * kept[1] + ghost[2] * deep


def slots(views):
    me = lax.axis_index("view")
    return lambda view: step_to(me, view, views)


def last_kernel(
    density, image_in_ref, base_ref, deep_ref, kept_ref, scale_ref, sum_ref, xright_ref,
    image_ref, level_ref, sums_ref,
):
    views, _, per_view, _ = image_ref.shape
    nx = views * per_view
    slot = slots(views)
    for view in range(views):
        image_ref[slot(view)] = image_in_ref[view]
    near = [-xright_ref[c, 0] for c in range(3)]
    far = [-8.0 * cells - xright_ref[c, 1] for c, cells in enumerate(near)]
    raws = [
        base_ref[k] + ghost_terms(ghost, kept_ref[2 + k], deep_ref[k]) * scale_ref[scale_ref.shape[0] - 1]
        for k, ghost in enumerate((near, far))
    ]
    two_rows(density, raws, level_ref, sums_ref, sum_ref, [put(image_ref, nx - 2 + k, slot) for k in range(2)])


def edged(density, image, base, *rest):
    return pl.pallas_call(
        functools.partial(last_kernel, density),
        out_shape=jax.ShapeDtypeStruct(image.shape, jnp.float32),
        in_specs=[VMEM] * (2 + len(rest)),
        out_specs=VMEM,
        scratch_shapes=[pltpu.VMEM(base.shape, jnp.float32)] * 2,
        compiler_params=PARAMS,
        cost_estimate=COST,
    )(image, base, *rest)


def turn(block, axis, by):
    count = lax.axis_size(axis)
    return lax.ppermute(block, axis, [(i, (i + by) % count) for i in range(count)])


def both_sides(block, axis):
    before = turn(block, axis, 1)
    return before, before if lax.axis_size(axis) == 2 else turn(block, axis, -1)


def exchange(count):
    if count == 4:
        return [(2, 3, 1, 0), (3, 2, 0, 1), (1, 0, 3, 2)]
    if count & (count - 1) == 0:
        return [tuple(i ^ step for i in range(count)) for step in range(count - 1, 0, -1)]
    return [tuple((i + step) % count for i in range(count)) for step in range(1, count)]


def looked_up(index, table):
    found = jnp.int32(table[0])
    for place, entry in enumerate(table[1:], 1):
        found = jnp.where(index == place, entry, found)
    return found


def step_to(me, other, count):
    steps = [(i,) + targets for i, targets in enumerate(zip(*exchange(count)))]
    return looked_up(me, [targets.index(other) for targets in steps])


def exchanged(blocks, axis):
    routes = exchange(lax.axis_size(axis))
    return [blocks[0]] + [lax.ppermute(blocks[k], axis, list(enumerate(route))) for k, route in enumerate(routes, 1)]


def composite_kernel(*refs):
    *image_refs, out_ref = refs
    count = len(image_refs)
    me = lax.axis_index("view")
    sources = [me] + [looked_up(me, [route.index(i) for i in range(count)]) for route in exchange(count)]
    red = square = 0.0
    through = 1.0
    for source, image_ref in zip(sources, image_refs):
        passing = 1.0
        for other, front_ref in zip(sources, image_refs):
            passing = passing * jnp.where(other < source, front_ref[2], 1.0)
        red = red + passing * image_ref[0]
        square = square + passing * image_ref[1]
        through = through * image_ref[2]
    for k, values in enumerate((red, 4.0 * (red - square), 1.0 - through - red, 1.0 - through)):
        out_ref[0, 0, k] = values


def composited(images):
    return pl.pallas_call(
        composite_kernel,
        out_shape=jax.ShapeDtypeStruct((1, 1, 4) + images[0].shape[1:], jnp.float32),
        in_specs=[VMEM] * len(images),
        out_specs=VMEM,
        compiler_params=PARAMS,
        cost_estimate=COST,
    )(*images)


def local(velocity, occupied, q_floor, q_span):
    comps, nx, ny, nz = velocity.shape
    views = lax.axis_size("view")
    density = 5.0 / (nz * views)
    xleft = turn(tail(velocity), "gx", 1)
    u, parts, xhead, yface, ztail, zhead = faces(velocity)
    xright = turn(xhead, "gx", -1)
    zleft = turn(ztail, "view", 1)
    zright = turn(zhead, "view", -1)
    yleft, yright = both_sides(yface, "gy")
    raw, pack, kept, scale = shaded(u, parts, yleft, yright, occupied[:, :, 0], q_floor, q_span)
    image, base, deep, summer = blended(density, views, raw, pack, kept, scale, zleft, zright, xleft)
    blocks = edged(density, image, base, deep, kept, scale, summer, xright)
    return composited(exchanged(blocks, "view"))


def solution(mesh):
    placed = (P(None, "gx", "gy", "view"), P("gx", "gy", "view"), P(), P())
    return jax.shard_map(
        local,
        mesh=mesh,
        in_specs=placed,
        out_specs=P("gx", "gy", None, "view", None),
        check_vma=False,
    )
```

```python
import functools
import math

import jax
import jax.numpy as jnp
from jax import lax
from jax.experimental import pallas as pl
from jax.experimental.pallas import tpu as pltpu
from jax.sharding import PartitionSpec as P

SUB = 8
ROWS = 32
VMEM = pl.BlockSpec(memory_space=pltpu.VMEM)
HBM = pl.BlockSpec(memory_space=pltpu.HBM)
COST = pl.CostEstimate(flops=1 << 20, bytes_accessed=1 << 20, transcendentals=0)
PARAMS = pltpu.CompilerParams(vmem_limit_bytes=16 << 20)


def split(values):
    high = values.astype(jnp.bfloat16)
    low = (values - high.astype(jnp.float32)).astype(jnp.bfloat16)
    return high, low


def iota(shape, dim):
    return lax.broadcasted_iota(jnp.int32, shape, dim)


def faces_kernel(u_hbm, u_ref, parts_ref, xhead_ref, yface_ref, tail_ref, head_ref, packed_ref, sems):
    comps, nx, ny, nz = u_ref.shape
    quarters = sems.shape[1]
    rows = ny // quarters

    def fetch(c, k):
        span = pl.ds(k * rows if isinstance(k, int) else pl.multiple_of(k * rows, rows), rows)
        return pltpu.make_async_copy(u_hbm.at[c, :, span], u_ref.at[c, :, span], sems.at[c, k])

    for c in range(comps):
        for k in range(quarters):
            fetch(c, k).start()
    slot = iota((8, nz), 1) // 4
    for c in range(comps):

        def quarter(k, carry):
            fetch(c, k).wait()
            start = pl.multiple_of(k * rows, rows)
            packed = [jnp.zeros((8, nz), jnp.float32)] * (rows // 8)
            for x in range(nx):
                cells = u_ref[c, x, pl.ds(start, rows), :]
                high, low = split(cells)
                parts_ref[c, x, pl.ds(start, rows), pl.ds(0, nz)] = high
                parts_ref[c, x, pl.ds(start, rows), pl.ds(nz, nz)] = low
                mine = slot == x
                for n in range(rows // 8):
                    packed[n] = jnp.where(mine, pltpu.roll(cells[8 * n : 8 * n + 8], (4 * x + 2) % nz, 1), packed[n])
            for n in range(rows // 8):
                packed_ref[c, pl.ds(pl.multiple_of(start + 8 * n, 8), 8), :] = packed[n]
            return carry

        lax.fori_loop(0, quarters, quarter, 0)
    sub = iota((8, nz), 0)
    for c in range(comps):
        xhead_ref[c] = u_ref[c, pl.ds(0, 2)]
        for x in range(nx):
            lines = jnp.where(sub >= 6, u_ref[c, x, pl.ds(ny - 8, 8), :], u_ref[c, x, pl.ds(0, 8), :])
            yface_ref[c, x] = pltpu.roll(lines, 2, 0)[:4]
    tails, heads = fold([packed_ref[c] for c in range(comps)], ny, nz)
    tail_ref[...] = tails
    head_ref[...] = heads


def fold(packed, ny, nz):
    early = iota((ny, nz), 1) % 4 < 2
    early2 = early[: ny // 2]
    third, fourth = packed[2][: ny // 2], packed[2][ny // 2 :]
    tails = jnp.where(early, packed[0], pltpu.roll(packed[1], 2, 1))
    tails2 = jnp.where(early2, third, pltpu.roll(fourth, 2, 1))
    heads = jnp.where(early, pltpu.roll(packed[0], nz - 2, 1), packed[1])
    heads2 = jnp.where(early2, pltpu.roll(third, nz - 2, 1), fourth)
    return jnp.concatenate([tails, tails2], axis=0), jnp.concatenate([heads, heads2], axis=0)


def unfold(left, right, ny, nz):
    early = iota((ny, nz), 1) % 4 < 2
    early2 = early[: ny // 2]
    left2, right2 = left[ny:], right[ny:]
    left, right = left[:ny], right[:ny]
    first = jnp.where(early, left, pltpu.roll(right, 2, 1))
    second = jnp.where(early, pltpu.roll(left, nz - 2, 1), right)
    third = jnp.where(early2, left2, pltpu.roll(right2, 2, 1))
    fourth = jnp.where(early2, pltpu.roll(left2, nz - 2, 1), right2)
    return first, second, jnp.concatenate([third, fourth], axis=0)


def faces(u):
    comps, nx, ny, nz = u.shape
    message = jax.ShapeDtypeStruct((ny + ny // 2, nz), jnp.float32)
    return pl.pallas_call(
        faces_kernel,
        out_shape=(
            jax.ShapeDtypeStruct(u.shape, jnp.float32),
            jax.ShapeDtypeStruct((comps, nx, ny, 2 * nz), jnp.bfloat16),
            jax.ShapeDtypeStruct((comps, 2, ny, nz), jnp.float32),
            jax.ShapeDtypeStruct((comps, nx, 4, nz), jnp.float32),
            message,
            message,
        ),
        in_specs=[HBM],
        out_specs=(VMEM,) * 6,
        scratch_shapes=[pltpu.VMEM((comps, ny, nz), jnp.float32), pltpu.SemaphoreType.DMA((comps, 4))],
        compiler_params=pltpu.CompilerParams(vmem_limit_bytes=37 << 20),
        cost_estimate=COST,
    )(u)


def stencil(far):
    one = jnp.where(far == 1, 8.0, 0.0) - jnp.where(far == -1, 8.0, 0.0)
    return (one - jnp.where(far == 2, 1.0, 0.0) + jnp.where(far == -2, 1.0, 0.0)).astype(jnp.bfloat16)


def shading(occupied_ref, floor, span, scale_ref, offset_ref):
    blocks, ny, nz = scale_ref.shape
    groups = ny // SUB
    mine = iota((ny, groups), 0) // SUB == iota((ny, groups), 1)
    shrink = 1.0 / span
    for block in range(blocks):
        row = occupied_ref[block : block + 1, :].astype(jnp.float32)
        column = jnp.sum(jnp.where(mine, row, 0.0), axis=1, keepdims=True)
        scale_ref[block] = jnp.broadcast_to(column * (shrink * (-1.0 / 144.0)), (ny, nz))
        offset_ref[block] = jnp.broadcast_to(column * (shrink * -floor), (ny, nz))


def lane_shift(x, nz, back):
    if isinstance(x, int):
        return (4 * x + 2 if back else 2 * nz - 2 - 4 * x) % nz
    return lax.rem(4 * x + 2 if back else 2 * nz - 2 - 4 * x, nz)


def slopes(parts_ref, x, tables, slope_ref):
    yleft_ref, yright_ref, dz_ref, dy_ref = tables
    comps, ny, nz = slope_ref.shape[2:]
    sub = iota((8, nz), 0)

    def top(left):
        lines = jnp.concatenate([left, left], axis=0)
        return jnp.where(sub < 2, lines - jnp.where(sub == 0, 8.0 * pltpu.roll(lines, 7, 0), 0.0), 0.0)

    def low(right):
        lines = jnp.concatenate([right, right], axis=0)
        return jnp.where(sub >= 6, jnp.where(sub == 7, 8.0 * pltpu.roll(lines, 1, 0), 0.0) - lines, 0.0)

    parts = [[parts_ref[c, x + k] for k in range(2)] for c in range(comps)]
    depth = jnp.dot(
        jnp.concatenate([part for pair in parts for part in pair], axis=0),
        dz_ref[...],
        preferred_element_type=jnp.float32,
    )
    for c in range(comps):
        both = jnp.concatenate(
            [jnp.concatenate([part[:, half : half + nz] for part in parts[c]], axis=1) for half in (0, nz)], axis=0
        )
        down = jnp.dot(dy_ref[...], both, preferred_element_type=jnp.float32)
        for k in range(2):
            slope_ref[1, k, c] = depth[(2 * c + k) * ny : (2 * c + k + 1) * ny]
            mine = down[:, k * nz : (k + 1) * nz]
            slope_ref[0, k, c, pl.ds(0, 8), :] = mine[:8] + top(yleft_ref[c, x + k])
            slope_ref[0, k, c, pl.ds(8, ny - 16), :] = mine[8 : ny - 8]
            slope_ref[0, k, c, pl.ds(ny - 8, 8), :] = mine[ny - 8 :] + low(yright_ref[c, x + k])


def shade(u_ref, x, slope_ref, scale_ref, offset_ref, raw_ref, pack_ref, kept_ref=None, place=None):
    comps, nx, ny, nz = u_ref.shape
    block = x // SUB

    def difference(high, low):
        if high is None:
            return 0.0 if low is None else -low
        return high if low is None else high - low

    for y in range(0, ny, ROWS):
        rows = pl.ds(y, ROWS)
        slots = iota((ROWS, nz), 1) // 4
        across = []
        for c in range(comps):
            near = [
                u_ref[c, x + d, rows, :] if not isinstance(x, int) or 0 <= x + d < nx else None for d in range(-2, 4)
            ]
            across.append(
                [8.0 * difference(near[k + 3], near[k + 1]) - difference(near[k + 4], near[k]) for k in range(2)]
            )
        packs = [pack_ref[k, rows, :] for k in range(3)]
        for k in range(2):
            side = [across[c][k] for c in range(comps)]
            down = [slope_ref[0, k, c, rows, :] for c in range(comps)]
            depth = [slope_ref[1, k, c, rows, :] for c in range(comps)]
            total = 0.5 * (side[0] * side[0] + down[1] * down[1] + depth[2] * depth[2])
            total = total + side[1] * down[0] + side[2] * depth[0] + down[2] * depth[1]
            raw_ref[x + k, rows, :] = total * scale_ref[block, rows, :] + offset_ref[block, rows, :]
            back = lane_shift(x + k, nz, True)
            packs = [
                jnp.where(slots == x + k, pltpu.roll(values, back, 1), pack)
                for values, pack in zip((side[2], down[2], depth[2]), packs)
            ]
            if kept_ref is not None:
                for n, values in enumerate((side[0], down[0], depth[0])):
                    kept_ref[place + k, n, rows, :] = values
        for k in range(3):
            pack_ref[k, rows, :] = packs[k]


def shade_kernel(
    u_ref, parts_ref, yleft_ref, yright_ref, occupied_ref, floor_ref, span_ref,
    raw_ref, pack_ref, kept_ref, scale_ref, offset_ref, dz_ref, dy_ref, slope0_ref, slope1_ref,
):
    comps, nx, ny, nz = u_ref.shape
    dz_ref[...] = stencil(iota((2 * nz, nz), 0) % nz - iota((2 * nz, nz), 1))
    dy_ref[...] = stencil(iota((ny, 2 * ny), 1) % ny - iota((ny, 2 * ny), 0))
    shading(occupied_ref, floor_ref[...].reshape(1, 1), span_ref[...].reshape(1, 1), scale_ref, offset_ref)
    pack_ref[...] = jnp.zeros(pack_ref.shape, jnp.float32)
    tables = (yleft_ref, yright_ref, dz_ref, dy_ref)
    outs = (scale_ref, offset_ref, raw_ref, pack_ref)
    slopes(parts_ref, 0, tables, slope0_ref)
    slopes(parts_ref, 2, tables, slope1_ref)
    shade(u_ref, 0, slope0_ref, *outs, kept_ref, 0)

    def pairs(i, carry):
        x = 4 * i + 2
        slopes(parts_ref, x + 2, tables, slope0_ref)
        shade(u_ref, x, slope1_ref, *outs)
        slopes(parts_ref, x + 4, tables, slope1_ref)
        shade(u_ref, x + 2, slope0_ref, *outs)
        return carry

    lax.fori_loop(0, (nx - 4) // 4, pairs, 0)
    shade(u_ref, nx - 2, slope1_ref, *outs, kept_ref, 2)


def shaded(u, *rest):
    comps, nx, ny, nz = u.shape
    return pl.pallas_call(
        shade_kernel,
        out_shape=(
            jax.ShapeDtypeStruct((nx, ny, nz), jnp.float32),
            jax.ShapeDtypeStruct((comps, ny, nz), jnp.float32),
            jax.ShapeDtypeStruct((4, comps, ny, nz), jnp.float32),
            jax.ShapeDtypeStruct((nx // SUB, ny, nz), jnp.float32),
        ),
        in_specs=[VMEM] * 7,
        out_specs=(VMEM,) * 4,
        scratch_shapes=[
            pltpu.VMEM((nx // SUB, ny, nz), jnp.float32),
            pltpu.VMEM((2 * nz, nz), jnp.bfloat16),
            pltpu.VMEM((ny, 2 * ny), jnp.bfloat16),
            pltpu.VMEM((2, 2, comps, ny, nz), jnp.float32),
            pltpu.VMEM((2, 2, comps, ny, nz), jnp.float32),
        ],
        compiler_params=PARAMS,
        cost_estimate=COST,
    )(u, *rest)


def sides_deep(nx, ny, nz, zleft_ref, zright_ref):
    source, target = iota((2 * nz, nz), 0) % nz, iota((2 * nz, nz), 1)
    where = jnp.where(source // 4 == target // 4, source % 4 + 10 * (target % 4), -1)
    weights = jnp.zeros((2 * nz, nz), jnp.float32)
    for value, m, t in ((1.0, 0, 2), (-8.0, 1, 2), (1.0, 1, 3), (-1.0, 2, 0), (8.0, 2, 1), (-1.0, 3, 1)):
        weights = jnp.where(where == m + 10 * t, value, weights)
    weights = weights.astype(jnp.bfloat16)
    return [
        jnp.dot(jnp.concatenate(split(ghost), axis=1), weights, preferred_element_type=jnp.float32)
        for ghost in unfold(zleft_ref[...], zright_ref[...], ny, nz)
    ]


def on_border(packed, x, rows=None):
    ny, nz = packed.shape
    lane = iota((ny, nz), 1)
    return jnp.where((lane >= nz - 2) | (lane < 2), pltpu.roll(packed, lane_shift(x, nz, False), 1), 0.0)


def gather(density, raws, level_ref, sums_ref, sum_ref):
    parts = []
    for k, raw in enumerate(raws):
        level = jnp.clip(raw, 0.0, 1.0)
        level_ref[k] = level
        parts.append(jnp.concatenate(split((density / math.log(2.0)) * level), axis=1))
    ny, nz = level_ref.shape[1:]
    sums = jnp.dot(jnp.concatenate(parts, axis=0), sum_ref[...], preferred_element_type=jnp.float32)
    for k in range(len(raws)):
        sums_ref[k] = sums[k * ny : (k + 1) * ny]


def blend(level_ref, sums_ref, k, store):
    ny, nz = level_ref.shape[1:]
    lane_group = iota((8, ny), 1) // 8
    eye = iota((8, ny), 1) % 8 == iota((8, ny), 0)
    totals = [jnp.zeros((8, ny), jnp.float32)] * 3
    for group in range(ny // 8):
        rows = pl.ds(8 * group, 8)
        level = level_ref[k, rows, :]
        passing = jnp.exp2(sums_ref[k, rows, pl.ds(0, nz)])
        first = (passing - jnp.exp2(sums_ref[k, rows, pl.ds(nz, nz)])) * level
        red = jnp.sum(first, axis=1, keepdims=True)
        square = jnp.sum(first * level, axis=1, keepdims=True)
        whole = sums_ref[k, rows, pl.ds(2 * nz, ny)]
        totals = [jnp.where(lane_group == group, part, total) for part, total in zip((red, square, whole), totals)]
    red, square, whole = [jnp.sum(jnp.where(eye, total, 0.0), axis=0, keepdims=True) for total in totals]
    through = jnp.exp2(whole)
    store(red, square, through)


def put(image_ref, x, slot=lambda view: view):
    per_view = image_ref.shape[2]
    view, row = (x // per_view, x % per_view) if isinstance(x, int) else (lax.div(x, per_view), lax.rem(x, per_view))

    def store(*channels):
        for k, values in enumerate(channels):
            image_ref[slot(view), k, pl.ds(row, 1), :] = values

    return store


def summing(sum_ref):
    nz = sum_ref.shape[0] // 2
    row = iota(sum_ref.shape, 0) % nz
    col = iota(sum_ref.shape, 1)
    sum_ref[...] = jnp.where((row < col) & (col < nz) | (row <= col - nz), -1.0, 0.0).astype(jnp.bfloat16)


def blend_kernel(
    density, raw_ref, pack_ref, kept_ref, scale_ref, zleft_ref, zright_ref, xleft_ref,
    image_ref, base_ref, deep_ref, sum_ref, level0_ref, level1_ref, sums0_ref, sums1_ref,
    fix_ref, first_ref, edge_level_ref, edge_sums_ref,
):
    nx, ny, nz = raw_ref.shape
    summing(sum_ref)
    ghosts = sides_deep(nx, ny, nz, zleft_ref, zright_ref)
    first_ref[...] = ghosts[0]
    fix = ghosts[2] * (0.5 * ghosts[2] + pack_ref[2]) + ghosts[0] * pack_ref[0] + ghosts[1] * pack_ref[1]
    per_block = 4 * SUB
    lane_block = iota((ny, nz), 1) // per_block
    scale = scale_ref[0]
    for block in range(1, nx // SUB):
        scale = jnp.where(lane_block == block, scale_ref[block], scale)
    fix_ref[...] = fix * scale
    image_ref[...] = jnp.zeros(image_ref.shape, jnp.float32)
    batch = level0_ref.shape[0]

    near = [xleft_ref[c, 1] for c in range(3)]
    far = [xleft_ref[c, 0] - 8.0 * cells for c, cells in enumerate(near)]

    def prepared(x, place):
        return raw_ref[x] + on_border(fix_ref[...], x), kept_ref[place, 2] + on_border(first_ref[...], x)

    raws = []
    for x, ghost in enumerate((far, near)):
        base, deep = prepared(x, x)
        raws.append(base + ghost_terms(ghost, kept_ref[x], deep) * scale_ref[0])
    for k in range(2):
        base_ref[k], deep_ref[k] = prepared(nx - 2 + k, 2 + k)

    def load(x, level_ref, sums_ref):
        raws = [raw_ref[x + k] + on_border(fix_ref[...], x + k) for k in range(batch)]
        gather(density, raws, level_ref, sums_ref, sum_ref)

    def mix(x, level_ref, sums_ref):
        for k in range(batch):
            blend(level_ref, sums_ref, k, put(image_ref, x + k))

    load(2, level0_ref, sums0_ref)
    two_rows(density, raws, edge_level_ref, edge_sums_ref, sum_ref, [put(image_ref, x) for x in range(2)])

    def batches(i, carry):
        x = 2 * batch * i + 2
        load(x + batch, level1_ref, sums1_ref)
        mix(x, level0_ref, sums0_ref)
        load(x + 2 * batch, level0_ref, sums0_ref)
        mix(x + batch, level1_ref, sums1_ref)
        return carry

    count = (nx - 4) // batch
    lax.fori_loop(0, (count - 1) // 2, batches, 0)
    if count % 2 == 0:
        load(nx - 2 - batch, level1_ref, sums1_ref)
        mix(nx - 2 - 2 * batch, level0_ref, sums0_ref)
        mix(nx - 2 - batch, level1_ref, sums1_ref)
    else:
        mix(nx - 2 - batch, level0_ref, sums0_ref)


def row_tables(batch, ny, nz, buffers):
    return (
        [pltpu.VMEM((batch, ny, nz), jnp.float32)] * buffers
        + [pltpu.VMEM((batch, ny, 2 * nz + ny), jnp.float32)] * buffers
    )


def blended(density, views, raw, *rest):
    nx, ny, nz = raw.shape
    return pl.pallas_call(
        functools.partial(blend_kernel, density),
        out_shape=(
            jax.ShapeDtypeStruct((views, 3, nx // views, ny), jnp.float32),
            jax.ShapeDtypeStruct((2, ny, nz), jnp.float32),
            jax.ShapeDtypeStruct((2, ny, nz), jnp.float32),
            jax.ShapeDtypeStruct((2 * nz, 2 * nz + ny), jnp.bfloat16),
        ),
        in_specs=[VMEM] * 7,
        out_specs=(VMEM,) * 4,
        scratch_shapes=row_tables(4, ny, nz, 2)
        + [pltpu.VMEM((ny, nz), jnp.float32)] * 2
        + [pltpu.VMEM((2, ny, nz), jnp.float32)] * 2,
        compiler_params=PARAMS,
        cost_estimate=COST,
    )(raw, *rest)


def two_rows(density, raws, level_ref, sums_ref, sum_ref, stores):
    ny, nz = raws[0].shape
    binary = density / math.log(2.0)
    parts = []
    for k, raw in enumerate(raws):
        level = jnp.clip(raw, 0.0, 1.0)
        level_ref[k] = level
        parts.append(jnp.concatenate(split(binary * level), axis=1))
    sums = jnp.dot(
        jnp.concatenate(parts, axis=0), sum_ref[:, pl.ds(nz, nz)], preferred_element_type=jnp.float32
    )
    lane_group = iota((8, ny), 1) // 8
    eye = iota((8, ny), 1) % 8 == iota((8, ny), 0)
    last = iota((8, nz), 1) == nz - 1
    for k, store in enumerate(stores):
        sums_ref[k] = sums[k * ny : (k + 1) * ny]
        totals = [jnp.zeros((8, ny), jnp.float32)] * 3
        for group in range(ny // 8):
            rows = pl.ds(8 * group, 8)
            level, behind = level_ref[k, rows, :], sums_ref[k, rows, :]
            left = jnp.exp2(behind)
            first = (jnp.exp2(behind + binary * level) - left) * level
            found = [jnp.sum(cells, axis=1, keepdims=True) for cells in (first, first * level, jnp.where(last, left, 0.0))]
            totals = [jnp.where(lane_group == group, part, total) for part, total in zip(found, totals)]
        store(*[jnp.sum(jnp.where(eye, total, 0.0), axis=0, keepdims=True) for total in totals])


def ghost_terms(ghost, kept, deep):
    return ghost[0] * (0.5 * ghost[0] + kept[0]) + ghost[1] * kept[1] + ghost[2] * deep


def slots(views):
    me = lax.axis_index("view")
    return lambda view: step_to(me, view, views)


def last_kernel(
    density, image_in_ref, base_ref, deep_ref, kept_ref, scale_ref, sum_ref, xright_ref,
    image_ref, level_ref, sums_ref,
):
    views, _, per_view, _ = image_ref.shape
    nx = views * per_view
    slot = slots(views)
    for view in range(views):
        image_ref[slot(view)] = image_in_ref[view]
    near = [-xright_ref[c, 0] for c in range(3)]
    far = [-8.0 * cells - xright_ref[c, 1] for c, cells in enumerate(near)]
    raws = [
        base_ref[k] + ghost_terms(ghost, kept_ref[2 + k], deep_ref[k]) * scale_ref[scale_ref.shape[0] - 1]
        for k, ghost in enumerate((near, far))
    ]
    two_rows(density, raws, level_ref, sums_ref, sum_ref, [put(image_ref, nx - 2 + k, slot) for k in range(2)])


def edged(density, image, base, *rest):
    return pl.pallas_call(
        functools.partial(last_kernel, density),
        out_shape=jax.ShapeDtypeStruct(image.shape, jnp.float32),
        in_specs=[VMEM] * (2 + len(rest)),
        out_specs=VMEM,
        scratch_shapes=[pltpu.VMEM(base.shape, jnp.float32)] * 2,
        compiler_params=PARAMS,
        cost_estimate=COST,
    )(image, base, *rest)


def turn(block, axis, by):
    count = lax.axis_size(axis)
    return lax.ppermute(block, axis, [(i, (i + by) % count) for i in range(count)])


def both_sides(block, axis):
    before = turn(block, axis, 1)
    return before, before if lax.axis_size(axis) == 2 else turn(block, axis, -1)


def exchange(count):
    if count == 4:
        return [(2, 3, 0, 1), (3, 2, 1, 0), (1, 0, 3, 2)]
    if count & (count - 1) == 0:
        return [tuple(i ^ step for i in range(count)) for step in range(count - 1, 0, -1)]
    return [tuple((i + step) % count for i in range(count)) for step in range(1, count)]


def looked_up(index, table):
    found = jnp.int32(table[0])
    for place, entry in enumerate(table[1:], 1):
        found = jnp.where(index == place, entry, found)
    return found


def step_to(me, other, count):
    steps = [(i,) + targets for i, targets in enumerate(zip(*exchange(count)))]
    return looked_up(me, [targets.index(other) for targets in steps])


def exchanged(blocks, axis):
    routes = exchange(lax.axis_size(axis))
    return [blocks[0]] + [lax.ppermute(blocks[k], axis, list(enumerate(route))) for k, route in enumerate(routes, 1)]


def composite_kernel(*refs):
    *image_refs, out_ref = refs
    count = len(image_refs)
    me = lax.axis_index("view")
    sources = [me] + [looked_up(me, [route.index(i) for i in range(count)]) for route in exchange(count)]
    red = square = 0.0
    through = 1.0
    for source, image_ref in zip(sources, image_refs):
        passing = 1.0
        for other, front_ref in zip(sources, image_refs):
            passing = passing * jnp.where(other < source, front_ref[2], 1.0)
        red = red + passing * image_ref[0]
        square = square + passing * image_ref[1]
        through = through * image_ref[2]
    for k, values in enumerate((red, 4.0 * (red - square), 1.0 - through - red, 1.0 - through)):
        out_ref[0, 0, k] = values


def composited(images):
    return pl.pallas_call(
        composite_kernel,
        out_shape=jax.ShapeDtypeStruct((1, 1, 4) + images[0].shape[1:], jnp.float32),
        in_specs=[VMEM] * len(images),
        out_specs=VMEM,
        compiler_params=PARAMS,
        cost_estimate=COST,
    )(*images)


def local(velocity, occupied, q_floor, q_span):
    comps, nx, ny, nz = velocity.shape
    views = lax.axis_size("view")
    density = 5.0 / (nz * views)
    xleft = turn(velocity[:, nx - 2 :], "gx", 1)
    u, parts, xhead, yface, ztail, zhead = faces(velocity)
    xright = turn(xhead, "gx", -1)
    zleft = turn(ztail, "view", 1)
    zright = turn(zhead, "view", -1)
    yleft, yright = both_sides(yface, "gy")
    raw, pack, kept, scale = shaded(u, parts, yleft, yright, occupied[:, :, 0], q_floor, q_span)
    image, base, deep, summer = blended(density, views, raw, pack, kept, scale, zleft, zright, xleft)
    blocks = edged(density, image, base, deep, kept, scale, summer, xright)
    return composited(exchanged(blocks, "view"))


def solution(mesh):
    placed = (P(None, "gx", "gy", "view"), P("gx", "gy", "view"), P(), P())
    return jax.shard_map(
        local,
        mesh=mesh,
        in_specs=placed,
        out_specs=P("gx", "gy", None, "view", None),
        check_vma=False,
    )
```

```python
import functools
import math

import jax
import jax.numpy as jnp
from jax import lax
from jax.experimental import pallas as pl
from jax.experimental.pallas import tpu as pltpu
from jax.sharding import PartitionSpec as P

SUB = 8
ROWS = 32
VMEM = pl.BlockSpec(memory_space=pltpu.VMEM)
HBM = pl.BlockSpec(memory_space=pltpu.HBM)
COST = pl.CostEstimate(flops=1 << 20, bytes_accessed=1 << 20, transcendentals=0)
PARAMS = pltpu.CompilerParams(vmem_limit_bytes=16 << 20)


def split(values):
    high = values.astype(jnp.bfloat16)
    low = (values - high.astype(jnp.float32)).astype(jnp.bfloat16)
    return high, low


def iota(shape, dim):
    return lax.broadcasted_iota(jnp.int32, shape, dim)


def faces_kernel(u_hbm, u_ref, parts_ref, xhead_ref, yface_ref, tail_ref, head_ref, packed_ref, sems):
    comps, nx, ny, nz = u_ref.shape
    quarters = sems.shape[1]
    rows = ny // quarters

    def fetch(c, k):
        span = pl.ds(k * rows if isinstance(k, int) else pl.multiple_of(k * rows, rows), rows)
        return pltpu.make_async_copy(u_hbm.at[c, :, span], u_ref.at[c, :, span], sems.at[c, k])

    for c in range(comps):
        for k in range(quarters):
            fetch(c, k).start()
    slot = iota((8, nz), 1) // 4
    for c in range(comps):

        def quarter(k, carry):
            fetch(c, k).wait()
            start = pl.multiple_of(k * rows, rows)
            packed = [jnp.zeros((8, nz), jnp.float32)] * (rows // 8)
            for x in range(nx):
                cells = u_ref[c, x, pl.ds(start, rows), :]
                high, low = split(cells)
                parts_ref[c, x, pl.ds(start, rows), pl.ds(0, nz)] = high
                parts_ref[c, x, pl.ds(start, rows), pl.ds(nz, nz)] = low
                mine = slot == x
                for n in range(rows // 8):
                    packed[n] = jnp.where(mine, pltpu.roll(cells[8 * n : 8 * n + 8], (4 * x + 2) % nz, 1), packed[n])
            for n in range(rows // 8):
                packed_ref[c, pl.ds(pl.multiple_of(start + 8 * n, 8), 8), :] = packed[n]
            return carry

        lax.fori_loop(0, quarters, quarter, 0)
    sub = iota((8, nz), 0)
    for c in range(comps):
        xhead_ref[c] = u_ref[c, pl.ds(0, 2)]
        for x in range(nx):
            lines = jnp.where(sub >= 6, u_ref[c, x, pl.ds(ny - 8, 8), :], u_ref[c, x, pl.ds(0, 8), :])
            yface_ref[c, x] = pltpu.roll(lines, 2, 0)[:4]
    tails, heads = fold([packed_ref[c] for c in range(comps)], ny, nz)
    tail_ref[...] = tails
    head_ref[...] = heads


def fold(packed, ny, nz):
    early = iota((ny, nz), 1) % 4 < 2
    early2 = early[: ny // 2]
    third, fourth = packed[2][: ny // 2], packed[2][ny // 2 :]
    tails = jnp.where(early, packed[0], pltpu.roll(packed[1], 2, 1))
    tails2 = jnp.where(early2, third, pltpu.roll(fourth, 2, 1))
    heads = jnp.where(early, pltpu.roll(packed[0], nz - 2, 1), packed[1])
    heads2 = jnp.where(early2, pltpu.roll(third, nz - 2, 1), fourth)
    return jnp.concatenate([tails, tails2], axis=0), jnp.concatenate([heads, heads2], axis=0)


def unfold(left, right, ny, nz):
    early = iota((ny, nz), 1) % 4 < 2
    early2 = early[: ny // 2]
    left2, right2 = left[ny:], right[ny:]
    left, right = left[:ny], right[:ny]
    first = jnp.where(early, left, pltpu.roll(right, 2, 1))
    second = jnp.where(early, pltpu.roll(left, nz - 2, 1), right)
    third = jnp.where(early2, left2, pltpu.roll(right2, 2, 1))
    fourth = jnp.where(early2, pltpu.roll(left2, nz - 2, 1), right2)
    return first, second, jnp.concatenate([third, fourth], axis=0)


def faces(u):
    comps, nx, ny, nz = u.shape
    message = jax.ShapeDtypeStruct((ny + ny // 2, nz), jnp.float32)
    return pl.pallas_call(
        faces_kernel,
        out_shape=(
            jax.ShapeDtypeStruct(u.shape, jnp.float32),
            jax.ShapeDtypeStruct((comps, nx, ny, 2 * nz), jnp.bfloat16),
            jax.ShapeDtypeStruct((comps, 2, ny, nz), jnp.float32),
            jax.ShapeDtypeStruct((comps, nx, 4, nz), jnp.float32),
            message,
            message,
        ),
        in_specs=[HBM],
        out_specs=(VMEM,) * 6,
        scratch_shapes=[pltpu.VMEM((comps, ny, nz), jnp.float32), pltpu.SemaphoreType.DMA((comps, 4))],
        compiler_params=pltpu.CompilerParams(vmem_limit_bytes=37 << 20),
        cost_estimate=COST,
    )(u)


def stencil(far):
    one = jnp.where(far == 1, 8.0, 0.0) - jnp.where(far == -1, 8.0, 0.0)
    return (one - jnp.where(far == 2, 1.0, 0.0) + jnp.where(far == -2, 1.0, 0.0)).astype(jnp.bfloat16)


def shading(occupied_ref, floor, span, scale_ref, offset_ref):
    blocks, ny, nz = scale_ref.shape
    groups = ny // SUB
    mine = iota((ny, groups), 0) // SUB == iota((ny, groups), 1)
    shrink = 1.0 / span
    for block in range(blocks):
        row = occupied_ref[block : block + 1, :].astype(jnp.float32)
        column = jnp.sum(jnp.where(mine, row, 0.0), axis=1, keepdims=True)
        scale_ref[block] = jnp.broadcast_to(column * (shrink * (-1.0 / 144.0)), (ny, nz))
        offset_ref[block] = jnp.broadcast_to(column * (shrink * -floor), (ny, nz))


def lane_shift(x, nz, back):
    if isinstance(x, int):
        return (4 * x + 2 if back else 2 * nz - 2 - 4 * x) % nz
    return lax.rem(4 * x + 2 if back else 2 * nz - 2 - 4 * x, nz)


def slopes(parts_ref, x, tables, slope_ref):
    yleft_ref, yright_ref, dz_ref, dy_ref = tables
    comps, ny, nz = slope_ref.shape[2:]
    sub = iota((8, nz), 0)

    def top(left):
        lines = jnp.concatenate([left, left], axis=0)
        return jnp.where(sub < 2, lines - jnp.where(sub == 0, 8.0 * pltpu.roll(lines, 7, 0), 0.0), 0.0)

    def low(right):
        lines = jnp.concatenate([right, right], axis=0)
        return jnp.where(sub >= 6, jnp.where(sub == 7, 8.0 * pltpu.roll(lines, 1, 0), 0.0) - lines, 0.0)

    parts = [[parts_ref[c, x + k] for k in range(2)] for c in range(comps)]
    depth = jnp.dot(
        jnp.concatenate([part for pair in parts for part in pair], axis=0),
        dz_ref[...],
        preferred_element_type=jnp.float32,
    )
    for c in range(comps):
        both = jnp.concatenate(
            [jnp.concatenate([part[:, half : half + nz] for part in parts[c]], axis=1) for half in (0, nz)], axis=0
        )
        down = jnp.dot(dy_ref[...], both, preferred_element_type=jnp.float32)
        for k in range(2):
            slope_ref[1, k, c] = depth[(2 * c + k) * ny : (2 * c + k + 1) * ny]
            mine = down[:, k * nz : (k + 1) * nz]
            slope_ref[0, k, c, pl.ds(0, 8), :] = mine[:8] + top(yleft_ref[c, x + k])
            slope_ref[0, k, c, pl.ds(8, ny - 16), :] = mine[8 : ny - 8]
            slope_ref[0, k, c, pl.ds(ny - 8, 8), :] = mine[ny - 8 :] + low(yright_ref[c, x + k])


def shade(u_ref, x, slope_ref, scale_ref, offset_ref, raw_ref, pack_ref, kept_ref=None, place=None):
    comps, nx, ny, nz = u_ref.shape
    block = x // SUB

    def difference(high, low):
        if high is None:
            return 0.0 if low is None else -low
        return high if low is None else high - low

    for y in range(0, ny, ROWS):
        rows = pl.ds(y, ROWS)
        slots = iota((ROWS, nz), 1) // 4
        across = []
        for c in range(comps):
            near = [
                u_ref[c, x + d, rows, :] if not isinstance(x, int) or 0 <= x + d < nx else None for d in range(-2, 4)
            ]
            across.append(
                [8.0 * difference(near[k + 3], near[k + 1]) - difference(near[k + 4], near[k]) for k in range(2)]
            )
        packs = [pack_ref[k, rows, :] for k in range(3)]
        for k in range(2):
            side = [across[c][k] for c in range(comps)]
            down = [slope_ref[0, k, c, rows, :] for c in range(comps)]
            depth = [slope_ref[1, k, c, rows, :] for c in range(comps)]
            total = 0.5 * (side[0] * side[0] + down[1] * down[1] + depth[2] * depth[2])
            total = total + side[1] * down[0] + side[2] * depth[0] + down[2] * depth[1]
            raw_ref[x + k, rows, :] = total * scale_ref[block, rows, :] + offset_ref[block, rows, :]
            back = lane_shift(x + k, nz, True)
            packs = [
                jnp.where(slots == x + k, pltpu.roll(values, back, 1), pack)
                for values, pack in zip((side[2], down[2], depth[2]), packs)
            ]
            if kept_ref is not None:
                for n, values in enumerate((side[0], down[0], depth[0])):
                    kept_ref[place + k, n, rows, :] = values
        for k in range(3):
            pack_ref[k, rows, :] = packs[k]


def shade_kernel(
    u_ref, parts_ref, yleft_ref, yright_ref, occupied_ref, floor_ref, span_ref,
    raw_ref, pack_ref, kept_ref, scale_ref, offset_ref, dz_ref, dy_ref, slope0_ref, slope1_ref,
):
    comps, nx, ny, nz = u_ref.shape
    dz_ref[...] = stencil(iota((2 * nz, nz), 0) % nz - iota((2 * nz, nz), 1))
    dy_ref[...] = stencil(iota((ny, 2 * ny), 1) % ny - iota((ny, 2 * ny), 0))
    shading(occupied_ref, floor_ref[...].reshape(1, 1), span_ref[...].reshape(1, 1), scale_ref, offset_ref)
    pack_ref[...] = jnp.zeros(pack_ref.shape, jnp.float32)
    tables = (yleft_ref, yright_ref, dz_ref, dy_ref)
    outs = (scale_ref, offset_ref, raw_ref, pack_ref)
    slopes(parts_ref, 0, tables, slope0_ref)
    slopes(parts_ref, 2, tables, slope1_ref)
    shade(u_ref, 0, slope0_ref, *outs, kept_ref, 0)

    def pairs(i, carry):
        x = 4 * i + 2
        slopes(parts_ref, x + 2, tables, slope0_ref)
        shade(u_ref, x, slope1_ref, *outs)
        slopes(parts_ref, x + 4, tables, slope1_ref)
        shade(u_ref, x + 2, slope0_ref, *outs)
        return carry

    lax.fori_loop(0, (nx - 4) // 4, pairs, 0)
    shade(u_ref, nx - 2, slope1_ref, *outs, kept_ref, 2)


def shaded(u, *rest):
    comps, nx, ny, nz = u.shape
    return pl.pallas_call(
        shade_kernel,
        out_shape=(
            jax.ShapeDtypeStruct((nx, ny, nz), jnp.float32),
            jax.ShapeDtypeStruct((comps, ny, nz), jnp.float32),
            jax.ShapeDtypeStruct((4, comps, ny, nz), jnp.float32),
            jax.ShapeDtypeStruct((nx // SUB, ny, nz), jnp.float32),
        ),
        in_specs=[VMEM] * 7,
        out_specs=(VMEM,) * 4,
        scratch_shapes=[
            pltpu.VMEM((nx // SUB, ny, nz), jnp.float32),
            pltpu.VMEM((2 * nz, nz), jnp.bfloat16),
            pltpu.VMEM((ny, 2 * ny), jnp.bfloat16),
            pltpu.VMEM((2, 2, comps, ny, nz), jnp.float32),
            pltpu.VMEM((2, 2, comps, ny, nz), jnp.float32),
        ],
        compiler_params=PARAMS,
        cost_estimate=COST,
    )(u, *rest)


def sides_deep(nx, ny, nz, zleft_ref, zright_ref):
    source, target = iota((2 * nz, nz), 0) % nz, iota((2 * nz, nz), 1)
    where = jnp.where(source // 4 == target // 4, source % 4 + 10 * (target % 4), -1)
    weights = jnp.zeros((2 * nz, nz), jnp.float32)
    for value, m, t in ((1.0, 0, 2), (-8.0, 1, 2), (1.0, 1, 3), (-1.0, 2, 0), (8.0, 2, 1), (-1.0, 3, 1)):
        weights = jnp.where(where == m + 10 * t, value, weights)
    weights = weights.astype(jnp.bfloat16)
    return [
        jnp.dot(jnp.concatenate(split(ghost), axis=1), weights, preferred_element_type=jnp.float32)
        for ghost in unfold(zleft_ref[...], zright_ref[...], ny, nz)
    ]


def on_border(packed, x, rows=None):
    ny, nz = packed.shape
    lane = iota((ny, nz), 1)
    return jnp.where((lane >= nz - 2) | (lane < 2), pltpu.roll(packed, lane_shift(x, nz, False), 1), 0.0)


def gather(density, raws, level_ref, sums_ref, sum_ref):
    parts = []
    for k, raw in enumerate(raws):
        level = jnp.clip(raw, 0.0, 1.0)
        level_ref[k] = level
        parts.append(jnp.concatenate(split((density / math.log(2.0)) * level), axis=1))
    ny, nz = level_ref.shape[1:]
    sums = jnp.dot(jnp.concatenate(parts, axis=0), sum_ref[...], preferred_element_type=jnp.float32)
    for k in range(len(raws)):
        sums_ref[k] = sums[k * ny : (k + 1) * ny]


def blend(level_ref, sums_ref, k, store):
    ny, nz = level_ref.shape[1:]
    lane_group = iota((8, ny), 1) // 8
    eye = iota((8, ny), 1) % 8 == iota((8, ny), 0)
    totals = [jnp.zeros((8, ny), jnp.float32)] * 3
    for group in range(ny // 8):
        rows = pl.ds(8 * group, 8)
        level = level_ref[k, rows, :]
        passing = jnp.exp2(sums_ref[k, rows, pl.ds(0, nz)])
        first = (passing - jnp.exp2(sums_ref[k, rows, pl.ds(nz, nz)])) * level
        red = jnp.sum(first, axis=1, keepdims=True)
        square = jnp.sum(first * level, axis=1, keepdims=True)
        whole = sums_ref[k, rows, pl.ds(2 * nz, ny)]
        totals = [jnp.where(lane_group == group, part, total) for part, total in zip((red, square, whole), totals)]
    red, square, whole = [jnp.sum(jnp.where(eye, total, 0.0), axis=0, keepdims=True) for total in totals]
    through = jnp.exp2(whole)
    store(red, square, through)


def put(image_ref, x, slot=lambda view: view):
    per_view = image_ref.shape[2]
    view, row = (x // per_view, x % per_view) if isinstance(x, int) else (lax.div(x, per_view), lax.rem(x, per_view))

    def store(*channels):
        for k, values in enumerate(channels):
            image_ref[slot(view), k, pl.ds(row, 1), :] = values

    return store


def summing(sum_ref):
    nz = sum_ref.shape[0] // 2
    row = iota(sum_ref.shape, 0) % nz
    col = iota(sum_ref.shape, 1)
    sum_ref[...] = jnp.where((row < col) & (col < nz) | (row <= col - nz), -1.0, 0.0).astype(jnp.bfloat16)


def blend_kernel(
    density, raw_ref, pack_ref, kept_ref, scale_ref, zleft_ref, zright_ref, xleft_ref,
    image_ref, base_ref, deep_ref, sum_ref, level0_ref, level1_ref, sums0_ref, sums1_ref,
    fix_ref, first_ref, edge_level_ref, edge_sums_ref,
):
    nx, ny, nz = raw_ref.shape
    summing(sum_ref)
    ghosts = sides_deep(nx, ny, nz, zleft_ref, zright_ref)
    first_ref[...] = ghosts[0]
    fix = ghosts[2] * (0.5 * ghosts[2] + pack_ref[2]) + ghosts[0] * pack_ref[0] + ghosts[1] * pack_ref[1]
    per_block = 4 * SUB
    lane_block = iota((ny, nz), 1) // per_block
    scale = scale_ref[0]
    for block in range(1, nx // SUB):
        scale = jnp.where(lane_block == block, scale_ref[block], scale)
    fix_ref[...] = fix * scale
    image_ref[...] = jnp.zeros(image_ref.shape, jnp.float32)
    batch = level0_ref.shape[0]

    near = [xleft_ref[c, 1] for c in range(3)]
    far = [xleft_ref[c, 0] - 8.0 * cells for c, cells in enumerate(near)]

    def prepared(x, place):
        return raw_ref[x] + on_border(fix_ref[...], x), kept_ref[place, 2] + on_border(first_ref[...], x)

    raws = []
    for x, ghost in enumerate((far, near)):
        base, deep = prepared(x, x)
        raws.append(base + ghost_terms(ghost, kept_ref[x], deep) * scale_ref[0])
    for k in range(2):
        base_ref[k], deep_ref[k] = prepared(nx - 2 + k, 2 + k)

    def load(x, level_ref, sums_ref):
        raws = [raw_ref[x + k] + on_border(fix_ref[...], x + k) for k in range(batch)]
        gather(density, raws, level_ref, sums_ref, sum_ref)

    def mix(x, level_ref, sums_ref):
        for k in range(batch):
            blend(level_ref, sums_ref, k, put(image_ref, x + k))

    load(2, level0_ref, sums0_ref)
    two_rows(density, raws, edge_level_ref, edge_sums_ref, sum_ref, [put(image_ref, x) for x in range(2)])

    def batches(i, carry):
        x = 2 * batch * i + 2
        load(x + batch, level1_ref, sums1_ref)
        mix(x, level0_ref, sums0_ref)
        load(x + 2 * batch, level0_ref, sums0_ref)
        mix(x + batch, level1_ref, sums1_ref)
        return carry

    count = (nx - 4) // batch
    lax.fori_loop(0, (count - 1) // 2, batches, 0)
    if count % 2 == 0:
        load(nx - 2 - batch, level1_ref, sums1_ref)
        mix(nx - 2 - 2 * batch, level0_ref, sums0_ref)
        mix(nx - 2 - batch, level1_ref, sums1_ref)
    else:
        mix(nx - 2 - batch, level0_ref, sums0_ref)


def row_tables(batch, ny, nz, buffers):
    return (
        [pltpu.VMEM((batch, ny, nz), jnp.float32)] * buffers
        + [pltpu.VMEM((batch, ny, 2 * nz + ny), jnp.float32)] * buffers
    )


def blended(density, views, raw, *rest):
    nx, ny, nz = raw.shape
    return pl.pallas_call(
        functools.partial(blend_kernel, density),
        out_shape=(
            jax.ShapeDtypeStruct((views, 3, nx // views, ny), jnp.float32),
            jax.ShapeDtypeStruct((2, ny, nz), jnp.float32),
            jax.ShapeDtypeStruct((2, ny, nz), jnp.float32),
            jax.ShapeDtypeStruct((2 * nz, 2 * nz + ny), jnp.bfloat16),
        ),
        in_specs=[VMEM] * 7,
        out_specs=(VMEM,) * 4,
        scratch_shapes=row_tables(4, ny, nz, 2)
        + [pltpu.VMEM((ny, nz), jnp.float32)] * 2
        + [pltpu.VMEM((2, ny, nz), jnp.float32)] * 2,
        compiler_params=PARAMS,
        cost_estimate=COST,
    )(raw, *rest)


def two_rows(density, raws, level_ref, sums_ref, sum_ref, stores):
    ny, nz = raws[0].shape
    binary = density / math.log(2.0)
    parts = []
    for k, raw in enumerate(raws):
        level = jnp.clip(raw, 0.0, 1.0)
        level_ref[k] = level
        parts.append(jnp.concatenate(split(binary * level), axis=1))
    lane_group = iota((8, ny), 1) // 8
    eye = iota((8, ny), 1) % 8 == iota((8, ny), 0)
    last = iota((8, nz), 1) == nz - 1
    for k, store in enumerate(stores):
        sums_ref[k] = jnp.dot(parts[k], sum_ref[:, pl.ds(nz, nz)], preferred_element_type=jnp.float32)
        totals = [jnp.zeros((8, ny), jnp.float32)] * 3
        for group in range(ny // 8):
            rows = pl.ds(8 * group, 8)
            level, behind = level_ref[k, rows, :], sums_ref[k, rows, :]
            left = jnp.exp2(behind)
            first = (jnp.exp2(behind + binary * level) - left) * level
            found = [jnp.sum(cells, axis=1, keepdims=True) for cells in (first, first * level, jnp.where(last, left, 0.0))]
            totals = [jnp.where(lane_group == group, part, total) for part, total in zip(found, totals)]
        store(*[jnp.sum(jnp.where(eye, total, 0.0), axis=0, keepdims=True) for total in totals])


def ghost_terms(ghost, kept, deep):
    return ghost[0] * (0.5 * ghost[0] + kept[0]) + ghost[1] * kept[1] + ghost[2] * deep


def slots(views):
    me = lax.axis_index("view")
    return lambda view: step_to(me, view, views)


def last_kernel(
    density, image_in_ref, base_ref, deep_ref, kept_ref, scale_ref, sum_ref, xright_ref,
    image_ref, level_ref, sums_ref,
):
    views, _, per_view, _ = image_ref.shape
    nx = views * per_view
    slot = slots(views)
    for view in range(views):
        image_ref[slot(view)] = image_in_ref[view]
    near = [-xright_ref[c, 0] for c in range(3)]
    far = [-8.0 * cells - xright_ref[c, 1] for c, cells in enumerate(near)]
    raws = [
        base_ref[k] + ghost_terms(ghost, kept_ref[2 + k], deep_ref[k]) * scale_ref[scale_ref.shape[0] - 1]
        for k, ghost in enumerate((near, far))
    ]
    two_rows(density, raws, level_ref, sums_ref, sum_ref, [put(image_ref, nx - 2 + k, slot) for k in range(2)])


def edged(density, image, base, *rest):
    return pl.pallas_call(
        functools.partial(last_kernel, density),
        out_shape=jax.ShapeDtypeStruct(image.shape, jnp.float32),
        in_specs=[VMEM] * (2 + len(rest)),
        out_specs=VMEM,
        scratch_shapes=[pltpu.VMEM(base.shape, jnp.float32)] * 2,
        compiler_params=PARAMS,
        cost_estimate=COST,
    )(image, base, *rest)


def turn(block, axis, by):
    count = lax.axis_size(axis)
    return lax.ppermute(block, axis, [(i, (i + by) % count) for i in range(count)])


def both_sides(block, axis):
    before = turn(block, axis, 1)
    return before, before if lax.axis_size(axis) == 2 else turn(block, axis, -1)


def exchange(count):
    if count == 4:
        return [(2, 3, 1, 0), (3, 2, 0, 1), (1, 0, 3, 2)]
    if count & (count - 1) == 0:
        return [tuple(i ^ step for i in range(count)) for step in range(count - 1, 0, -1)]
    return [tuple((i + step) % count for i in range(count)) for step in range(1, count)]


def looked_up(index, table):
    found = jnp.int32(table[0])
    for place, entry in enumerate(table[1:], 1):
        found = jnp.where(index == place, entry, found)
    return found


def step_to(me, other, count):
    steps = [(i,) + targets for i, targets in enumerate(zip(*exchange(count)))]
    return looked_up(me, [targets.index(other) for targets in steps])


def exchanged(blocks, axis):
    routes = exchange(lax.axis_size(axis))
    return [blocks[0]] + [lax.ppermute(blocks[k], axis, list(enumerate(route))) for k, route in enumerate(routes, 1)]


def composite_kernel(*refs):
    *image_refs, out_ref = refs
    count = len(image_refs)
    me = lax.axis_index("view")
    sources = [me] + [looked_up(me, [route.index(i) for i in range(count)]) for route in exchange(count)]
    red = square = 0.0
    through = 1.0
    for source, image_ref in zip(sources, image_refs):
        passing = 1.0
        for other, front_ref in zip(sources, image_refs):
            passing = passing * jnp.where(other < source, front_ref[2], 1.0)
        red = red + passing * image_ref[0]
        square = square + passing * image_ref[1]
        through = through * image_ref[2]
    for k, values in enumerate((red, 4.0 * (red - square), 1.0 - through - red, 1.0 - through)):
        out_ref[0, 0, k] = values


def composited(images):
    return pl.pallas_call(
        composite_kernel,
        out_shape=jax.ShapeDtypeStruct((1, 1, 4) + images[0].shape[1:], jnp.float32),
        in_specs=[VMEM] * len(images),
        out_specs=VMEM,
        compiler_params=PARAMS,
        cost_estimate=COST,
    )(*images)


def local(velocity, occupied, q_floor, q_span):
    comps, nx, ny, nz = velocity.shape
    views = lax.axis_size("view")
    density = 5.0 / (nz * views)
    xleft = turn(velocity[:, nx - 2 :], "gx", 1)
    u, parts, xhead, yface, ztail, zhead = faces(velocity)
    xright = turn(xhead, "gx", -1)
    zleft = turn(ztail, "view", 1)
    zright = turn(zhead, "view", -1)
    yleft, yright = both_sides(yface, "gy")
    raw, pack, kept, scale = shaded(u, parts, yleft, yright, occupied[:, :, 0], q_floor, q_span)
    image, base, deep, summer = blended(density, views, raw, pack, kept, scale, zleft, zright, xleft)
    blocks = edged(density, image, base, deep, kept, scale, summer, xright)
    return composited(exchanged(blocks, "view"))


def solution(mesh):
    placed = (P(None, "gx", "gy", "view"), P("gx", "gy", "view"), P(), P())
    return jax.shard_map(
        local,
        mesh=mesh,
        in_specs=placed,
        out_specs=P("gx", "gy", None, "view", None),
        check_vma=False,
    )
```

```python
import functools
import math

import jax
import jax.numpy as jnp
from jax import lax
from jax.experimental import pallas as pl
from jax.experimental.pallas import tpu as pltpu
from jax.sharding import PartitionSpec as P

SUB = 8
ROWS = 32
VMEM = pl.BlockSpec(memory_space=pltpu.VMEM)
HBM = pl.BlockSpec(memory_space=pltpu.HBM)
COST = pl.CostEstimate(flops=1 << 20, bytes_accessed=1 << 20, transcendentals=0)
PARAMS = pltpu.CompilerParams(vmem_limit_bytes=16 << 20)


def split(values):
    high = values.astype(jnp.bfloat16)
    low = (values - high.astype(jnp.float32)).astype(jnp.bfloat16)
    return high, low


def iota(shape, dim):
    return lax.broadcasted_iota(jnp.int32, shape, dim)


def tail_kernel(u_hbm, out_ref, sems):
    comps, nx, ny, _ = u_hbm.shape
    half = ny // 2
    copies = [
        pltpu.make_async_copy(
            u_hbm.at[c, nx - 2 + layer, pl.ds(part * half, half)],
            out_ref.at[c, layer, pl.ds(part * half, half)],
            sems.at[c, layer, part],
        )
        for c in range(comps)
        for layer in range(2)
        for part in range(2)
    ]
    for copy in copies:
        copy.start()
    for copy in copies:
        copy.wait()


def tail(u):
    comps, _, ny, nz = u.shape
    return pl.pallas_call(
        tail_kernel,
        out_shape=jax.ShapeDtypeStruct((comps, 2, ny, nz), jnp.float32),
        in_specs=[HBM],
        out_specs=VMEM,
        scratch_shapes=[pltpu.SemaphoreType.DMA((comps, 2, 2))],
        compiler_params=pltpu.CompilerParams(vmem_limit_bytes=50 << 20),
        cost_estimate=COST,
    )(u)


def faces_kernel(u_hbm, u_ref, parts_ref, xhead_ref, yface_ref, tail_ref, head_ref, packed_ref, sems):
    comps, nx, ny, nz = u_ref.shape
    quarters = sems.shape[1]
    rows = ny // quarters

    def fetch(c, k):
        span = pl.ds(k * rows if isinstance(k, int) else pl.multiple_of(k * rows, rows), rows)
        return pltpu.make_async_copy(u_hbm.at[c, :, span], u_ref.at[c, :, span], sems.at[c, k])

    for c in range(comps):
        for k in range(quarters):
            fetch(c, k).start()
    slot = iota((8, nz), 1) // 4
    for c in range(comps):

        def quarter(k, carry):
            fetch(c, k).wait()
            start = pl.multiple_of(k * rows, rows)
            packed = [jnp.zeros((8, nz), jnp.float32)] * (rows // 8)
            for x in range(nx):
                cells = u_ref[c, x, pl.ds(start, rows), :]
                high, low = split(cells)
                parts_ref[c, x, pl.ds(start, rows), pl.ds(0, nz)] = high
                parts_ref[c, x, pl.ds(start, rows), pl.ds(nz, nz)] = low
                mine = slot == x
                for n in range(rows // 8):
                    packed[n] = jnp.where(mine, pltpu.roll(cells[8 * n : 8 * n + 8], (4 * x + 2) % nz, 1), packed[n])
            for n in range(rows // 8):
                packed_ref[c, pl.ds(pl.multiple_of(start + 8 * n, 8), 8), :] = packed[n]
            return carry

        lax.fori_loop(0, quarters, quarter, 0)
    sub = iota((8, nz), 0)
    for c in range(comps):
        xhead_ref[c] = u_ref[c, pl.ds(0, 2)]
        for x in range(nx):
            lines = jnp.where(sub >= 6, u_ref[c, x, pl.ds(ny - 8, 8), :], u_ref[c, x, pl.ds(0, 8), :])
            yface_ref[c, x] = pltpu.roll(lines, 2, 0)[:4]
    tails, heads = fold([packed_ref[c] for c in range(comps)], ny, nz)
    tail_ref[...] = tails
    head_ref[...] = heads


def fold(packed, ny, nz):
    early = iota((ny, nz), 1) % 4 < 2
    early2 = early[: ny // 2]
    third, fourth = packed[2][: ny // 2], packed[2][ny // 2 :]
    tails = jnp.where(early, packed[0], pltpu.roll(packed[1], 2, 1))
    tails2 = jnp.where(early2, third, pltpu.roll(fourth, 2, 1))
    heads = jnp.where(early, pltpu.roll(packed[0], nz - 2, 1), packed[1])
    heads2 = jnp.where(early2, pltpu.roll(third, nz - 2, 1), fourth)
    return jnp.concatenate([tails, tails2], axis=0), jnp.concatenate([heads, heads2], axis=0)


def unfold(left, right, ny, nz):
    early = iota((ny, nz), 1) % 4 < 2
    early2 = early[: ny // 2]
    left2, right2 = left[ny:], right[ny:]
    left, right = left[:ny], right[:ny]
    first = jnp.where(early, left, pltpu.roll(right, 2, 1))
    second = jnp.where(early, pltpu.roll(left, nz - 2, 1), right)
    third = jnp.where(early2, left2, pltpu.roll(right2, 2, 1))
    fourth = jnp.where(early2, pltpu.roll(left2, nz - 2, 1), right2)
    return first, second, jnp.concatenate([third, fourth], axis=0)


def faces(u):
    comps, nx, ny, nz = u.shape
    message = jax.ShapeDtypeStruct((ny + ny // 2, nz), jnp.float32)
    return pl.pallas_call(
        faces_kernel,
        out_shape=(
            jax.ShapeDtypeStruct(u.shape, jnp.float32),
            jax.ShapeDtypeStruct((comps, nx, ny, 2 * nz), jnp.bfloat16),
            jax.ShapeDtypeStruct((comps, 2, ny, nz), jnp.float32),
            jax.ShapeDtypeStruct((comps, nx, 4, nz), jnp.float32),
            message,
            message,
        ),
        in_specs=[HBM],
        out_specs=(VMEM,) * 6,
        scratch_shapes=[pltpu.VMEM((comps, ny, nz), jnp.float32), pltpu.SemaphoreType.DMA((comps, 4))],
        compiler_params=pltpu.CompilerParams(vmem_limit_bytes=37 << 20),
        cost_estimate=COST,
    )(u)


def stencil(far):
    one = jnp.where(far == 1, 8.0, 0.0) - jnp.where(far == -1, 8.0, 0.0)
    return (one - jnp.where(far == 2, 1.0, 0.0) + jnp.where(far == -2, 1.0, 0.0)).astype(jnp.bfloat16)


def shading(occupied_ref, floor, span, scale_ref, offset_ref):
    blocks, ny, nz = scale_ref.shape
    groups = ny // SUB
    mine = iota((ny, groups), 0) // SUB == iota((ny, groups), 1)
    shrink = 1.0 / span
    for block in range(blocks):
        row = occupied_ref[block : block + 1, :].astype(jnp.float32)
        column = jnp.sum(jnp.where(mine, row, 0.0), axis=1, keepdims=True)
        scale_ref[block] = jnp.broadcast_to(column * (shrink * (-1.0 / 144.0)), (ny, nz))
        offset_ref[block] = jnp.broadcast_to(column * (shrink * -floor), (ny, nz))


def lane_shift(x, nz, back):
    if isinstance(x, int):
        return (4 * x + 2 if back else 2 * nz - 2 - 4 * x) % nz
    return lax.rem(4 * x + 2 if back else 2 * nz - 2 - 4 * x, nz)


def slopes(parts_ref, x, tables, slope_ref):
    yleft_ref, yright_ref, dz_ref, dy_ref = tables
    comps, ny, nz = slope_ref.shape[2:]
    sub = iota((8, nz), 0)

    def top(left):
        lines = jnp.concatenate([left, left], axis=0)
        return jnp.where(sub < 2, lines - jnp.where(sub == 0, 8.0 * pltpu.roll(lines, 7, 0), 0.0), 0.0)

    def low(right):
        lines = jnp.concatenate([right, right], axis=0)
        return jnp.where(sub >= 6, jnp.where(sub == 7, 8.0 * pltpu.roll(lines, 1, 0), 0.0) - lines, 0.0)

    parts = [[parts_ref[c, x + k] for k in range(2)] for c in range(comps)]
    depth = jnp.dot(
        jnp.concatenate([part for pair in parts for part in pair], axis=0),
        dz_ref[...],
        preferred_element_type=jnp.float32,
    )
    for c in range(comps):
        both = jnp.concatenate(
            [jnp.concatenate([part[:, half : half + nz] for part in parts[c]], axis=1) for half in (0, nz)], axis=0
        )
        down = jnp.dot(dy_ref[...], both, preferred_element_type=jnp.float32)
        for k in range(2):
            slope_ref[1, k, c] = depth[(2 * c + k) * ny : (2 * c + k + 1) * ny]
            mine = down[:, k * nz : (k + 1) * nz]
            slope_ref[0, k, c, pl.ds(0, 8), :] = mine[:8] + top(yleft_ref[c, x + k])
            slope_ref[0, k, c, pl.ds(8, ny - 16), :] = mine[8 : ny - 8]
            slope_ref[0, k, c, pl.ds(ny - 8, 8), :] = mine[ny - 8 :] + low(yright_ref[c, x + k])


def shade(u_ref, x, slope_ref, scale_ref, offset_ref, raw_ref, pack_ref, kept_ref=None, place=None):
    comps, nx, ny, nz = u_ref.shape
    block = x // SUB

    def difference(high, low):
        if high is None:
            return 0.0 if low is None else -low
        return high if low is None else high - low

    for y in range(0, ny, ROWS):
        rows = pl.ds(y, ROWS)
        slots = iota((ROWS, nz), 1) // 4
        across = []
        for c in range(comps):
            near = [
                u_ref[c, x + d, rows, :] if not isinstance(x, int) or 0 <= x + d < nx else None for d in range(-2, 4)
            ]
            across.append(
                [8.0 * difference(near[k + 3], near[k + 1]) - difference(near[k + 4], near[k]) for k in range(2)]
            )
        packs = [pack_ref[k, rows, :] for k in range(3)]
        for k in range(2):
            side = [across[c][k] for c in range(comps)]
            down = [slope_ref[0, k, c, rows, :] for c in range(comps)]
            depth = [slope_ref[1, k, c, rows, :] for c in range(comps)]
            total = 0.5 * (side[0] * side[0] + down[1] * down[1] + depth[2] * depth[2])
            total = total + side[1] * down[0] + side[2] * depth[0] + down[2] * depth[1]
            raw_ref[x + k, rows, :] = total * scale_ref[block, rows, :] + offset_ref[block, rows, :]
            back = lane_shift(x + k, nz, True)
            packs = [
                jnp.where(slots == x + k, pltpu.roll(values, back, 1), pack)
                for values, pack in zip((side[2], down[2], depth[2]), packs)
            ]
            if kept_ref is not None:
                for n, values in enumerate((side[0], down[0], depth[0])):
                    kept_ref[place + k, n, rows, :] = values
        for k in range(3):
            pack_ref[k, rows, :] = packs[k]


def shade_kernel(
    u_ref, parts_ref, yleft_ref, yright_ref, occupied_ref, floor_ref, span_ref,
    raw_ref, pack_ref, kept_ref, scale_ref, offset_ref, dz_ref, dy_ref, slope0_ref, slope1_ref,
):
    comps, nx, ny, nz = u_ref.shape
    dz_ref[...] = stencil(iota((2 * nz, nz), 0) % nz - iota((2 * nz, nz), 1))
    dy_ref[...] = stencil(iota((ny, 2 * ny), 1) % ny - iota((ny, 2 * ny), 0))
    shading(occupied_ref, floor_ref[...].reshape(1, 1), span_ref[...].reshape(1, 1), scale_ref, offset_ref)
    pack_ref[...] = jnp.zeros(pack_ref.shape, jnp.float32)
    tables = (yleft_ref, yright_ref, dz_ref, dy_ref)
    outs = (scale_ref, offset_ref, raw_ref, pack_ref)
    slopes(parts_ref, 0, tables, slope0_ref)
    slopes(parts_ref, 2, tables, slope1_ref)
    shade(u_ref, 0, slope0_ref, *outs, kept_ref, 0)

    def pairs(i, carry):
        x = 4 * i + 2
        slopes(parts_ref, x + 2, tables, slope0_ref)
        shade(u_ref, x, slope1_ref, *outs)
        slopes(parts_ref, x + 4, tables, slope1_ref)
        shade(u_ref, x + 2, slope0_ref, *outs)
        return carry

    lax.fori_loop(0, (nx - 4) // 4, pairs, 0)
    shade(u_ref, nx - 2, slope1_ref, *outs, kept_ref, 2)


def shaded(u, *rest):
    comps, nx, ny, nz = u.shape
    return pl.pallas_call(
        shade_kernel,
        out_shape=(
            jax.ShapeDtypeStruct((nx, ny, nz), jnp.float32),
            jax.ShapeDtypeStruct((comps, ny, nz), jnp.float32),
            jax.ShapeDtypeStruct((4, comps, ny, nz), jnp.float32),
            jax.ShapeDtypeStruct((nx // SUB, ny, nz), jnp.float32),
        ),
        in_specs=[VMEM] * 7,
        out_specs=(VMEM,) * 4,
        scratch_shapes=[
            pltpu.VMEM((nx // SUB, ny, nz), jnp.float32),
            pltpu.VMEM((2 * nz, nz), jnp.bfloat16),
            pltpu.VMEM((ny, 2 * ny), jnp.bfloat16),
            pltpu.VMEM((2, 2, comps, ny, nz), jnp.float32),
            pltpu.VMEM((2, 2, comps, ny, nz), jnp.float32),
        ],
        compiler_params=PARAMS,
        cost_estimate=COST,
    )(u, *rest)


def sides_deep(nx, ny, nz, zleft_ref, zright_ref):
    source, target = iota((2 * nz, nz), 0) % nz, iota((2 * nz, nz), 1)
    where = jnp.where(source // 4 == target // 4, source % 4 + 10 * (target % 4), -1)
    weights = jnp.zeros((2 * nz, nz), jnp.float32)
    for value, m, t in ((1.0, 0, 2), (-8.0, 1, 2), (1.0, 1, 3), (-1.0, 2, 0), (8.0, 2, 1), (-1.0, 3, 1)):
        weights = jnp.where(where == m + 10 * t, value, weights)
    weights = weights.astype(jnp.bfloat16)
    return [
        jnp.dot(jnp.concatenate(split(ghost), axis=1), weights, preferred_element_type=jnp.float32)
        for ghost in unfold(zleft_ref[...], zright_ref[...], ny, nz)
    ]


def on_border(packed, x, rows=None):
    ny, nz = packed.shape
    lane = iota((ny, nz), 1)
    return jnp.where((lane >= nz - 2) | (lane < 2), pltpu.roll(packed, lane_shift(x, nz, False), 1), 0.0)


def gather(density, raws, level_ref, sums_ref, sum_ref):
    parts = []
    for k, raw in enumerate(raws):
        level = jnp.clip(raw, 0.0, 1.0)
        level_ref[k] = level
        parts.append(jnp.concatenate(split((density / math.log(2.0)) * level), axis=1))
    ny, nz = level_ref.shape[1:]
    sums = jnp.dot(jnp.concatenate(parts, axis=0), sum_ref[...], preferred_element_type=jnp.float32)
    for k in range(len(raws)):
        sums_ref[k] = sums[k * ny : (k + 1) * ny]


def blend(level_ref, sums_ref, k, store):
    ny, nz = level_ref.shape[1:]
    lane_group = iota((8, ny), 1) // 8
    eye = iota((8, ny), 1) % 8 == iota((8, ny), 0)
    totals = [jnp.zeros((8, ny), jnp.float32)] * 3
    for group in range(ny // 8):
        rows = pl.ds(8 * group, 8)
        level = level_ref[k, rows, :]
        passing = jnp.exp2(sums_ref[k, rows, pl.ds(0, nz)])
        first = (passing - jnp.exp2(sums_ref[k, rows, pl.ds(nz, nz)])) * level
        red = jnp.sum(first, axis=1, keepdims=True)
        square = jnp.sum(first * level, axis=1, keepdims=True)
        whole = sums_ref[k, rows, pl.ds(2 * nz, ny)]
        totals = [jnp.where(lane_group == group, part, total) for part, total in zip((red, square, whole), totals)]
    red, square, whole = [jnp.sum(jnp.where(eye, total, 0.0), axis=0, keepdims=True) for total in totals]
    through = jnp.exp2(whole)
    store(red, square, through)


def put(image_ref, x, slot=lambda view: view):
    per_view = image_ref.shape[2]
    view, row = (x // per_view, x % per_view) if isinstance(x, int) else (lax.div(x, per_view), lax.rem(x, per_view))

    def store(*channels):
        for k, values in enumerate(channels):
            image_ref[slot(view), k, pl.ds(row, 1), :] = values

    return store


def summing(sum_ref):
    nz = sum_ref.shape[0] // 2
    row = iota(sum_ref.shape, 0) % nz
    col = iota(sum_ref.shape, 1)
    sum_ref[...] = jnp.where((row < col) & (col < nz) | (row <= col - nz), -1.0, 0.0).astype(jnp.bfloat16)


def blend_kernel(
    density, raw_ref, pack_ref, kept_ref, scale_ref, zleft_ref, zright_ref, xleft_ref,
    image_ref, base_ref, deep_ref, sum_ref, level0_ref, level1_ref, sums0_ref, sums1_ref,
    fix_ref, first_ref, edge_level_ref, edge_sums_ref,
):
    nx, ny, nz = raw_ref.shape
    summing(sum_ref)
    ghosts = sides_deep(nx, ny, nz, zleft_ref, zright_ref)
    first_ref[...] = ghosts[0]
    fix = ghosts[2] * (0.5 * ghosts[2] + pack_ref[2]) + ghosts[0] * pack_ref[0] + ghosts[1] * pack_ref[1]
    per_block = 4 * SUB
    lane_block = iota((ny, nz), 1) // per_block
    scale = scale_ref[0]
    for block in range(1, nx // SUB):
        scale = jnp.where(lane_block == block, scale_ref[block], scale)
    fix_ref[...] = fix * scale
    image_ref[...] = jnp.zeros(image_ref.shape, jnp.float32)
    batch = level0_ref.shape[0]

    near = [xleft_ref[c, 1] for c in range(3)]
    far = [xleft_ref[c, 0] - 8.0 * cells for c, cells in enumerate(near)]

    def prepared(x, place):
        return raw_ref[x] + on_border(fix_ref[...], x), kept_ref[place, 2] + on_border(first_ref[...], x)

    raws = []
    for x, ghost in enumerate((far, near)):
        base, deep = prepared(x, x)
        raws.append(base + ghost_terms(ghost, kept_ref[x], deep) * scale_ref[0])
    for k in range(2):
        base_ref[k], deep_ref[k] = prepared(nx - 2 + k, 2 + k)

    def load(x, level_ref, sums_ref):
        raws = [raw_ref[x + k] + on_border(fix_ref[...], x + k) for k in range(batch)]
        gather(density, raws, level_ref, sums_ref, sum_ref)

    def mix(x, level_ref, sums_ref):
        for k in range(batch):
            blend(level_ref, sums_ref, k, put(image_ref, x + k))

    load(2, level0_ref, sums0_ref)
    two_rows(density, raws, edge_level_ref, edge_sums_ref, sum_ref, [put(image_ref, x) for x in range(2)])

    def batches(i, carry):
        x = 2 * batch * i + 2
        load(x + batch, level1_ref, sums1_ref)
        mix(x, level0_ref, sums0_ref)
        load(x + 2 * batch, level0_ref, sums0_ref)
        mix(x + batch, level1_ref, sums1_ref)
        return carry

    count = (nx - 4) // batch
    lax.fori_loop(0, (count - 1) // 2, batches, 0)
    if count % 2 == 0:
        load(nx - 2 - batch, level1_ref, sums1_ref)
        mix(nx - 2 - 2 * batch, level0_ref, sums0_ref)
        mix(nx - 2 - batch, level1_ref, sums1_ref)
    else:
        mix(nx - 2 - batch, level0_ref, sums0_ref)


def row_tables(batch, ny, nz, buffers):
    return (
        [pltpu.VMEM((batch, ny, nz), jnp.float32)] * buffers
        + [pltpu.VMEM((batch, ny, 2 * nz + ny), jnp.float32)] * buffers
    )


def blended(density, views, raw, *rest):
    nx, ny, nz = raw.shape
    return pl.pallas_call(
        functools.partial(blend_kernel, density),
        out_shape=(
            jax.ShapeDtypeStruct((views, 3, nx // views, ny), jnp.float32),
            jax.ShapeDtypeStruct((2, ny, nz), jnp.float32),
            jax.ShapeDtypeStruct((2, ny, nz), jnp.float32),
            jax.ShapeDtypeStruct((2 * nz, 2 * nz + ny), jnp.bfloat16),
        ),
        in_specs=[VMEM] * 7,
        out_specs=(VMEM,) * 4,
        scratch_shapes=row_tables(4, ny, nz, 2)
        + [pltpu.VMEM((ny, nz), jnp.float32)] * 2
        + [pltpu.VMEM((2, ny, nz), jnp.float32)] * 2,
        compiler_params=PARAMS,
        cost_estimate=COST,
    )(raw, *rest)


def two_rows(density, raws, level_ref, sums_ref, sum_ref, stores):
    ny, nz = raws[0].shape
    binary = density / math.log(2.0)
    parts = []
    for k, raw in enumerate(raws):
        level = jnp.clip(raw, 0.0, 1.0)
        level_ref[k] = level
        parts.append(jnp.concatenate(split(binary * level), axis=1))
    sums = jnp.dot(
        jnp.concatenate(parts, axis=0), sum_ref[:, pl.ds(nz, nz)], preferred_element_type=jnp.float32
    )
    lane_group = iota((8, ny), 1) // 8
    eye = iota((8, ny), 1) % 8 == iota((8, ny), 0)
    last = iota((8, nz), 1) == nz - 1
    for k, store in enumerate(stores):
        sums_ref[k] = sums[k * ny : (k + 1) * ny]
        totals = [jnp.zeros((8, ny), jnp.float32)] * 3
        for group in range(ny // 8):
            rows = pl.ds(8 * group, 8)
            level, behind = level_ref[k, rows, :], sums_ref[k, rows, :]
            left = jnp.exp2(behind)
            first = (jnp.exp2(behind + binary * level) - left) * level
            found = [jnp.sum(cells, axis=1, keepdims=True) for cells in (first, first * level, jnp.where(last, left, 0.0))]
            totals = [jnp.where(lane_group == group, part, total) for part, total in zip(found, totals)]
        store(*[jnp.sum(jnp.where(eye, total, 0.0), axis=0, keepdims=True) for total in totals])


def ghost_terms(ghost, kept, deep):
    return ghost[0] * (0.5 * ghost[0] + kept[0]) + ghost[1] * kept[1] + ghost[2] * deep


def slots(views):
    me = lax.axis_index("view")
    return lambda view: step_to(me, view, views)


def last_kernel(
    density, image_in_ref, base_ref, deep_ref, kept_ref, scale_ref, sum_ref, xright_ref,
    image_ref, level_ref, sums_ref,
):
    views, _, per_view, _ = image_ref.shape
    nx = views * per_view
    slot = slots(views)
    for view in range(views):
        image_ref[slot(view)] = image_in_ref[view]
    near = [-xright_ref[c, 0] for c in range(3)]
    far = [-8.0 * cells - xright_ref[c, 1] for c, cells in enumerate(near)]
    raws = [
        base_ref[k] + ghost_terms(ghost, kept_ref[2 + k], deep_ref[k]) * scale_ref[scale_ref.shape[0] - 1]
        for k, ghost in enumerate((near, far))
    ]
    two_rows(density, raws, level_ref, sums_ref, sum_ref, [put(image_ref, nx - 2 + k, slot) for k in range(2)])


def edged(density, image, base, *rest):
    return pl.pallas_call(
        functools.partial(last_kernel, density),
        out_shape=jax.ShapeDtypeStruct(image.shape, jnp.float32),
        in_specs=[VMEM] * (2 + len(rest)),
        out_specs=VMEM,
        scratch_shapes=[pltpu.VMEM(base.shape, jnp.float32)] * 2,
        compiler_params=PARAMS,
        cost_estimate=COST,
    )(image, base, *rest)


def turn(block, axis, by):
    count = lax.axis_size(axis)
    return lax.ppermute(block, axis, [(i, (i + by) % count) for i in range(count)])


def both_sides(block, axis):
    before = turn(block, axis, 1)
    return before, before if lax.axis_size(axis) == 2 else turn(block, axis, -1)


def exchange(count):
    if count == 4:
        return [(2, 3, 1, 0), (3, 2, 0, 1), (1, 0, 3, 2)]
    if count & (count - 1) == 0:
        return [tuple(i ^ step for i in range(count)) for step in range(count - 1, 0, -1)]
    return [tuple((i + step) % count for i in range(count)) for step in range(1, count)]


def looked_up(index, table):
    found = jnp.int32(table[0])
    for place, entry in enumerate(table[1:], 1):
        found = jnp.where(index == place, entry, found)
    return found


def step_to(me, other, count):
    steps = [(i,) + targets for i, targets in enumerate(zip(*exchange(count)))]
    return looked_up(me, [targets.index(other) for targets in steps])


def exchanged(blocks, axis):
    routes = exchange(lax.axis_size(axis))
    return [blocks[0]] + [lax.ppermute(blocks[k], axis, list(enumerate(route))) for k, route in enumerate(routes, 1)]


def composite_kernel(*refs):
    *image_refs, out_ref = refs
    count = len(image_refs)
    me = lax.axis_index("view")
    sources = [me] + [looked_up(me, [route.index(i) for i in range(count)]) for route in exchange(count)]
    red = square = 0.0
    through = 1.0
    for source, image_ref in zip(sources, image_refs):
        passing = 1.0
        for other, front_ref in zip(sources, image_refs):
            passing = passing * jnp.where(other < source, front_ref[2], 1.0)
        red = red + passing * image_ref[0]
        square = square + passing * image_ref[1]
        through = through * image_ref[2]
    for k, values in enumerate((red, 4.0 * (red - square), 1.0 - through - red, 1.0 - through)):
        out_ref[0, 0, k] = values


def composited(images):
    return pl.pallas_call(
        composite_kernel,
        out_shape=jax.ShapeDtypeStruct((1, 1, 4) + images[0].shape[1:], jnp.float32),
        in_specs=[VMEM] * len(images),
        out_specs=VMEM,
        compiler_params=PARAMS,
        cost_estimate=COST,
    )(*images)


def local(velocity, occupied, q_floor, q_span):
    comps, nx, ny, nz = velocity.shape
    views = lax.axis_size("view")
    density = 5.0 / (nz * views)
    xleft = turn(tail(velocity), "gx", 1)
    u, parts, xhead, yface, ztail, zhead = faces(velocity)
    xright = turn(xhead, "gx", -1)
    zleft = turn(ztail, "view", 1)
    zright = turn(zhead, "view", -1)
    yleft, yright = both_sides(yface, "gy")
    raw, pack, kept, scale = shaded(u, parts, yleft, yright, occupied[:, :, 0], q_floor, q_span)
    image, base, deep, summer = blended(density, views, raw, pack, kept, scale, zleft, zright, xleft)
    blocks = edged(density, image, base, deep, kept, scale, summer, xright)
    return composited(exchanged(blocks, "view"))


def solution(mesh):
    placed = (P(None, "gx", "gy", "view"), P("gx", "gy", "view"), P(), P())
    return jax.shard_map(
        local,
        mesh=mesh,
        in_specs=placed,
        out_specs=P("gx", "gy", None, "view", None),
        check_vma=False,
    )
```
